128 devices in a mesh: batch: 16 (over x, y), keys: 8 (over z, core).
Axes of the slice: x: 4, y: 4, z: 4, core: 2. Of those that a mesh axis runs over, the one named last changes fastest.
Arguments:
- hidden_in: bfloat16 [16384, 768], P(('batch', 'keys')), may hold values from -6 to 6
- prev_logits: bfloat16 [12, 16384, 1024], P(None, 'batch', 'keys'), may hold values from -6 to 6
- seq_lengths: int32 [16, 16], P('batch'), may hold values from 0 to 512, as said below
- grad_out: bfloat16 [16384, 768], P(('batch', 'keys')), may hold values from -6 to 6
- w_query: bfloat16 [768, 768], replicated, may hold values from -0.21875 to 0.21875
- w_key: bfloat16 [768, 768], replicated, may hold values from -0.21875 to 0.21875
- w_value: bfloat16 [768, 768], replicated, may hold values from -0.21875 to 0.21875
- w_output: bfloat16 [768, 768], replicated, may hold values from -0.625 to 0.625
- w_inner: bfloat16 [768, 3072], replicated, may hold values from -0.21875 to 0.21875
- w_outer: bfloat16 [3072, 768], replicated, may hold values from -0.109375 to 0.109375
- b_query: float32 [768], replicated, may hold values from -3 to 3
- b_value: float32 [768], replicated, may hold values from -3 to 3
- b_output: float32 [768], replicated, may hold values from -2 to 2
- b_inner: float32 [3072], replicated, may hold values from -3 to 3
- b_outer: float32 [768], replicated, may hold values from -2 to 2
- gain_attn: float32 [768], replicated, may hold values from 0.5 to 1.5
- bias_attn: float32 [768], replicated, may hold values from -2 to 2
- gain_ffn: float32 [768], replicated, may hold values from 0.5 to 1.5
- bias_ffn: float32 [768], replicated, may hold values from -2 to 2
Outputs:
- out_hidden: bfloat16 [16384, 768], P(('batch', 'keys'))
- grad_hidden: bfloat16 [16384, 768], P(('batch', 'keys'))
- grad_logits: bfloat16 [12, 16384, 1024], P(None, 'batch', 'keys')
- grad_w_query: float32 [768, 768], P(('batch', 'keys'))
- grad_w_key: float32 [768, 768], P(('batch', 'keys'))
- grad_w_value: float32 [768, 768], P(('batch', 'keys'))
- grad_w_output: float32 [768, 768], P(('batch', 'keys'))
- grad_w_inner: float32 [768, 3072], P(('batch', 'keys'))
- grad_w_outer: float32 [3072, 768], P(('batch', 'keys'))
- grad_b_query: float32 [768], P(('batch', 'keys'))
- grad_b_value: float32 [768], P(('batch', 'keys'))
- grad_b_output: float32 [768], P(('batch', 'keys'))
- grad_b_inner: float32 [3072], P(('batch', 'keys'))
- grad_b_outer: float32 [768], P(('batch', 'keys'))
- grad_gain_attn: float32 [768], P(('batch', 'keys'))
- grad_bias_attn: float32 [768], P(('batch', 'keys'))
- grad_gain_ffn: float32 [768], P(('batch', 'keys'))
- grad_bias_ffn: float32 [768], P(('batch', 'keys'))
The draws below stay inside these ranges and needn't reach their ends.
Inputs may be any that keep to these rules, and one draw needn't show every extreme that they name: `seq_lengths`: each row sums to at most 1024 and has at least one entry equal to 512.
All inputs are finite; a program needn't handle non-finite values.
Results may differ from the reference program's by a relative error of at most 0.04.
Values may be sent and summed in bfloat16 or wider, within the bound.
A program may use at most 192 MiB of HBM per device.

```python
import jax
import jax.numpy as jnp
from jax import lax

D = 768
HEADS = 12
HEAD = 64
FF = 3072
TOK_DEV = 128
SEQS = 16
GROUP = 1024
SEQ_MAX = 512
TOKENS = 16384
N_BATCH = 16
N_KEYS = 8


def draw_seq_lengths(key, part):
    key = jax.random.fold_in(key, 11)
    budget_key, long_key, short_key, choose_key, order_key, full_key = jax.random.split(key, 6)
    budgets = jax.random.randint(budget_key, (N_BATCH,), max(SEQ_MAX, GROUP // 4), GROUP + 1)
    full_group = jax.random.randint(full_key, (), 0, N_BATCH)
    budgets = jnp.where(jnp.arange(N_BATCH) == full_group, GROUP, budgets)
    long_lengths = jax.random.randint(long_key, (N_BATCH, SEQS - 1), 1, SEQ_MAX + 1)
    short_lengths = jax.random.randint(short_key, (N_BATCH, SEQS - 1), 1, max(2, SEQ_MAX // 8) + 1)
    choose_long = jax.random.randint(choose_key, (N_BATCH, SEQS - 1), 0, 4)
    raw_lengths = jnp.where(choose_long == 0, long_lengths, short_lengths)
    ends_at = SEQ_MAX + jnp.cumsum(raw_lengths, axis=1)
    kept_lengths = jnp.where(ends_at <= budgets[:, None], raw_lengths, 0).astype(jnp.int32)
    full_rows = jnp.concatenate([jnp.full((N_BATCH, 1), SEQ_MAX, jnp.int32), kept_lengths], axis=1)
    scores_int = jax.random.randint(order_key, (N_BATCH, SEQS), 0, 1 << 20) * SEQS + jnp.arange(SEQS, dtype=jnp.int32)[None, :]
    shuffle = jnp.argsort(scores_int, axis=1, stable=True)
    return jnp.take_along_axis(full_rows, shuffle, axis=1).astype(jnp.int32)


def block_scale(stream_key, extent, shards, low, high):
    def one(dim, blocks):
        heights = jax.random.uniform(jax.random.fold_in(jax.random.fold_in(stream_key, 6), dim), (blocks,), jnp.float32, low / len(shards), high / len(shards))
        return jnp.repeat(jnp.exp(heights), extent[dim] // blocks).reshape((-1,) + (1,) * (len(extent) - dim - 1))

    factor_of = one(*shards[0])
    for cut in shards[1:]:
        factor_of = factor_of * one(*cut)
    return factor_of


def noise(own_key, shape, deviation, limit, cuts=(), held_as=jnp.bfloat16):
    gain = block_scale(own_key, shape, cuts, -0.22, 0.18) if cuts else 1.0
    array = jax.random.normal(own_key, shape, jnp.float32) * deviation * gain
    return jnp.minimum(jnp.maximum(array, -limit), limit).astype(held_as)


def setup_inputs(seed: int = 0) -> dict:
    key_of = jax.random.split(jax.random.key(seed), 20)
    hidden_in = noise(key_of[0], (TOKENS, D), 1.0, 6.0, ((0, 128),))
    prev_logits = noise(key_of[1], (HEADS, TOKENS, GROUP), 1.0, 6.0, ((1, 16), (2, 8)))
    seq_lengths = draw_seq_lengths(jax.random.fold_in(key_of[19], 71), 0)
    grad_out = noise(key_of[3], (TOKENS, D), 1.0, 6.0, ((0, 128),))
    w_query = noise(key_of[4], (D, D), D ** -0.5, 0.21875)
    w_key = noise(key_of[5], (D, D), D ** -0.5, 0.21875)
    w_value = noise(key_of[6], (D, D), D ** -0.5, 0.21875)
    w_output = noise(key_of[7], (D, D), (D // 8) ** -0.5, 0.625)
    w_inner = noise(key_of[8], (D, FF), D ** -0.5, 0.21875)
    w_outer = noise(key_of[9], (FF, D), FF ** -0.5, 0.109375)
    b_query = noise(key_of[10], (D,), 0.5, 3.0, (), jnp.float32)
    b_value = noise(key_of[11], (D,), 0.5, 3.0, (), jnp.float32)
    b_output = noise(key_of[12], (D,), 0.3, 2.0, (), jnp.float32)
    b_inner = noise(key_of[13], (FF,), 0.5, 3.0, (), jnp.float32)
    b_outer = noise(key_of[14], (D,), 0.3, 2.0, (), jnp.float32)
    gain_attn = jnp.clip(1.0 + 0.1 * jax.random.normal(key_of[15], (D,), jnp.float32), 0.5, 1.5)
    bias_attn = noise(key_of[16], (D,), 0.3, 2.0, (), jnp.float32)
    gain_ffn = jnp.clip(1.0 + 0.1 * jax.random.normal(key_of[17], (D,), jnp.float32), 0.5, 1.5)
    bias_ffn = noise(key_of[18], (D,), 0.3, 2.0, (), jnp.float32)
    return dict(hidden_in=hidden_in, prev_logits=prev_logits, seq_lengths=seq_lengths, grad_out=grad_out, w_query=w_query, w_key=w_key, w_value=w_value, w_output=w_output, w_inner=w_inner, w_outer=w_outer, b_query=b_query, b_value=b_value, b_output=b_output, b_inner=b_inner, b_outer=b_outer, gain_attn=gain_attn, bias_attn=bias_attn, gain_ffn=gain_ffn, bias_ffn=bias_ffn)


EPSILON = 1e-05
NEGATIVE = -1e+30
HIGHEST = lax.Precision.HIGHEST

@jax.custom_vjp
def low(v):
    return lax.optimization_barrier(v.astype(jnp.bfloat16)).astype(jnp.float32)

@jax.custom_vjp
def low_back(v):
    return v

def low_keep(v):
    return (low(v), None)

def low_pass(kept, grad):
    return (grad,)

def back_keep(v):
    return (v, None)

def back_low(kept, grad):
    return (low(grad),)
low.defvjp(low_keep, low_pass)
low_back.defvjp(back_keep, back_low)

def segments_for(lengths_row, tok_rows, key_count):
    group_rows = tok_rows * key_count
    indices = jnp.arange(group_rows, dtype=jnp.int32)
    places = indices % tok_rows * key_count + indices // tok_rows
    bounds = jnp.cumsum(lengths_row).astype(jnp.int32)
    counted = lax.optimization_barrier(jnp.sum((places[:, None] >= bounds[None, :]).astype(jnp.int32), axis=1))
    return jnp.where(places < bounds[-1], counted, -1 - places).astype(jnp.int32)

def normalize(values, gain_vec, offset):
    average = lax.optimization_barrier(jnp.mean(values, axis=-1, keepdims=True))
    centered = values - average
    variance = lax.optimization_barrier(jnp.mean(centered * centered, axis=-1, keepdims=True))
    return centered * lax.rsqrt(variance + EPSILON) * gain_vec + offset

def group_layer(params, hidden_rows, logit_rows, segment):
    w_query, w_key, w_value, w_output, w_inner, w_outer, b_query, b_value, b_output, b_inner, b_outer, gain_attn, bias_attn, gain_ffn, bias_ffn = params
    group_rows = hidden_rows.shape[0]
    block_rows = min(512, group_rows)
    blocks = group_rows // block_rows
    queries = low(low_back(jnp.dot(hidden_rows, w_query, precision=HIGHEST) + b_query))
    key_rows = low(low_back(jnp.dot(hidden_rows, w_key, precision=HIGHEST)))
    value_rows = low(low_back(jnp.dot(hidden_rows, w_value, precision=HIGHEST) + b_value))
    key_heads = key_rows.reshape(group_rows, HEADS, HEAD)
    value_heads = value_rows.reshape(group_rows, HEADS, HEAD)

    def attend(pieces):
        query_block, logit_block, seg_block = pieces
        raw_scores = jnp.einsum('qhd,khd->hqk', query_block, key_heads, precision=HIGHEST)
        scores = low_back(raw_scores * HEAD ** (-0.5) + logit_block)
        allowed = seg_block[:, None] == segment[None, :]
        masked = jnp.where(allowed[None], scores, NEGATIVE)
        larger = lax.optimization_barrier(jnp.max(masked, axis=2, keepdims=True))
        weights = jnp.where(allowed[None], jnp.exp(masked - larger), 0.0)
        probs = low(weights / lax.optimization_barrier(jnp.sum(weights, axis=2, keepdims=True)))
        return jnp.einsum('hqk,khd->qhd', probs, value_heads, precision=HIGHEST)
    query_blocks = queries.reshape(blocks, block_rows, HEADS, HEAD)
    logit_blocks = jnp.moveaxis(logit_rows.reshape(HEADS, blocks, block_rows, group_rows), 1, 0)
    seg_blocks = segment.reshape(blocks, block_rows)
    mixed = lax.map(jax.checkpoint(attend), (query_blocks, logit_blocks, seg_blocks))
    attn = low(low_back(mixed.reshape(group_rows, D)))
    branch = low_back(jnp.dot(attn, w_output, precision=HIGHEST) + b_output)
    first = normalize(hidden_rows + branch, gain_attn, bias_attn)
    inner = low_back(jnp.dot(low(first), w_inner, precision=HIGHEST) + b_inner)
    active = low(jax.nn.gelu(inner, approximate=False))
    outer = low_back(jnp.dot(active, w_outer, precision=HIGHEST) + b_outer)
    return normalize(first + outer, gain_ffn, bias_ffn)

def reference(hidden_in, prev_logits, seq_lengths, grad_out, w_query, w_key, w_value, w_output, w_inner, w_outer, b_query, b_value, b_output, b_inner, b_outer, gain_attn, bias_attn, gain_ffn, bias_ffn):
    params = tuple((entry.astype(jnp.float32) for entry in (w_query, w_key, w_value, w_output, w_inner, w_outer, b_query, b_value, b_output, b_inner, b_outer, gain_attn, bias_attn, gain_ffn, bias_ffn)))
    group_rows = TOK_DEV * N_KEYS

    def step(carry, index):
        sums, out_rows, grad_rows, grad_logit_rows = carry
        start = (index * group_rows).astype(jnp.int32)
        hidden_rows = lax.dynamic_slice_in_dim(hidden_in, start, group_rows, 0).astype(jnp.float32)
        logit_rows = lax.dynamic_slice_in_dim(prev_logits, start, group_rows, 1).astype(jnp.float32)
        lengths_row = lax.dynamic_index_in_dim(seq_lengths, index, 0, keepdims=False)
        segment = segments_for(lengths_row, TOK_DEV, N_KEYS)
        cotangent = lax.dynamic_slice_in_dim(grad_out, start, group_rows, 0).astype(jnp.float32)

        def layer_of(param_set, hidden_set, logit_set):
            return group_layer(param_set, hidden_set, logit_set, segment)
        result, pullback = jax.vjp(layer_of, params, hidden_rows, logit_rows)
        grad_params, grad_hidden_rows, grad_logit_group = pullback(cotangent)
        sums = jax.tree.map(lambda total, piece: total + piece, sums, grad_params)
        out_rows = lax.dynamic_update_slice_in_dim(out_rows, result.astype(jnp.bfloat16), start, 0)
        grad_rows = lax.dynamic_update_slice_in_dim(grad_rows, grad_hidden_rows.astype(jnp.bfloat16), start, 0)
        grad_logit_rows = lax.dynamic_update_slice_in_dim(grad_logit_rows, grad_logit_group.astype(jnp.bfloat16), start, 1)
        return ((sums, out_rows, grad_rows, grad_logit_rows), None)
    zeros_params = tuple((jnp.zeros(entry.shape, jnp.float32) for entry in params))
    start_carry = (zeros_params, jnp.zeros(hidden_in.shape, jnp.bfloat16), jnp.zeros(hidden_in.shape, jnp.bfloat16), jnp.zeros(prev_logits.shape, jnp.bfloat16))
    final, unused = lax.scan(step, start_carry, jnp.arange(N_BATCH, dtype=jnp.int32))
    sums, out_rows, grad_rows, grad_logit_rows = final
    return (out_rows, grad_rows, grad_logit_rows, sums[0], sums[1], sums[2], sums[3], sums[4], sums[5], sums[6], sums[7], sums[8], sums[9], sums[10], sums[11], sums[12], sums[13], sums[14])
```

```python
import jax
import jax.numpy as jnp
from jax import lax
from jax.experimental import pallas as pl
from jax.experimental.pallas import tpu as pltpu
from jax.sharding import PartitionSpec as P

EPSILON = 1e-05
NEGATIVE = -1e30
MESH = pl.DeviceIdType.MESH
BF = jnp.bfloat16
F32 = jnp.float32

TOK = 128
D = 768
HALF = 384
HEADS = 6
FF = 3072
SEQS = 16
BLOCKS = 8


def dot(a, b):
    return lax.dot_general(a, b, (((1,), (0,)), ((), ())), preferred_element_type=F32)


def dot_nt(a, b):
    return lax.dot_general(a, b, (((1,), (1,)), ((), ())), preferred_element_type=F32)


def dot_tn(a, b):
    return lax.dot_general(a, b, (((0,), (0,)), ((), ())), preferred_element_type=F32)


def iota(shape, dim):
    return lax.broadcasted_iota(jnp.int32, shape, dim)


def split_hi_lo(v):
    hi = v.astype(BF)
    lo = (v - hi.astype(F32)).astype(BF)
    return jnp.concatenate([hi.astype(F32), lo.astype(F32)], axis=0).astype(BF)


def head_rows():
    return jnp.where(iota((16, HALF), 1) // 64 == iota((16, HALF), 0) % 8, 1.0, 0.0).astype(BF)


def unit_rows():
    return jnp.where(iota((16, 128), 1) == iota((16, 128), 0), 1.0, 0.0).astype(BF)


def row_sums(v):
    return jnp.sum(v, axis=0, keepdims=True)


def norm(values):
    average = jnp.mean(values, axis=-1, keepdims=True)
    centered = values - average
    variance = jnp.mean(centered * centered, axis=-1, keepdims=True)
    inverse = lax.rsqrt(variance + EPSILON)
    return centered * inverse, inverse


def norm_back(upstream, normed, inverse, gain):
    scaled = upstream * gain
    return inverse * (
        scaled
        - jnp.mean(scaled, axis=-1, keepdims=True)
        - normed * jnp.mean(scaled * normed, axis=-1, keepdims=True)
    )


ARGS = ("hidden", "prev", "lengths", "gout", "w_q", "w_k", "w_v", "w_o", "w_i", "w_u")
ARGS += ("b_q", "b_v", "b_o", "b_i", "b_u", "g_a", "b_a", "g_f", "b_f")
OUTS = ("out_hidden", "grad_hidden", "gl", "zr")

SCRATCH = dict(
    wq=((2, D, HALF), BF),
    wk=((2, D, HALF), BF),
    wv=((2, D, HALF), BF),
    wo=((D, D), BF),
    wi=((4, D, D), BF),
    wu=((4, D, D), BF),
    vq=((D,), F32),
    vv=((D,), F32),
    vo=((D,), F32),
    vi=((FF,), F32),
    vu=((D,), F32),
    ga=((D,), F32),
    ba=((D,), F32),
    gf=((D,), F32),
    bf=((D,), F32),
    go=((TOK, D), BF),
    hid=((BLOCKS, TOK, D), BF),
    pv=((2, HEADS, BLOCKS * TOK, 128), BF),
    qs=((BLOCKS, TOK, HALF), BF),
    km=((HEADS, 256, 128), BF),
    ve=((HEADS, 256, 256), BF),
    madd=((TOK, 256), F32),
    obuf=((BLOCKS, TOK, HALF), BF),
    orecv=((BLOCKS, TOK, HALF), BF),
    st=((BLOCKS, 16, 128), F32),
    strecv=((BLOCKS, 16, 128), F32),
    at=((2, TOK, HALF), F32),
    atx=((2, TOK, D), BF),
    fx=((2, TOK, D), BF),
    n1=((TOK, D), F32),
    gs=((TOK, D), F32),
    gp=((4, TOK, D), F32),
    ax=((2, TOK, FF), BF),
    igs=((2, TOK, FF // 2), BF),
    igr=((TOK, FF // 2), BF),
    ogs=((2, TOK, HALF), BF),
    ogr=((TOK, HALF), BF),
    brs=((2, TOK, HALF), BF),
    brr=((TOK, HALF), BF),
    brow=((2, 16, HALF), F32),
    ags=((2, TOK, HALF), BF),
    dorecv=((BLOCKS, TOK, HALF), BF),
    s2=((2, 16, 128), F32),
    s2recv=((BLOCKS, 16, 128), F32),
    dkt=((HALF, 256), F32),
    dvt=((HALF, 256), F32),
    dq=((BLOCKS, TOK, HALF), BF),
    dqrecv=((BLOCKS, TOK, HALF), BF),
    kgs=((2, TOK, HALF), BF),
    kgr=((TOK, HALF), BF),
    vgs=((2, TOK, HALF), BF),
    vgr=((TOK, HALF), BF),
    a1s=((4, 192, 1920), BF),
    a1r=((3, 192, 1920), BF),
    a1t=((4, 48, 1920), BF),
    a1u=((3, 48, 1920), BF),
    a2s=((4, 192, 512), BF),
    a2r=((3, 192, 512), BF),
    a2t=((4, 48, 512), BF),
    a2u=((3, 48, 512), BF),
    b1s=((4, 4, 192, HALF), BF),
    b1r=((3, 4, 192, HALF), BF),
    b1t=((4, 192, HALF), BF),
    b1u=((3, 192, HALF), BF),
    b2s=((4, 4, 48, D), BF),
    b2r=((3, 4, 48, D), BF),
    b2t=((4, 48, D), BF),
    b2u=((3, 48, D), BF),
    fa1=((48, 1920), F32),
    fa2=((48, 512), F32),
    fb1=((192, HALF), F32),
    fb2=((48, D), F32),
    zf=((BLOCKS, 80, HALF), F32),
    zs=((BLOCKS, 80, HALF), BF),
)
SEMS = dict(
    ld=24,
    hs=8,
    hr=8,
    pl_=4,
    ps=4,
    pr=4,
    os=8,
    or_=8,
    ss=8,
    sr=8,
    xs=6,
    xr=6,
    ds=8,
    dr=8,
    es=8,
    er=8,
    qs_=8,
    qr=8,
    gl_=8,
    gs_=8,
    gr=8,
    ks=2,
    kr=2,
    rs=24,
    rr=24,
    zs_=8,
    zr_=8,
    outs=3,
)


def body(*refs):
    na, no, nsc = len(ARGS), len(OUTS), len(SCRATCH)
    A = dict(zip(ARGS, refs[:na]))
    O = dict(zip(OUTS, refs[na : na + no]))
    S = dict(zip(SCRATCH, refs[na + no : na + no + nsc]))
    M = dict(zip(SEMS, refs[na + no + nsc :]))

    bi = lax.axis_index("batch")
    ki = lax.axis_index("keys")
    x, y = bi // 4, lax.rem(bi, 4)
    z, c = ki // 2, lax.rem(ki, 2)
    oc = 1 - c

    def dev(dx=0, dy=0, dz=0, dc=0):
        nb = lax.rem(x + dx, 4) * 4 + lax.rem(y + dy, 4)
        return (nb, lax.rem(z + dz, 4) * 2 + lax.rem(c + dc, 2))

    def key_of(dz, dc):
        return lax.rem(z + dz, 4) * 2 + lax.rem(c + dc, 2)

    def far(d):
        return d + (d // 2) * (1 - 2 * lax.rem(d, 2))

    def remote(src, dst, ssem, rsem, to):
        return pltpu.make_async_remote_copy(
            src_ref=src, dst_ref=dst, send_sem=ssem, recv_sem=rsem, device_id=to, device_id_type=MESH
        )

    def local(src, dst, sem):
        return pltpu.make_async_copy(src, dst, sem)

    loads = [
        local(A["hidden"], S["hid"].at[ki], M["ld"].at[0]),
        local(A["w_k"].at[:, pl.ds(pl.multiple_of(c * HALF, 128), HALF)], S["wk"].at[c], M["ld"].at[1]),
        local(A["w_v"].at[:, pl.ds(pl.multiple_of(c * HALF, 128), HALF)], S["wv"].at[c], M["ld"].at[2]),
        local(A["w_q"].at[:, pl.ds(pl.multiple_of(c * HALF, 128), HALF)], S["wq"].at[c], M["ld"].at[3]),
        local(A["b_q"], S["vq"], M["ld"].at[4]),
        local(A["b_v"], S["vv"], M["ld"].at[5]),
    ]
    early = len(loads)
    later = [
        local(A["w_o"], S["wo"], M["ld"].at[6]),
        local(A["b_o"], S["vo"], M["ld"].at[7]),
        local(A["b_i"], S["vi"], M["ld"].at[8]),
        local(A["b_u"], S["vu"], M["ld"].at[9]),
        local(A["g_a"], S["ga"], M["ld"].at[10]),
        local(A["b_a"], S["ba"], M["ld"].at[11]),
        local(A["g_f"], S["gf"], M["ld"].at[12]),
        local(A["b_f"], S["bf"], M["ld"].at[13]),
        local(A["gout"], S["go"], M["ld"].at[14]),
    ]
    for j in range(4):
        later.append(local(A["w_i"].at[:, pl.ds(D * j, D)], S["wi"].at[j], M["ld"].at[15 + j]))
    for j in range(2):
        later.append(local(A["w_u"].at[pl.ds(2 * D * j, D)], S["wu"].at[2 * j], M["ld"].at[19 + 2 * j]))
        later.append(
            local(A["w_u"].at[pl.ds(2 * D * j + D, D)], S["wu"].at[2 * j + 1], M["ld"].at[20 + 2 * j])
        )
    last = [
        local(
            A[n].at[:, pl.ds(pl.multiple_of(oc * HALF, 128), HALF)], S[s].at[oc], M["outs"].at[i]
        )
        for i, (n, s) in enumerate((("w_q", "wq"), ("w_k", "wk"), ("w_v", "wv")))
    ]
    for cp in loads:
        cp.start()

    def prev_rows(dz):
        return pl.ds(pl.multiple_of(lax.rem(z + dz, 4) * 256, 256), 256)

    def prev_local(dz):
        rows = prev_rows(dz)
        return local(
            A["prev"].at[pl.ds(c * HEADS, HEADS), rows, :], S["pv"].at[c, :, rows, :], M["pl_"].at[dz]
        )

    def prev_remote(dz):
        rows = prev_rows(dz)
        return remote(
            A["prev"].at[pl.ds(oc * HEADS, HEADS), rows, :],
            S["pv"].at[c, :, rows, :],
            M["ps"].at[dz],
            M["pr"].at[dz],
            dev(dc=1),
        )

    for dz in (0, 1, 3, 2):
        prev_local(dz).start()

    peers = [(0, 0, dz, dc) for dz in range(4) for dc in range(2) if dz or dc]
    peers += [(d, 0, 0, 0) for d in (1, 2, 3)] + [(0, d, 0, 0) for d in (1, 2, 3)]
    barrier = pltpu.get_barrier_semaphore()
    for off in peers:
        pl.semaphore_signal(barrier, inc=1, device_id=dev(*off), device_id_type=MESH)
    pl.semaphore_wait(barrier, len(peers))

    def hid_send(i, to):
        return remote(A["hidden"], S["hid"].at[ki], M["hs"].at[i], M["hr"].at[ki], to)

    def hid_arrival(k):
        return remote(A["hidden"], S["hid"].at[k], M["hs"].at[0], M["hr"].at[k], dev(dc=1))

    def hid_forward(d, k):
        return remote(S["hid"].at[k], S["hid"].at[k], M["hs"].at[3 + d], M["hr"].at[k], dev(dc=1))

    hid_sends = [hid_send(0, dev(dc=1)), hid_send(1, dev(dz=1)), hid_send(2, dev(dz=3)), hid_send(3, dev(dz=2))]
    for cp in hid_sends:
        cp.start()
    prev_remote(0).start()
    prev_remote(1).start()
    prev_remote(3).start()
    prev_remote(2).start()

    bounds = []
    running = jnp.int32(0)
    for j in range(SEQS):
        running = running + A["lengths"][0, j]
        bounds.append(running)

    def segment_of(places):
        counted = jnp.zeros(places.shape, jnp.int32)
        for bound in bounds:
            counted = counted + jnp.where(places >= bound, 1, 0)
        return jnp.where(places < bounds[-1], counted, -1 - places)

    lane8 = iota((8, 128), 1)
    key_segment = [segment_of(lane8 * BLOCKS + z * 2 + half)[0:1, :] for half in range(2)]
    lane = iota((TOK, 128), 1)

    for cp in loads[:1] + loads[1:3] + loads[5:6]:
        cp.wait()
    hid_arrival(key_of(0, 1)).wait_recv()
    pair = pl.ds(z * 2, 2)
    hid_pair = S["hid"][pair].reshape(256, D)
    key_rows = dot(hid_pair, S["wk"][c]).astype(BF).astype(F32)
    bias_v = S["vv"][...].reshape(1, D)
    bias_q = S["vq"]
    bv = jnp.where(c == 0, bias_v[:, :HALF], bias_v[:, HALF:])
    value_rows = (dot(hid_pair, S["wv"][c]) + bv).astype(BF).astype(F32)
    lane2 = iota((256, 128), 1)
    for h in range(HEADS):
        g, e = h // 2, h % 2
        mine = lane2 // 64 == e
        S["km"][h] = jnp.where(mine, key_rows[:, 128 * g : 128 * g + 128], 0.0).astype(BF)
        S["ve"][h, :, :128] = jnp.where(mine, value_rows[:, 128 * g : 128 * g + 128], 0.0).astype(BF)
        S["ve"][h, :, 128:] = jnp.where((lane2 == h) | (lane2 == 8 + h), 1.0, 0.0).astype(BF)
    loads[3].wait()
    loads[4].wait()
    bias_q = S["vq"][...].reshape(1, D)
    S["brow"][...] = jnp.zeros((2, 16, HALF), F32)
    for cp in later + last:
        cp.start()

    def out_send(i, k, to):
        return remote(S["obuf"].at[k], S["orecv"].at[ki], M["os"].at[i], M["or_"].at[ki], to)

    def st_send(i, k, to):
        return remote(S["st"].at[k], S["strecv"].at[ki], M["ss"].at[i], M["sr"].at[ki], to)

    def forward(i, carry):
        d = i // 2
        dc = lax.rem(i, 2)
        dz = far(d)
        k = key_of(dz, dc)

        @pl.when(jnp.logical_and(dc == 0, d > 0))
        def _():
            hid_arrival(k).wait_recv()
            hid_forward(d, k).start()

        @pl.when(jnp.logical_and(dc == 1, d > 0))
        def _():
            hid_arrival(k).wait_recv()

        @pl.when(dc == 0)
        def _():
            prev_local(dz).wait()
            prev_remote(dz).wait_recv()

        bq = jnp.where(c == 0, bias_q[:, :HALF], bias_q[:, HALF:])
        queries = (dot(S["hid"][k], S["wq"][c]) + bq).astype(BF).astype(F32) * 0.125
        S["qs"][k] = queries.astype(BF)
        row_segment = segment_of(iota((TOK, 128), 0) * BLOCKS + k)
        for half in range(2):
            S["madd"][:, 128 * half : 128 * half + 128] = jnp.where(
                row_segment == key_segment[half], 0.0, NEGATIVE
            )
        rows = pl.ds(pl.multiple_of(k * TOK, TOK), TOK)
        totals = jnp.zeros((TOK, 128), F32)
        tops = jnp.zeros((TOK, 128), F32)
        for g in range(3):
            two = S["qs"][k, :, 128 * g : 128 * g + 128]
            mixed = jnp.zeros((TOK, 128), F32)
            for h in (2 * g, 2 * g + 1):
                before = jnp.concatenate([S["pv"][0, h, rows, :], S["pv"][1, h, rows, :]], axis=1)
                s = dot_nt(two, S["km"][h]) + before.astype(F32) + S["madd"][...]
                top = jnp.max(s, axis=1, keepdims=True)
                p = jnp.exp(s - top).astype(BF)
                S["pv"][0, h, rows, :] = p[:, :128]
                S["pv"][1, h, rows, :] = p[:, 128:]
                o = dot(p, S["ve"][h])
                mixed = mixed + o[:, :128]
                totals = totals + o[:, 128:]
                tops = jnp.where(lane == 8 + h, top, tops)
            S["obuf"][k, :, 128 * g : 128 * g + 128] = mixed.astype(BF)
        stats = jnp.where(lane < 8, totals, tops)
        S["st"][k] = stats.T[:16, :]

        @pl.when(i > 0)
        def _():
            to = dev(dz=dz, dc=dc)
            out_send(i, k, to).start()
            st_send(i, k, to).start()

        return carry

    lax.fori_loop(0, BLOCKS, forward, 0)

    S["orecv"][ki] = S["obuf"][ki]
    S["strecv"][ki] = S["st"][ki]

    def await_parts(i, carry):
        k = key_of(far(i // 2), lax.rem(i, 2))
        remote(S["obuf"].at[k], S["orecv"].at[k], M["os"].at[i], M["or_"].at[k], dev(dc=1)).wait_recv()
        remote(S["st"].at[k], S["strecv"].at[k], M["ss"].at[i], M["sr"].at[k], dev(dc=1)).wait_recv()
        return carry

    lax.fori_loop(1, BLOCKS, await_parts, 0)
    row8 = iota((8, 128), 0)
    spread = head_rows()
    lse = []
    for half in range(2):
        tops = [S["strecv"][2 * zz + half, 8:16, :] for zz in range(4)]
        sums = [S["strecv"][2 * zz + half, 0:8, :] for zz in range(4)]
        top = jnp.maximum(jnp.maximum(tops[0], tops[1]), jnp.maximum(tops[2], tops[3]))
        shares = [jnp.exp(t - top) for t in tops]
        total = shares[0] * sums[0] + shares[1] * sums[1] + shares[2] * sums[2] + shares[3] * sums[3]
        total = jnp.where(row8 < HEADS, total, 1.0)
        lse.append(jnp.where(row8 < HEADS, top + jnp.log(total), 0.0))
        acc = jnp.zeros((TOK, HALF), F32)
        for zz in range(4):
            factor = dot_tn(split_hi_lo(jnp.where(row8 < HEADS, shares[zz] / total, 0.0)), spread)
            acc = acc + S["orecv"][2 * zz + half].astype(F32) * factor
        S["at"][half] = acc
        S["atx"][0, :, HALF * half : HALF * half + HALF] = acc.astype(BF)

    def vec(name):
        return S[name][...].reshape(1, -1)

    for cp in later:
        cp.wait()
    attn_low = S["atx"][0]
    first_sum = S["hid"][ki].astype(F32) + dot(attn_low, S["wo"][...]) + vec("vo")
    normed, inverse_a = norm(first_sum)
    S["n1"][...] = normed
    S["fx"][0] = (normed * vec("ga") + vec("ba")).astype(BF)
    second = normed * vec("ga") + vec("ba") + vec("vu")
    bias_i = vec("vi")
    for j in range(4):
        inner = dot(S["fx"][0], S["wi"][j]) + bias_i[:, D * j : D * j + D]
        cdf = 0.5 + 0.5 * lax.erf(inner * 0.7071067811865476)
        density = jnp.exp(inner * inner * -0.5) * 0.3989422804014327
        S["gp"][j] = cdf + inner * density
        S["ax"][0, :, D * j : D * j + D] = (inner * cdf).astype(BF)
        second = second + dot(S["ax"][0, :, D * j : D * j + D], S["wu"][j])
    normed_f, inverse_f = norm(second)
    O["out_hidden"][...] = (normed_f * vec("gf") + vec("bf")).astype(BF)
    upstream = S["go"][...].astype(F32)

    def put_row(r, values):
        sums = row_sums(values)
        S["brow"][0, r : r + 1, :] = sums[:, :HALF]
        S["brow"][1, r : r + 1, :] = sums[:, HALF:]

    put_row(6, upstream * normed_f)
    put_row(7, upstream)
    grad_second = norm_back(upstream, normed_f, inverse_f, vec("gf"))
    og = grad_second.astype(BF)
    put_row(3, og.astype(F32))
    S["ogs"][0] = og[:, :HALF]
    S["ogs"][1] = og[:, HALF:]
    S["gs"][...] = grad_second
    bsum = []
    for j in range(4):
        ig = (dot_nt(og, S["wu"][j]) * S["gp"][j]).astype(BF)
        S["igs"][j // 2, :, D * (j % 2) : D * (j % 2) + D] = ig
        bsum.append(row_sums(ig.astype(F32)))
        S["gs"][...] = S["gs"][...] + dot_nt(ig, S["wi"][j])
    grad_first = S["gs"][...]
    normed = S["n1"][...]
    put_row(4, grad_first * normed)
    put_row(5, grad_first)
    grad_first_sum = norm_back(grad_first, normed, inverse_a, vec("ga"))
    S["gs"][...] = grad_first_sum
    br = grad_first_sum.astype(BF)
    put_row(2, br.astype(F32))
    S["brs"][0] = br[:, :HALF]
    S["brs"][1] = br[:, HALF:]
    ag = dot_nt(br, S["wo"][...]).astype(BF)
    for half in range(2):
        S["ags"][half] = ag[:, HALF * half : HALF * half + HALF]
        product = S["at"][half] * ag[:, HALF * half : HALF * half + HALF].astype(F32)
        dots = jnp.zeros((16, TOK), F32)
        hi = product.astype(BF)
        lo = (product - hi.astype(F32)).astype(BF)
        dots = dot_nt(spread, hi) + dot_nt(spread, lo)
        S["s2"][half, 0:8, :] = dots[0:8, :]
        S["s2"][half, 8:16, :] = lse[half]

    def ag_send(i, k, to):
        half = lax.rem(k, 2)
        return remote(S["ags"].at[half], S["dorecv"].at[ki], M["ds"].at[i], M["dr"].at[ki], to)

    def s2_send(i, k, to):
        half = lax.rem(k, 2)
        return remote(S["s2"].at[half], S["s2recv"].at[ki], M["es"].at[i], M["er"].at[ki], to)

    def send_grads(i, carry):
        dz, dc = far(i // 2), lax.rem(i, 2)
        k = key_of(dz, dc)
        to = dev(dz=dz, dc=dc)
        ag_send(i, k, to).start()
        s2_send(i, k, to).start()
        return carry

    lax.fori_loop(1, BLOCKS, send_grads, 0)
    S["dorecv"][ki] = S["ags"][c]
    S["s2recv"][ki] = S["s2"][c]

    other = dev(dc=1)
    swaps = [
        remote(S["fx"].at[0], S["fx"].at[1], M["xs"].at[0], M["xr"].at[0], other),
        remote(S["igs"].at[oc], S["igr"], M["xs"].at[1], M["xr"].at[1], other),
        remote(S["ax"].at[0], S["ax"].at[1], M["xs"].at[2], M["xr"].at[2], other),
        remote(S["ogs"].at[oc], S["ogr"], M["xs"].at[3], M["xr"].at[3], other),
        remote(S["atx"].at[0], S["atx"].at[1], M["xs"].at[4], M["xr"].at[4], other),
        remote(S["brs"].at[oc], S["brr"], M["xs"].at[5], M["xr"].at[5], other),
    ]
    for cp in swaps:
        cp.start()

    lane512 = iota((8, 512), 1)
    sub512 = iota((8, 512), 0)
    pick = jnp.where(
        iota((512, 128), 1) == (iota((512, 128), 0) // 128) * 32 + lax.rem(iota((512, 128), 0), 128) // 4,
        1.0,
        0.0,
    ).astype(BF)
    flat = jnp.concatenate(bsum, axis=1)
    for g in range(6):
        spread_out = jnp.where(lax.rem(lane512, 4) == sub512, flat[:, 512 * g : 512 * g + 512], 0.0)
        S["brow"][g // 3, 8:16, 128 * (g % 3) : 128 * (g % 3) + 128] = dot(spread_out.astype(BF), pick)

    for cp in swaps:
        cp.wait()

    def weight_grad(left, right):
        return dot_tn(left, right).astype(BF)

    first_two = S["fx"][...].reshape(256, D)
    for j in range(4):
        col = slice(HALF * j, HALF * j + HALF)
        right = jnp.concatenate([S["igs"][c, :, col], S["igr"][:, col]], axis=0)
        S["a1s"][:, :, col] = weight_grad(first_two, right).reshape(4, 192, HALF)
    right = jnp.concatenate([S["brs"][c], S["brr"][...]], axis=0)
    S["a1s"][:, :, 1536:1920] = weight_grad(S["atx"][...].reshape(256, D), right).reshape(4, 192, HALF)

    def along(axis, d):
        return dev(dx=d) if axis == 0 else dev(dy=d)

    def at_place(axis, d):
        return lax.rem((x if axis == 0 else y) + d, 4)

    def scatter(n, axis, src, dst, inner):
        out = []
        for d in (1, 2, 3):
            there = at_place(axis, d)
            piece = src.at[:, there] if inner else src.at[there]
            sem = 3 * n + d - 1
            out.append(remote(piece, dst.at[d - 1], M["rs"].at[sem], M["rr"].at[sem], along(axis, d)))
        return out

    all_sends = []
    ra1 = scatter(0, 0, S["a1s"], S["a1r"], False)
    for cp in ra1:
        cp.start()
    right = jnp.concatenate([S["ogs"][c], S["ogr"][...]], axis=0)
    for j in range(4):
        left = S["ax"][:, :, D * j : D * j + D].reshape(256, D)
        S["b1s"][j] = weight_grad(left, right).reshape(4, 192, HALF)
    rb1 = scatter(1, 1, S["b1s"], S["b1r"], True)
    for cp in rb1:
        cp.start()

    S["dkt"][...] = jnp.zeros((HALF, 256), F32)
    S["dvt"][...] = jnp.zeros((HALF, 256), F32)
    units = unit_rows()

    def dq_send(i, k, to):
        return remote(S["dq"].at[k], S["dqrecv"].at[ki], M["qs_"].at[i], M["qr"].at[ki], to)

    def gl_rows(k):
        return pl.ds(pl.multiple_of(k * TOK, TOK), TOK)

    def gl_local(i, k):
        rows = gl_rows(k)
        return local(
            S["pv"].at[c, :, rows, :], O["gl"].at[pl.ds(c * HEADS, HEADS), rows, :], M["gl_"].at[i]
        )

    def gl_remote(i, k):
        rows = gl_rows(k)
        return remote(
            S["pv"].at[oc, :, rows, :],
            O["gl"].at[pl.ds(c * HEADS, HEADS), rows, :],
            M["gs_"].at[i],
            M["gr"].at[k],
            dev(dc=1),
        )

    def backward(i, carry):
        dz, dc = far(i // 2), lax.rem(i, 2)
        k = key_of(dz, dc)

        @pl.when(i > 0)
        def _():
            remote(S["ags"].at[0], S["dorecv"].at[k], M["ds"].at[i], M["dr"].at[k], dev(dc=1)).wait_recv()
            remote(S["s2"].at[0], S["s2recv"].at[k], M["es"].at[i], M["er"].at[k], dev(dc=1)).wait_recv()

        rows = pl.ds(pl.multiple_of(k * TOK, TOK), TOK)
        share = jnp.exp(S["st"][k, 8:16, :] - S["s2recv"][k, 8:16, :])
        share = jnp.where(row8 < HEADS, share, 0.0)
        minus = dot_tn(split_hi_lo(S["s2recv"][k, 0:8, :] * share * -1.0), units).astype(BF)
        factor = dot_tn(split_hi_lo(share), spread)
        scaled = S["dorecv"][k].astype(F32) * factor
        scaled_t = scaled.T.astype(BF)
        scaled = scaled.astype(BF)
        queries_t = S["qs"][k].astype(F32).T.astype(BF)
        for g in range(3):
            left = jnp.concatenate([scaled[:, 128 * g : 128 * g + 128], minus], axis=1)
            partial = jnp.zeros((TOK, 128), F32)
            for h in (2 * g, 2 * g + 1):
                p = jnp.concatenate([S["pv"][0, h, rows, :], S["pv"][1, h, rows, :]], axis=1)
                grad = (p.astype(F32) * dot_nt(left, S["ve"][h])).astype(BF)
                S["pv"][0, h, rows, :] = grad[:, :128]
                S["pv"][1, h, rows, :] = grad[:, 128:]
                at = slice(64 * h, 64 * h + 64)
                S["dvt"][at, :] = S["dvt"][at, :] + dot(scaled_t[at, :], p)
                S["dkt"][at, :] = S["dkt"][at, :] + dot(queries_t[at, :], grad)
                partial = partial + dot(grad, S["km"][h])
            S["dq"][k, :, 128 * g : 128 * g + 128] = (partial * 0.125).astype(BF)

        @pl.when(i > 0)
        def _():
            dq_send(i, k, dev(dz=dz, dc=dc)).start()

        gl_local(i, k).start()
        gl_remote(i, k).start()
        return carry

    lax.fori_loop(0, BLOCKS, backward, 0)
    S["dqrecv"][ki] = S["dq"][ki]

    key_grad = S["dkt"][...].T.astype(BF)
    value_grad = S["dvt"][...].T.astype(BF)
    S["kgs"][...] = key_grad.reshape(2, TOK, HALF)
    S["vgs"][...] = value_grad.reshape(2, TOK, HALF)
    kv_swaps = [
        remote(S["kgs"].at[oc], S["kgr"], M["ks"].at[0], M["kr"].at[0], other),
        remote(S["vgs"].at[oc], S["vgr"], M["ks"].at[1], M["kr"].at[1], other),
    ]
    for cp in kv_swaps:
        cp.start()
    hid_pair = S["hid"][pair].reshape(256, D)
    S["b2s"][:, :, :, :HALF] = weight_grad(hid_pair, key_grad).reshape(4, 4, 48, HALF)
    S["b2s"][:, :, :, HALF:] = weight_grad(hid_pair, value_grad).reshape(4, 4, 48, HALF)
    rb2 = scatter(2, 1, S["b2s"], S["b2r"], True)
    for cp in rb2:
        cp.start()
    query_grad = S["dq"][...].reshape(BLOCKS * TOK, HALF)
    S["brow"][c, 0:1, :] = row_sums(query_grad.astype(F32))
    S["brow"][c, 1:2, :] = row_sums(value_grad.astype(F32))
    S["a2s"][:, :, :HALF] = weight_grad(S["hid"][...].reshape(BLOCKS * TOK, D), query_grad).reshape(
        4, 192, HALF
    )
    for half in range(2):
        columns = dot_tn(S["brow"][half].astype(BF), units).astype(BF)
        S["a2s"][2 * half : 2 * half + 2, :, HALF:] = columns.reshape(2, 192, 128)
    ra2 = scatter(3, 0, S["a2s"], S["a2r"], False)
    for cp in ra2:
        cp.start()

    for cp in ra1:
        cp.wait_recv()

    def sum_a(src, recv, dst):
        def step(j, carry):
            part = pl.ds(pl.multiple_of(j * 48, 16), 48)
            total = src[x, part, :].astype(F32)
            for d in range(3):
                total = total + recv[d, part, :].astype(F32)
            dst[j] = total.astype(BF)
            return carry

        lax.fori_loop(0, 4, step, 0)

    def sum_b(src, recv, dst):
        def step(j, carry):
            total = src[j, y].astype(F32)
            for d in range(3):
                total = total + recv[d, j].astype(F32)
            dst[j] = total.astype(BF)
            return carry

        lax.fori_loop(0, 4, step, 0)

    sum_a(S["a1s"], S["a1r"], S["a1t"])
    ta1 = scatter(4, 1, S["a1t"], S["a1u"], False)
    for cp in ta1:
        cp.start()
    for cp in rb1:
        cp.wait_recv()
    sum_b(S["b1s"], S["b1r"], S["b1t"])
    tb1 = scatter(5, 0, S["b1t"], S["b1u"], False)
    for cp in tb1:
        cp.start()

    def await_queries(i, carry):
        k = key_of(far(i // 2), lax.rem(i, 2))
        remote(S["dq"].at[k], S["dqrecv"].at[k], M["qs_"].at[i], M["qr"].at[k], dev(dc=1)).wait_recv()
        return carry

    lax.fori_loop(1, BLOCKS, await_queries, 0)
    for cp in last:
        cp.wait()
    for cp in kv_swaps:
        cp.wait()
    total = S["gs"][...]
    for half in range(2):
        parts = [S["dqrecv"][2 * zz + half].astype(F32) for zz in range(4)]
        grad = (parts[0] + parts[1] + parts[2] + parts[3]).astype(BF)
        total = total + dot_nt(grad, S["wq"][half])
    total = total + dot_nt(S["kgs"][c], S["wk"][c]) + dot_nt(S["kgr"][...], S["wk"][oc])
    total = total + dot_nt(S["vgs"][c], S["wv"][c]) + dot_nt(S["vgr"][...], S["wv"][oc])
    O["grad_hidden"][...] = total.astype(BF)

    for cp in rb2:
        cp.wait_recv()
    sum_b(S["b2s"], S["b2r"], S["b2t"])
    tb2 = scatter(6, 0, S["b2t"], S["b2u"], False)
    for cp in tb2:
        cp.start()
    for cp in ra2:
        cp.wait_recv()
    sum_a(S["a2s"], S["a2r"], S["a2t"])
    ta2 = scatter(7, 1, S["a2t"], S["a2u"], False)
    for cp in ta2:
        cp.start()

    def finish(copies, own, recv, dst):
        for cp in copies:
            cp.wait_recv()
        total = own.astype(F32)
        for d in range(3):
            total = total + recv[d].astype(F32)
        dst[...] = total

    finish(ta1, S["a1t"][y], S["a1u"], S["fa1"])
    finish(tb1, S["b1t"][x], S["b1u"], S["fb1"])
    finish(tb2, S["b2t"][x], S["b2u"], S["fb2"])
    finish(ta2, S["a2t"][y], S["a2u"], S["fa2"])

    S["zf"][:, 72:80, :] = jnp.zeros((BLOCKS, 8, HALF), F32)
    for p in range(BLOCKS):
        six = slice(6 * p, 6 * p + 6)
        groups = [S["fa2"][six, :HALF], S["fb2"][six, :HALF], S["fb2"][six, HALF:]]
        groups += [S["fa1"][six, 1536:1920]]
        groups += [S["fa1"][six, HALF * j : HALF * j + HALF] for j in range(4)]
        for g, rows6 in enumerate(groups):
            S["zf"][p, 6 * g : 6 * g + 6, :] = rows6
        S["zf"][p, 48:72, :] = S["fb1"][24 * p : 24 * p + 24, :]
        S["zf"][p, 72:78, :128] = S["fa2"][six, HALF:]
        S["zs"][p] = S["zf"][p].astype(BF)

    def z_send(i, k, to):
        return remote(S["zs"].at[k], O["zr"].at[ki], M["zs_"].at[i], M["zr_"].at[ki], to)

    def last_sends(i, carry):
        dz, dc = far(i // 2), lax.rem(i, 2)
        z_send(i, key_of(dz, dc), dev(dz=dz, dc=dc)).start()
        return carry

    lax.fori_loop(1, BLOCKS, last_sends, 0)
    own = local(S["zs"].at[ki], O["zr"].at[ki], M["zs_"].at[0])
    own.start()
    own.wait()

    def drain(i, carry):
        dz, dc = far(i // 2), lax.rem(i, 2)
        k = key_of(dz, dc)
        to = dev(dz=dz, dc=dc)
        out_send(i, k, to).wait_send()
        st_send(i, k, to).wait_send()
        ag_send(i, k, to).wait_send()
        s2_send(i, k, to).wait_send()
        dq_send(i, k, to).wait_send()
        remote(S["zs"].at[k], O["zr"].at[k], M["zs_"].at[i], M["zr_"].at[k], to).wait()
        return carry

    lax.fori_loop(1, BLOCKS, drain, 0)

    def drain_logits(i, carry):
        k = key_of(far(i // 2), lax.rem(i, 2))
        gl_local(i, k).wait()
        gl_remote(i, k).wait()
        return carry

    lax.fori_loop(0, BLOCKS, drain_logits, 0)
    for cp in hid_sends:
        cp.wait_send()
    for d in (1, 2, 3):
        hid_forward(d, key_of(far(jnp.int32(d)), 0)).wait_send()
    for dz in range(4):
        prev_remote(dz).wait_send()
    for cp in ra1 + rb1 + ra2 + rb2 + ta1 + tb1 + ta2 + tb2:
        cp.wait_send()


def main_kernel(args):
    any_space = pl.BlockSpec(memory_space=pl.ANY)
    in_specs = [
        pl.BlockSpec(memory_space=pltpu.SMEM) if name == "lengths" else any_space for name in ARGS
    ]
    vmem = pl.BlockSpec(memory_space=pltpu.VMEM)
    return pl.pallas_call(
        body,
        out_shape=[
            jax.ShapeDtypeStruct((TOK, D), BF),
            jax.ShapeDtypeStruct((TOK, D), BF),
            jax.ShapeDtypeStruct((2 * HEADS, BLOCKS * TOK, 128), BF),
            jax.ShapeDtypeStruct((BLOCKS, 80, HALF), BF),
        ],
        in_specs=in_specs,
        out_specs=[vmem, vmem, any_space, any_space],
        scratch_shapes=[pltpu.VMEM(s, t) for s, t in SCRATCH.values()]
        + [pltpu.SemaphoreType.DMA((n,)) for n in SEMS.values()],
        compiler_params=pltpu.CompilerParams(
            collective_id=0, has_side_effects=True, vmem_limit_bytes=60 * 2**20
        ),
        name="layer",
    )(*args)


def lay_out(oh, gh, gl, zr, *refs):
    outs, sem = refs[:18], refs[18]
    copy = pltpu.make_async_copy(gl, outs[2], sem)
    copy.start()
    outs[0][...] = oh[...]
    outs[1][...] = gh[...]
    sums = []
    for half in range(2):
        total = zr[half].astype(F32)
        for zz in range(1, 4):
            total = total + zr[2 * zz + half].astype(F32)
        sums.append(total)
    both = jnp.concatenate(sums, axis=1)
    for g in range(4):
        outs[3 + g][...] = both[6 * g : 6 * g + 6, :]
    for half in range(2):
        for j in range(4):
            at = (4 * half + j) * HALF
            outs[7][:, at : at + HALF] = sums[half][24 + 6 * j : 30 + 6 * j, :]
    outs[8][...] = both[48:72, :]
    tail = sums[0][72:80, :128] + sums[1][72:80, :128]
    flipped = jnp.concatenate([tail, jnp.zeros((120, 128), F32)], axis=0).T
    for slot, row in ((9, 0), (10, 1), (11, 2), (13, 3), (14, 4), (15, 5), (16, 6), (17, 7)):
        outs[slot][...] = flipped[row, 0:6]
    inner = jnp.zeros((1, 128), F32)
    lane = iota((1, 128), 1)
    for i in range(6):
        for j in range(4):
            inner = jnp.where(lane == 4 * i + j, flipped[8 + j : 9 + j, i : i + 1], inner)
    outs[12][...] = inner[0, 0:24]
    copy.wait()


def out_kernel(oh, gh, gl, zr):
    vmem = pl.BlockSpec(memory_space=pltpu.VMEM)
    any_space = pl.BlockSpec(memory_space=pl.ANY)
    f = lambda *s: jax.ShapeDtypeStruct(s, F32)
    return pl.pallas_call(
        lay_out,
        out_shape=[
            jax.ShapeDtypeStruct((TOK, D), BF),
            jax.ShapeDtypeStruct((TOK, D), BF),
            jax.ShapeDtypeStruct((2 * HEADS, BLOCKS * TOK, 128), BF),
            f(6, D),
            f(6, D),
            f(6, D),
            f(6, D),
            f(6, FF),
            f(24, D),
            f(6),
            f(6),
            f(6),
            f(24),
            f(6),
            f(6),
            f(6),
            f(6),
            f(6),
        ],
        in_specs=[vmem, vmem, any_space, vmem],
        out_specs=[vmem, vmem, any_space] + [vmem] * 15,
        scratch_shapes=[pltpu.SemaphoreType.DMA],
        name="lay_out",
    )(oh, gh, gl, zr)


def on_device(*args):
    return tuple(out_kernel(*main_kernel(args)))


def solution(mesh):
    rows = P(("batch", "keys"), None)
    logits = P(None, "batch", "keys")
    flat = P(("batch", "keys"))
    return jax.shard_map(
        on_device,
        mesh=mesh,
        in_specs=(rows, logits, P("batch", None), rows) + (P(),) * 15,
        out_specs=(rows, rows, logits) + (rows,) * 6 + (flat,) * 9,
        check_vma=False,
    )
```

```python
from types import SimpleNamespace
from typing import Any, NamedTuple

import jax
import jax.numpy as jnp
from jax import lax
from jax.experimental import pallas as pl
from jax.experimental.pallas import tpu as pltpu
from jax.sharding import PartitionSpec as P

EPSILON = 1e-05
NEGATIVE = -1e30
MESH = pl.DeviceIdType.MESH
BF = jnp.bfloat16
F32 = jnp.float32

TOK = 128
D = 768
HALF = 384
HEADS = 6
FF = 3072
SEQS = 16
BLOCKS = 8
PARTS = 4


def dot(a, b):
    return lax.dot_general(a, b, (((1,), (0,)), ((), ())), preferred_element_type=F32)


def dot_nt(a, b):
    return lax.dot_general(a, b, (((1,), (1,)), ((), ())), preferred_element_type=F32)


def dot_tn(a, b):
    return lax.dot_general(a, b, (((0,), (0,)), ((), ())), preferred_element_type=F32)


def iota(shape, dim):
    return lax.broadcasted_iota(jnp.int32, shape, dim)


def split_hi_lo(v):
    hi = v.astype(BF)
    lo = (v - hi.astype(F32)).astype(BF)
    return jnp.concatenate([hi.astype(F32), lo.astype(F32)], axis=0).astype(BF)


def head_rows():
    return jnp.where(iota((16, HALF), 1) // 64 == iota((16, HALF), 0) % 8, 1.0, 0.0).astype(BF)


def unit_rows():
    return jnp.where(iota((16, 128), 1) == iota((16, 128), 0), 1.0, 0.0).astype(BF)


def row_sums(v):
    return jnp.sum(v, axis=0, keepdims=True)


def norm(values):
    average = jnp.mean(values, axis=-1, keepdims=True)
    centered = values - average
    variance = jnp.mean(centered * centered, axis=-1, keepdims=True)
    inverse = lax.rsqrt(variance + EPSILON)
    return centered * inverse, inverse


def norm_back(upstream, normed, inverse, gain):
    scaled = upstream * gain
    return inverse * (
        scaled
        - jnp.mean(scaled, axis=-1, keepdims=True)
        - normed * jnp.mean(scaled * normed, axis=-1, keepdims=True)
    )


class Args(NamedTuple):
    hidden: Any
    prev: Any
    lengths: Any
    gout: Any
    w_q: Any
    w_k: Any
    w_v: Any
    w_o: Any
    w_i: Any
    w_u: Any
    b_q: Any
    b_v: Any
    b_o: Any
    b_i: Any
    b_u: Any
    g_a: Any
    b_a: Any
    g_f: Any
    b_f: Any


class Outs(NamedTuple):
    out_hidden: Any
    grad_hidden: Any
    gl: Any
    zr: Any


SCRATCH = dict(
    wq=((2, D, HALF), BF),
    wk=((2, D, HALF), BF),
    wv=((2, D, HALF), BF),
    wo=((D, D), BF),
    wi=((4, D, D), BF),
    wu=((4, D, D), BF),
    vq=((D,), F32),
    vv=((D,), F32),
    vo=((D,), F32),
    vi=((FF,), F32),
    vu=((D,), F32),
    ga=((D,), F32),
    ba=((D,), F32),
    gf=((D,), F32),
    bf=((D,), F32),
    go=((TOK, D), BF),
    hid=((BLOCKS, TOK, D), BF),
    pv=((2, HEADS, BLOCKS * TOK, 128), BF),
    qs=((BLOCKS, TOK, HALF), BF),
    km=((HEADS, 256, 128), BF),
    ve=((HEADS, 256, 256), BF),
    madd=((TOK, 256), F32),
    obuf=((BLOCKS, TOK, HALF), BF),
    orecv=((BLOCKS, TOK, HALF), BF),
    st=((BLOCKS, 16, 128), F32),
    strecv=((BLOCKS, 16, 128), F32),
    at=((2, TOK, HALF), F32),
    atx=((2, TOK, D), BF),
    fx=((2, TOK, D), BF),
    n1=((TOK, D), F32),
    gs=((TOK, D), F32),
    gp=((4, TOK, D), F32),
    ax=((2, TOK, FF), BF),
    igs=((2, TOK, FF // 2), BF),
    igr=((TOK, FF // 2), BF),
    ogs=((2, TOK, HALF), BF),
    ogr=((TOK, HALF), BF),
    brs=((2, TOK, HALF), BF),
    brr=((TOK, HALF), BF),
    brow=((2, 16, HALF), F32),
    ags=((2, TOK, HALF), BF),
    dorecv=((BLOCKS, TOK, HALF), BF),
    s2=((2, 16, 128), F32),
    s2recv=((BLOCKS, 16, 128), F32),
    dkt=((HALF, 256), F32),
    dvt=((HALF, 256), F32),
    dq=((BLOCKS, TOK, HALF), BF),
    dqrecv=((BLOCKS, TOK, HALF), BF),
    kgs=((2, TOK, HALF), BF),
    kgr=((TOK, HALF), BF),
    vgs=((2, TOK, HALF), BF),
    vgr=((TOK, HALF), BF),
    a1s=((4, 192, 1920), BF),
    a1r=((3, 192, 1920), BF),
    a1t=((4, 48, 1920), BF),
    a1u=((3, 48, 1920), BF),
    a2s=((4, 192, 512), BF),
    a2r=((3, 192, 512), BF),
    a2t=((4, 48, 512), BF),
    a2u=((3, 48, 512), BF),
    b1s=((4, 4, 192, HALF), BF),
    b1r=((3, 4, 192, HALF), BF),
    b1t=((4, 192, HALF), BF),
    b1u=((3, 192, HALF), BF),
    b2s=((4, 4, 48, D), BF),
    b2r=((3, 4, 48, D), BF),
    b2t=((4, 48, D), BF),
    b2u=((3, 48, D), BF),
    fa1=((48, 1920), F32),
    fa2=((48, 512), F32),
    fb1=((192, HALF), F32),
    fb2=((48, D), F32),
    zf=((BLOCKS, 80, HALF), F32),
    zs=((BLOCKS, 80, HALF), BF),
)
SEMS = dict(
    ld=24,
    hs=8,
    hr=8,
    pl_=4,
    ps=4,
    pr=4,
    os=8,
    or_=8,
    ss=8,
    sr=8,
    xs=6,
    xr=6,
    ds=8,
    dr=8,
    es=8,
    er=8,
    qs_=8,
    qr=8,
    gl_=8,
    gs_=8,
    gr=8,
    ks=2,
    kr=2,
    rs=24,
    rr=24,
    zs_=8,
    zr_=8,
    outs=3,
)


def body(*refs):
    na, no, nsc = len(Args._fields), len(Outs._fields), len(SCRATCH)
    A = Args(*refs[:na])
    O = Outs(*refs[na : na + no])
    S = SimpleNamespace(**dict(zip(SCRATCH, refs[na + no : na + no + nsc])))
    M = SimpleNamespace(**dict(zip(SEMS, refs[na + no + nsc :])))

    bi = lax.axis_index("batch")
    ki = lax.axis_index("keys")
    x, y = bi // 4, lax.rem(bi, 4)
    z, c = ki // 2, lax.rem(ki, 2)
    oc = 1 - c

    def dev(dx=0, dy=0, dz=0, dc=0):
        nb = lax.rem(x + dx, 4) * 4 + lax.rem(y + dy, 4)
        return (nb, lax.rem(z + dz, 4) * 2 + lax.rem(c + dc, 2))

    def key_of(dz, dc):
        return lax.rem(z + dz, 4) * 2 + lax.rem(c + dc, 2)

    def far(d):
        return d + (d // 2) * (1 - 2 * lax.rem(d, 2))

    def remote(src, dst, ssem, rsem, to):
        return pltpu.make_async_remote_copy(
            src_ref=src, dst_ref=dst, send_sem=ssem, recv_sem=rsem, device_id=to, device_id_type=MESH
        )

    def local(src, dst, sem):
        return pltpu.make_async_copy(src, dst, sem)

    loads = [
        local(A.hidden, S.hid.at[ki], M.ld.at[0]),
        local(A.w_k.at[:, pl.ds(pl.multiple_of(c * HALF, 128), HALF)], S.wk.at[c], M.ld.at[1]),
        local(A.w_v.at[:, pl.ds(pl.multiple_of(c * HALF, 128), HALF)], S.wv.at[c], M.ld.at[2]),
        local(A.w_q.at[:, pl.ds(pl.multiple_of(c * HALF, 128), HALF)], S.wq.at[c], M.ld.at[3]),
        local(A.b_q, S.vq, M.ld.at[4]),
        local(A.b_v, S.vv, M.ld.at[5]),
    ]
    early = len(loads)
    later = [
        local(A.w_o, S.wo, M.ld.at[6]),
        local(A.b_o, S.vo, M.ld.at[7]),
        local(A.b_i, S.vi, M.ld.at[8]),
        local(A.b_u, S.vu, M.ld.at[9]),
        local(A.g_a, S.ga, M.ld.at[10]),
        local(A.b_a, S.ba, M.ld.at[11]),
        local(A.g_f, S.gf, M.ld.at[12]),
        local(A.b_f, S.bf, M.ld.at[13]),
        local(A.gout, S.go, M.ld.at[14]),
    ]
    for j in range(4):
        later.append(local(A.w_i.at[:, pl.ds(D * j, D)], S.wi.at[j], M.ld.at[15 + j]))
    for j in range(2):
        later.append(local(A.w_u.at[pl.ds(2 * D * j, D)], S.wu.at[2 * j], M.ld.at[19 + 2 * j]))
        later.append(
            local(A.w_u.at[pl.ds(2 * D * j + D, D)], S.wu.at[2 * j + 1], M.ld.at[20 + 2 * j])
        )
    last = [
        local(a.at[:, pl.ds(pl.multiple_of(oc * HALF, 128), HALF)], s.at[oc], M.outs.at[i])
        for i, (a, s) in enumerate(((A.w_q, S.wq), (A.w_k, S.wk), (A.w_v, S.wv)))
    ]
    for cp in loads:
        cp.start()

    def prev_rows(dz):
        return pl.ds(pl.multiple_of(lax.rem(z + dz, 4) * 256, 256), 256)

    def prev_local(dz):
        rows = prev_rows(dz)
        return local(
            A.prev.at[pl.ds(c * HEADS, HEADS), rows, :], S.pv.at[c, :, rows, :], M.pl_.at[dz]
        )

    def prev_remote(dz):
        rows = prev_rows(dz)
        return remote(
            A.prev.at[pl.ds(oc * HEADS, HEADS), rows, :],
            S.pv.at[c, :, rows, :],
            M.ps.at[dz],
            M.pr.at[dz],
            dev(dc=1),
        )

    for dz in (0, 1, 3, 2):
        prev_local(dz).start()

    peers = [(0, 0, dz, dc) for dz in range(4) for dc in range(2) if dz or dc]
    peers += [(d, 0, 0, 0) for d in (1, 2, 3)] + [(0, d, 0, 0) for d in (1, 2, 3)]
    barrier = pltpu.get_barrier_semaphore()
    for off in peers:
        pl.semaphore_signal(barrier, inc=1, device_id=dev(*off), device_id_type=MESH)
    pl.semaphore_wait(barrier, len(peers))

    def hid_send(i, to):
        return remote(A.hidden, S.hid.at[ki], M.hs.at[i], M.hr.at[ki], to)

    def hid_arrival(k):
        return remote(A.hidden, S.hid.at[k], M.hs.at[0], M.hr.at[k], dev(dc=1))

    def hid_forward(d, k):
        return remote(S.hid.at[k], S.hid.at[k], M.hs.at[3 + d], M.hr.at[k], dev(dc=1))

    hid_sends = [hid_send(0, dev(dc=1)), hid_send(1, dev(dz=1)), hid_send(2, dev(dz=3)), hid_send(3, dev(dz=2))]
    for cp in hid_sends:
        cp.start()
    prev_remote(0).start()
    prev_remote(1).start()
    prev_remote(3).start()
    prev_remote(2).start()

    bounds = []
    running = jnp.int32(0)
    for j in range(SEQS):
        running = running + A.lengths[0, j]
        bounds.append(running)

    def segment_of(places):
        counted = jnp.zeros(places.shape, jnp.int32)
        for bound in bounds:
            counted = counted + jnp.where(places >= bound, 1, 0)
        return jnp.where(places < bounds[-1], counted, -1 - places)

    lane8 = iota((8, 128), 1)
    key_segment = [segment_of(lane8 * BLOCKS + z * 2 + half)[0:1, :] for half in range(2)]
    lane = iota((TOK, 128), 1)

    for cp in loads[:1] + loads[1:3] + loads[5:6]:
        cp.wait()
    hid_arrival(key_of(0, 1)).wait_recv()
    pair = pl.ds(z * 2, 2)
    hid_pair = S.hid[pair].reshape(256, D)
    key_rows = dot(hid_pair, S.wk[c]).astype(BF).astype(F32)
    bias_v = S.vv[...].reshape(1, D)
    bias_q = S.vq
    bv = jnp.where(c == 0, bias_v[:, :HALF], bias_v[:, HALF:])
    value_rows = (dot(hid_pair, S.wv[c]) + bv).astype(BF).astype(F32)
    lane2 = iota((256, 128), 1)
    for h in range(HEADS):
        g, e = h // 2, h % 2
        mine = lane2 // 64 == e
        S.km[h] = jnp.where(mine, key_rows[:, 128 * g : 128 * g + 128], 0.0).astype(BF)
        S.ve[h, :, :128] = jnp.where(mine, value_rows[:, 128 * g : 128 * g + 128], 0.0).astype(BF)
        S.ve[h, :, 128:] = jnp.where((lane2 == h) | (lane2 == 8 + h), 1.0, 0.0).astype(BF)
    loads[3].wait()
    loads[4].wait()
    bias_q = S.vq[...].reshape(1, D)
    S.brow[...] = jnp.zeros((2, 16, HALF), F32)
    for cp in later + last:
        cp.start()

    def out_send(i, k, to):
        return remote(S.obuf.at[k], S.orecv.at[ki], M.os.at[i], M.or_.at[ki], to)

    def st_send(i, k, to):
        return remote(S.st.at[k], S.strecv.at[ki], M.ss.at[i], M.sr.at[ki], to)

    def forward(i, carry):
        d = i // 2
        dc = lax.rem(i, 2)
        dz = far(d)
        k = key_of(dz, dc)

        @pl.when(jnp.logical_and(dc == 0, d > 0))
        def _():
            hid_arrival(k).wait_recv()
            hid_forward(d, k).start()

        @pl.when(jnp.logical_and(dc == 1, d > 0))
        def _():
            hid_arrival(k).wait_recv()

        @pl.when(dc == 0)
        def _():
            prev_local(dz).wait()
            prev_remote(dz).wait_recv()

        bq = jnp.where(c == 0, bias_q[:, :HALF], bias_q[:, HALF:])
        queries = (dot(S.hid[k], S.wq[c]) + bq).astype(BF).astype(F32) * 0.125
        S.qs[k] = queries.astype(BF)
        row_segment = segment_of(iota((TOK, 128), 0) * BLOCKS + k)
        for half in range(2):
            S.madd[:, 128 * half : 128 * half + 128] = jnp.where(
                row_segment == key_segment[half], 0.0, NEGATIVE
            )
        rows = pl.ds(pl.multiple_of(k * TOK, TOK), TOK)
        totals = jnp.zeros((TOK, 128), F32)
        tops = jnp.zeros((TOK, 128), F32)
        for g in range(3):
            two = S.qs[k, :, 128 * g : 128 * g + 128]
            mixed = jnp.zeros((TOK, 128), F32)
            for h in (2 * g, 2 * g + 1):
                before = jnp.concatenate([S.pv[0, h, rows, :], S.pv[1, h, rows, :]], axis=1)
                s = dot_nt(two, S.km[h]) + before.astype(F32) + S.madd[...]
                top = jnp.max(s, axis=1, keepdims=True)
                p = jnp.exp(s - top).astype(BF)
                S.pv[0, h, rows, :] = p[:, :128]
                S.pv[1, h, rows, :] = p[:, 128:]
                o = dot(p, S.ve[h])
                mixed = mixed + o[:, :128]
                totals = totals + o[:, 128:]
                tops = jnp.where(lane == 8 + h, top, tops)
            S.obuf[k, :, 128 * g : 128 * g + 128] = mixed.astype(BF)
        stats = jnp.where(lane < 8, totals, tops)
        S.st[k] = stats.T[:16, :]

        @pl.when(i > 0)
        def _():
            to = dev(dz=dz, dc=dc)
            out_send(i, k, to).start()
            st_send(i, k, to).start()

        return carry

    lax.fori_loop(0, BLOCKS, forward, 0)

    S.orecv[ki] = S.obuf[ki]
    S.strecv[ki] = S.st[ki]

    def await_parts(i, carry):
        k = key_of(far(i // 2), lax.rem(i, 2))
        remote(S.obuf.at[k], S.orecv.at[k], M.os.at[i], M.or_.at[k], dev(dc=1)).wait_recv()
        remote(S.st.at[k], S.strecv.at[k], M.ss.at[i], M.sr.at[k], dev(dc=1)).wait_recv()
        return carry

    lax.fori_loop(1, BLOCKS, await_parts, 0)
    row8 = iota((8, 128), 0)
    spread = head_rows()
    lse = []
    for half in range(2):
        tops = [S.strecv[2 * zz + half, 8:16, :] for zz in range(4)]
        sums = [S.strecv[2 * zz + half, 0:8, :] for zz in range(4)]
        top = jnp.maximum(jnp.maximum(tops[0], tops[1]), jnp.maximum(tops[2], tops[3]))
        shares = [jnp.exp(t - top) for t in tops]
        total = shares[0] * sums[0] + shares[1] * sums[1] + shares[2] * sums[2] + shares[3] * sums[3]
        total = jnp.where(row8 < HEADS, total, 1.0)
        lse.append(jnp.where(row8 < HEADS, top + jnp.log(total), 0.0))
        acc = jnp.zeros((TOK, HALF), F32)
        for zz in range(4):
            factor = dot_tn(split_hi_lo(jnp.where(row8 < HEADS, shares[zz] / total, 0.0)), spread)
            acc = acc + S.orecv[2 * zz + half].astype(F32) * factor
        S.at[half] = acc
        S.atx[0, :, HALF * half : HALF * half + HALF] = acc.astype(BF)

    def vec(ref):
        return ref[...].reshape(1, -1)

    for cp in later:
        cp.wait()
    attn_low = S.atx[0]
    first_sum = S.hid[ki].astype(F32) + dot(attn_low, S.wo[...]) + vec(S.vo)
    normed, inverse_a = norm(first_sum)
    S.n1[...] = normed
    S.fx[0] = (normed * vec(S.ga) + vec(S.ba)).astype(BF)
    second = normed * vec(S.ga) + vec(S.ba) + vec(S.vu)
    bias_i = vec(S.vi)
    for j in range(4):
        inner = dot(S.fx[0], S.wi[j]) + bias_i[:, D * j : D * j + D]
        cdf = 0.5 + 0.5 * lax.erf(inner * 0.7071067811865476)
        density = jnp.exp(inner * inner * -0.5) * 0.3989422804014327
        S.gp[j] = cdf + inner * density
        S.ax[0, :, D * j : D * j + D] = (inner * cdf).astype(BF)
        second = second + dot(S.ax[0, :, D * j : D * j + D], S.wu[j])
    normed_f, inverse_f = norm(second)
    O.out_hidden[...] = (normed_f * vec(S.gf) + vec(S.bf)).astype(BF)
    upstream = S.go[...].astype(F32)

    def put_row(r, values):
        sums = row_sums(values)
        S.brow[0, r : r + 1, :] = sums[:, :HALF]
        S.brow[1, r : r + 1, :] = sums[:, HALF:]

    put_row(6, upstream * normed_f)
    put_row(7, upstream)
    grad_second = norm_back(upstream, normed_f, inverse_f, vec(S.gf))
    og = grad_second.astype(BF)
    put_row(3, og.astype(F32))
    S.ogs[0] = og[:, :HALF]
    S.ogs[1] = og[:, HALF:]
    S.gs[...] = grad_second
    bsum = []
    for j in range(4):
        ig = (dot_nt(og, S.wu[j]) * S.gp[j]).astype(BF)
        S.igs[j // 2, :, D * (j % 2) : D * (j % 2) + D] = ig
        bsum.append(row_sums(ig.astype(F32)))
        S.gs[...] = S.gs[...] + dot_nt(ig, S.wi[j])
    grad_first = S.gs[...]
    normed = S.n1[...]
    put_row(4, grad_first * normed)
    put_row(5, grad_first)
    grad_first_sum = norm_back(grad_first, normed, inverse_a, vec(S.ga))
    S.gs[...] = grad_first_sum
    br = grad_first_sum.astype(BF)
    put_row(2, br.astype(F32))
    S.brs[0] = br[:, :HALF]
    S.brs[1] = br[:, HALF:]
    ag = dot_nt(br, S.wo[...]).astype(BF)
    for half in range(2):
        S.ags[half] = ag[:, HALF * half : HALF * half + HALF]
        product = S.at[half] * ag[:, HALF * half : HALF * half + HALF].astype(F32)
        dots = jnp.zeros((16, TOK), F32)
        hi = product.astype(BF)
        lo = (product - hi.astype(F32)).astype(BF)
        dots = dot_nt(spread, hi) + dot_nt(spread, lo)
        S.s2[half, 0:8, :] = dots[0:8, :]
        S.s2[half, 8:16, :] = lse[half]

    def ag_send(i, k, to):
        half = lax.rem(k, 2)
        return remote(S.ags.at[half], S.dorecv.at[ki], M.ds.at[i], M.dr.at[ki], to)

    def s2_send(i, k, to):
        half = lax.rem(k, 2)
        return remote(S.s2.at[half], S.s2recv.at[ki], M.es.at[i], M.er.at[ki], to)

    def send_grads(i, carry):
        dz, dc = far(i // 2), lax.rem(i, 2)
        k = key_of(dz, dc)
        to = dev(dz=dz, dc=dc)
        ag_send(i, k, to).start()
        s2_send(i, k, to).start()
        return carry

    lax.fori_loop(1, BLOCKS, send_grads, 0)
    S.dorecv[ki] = S.ags[c]
    S.s2recv[ki] = S.s2[c]

    other = dev(dc=1)
    swaps = [
        remote(S.fx.at[0], S.fx.at[1], M.xs.at[0], M.xr.at[0], other),
        remote(S.igs.at[oc], S.igr, M.xs.at[1], M.xr.at[1], other),
        remote(S.ax.at[0], S.ax.at[1], M.xs.at[2], M.xr.at[2], other),
        remote(S.ogs.at[oc], S.ogr, M.xs.at[3], M.xr.at[3], other),
        remote(S.atx.at[0], S.atx.at[1], M.xs.at[4], M.xr.at[4], other),
        remote(S.brs.at[oc], S.brr, M.xs.at[5], M.xr.at[5], other),
    ]
    for cp in swaps:
        cp.start()

    lane512 = iota((8, 512), 1)
    sub512 = iota((8, 512), 0)
    pick = jnp.where(
        iota((512, 128), 1) == (iota((512, 128), 0) // 128) * 32 + lax.rem(iota((512, 128), 0), 128) // 4,
        1.0,
        0.0,
    ).astype(BF)
    flat = jnp.concatenate(bsum, axis=1)
    for g in range(6):
        spread_out = jnp.where(lax.rem(lane512, 4) == sub512, flat[:, 512 * g : 512 * g + 512], 0.0)
        S.brow[g // 3, 8:16, 128 * (g % 3) : 128 * (g % 3) + 128] = dot(spread_out.astype(BF), pick)

    for cp in swaps:
        cp.wait()

    def weight_grad(left, right):
        return dot_tn(left, right).astype(BF)

    first_two = S.fx[...].reshape(256, D)
    for j in range(4):
        col = slice(HALF * j, HALF * j + HALF)
        right = jnp.concatenate([S.igs[c, :, col], S.igr[:, col]], axis=0)
        S.a1s[:, :, col] = weight_grad(first_two, right).reshape(4, 192, HALF)
    right = jnp.concatenate([S.brs[c], S.brr[...]], axis=0)
    S.a1s[:, :, 1536:1920] = weight_grad(S.atx[...].reshape(256, D), right).reshape(4, 192, HALF)

    def along(axis, d):
        return dev(dx=d) if axis == 0 else dev(dy=d)

    def at_place(axis, d):
        return lax.rem((x if axis == 0 else y) + d, 4)

    def scatter(n, axis, src, dst, inner):
        out = []
        for d in (1, 2, 3):
            there = at_place(axis, d)
            piece = src.at[:, there] if inner else src.at[there]
            sem = 3 * n + d - 1
            out.append(remote(piece, dst.at[d - 1], M.rs.at[sem], M.rr.at[sem], along(axis, d)))
        return out

    all_sends = []
    ra1 = scatter(0, 0, S.a1s, S.a1r, False)
    for cp in ra1:
        cp.start()
    right = jnp.concatenate([S.ogs[c], S.ogr[...]], axis=0)
    for j in range(4):
        left = S.ax[:, :, D * j : D * j + D].reshape(256, D)
        S.b1s[j] = weight_grad(left, right).reshape(4, 192, HALF)
    rb1 = scatter(1, 1, S.b1s, S.b1r, True)
    for cp in rb1:
        cp.start()

    S.dkt[...] = jnp.zeros((HALF, 256), F32)
    S.dvt[...] = jnp.zeros((HALF, 256), F32)
    units = unit_rows()

    def dq_send(i, k, to):
        return remote(S.dq.at[k], S.dqrecv.at[ki], M.qs_.at[i], M.qr.at[ki], to)

    def gl_rows(k):
        return pl.ds(pl.multiple_of(k * TOK, TOK), TOK)

    def gl_local(i, k):
        rows = gl_rows(k)
        return local(
            S.pv.at[c, :, rows, :], O.gl.at[pl.ds(c * HEADS, HEADS), rows, :], M.gl_.at[i]
        )

    def gl_remote(i, k):
        rows = gl_rows(k)
        return remote(
            S.pv.at[oc, :, rows, :],
            O.gl.at[pl.ds(c * HEADS, HEADS), rows, :],
            M.gs_.at[i],
            M.gr.at[k],
            dev(dc=1),
        )

    def backward(i, carry):
        dz, dc = far(i // 2), lax.rem(i, 2)
        k = key_of(dz, dc)

        @pl.when(i > 0)
        def _():
            remote(S.ags.at[0], S.dorecv.at[k], M.ds.at[i], M.dr.at[k], dev(dc=1)).wait_recv()
            remote(S.s2.at[0], S.s2recv.at[k], M.es.at[i], M.er.at[k], dev(dc=1)).wait_recv()

        rows = pl.ds(pl.multiple_of(k * TOK, TOK), TOK)
        share = jnp.exp(S.st[k, 8:16, :] - S.s2recv[k, 8:16, :])
        share = jnp.where(row8 < HEADS, share, 0.0)
        minus = dot_tn(split_hi_lo(S.s2recv[k, 0:8, :] * share * -1.0), units).astype(BF)
        factor = dot_tn(split_hi_lo(share), spread)
        scaled = S.dorecv[k].astype(F32) * factor
        scaled_t = scaled.T.astype(BF)
        scaled = scaled.astype(BF)
        queries_t = S.qs[k].astype(F32).T.astype(BF)
        for g in range(3):
            left = jnp.concatenate([scaled[:, 128 * g : 128 * g + 128], minus], axis=1)
            partial = jnp.zeros((TOK, 128), F32)
            for h in (2 * g, 2 * g + 1):
                p = jnp.concatenate([S.pv[0, h, rows, :], S.pv[1, h, rows, :]], axis=1)
                grad = (p.astype(F32) * dot_nt(left, S.ve[h])).astype(BF)
                S.pv[0, h, rows, :] = grad[:, :128]
                S.pv[1, h, rows, :] = grad[:, 128:]
                at = slice(64 * h, 64 * h + 64)
                S.dvt[at, :] = S.dvt[at, :] + dot(scaled_t[at, :], p)
                S.dkt[at, :] = S.dkt[at, :] + dot(queries_t[at, :], grad)
                partial = partial + dot(grad, S.km[h])
            S.dq[k, :, 128 * g : 128 * g + 128] = (partial * 0.125).astype(BF)

        @pl.when(i > 0)
        def _():
            dq_send(i, k, dev(dz=dz, dc=dc)).start()

        gl_local(i, k).start()
        gl_remote(i, k).start()
        return carry

    lax.fori_loop(0, BLOCKS, backward, 0)
    S.dqrecv[ki] = S.dq[ki]

    key_grad = S.dkt[...].T.astype(BF)
    value_grad = S.dvt[...].T.astype(BF)
    S.kgs[...] = key_grad.reshape(2, TOK, HALF)
    S.vgs[...] = value_grad.reshape(2, TOK, HALF)
    kv_swaps = [
        remote(S.kgs.at[oc], S.kgr, M.ks.at[0], M.kr.at[0], other),
        remote(S.vgs.at[oc], S.vgr, M.ks.at[1], M.kr.at[1], other),
    ]
    for cp in kv_swaps:
        cp.start()
    hid_pair = S.hid[pair].reshape(256, D)
    S.b2s[:, :, :, :HALF] = weight_grad(hid_pair, key_grad).reshape(4, 4, 48, HALF)
    S.b2s[:, :, :, HALF:] = weight_grad(hid_pair, value_grad).reshape(4, 4, 48, HALF)
    rb2 = scatter(2, 1, S.b2s, S.b2r, True)
    for cp in rb2:
        cp.start()
    query_grad = S.dq[...].reshape(BLOCKS * TOK, HALF)
    S.brow[c, 0:1, :] = row_sums(query_grad.astype(F32))
    S.brow[c, 1:2, :] = row_sums(value_grad.astype(F32))
    S.a2s[:, :, :HALF] = weight_grad(S.hid[...].reshape(BLOCKS * TOK, D), query_grad).reshape(
        4, 192, HALF
    )
    for half in range(2):
        columns = dot_tn(S.brow[half].astype(BF), units).astype(BF)
        S.a2s[2 * half : 2 * half + 2, :, HALF:] = columns.reshape(2, 192, 128)
    ra2 = scatter(3, 0, S.a2s, S.a2r, False)
    for cp in ra2:
        cp.start()

    for cp in ra1:
        cp.wait_recv()

    def sum_a(src, recv, dst):
        def step(j, carry):
            part = pl.ds(pl.multiple_of(j * 48, 16), 48)
            total = src[x, part, :].astype(F32)
            for d in range(3):
                total = total + recv[d, part, :].astype(F32)
            dst[j] = total.astype(BF)
            return carry

        lax.fori_loop(0, 4, step, 0)

    def sum_b(src, recv, dst):
        def step(j, carry):
            total = src[j, y].astype(F32)
            for d in range(3):
                total = total + recv[d, j].astype(F32)
            dst[j] = total.astype(BF)
            return carry

        lax.fori_loop(0, 4, step, 0)

    sum_a(S.a1s, S.a1r, S.a1t)
    ta1 = scatter(4, 1, S.a1t, S.a1u, False)
    for cp in ta1:
        cp.start()
    for cp in rb1:
        cp.wait_recv()
    sum_b(S.b1s, S.b1r, S.b1t)
    tb1 = scatter(5, 0, S.b1t, S.b1u, False)
    for cp in tb1:
        cp.start()

    def await_queries(i, carry):
        k = key_of(far(i // 2), lax.rem(i, 2))
        remote(S.dq.at[k], S.dqrecv.at[k], M.qs_.at[i], M.qr.at[k], dev(dc=1)).wait_recv()
        return carry

    lax.fori_loop(1, BLOCKS, await_queries, 0)
    for cp in last:
        cp.wait()
    for cp in kv_swaps:
        cp.wait()
    total = S.gs[...]
    for half in range(2):
        parts = [S.dqrecv[2 * zz + half].astype(F32) for zz in range(4)]
        grad = (parts[0] + parts[1] + parts[2] + parts[3]).astype(BF)
        total = total + dot_nt(grad, S.wq[half])
    total = total + dot_nt(S.kgs[c], S.wk[c]) + dot_nt(S.kgr[...], S.wk[oc])
    total = total + dot_nt(S.vgs[c], S.wv[c]) + dot_nt(S.vgr[...], S.wv[oc])
    O.grad_hidden[...] = total.astype(BF)

    for cp in rb2:
        cp.wait_recv()
    sum_b(S.b2s, S.b2r, S.b2t)
    tb2 = scatter(6, 0, S.b2t, S.b2u, False)
    for cp in tb2:
        cp.start()
    for cp in ra2:
        cp.wait_recv()
    sum_a(S.a2s, S.a2r, S.a2t)
    ta2 = scatter(7, 1, S.a2t, S.a2u, False)
    for cp in ta2:
        cp.start()

    def finish(copies, own, recv, dst):
        for cp in copies:
            cp.wait_recv()
        total = own.astype(F32)
        for d in range(3):
            total = total + recv[d].astype(F32)
        dst[...] = total

    finish(ta1, S.a1t[y], S.a1u, S.fa1)
    finish(tb1, S.b1t[x], S.b1u, S.fb1)
    finish(tb2, S.b2t[x], S.b2u, S.fb2)
    finish(ta2, S.a2t[y], S.a2u, S.fa2)

    S.zf[:, 72:80, :] = jnp.zeros((BLOCKS, 8, HALF), F32)
    for p in range(BLOCKS):
        six = slice(6 * p, 6 * p + 6)
        groups = [S.fa2[six, :HALF], S.fb2[six, :HALF], S.fb2[six, HALF:]]
        groups += [S.fa1[six, 1536:1920]]
        groups += [S.fa1[six, HALF * j : HALF * j + HALF] for j in range(4)]
        for g, rows6 in enumerate(groups):
            S.zf[p, 6 * g : 6 * g + 6, :] = rows6
        S.zf[p, 48:72, :] = S.fb1[24 * p : 24 * p + 24, :]
        S.zf[p, 72:78, :128] = S.fa2[six, HALF:]
        S.zs[p] = S.zf[p].astype(BF)

    def z_send(i, k, to):
        return remote(S.zs.at[k], O.zr.at[ki], M.zs_.at[i], M.zr_.at[ki], to)

    def last_sends(i, carry):
        dz, dc = far(i // 2), lax.rem(i, 2)
        z_send(i, key_of(dz, dc), dev(dz=dz, dc=dc)).start()
        return carry

    lax.fori_loop(1, BLOCKS, last_sends, 0)
    own = local(S.zs.at[ki], O.zr.at[ki], M.zs_.at[0])
    own.start()
    own.wait()

    def drain(i, carry):
        dz, dc = far(i // 2), lax.rem(i, 2)
        k = key_of(dz, dc)
        to = dev(dz=dz, dc=dc)
        out_send(i, k, to).wait_send()
        st_send(i, k, to).wait_send()
        ag_send(i, k, to).wait_send()
        s2_send(i, k, to).wait_send()
        dq_send(i, k, to).wait_send()
        remote(S.zs.at[k], O.zr.at[k], M.zs_.at[i], M.zr_.at[k], to).wait()
        return carry

    lax.fori_loop(1, BLOCKS, drain, 0)

    def drain_logits(i, carry):
        k = key_of(far(i // 2), lax.rem(i, 2))
        gl_local(i, k).wait()
        gl_remote(i, k).wait()
        return carry

    lax.fori_loop(0, BLOCKS, drain_logits, 0)
    for cp in hid_sends:
        cp.wait_send()
    for d in (1, 2, 3):
        hid_forward(d, key_of(far(jnp.int32(d)), 0)).wait_send()
    for dz in range(4):
        prev_remote(dz).wait_send()
    for cp in ra1 + rb1 + ra2 + rb2 + ta1 + tb1 + ta2 + tb2:
        cp.wait_send()


def main_kernel(args):
    any_space = pl.BlockSpec(memory_space=pl.ANY)
    in_specs = Args(*([any_space] * len(args)))._replace(
        lengths=pl.BlockSpec(memory_space=pltpu.SMEM)
    )
    vmem = pl.BlockSpec(memory_space=pltpu.VMEM)
    return pl.pallas_call(
        body,
        out_shape=[
            jax.ShapeDtypeStruct((TOK, D), BF),
            jax.ShapeDtypeStruct((TOK, D), BF),
            jax.ShapeDtypeStruct((2 * HEADS, BLOCKS * TOK, 128), BF),
            jax.ShapeDtypeStruct((BLOCKS, 80, HALF), BF),
        ],
        in_specs=list(in_specs),
        out_specs=[vmem, vmem, any_space, any_space],
        scratch_shapes=[pltpu.VMEM(s, t) for s, t in SCRATCH.values()]
        + [pltpu.SemaphoreType.DMA((n,)) for n in SEMS.values()],
        compiler_params=pltpu.CompilerParams(
            collective_id=0, has_side_effects=True, vmem_limit_bytes=60 * 2**20
        ),
        name="layer",
    )(*args)


def lay_out(oh, gh, gl, zr, *refs):
    outs, hold, sem = refs[:18], refs[18], refs[19]
    copies = []
    for i in range(PARTS):
        heads = pl.ds(2 * HEADS // PARTS * i, 2 * HEADS // PARTS)
        copies.append(pltpu.make_async_copy(gl.at[heads], hold.at[i], sem.at[0, i]))
        copies[-1].start()
    outs[0][...] = oh[...]
    outs[1][...] = gh[...]
    sums = []
    for half in range(2):
        total = zr[half].astype(F32)
        for zz in range(1, 4):
            total = total + zr[2 * zz + half].astype(F32)
        sums.append(total)
    both = jnp.concatenate(sums, axis=1)
    for g in range(4):
        outs[3 + g][...] = both[6 * g : 6 * g + 6, :]
    for half in range(2):
        for j in range(4):
            at = (4 * half + j) * HALF
            outs[7][:, at : at + HALF] = sums[half][24 + 6 * j : 30 + 6 * j, :]
    outs[8][...] = both[48:72, :]
    tail = sums[0][72:80, :128] + sums[1][72:80, :128]
    flipped = jnp.concatenate([tail, jnp.zeros((120, 128), F32)], axis=0).T
    for slot, row in ((9, 0), (10, 1), (11, 2), (13, 3), (14, 4), (15, 5), (16, 6), (17, 7)):
        outs[slot][...] = flipped[row, 0:6]
    inner = jnp.zeros((1, 128), F32)
    lane = iota((1, 128), 1)
    for i in range(6):
        for j in range(4):
            inner = jnp.where(lane == 4 * i + j, flipped[8 + j : 9 + j, i : i + 1], inner)
    outs[12][...] = inner[0, 0:24]
    for i in range(PARTS):
        heads = pl.ds(2 * HEADS // PARTS * i, 2 * HEADS // PARTS)
        copies[i].wait()
        copies[i] = pltpu.make_async_copy(hold.at[i], outs[2].at[heads], sem.at[1, i])
        copies[i].start()
    for copy in copies:
        copy.wait()


def out_kernel(oh, gh, gl, zr):
    vmem = pl.BlockSpec(memory_space=pltpu.VMEM)
    any_space = pl.BlockSpec(memory_space=pl.ANY)
    f = lambda *s: jax.ShapeDtypeStruct(s, F32)
    return pl.pallas_call(
        lay_out,
        out_shape=[
            jax.ShapeDtypeStruct((TOK, D), BF),
            jax.ShapeDtypeStruct((TOK, D), BF),
            jax.ShapeDtypeStruct((2 * HEADS, BLOCKS * TOK, 128), BF),
            f(6, D),
            f(6, D),
            f(6, D),
            f(6, D),
            f(6, FF),
            f(24, D),
            f(6),
            f(6),
            f(6),
            f(24),
            f(6),
            f(6),
            f(6),
            f(6),
            f(6),
        ],
        in_specs=[vmem, vmem, any_space, vmem],
        out_specs=[vmem, vmem, any_space] + [vmem] * 15,
        scratch_shapes=[
            pltpu.VMEM((PARTS, 2 * HEADS // PARTS, BLOCKS * TOK, 128), BF),
            pltpu.SemaphoreType.DMA((2, PARTS)),
        ],
        compiler_params=pltpu.CompilerParams(vmem_limit_bytes=60 * 2**20),
        name="lay_out",
    )(oh, gh, gl, zr)


def on_device(*args):
    return tuple(out_kernel(*main_kernel(args)))


def solution(mesh):
    rows = P(("batch", "keys"), None)
    logits = P(None, "batch", "keys")
    flat = P(("batch", "keys"))
    return jax.shard_map(
        on_device,
        mesh=mesh,
        in_specs=(rows, logits, P("batch", None), rows) + (P(),) * 15,
        out_specs=(rows, rows, logits) + (rows,) * 6 + (flat,) * 9,
        check_vma=False,
    )
```

```python
from types import SimpleNamespace
from typing import Any, NamedTuple

import jax
import jax.numpy as jnp
from jax import lax
from jax.experimental import pallas as pl
from jax.experimental.pallas import tpu as pltpu
from jax.sharding import PartitionSpec as P

EPSILON = 1e-05
NEGATIVE = -1e30
MESH = pl.DeviceIdType.MESH
BF = jnp.bfloat16
F32 = jnp.float32

TOK = 128
D = 768
HALF = 384
HEADS = 6
FF = 3072
SEQS = 16
BLOCKS = 8
PARTS = 4


def dot(a, b):
    return lax.dot_general(a, b, (((1,), (0,)), ((), ())), preferred_element_type=F32)


def dot_nt(a, b):
    return lax.dot_general(a, b, (((1,), (1,)), ((), ())), preferred_element_type=F32)


def dot_tn(a, b):
    return lax.dot_general(a, b, (((0,), (0,)), ((), ())), preferred_element_type=F32)


def iota(shape, dim):
    return lax.broadcasted_iota(jnp.int32, shape, dim)


def split_hi_lo(v):
    hi = v.astype(BF)
    lo = (v - hi.astype(F32)).astype(BF)
    return jnp.concatenate([hi.astype(F32), lo.astype(F32)], axis=0).astype(BF)


def head_rows():
    return jnp.where(iota((16, HALF), 1) // 64 == iota((16, HALF), 0) % 8, 1.0, 0.0).astype(BF)


def unit_rows():
    return jnp.where(iota((16, 128), 1) == iota((16, 128), 0), 1.0, 0.0).astype(BF)


def row_sums(v):
    return jnp.sum(v, axis=0, keepdims=True)


def norm(values):
    average = jnp.mean(values, axis=-1, keepdims=True)
    centered = values - average
    variance = jnp.mean(centered * centered, axis=-1, keepdims=True)
    inverse = lax.rsqrt(variance + EPSILON)
    return centered * inverse, inverse


def norm_back(upstream, normed, inverse, gain):
    scaled = upstream * gain
    return inverse * (
        scaled
        - jnp.mean(scaled, axis=-1, keepdims=True)
        - normed * jnp.mean(scaled * normed, axis=-1, keepdims=True)
    )


class Args(NamedTuple):
    hidden: Any
    prev: Any
    lengths: Any
    gout: Any
    w_q: Any
    w_k: Any
    w_v: Any
    w_o: Any
    w_i: Any
    w_u: Any
    b_q: Any
    b_v: Any
    b_o: Any
    b_i: Any
    b_u: Any
    g_a: Any
    b_a: Any
    g_f: Any
    b_f: Any


class Outs(NamedTuple):
    out_hidden: Any
    grad_hidden: Any
    gl: Any
    zrb: Any
    zra: Any
    wr: Any


SCRATCH = dict(
    wq=((2, D, HALF), BF),
    wk=((2, D, HALF), BF),
    wv=((2, D, HALF), BF),
    wo=((D, D), BF),
    wi=((4, D, D), BF),
    wu=((4, D, D), BF),
    vq=((D,), F32),
    vv=((D,), F32),
    vo=((D,), F32),
    vi=((FF,), F32),
    vu=((D,), F32),
    ga=((D,), F32),
    ba=((D,), F32),
    gf=((D,), F32),
    bf=((D,), F32),
    go=((TOK, D), BF),
    hid=((BLOCKS, TOK, D), BF),
    pv=((2, HEADS, BLOCKS * TOK, 128), BF),
    qs=((BLOCKS, TOK, HALF), BF),
    km=((HEADS, 256, 128), BF),
    ve=((HEADS, 256, 256), BF),
    madd=((TOK, 256), F32),
    obuf=((BLOCKS, TOK, HALF), BF),
    orecv=((BLOCKS, TOK, HALF), BF),
    st=((BLOCKS, 16, 128), F32),
    strecv=((BLOCKS, 16, 128), F32),
    at=((2, TOK, HALF), F32),
    atx=((2, TOK, D), BF),
    fx=((2, TOK, D), BF),
    n1=((TOK, D), F32),
    gs=((TOK, D), F32),
    gp=((4, TOK, D), F32),
    ax=((2, TOK, FF), BF),
    igs=((2, TOK, FF // 2), BF),
    igr=((TOK, FF // 2), BF),
    ogs=((2, TOK, HALF), BF),
    ogr=((TOK, HALF), BF),
    brs=((2, TOK, HALF), BF),
    brr=((TOK, HALF), BF),
    brow=((2, 16, HALF), F32),
    ags=((2, TOK, HALF), BF),
    dorecv=((BLOCKS, TOK, HALF), BF),
    s2=((2, 16, 128), F32),
    s2recv=((BLOCKS, 16, 128), F32),
    dkt=((HALF, 256), F32),
    dvt=((HALF, 256), F32),
    dq=((BLOCKS, TOK, HALF), BF),
    dqr=((2, 2, TOK, HALF), BF),
    dqo=((2, TOK, HALF), BF),
    dqh=((2, 2, 64, HALF), BF),
    kgs=((2, TOK, HALF), BF),
    kgr=((TOK, HALF), BF),
    vgs=((2, TOK, HALF), BF),
    vgr=((TOK, HALF), BF),
    a1s=((4, 192, 1920), BF),
    a1p=((2, 96, 1920), BF),
    a1r=((2, 192, 1920), BF),
    a1t=((4, 48, 1920), BF),
    a1u=((3, 48, 1920), BF),
    a2s=((4, 192, 128), BF),
    a2r=((3, 192, 128), BF),
    a2t=((4, 48, 128), BF),
    a2u=((3, 48, 128), BF),
    b1s=((4, 4, 192, HALF), BF),
    b1p=((2, 2, 192, HALF), BF),
    b1r=((2, 4, 192, HALF), BF),
    b1t=((4, 192, HALF), BF),
    b1u=((3, 192, HALF), BF),
    b2s=((4, 4, 48, 256), BF),
    b2r=((3, 4, 48, 256), BF),
    b2t=((4, 48, 256), BF),
    b2u=((3, 48, 256), BF),
    fa1=((48, 1920), F32),
    fa2=((48, 128), F32),
    fb1=((192, HALF), F32),
    fb2=((48, 256), F32),
    zf=((32, HALF), F32),
    zsb=((BLOCKS, 32, HALF), BF),
    zsa=((BLOCKS, 32, HALF), BF),
    zf2=((16, HALF), F32),
    zs2=((BLOCKS, 16, HALF), BF),
    qt=((BLOCKS, HALF, TOK), BF),
    kvt=((2, HALF, 256), BF),
    qgt=((2, HALF, TOK), BF),
    ykv=((256, BLOCKS * TOK), BF),
    yq=((128, BLOCKS * TOK), BF),
)
SEMS = dict(
    ld=21,
    outs=3,
    pl_=4,
    ps=1,
    pr=4,
    hs=1,
    hr=9,
    os=1,
    or_=1,
    ss=1,
    sr=1,
    xs=6,
    xr=6,
    ds=1,
    dr=6,
    es=1,
    er=4,
    rs=2,
    rh=4,
    rr=2,
    ts=6,
    tr=6,
    qs_=1,
    qr=4,
    gl_=1,
    gs_=1,
    gr=1,
    ks=1,
    kr=1,
    ys=1,
    yr=1,
    us=1,
    ur=1,
    zs_=1,
    zr_=1,
    vs=1,
    vr=1,
    ws=1,
    wr=1,
    own=3,
)


def body(*refs):
    na, no, nsc = len(Args._fields), len(Outs._fields), len(SCRATCH)
    A = Args(*refs[:na])
    O = Outs(*refs[na : na + no])
    S = SimpleNamespace(**dict(zip(SCRATCH, refs[na + no : na + no + nsc])))
    M = SimpleNamespace(**dict(zip(SEMS, refs[na + no + nsc : -1])))
    LEN = refs[-1]

    bi = lax.axis_index("batch")
    ki = lax.axis_index("keys")
    x, y = bi // 4, lax.rem(bi, 4)
    z, c = ki // 2, lax.rem(ki, 2)
    oc = 1 - c

    def dev(dx=0, dy=0, dz=0, dc=0):
        nb = lax.rem(x + dx, 4) * 4 + lax.rem(y + dy, 4)
        return (nb, lax.rem(z + dz, 4) * 2 + lax.rem(c + dc, 2))

    def key_of(dz, dc):
        return lax.rem(z + dz, 4) * 2 + lax.rem(c + dc, 2)

    def far(d):
        return d + (d // 2) * (1 - 2 * lax.rem(d, 2))

    def remote(src, dst, ssem, rsem, to):
        return pltpu.make_async_remote_copy(
            src_ref=src, dst_ref=dst, send_sem=ssem, recv_sem=rsem, device_id=to, device_id_type=MESH
        )

    def sent(sem, like):
        remote(like, like, sem, sem, dev(dc=1)).wait_send()

    def arrived(sem, like):
        remote(like, like, sem, sem, dev(dc=1)).wait_recv()

    def local(src, dst, sem):
        return pltpu.make_async_copy(src, dst, sem)

    loads = [
        local(A.hidden, S.hid.at[ki], M.ld.at[0]),
        local(A.w_k.at[:, pl.ds(pl.multiple_of(c * HALF, 128), HALF)], S.wk.at[c], M.ld.at[1]),
        local(A.w_v.at[:, pl.ds(pl.multiple_of(c * HALF, 128), HALF)], S.wv.at[c], M.ld.at[2]),
        local(A.w_q.at[:, pl.ds(pl.multiple_of(c * HALF, 128), HALF)], S.wq.at[c], M.ld.at[3]),
        local(A.b_q, S.vq, M.ld.at[4]),
        local(A.b_v, S.vv, M.ld.at[5]),
    ]
    lengths = local(A.lengths, LEN, M.ld.at[17])
    lengths.start()
    later = [
        local(A.w_o, S.wo, M.ld.at[6]),
        local(A.b_o, S.vo, M.ld.at[7]),
        local(A.b_i, S.vi, M.ld.at[8]),
        local(A.b_u, S.vu, M.ld.at[9]),
        local(A.g_a, S.ga, M.ld.at[10]),
        local(A.b_a, S.ba, M.ld.at[11]),
        local(A.g_f, S.gf, M.ld.at[12]),
        local(A.b_f, S.bf, M.ld.at[13]),
        local(A.gout, S.go, M.ld.at[14]),
    ]
    for j in range(4):
        later.append(local(A.w_i.at[:, pl.ds(D * j, D)], S.wi.at[j], M.ld.at[15]))
        later.append(local(A.w_u.at[pl.ds(D * j, D)], S.wu.at[j], M.ld.at[16]))
    last = [
        local(a.at[:, pl.ds(pl.multiple_of(oc * HALF, 128), HALF)], s.at[oc], M.outs.at[i])
        for i, (a, s) in enumerate(((A.w_q, S.wq), (A.w_k, S.wk), (A.w_v, S.wv)))
    ]
    for cp in loads:
        cp.start()

    def prev_rows(dz):
        return pl.ds(pl.multiple_of(lax.rem(z + dz, 4) * 256, 256), 256)

    def prev_local(dz):
        rows = prev_rows(dz)
        return local(
            A.prev.at[pl.ds(c * HEADS, HEADS), rows, :], S.pv.at[c, :, rows, :], M.pl_.at[dz]
        )

    def prev_remote(dz):
        rows = prev_rows(dz)
        return remote(
            A.prev.at[pl.ds(oc * HEADS, HEADS), rows, :],
            S.pv.at[c, :, rows, :],
            M.ps.at[0],
            M.pr.at[dz],
            dev(dc=1),
        )

    for dz in (0, 1, 3, 2):
        prev_local(dz).start()

    peers = [(0, 0, dz, dc) for dz in range(4) for dc in range(2) if dz or dc]
    peers += [(d, 0, 0, 0) for d in (1, 2, 3)] + [(0, d, 0, 0) for d in (1, 2, 3)]
    barrier = pltpu.get_barrier_semaphore()
    for off in peers:
        pl.semaphore_signal(barrier, inc=1, device_id=dev(*off), device_id_type=MESH)
    pl.semaphore_wait(barrier, len(peers))

    def rows_half(h):
        return pl.ds(64 * h, 64)

    def hid_send(i, src, k, rows, dz, dc):
        remote(src, S.hid.at[k, rows], M.hs.at[0], M.hr.at[i], dev(dz=dz, dc=dc)).start()

    def hid_arrival(i, k, rows):
        arrived(M.hr.at[i], S.hid.at[k, rows])

    low, high, whole = rows_half(0), rows_half(1), pl.ds(0, TOK)
    hid_send(3, A.hidden.at[low], ki, low, 1, 0)
    hid_send(2, A.hidden.at[high], ki, high, 3, 0)
    hid_send(0, A.hidden, ki, whole, 0, 1)
    hid_send(4, A.hidden.at[high], ki, high, 1, 0)
    hid_send(1, A.hidden.at[low], ki, low, 3, 0)
    prev_remote(0).start()
    prev_remote(1).start()
    prev_remote(3).start()
    prev_remote(2).start()

    bounds = []
    running = jnp.int32(0)
    lengths.wait()
    for j in range(SEQS):
        running = running + LEN[0, j]
        bounds.append(running)

    def segment_of(places):
        counted = jnp.zeros(places.shape, jnp.int32)
        for bound in bounds:
            counted = counted + jnp.where(places >= bound, 1, 0)
        return jnp.where(places < bounds[-1], counted, -1 - places)

    lane8 = iota((8, 128), 1)
    key_segment = [segment_of(lane8 * BLOCKS + z * 2 + half)[0:1, :] for half in range(2)]
    lane = iota((TOK, 128), 1)

    for cp in loads[:1] + loads[1:3] + loads[5:6]:
        cp.wait()
    hid_arrival(0, key_of(0, 1), whole)
    pair = pl.ds(z * 2, 2)
    hid_pair = S.hid[pair].reshape(256, D)
    key_rows = dot(hid_pair, S.wk[c]).astype(BF).astype(F32)
    bias_v = S.vv[...].reshape(1, D)
    bias_q = S.vq
    bv = jnp.where(c == 0, bias_v[:, :HALF], bias_v[:, HALF:])
    value_rows = (dot(hid_pair, S.wv[c]) + bv).astype(BF).astype(F32)
    lane2 = iota((256, 128), 1)
    for h in range(HEADS):
        g, e = h // 2, h % 2
        mine = lane2 // 64 == e
        S.km[h] = jnp.where(mine, key_rows[:, 128 * g : 128 * g + 128], 0.0).astype(BF)
        S.ve[h, :, :128] = jnp.where(mine, value_rows[:, 128 * g : 128 * g + 128], 0.0).astype(BF)
        S.ve[h, :, 128:] = jnp.where((lane2 == h) | (lane2 == 8 + h), 1.0, 0.0).astype(BF)
    loads[3].wait()
    loads[4].wait()
    bias_q = S.vq[...].reshape(1, D)
    S.brow[...] = jnp.zeros((2, 16, HALF), F32)
    S.ykv[...] = jnp.zeros((256, BLOCKS * TOK), BF)
    S.yq[...] = jnp.zeros((128, BLOCKS * TOK), BF)
    S.zf[...] = jnp.zeros((32, HALF), F32)
    S.zf2[...] = jnp.zeros((16, HALF), F32)
    for cp in later + last:
        cp.start()

    def out_send(k, to):
        return remote(S.obuf.at[k], S.orecv.at[ki], M.os.at[0], M.or_.at[0], to)

    def st_send(k, to):
        return remote(S.st.at[k], S.strecv.at[ki], M.ss.at[0], M.sr.at[0], to)

    def forward(i, carry):
        ring = (i + 2) // 4
        odd = lax.rem(ring, 2)
        dz = ring + odd * 2 * lax.rem(i, 2)
        dc = (1 - odd) * lax.rem(i, 2) + odd * (i // 4)
        k = key_of(dz, dc)

        @pl.when(i == 2)
        def _():
            above, below = key_of(1, 0), key_of(3, 0)
            hid_arrival(3, below, low)
            hid_send(7, S.hid.at[below, low], below, low, 1, 0)
            hid_arrival(2, above, high)
            hid_send(7, S.hid.at[above, high], above, high, 3, 0)
            hid_arrival(1, above, low)
            hid_send(5, S.hid.at[above], above, whole, 0, 1)

        @pl.when(i == 3)
        def _():
            hid_arrival(4, k, high)
            hid_send(6, S.hid.at[k], k, whole, 0, 1)

        @pl.when(i >= 4)
        def _():
            hid_arrival(i + 1, k, whole)

        @pl.when(i == 6)
        def _():
            hid_send(8, S.hid.at[k], k, whole, 0, 1)

        @pl.when(dc == 0)
        def _():
            prev_local(dz).wait()
            prev_remote(dz).wait_recv()

        bq = jnp.where(c == 0, bias_q[:, :HALF], bias_q[:, HALF:])
        queries = (dot(S.hid[k], S.wq[c]) + bq).astype(BF).astype(F32) * 0.125
        S.qs[k] = queries.astype(BF)
        S.qt[k] = queries.T.astype(BF)
        row_segment = segment_of(iota((TOK, 128), 0) * BLOCKS + k)
        for half in range(2):
            S.madd[:, 128 * half : 128 * half + 128] = jnp.where(
                row_segment == key_segment[half], 0.0, NEGATIVE
            )
        rows = pl.ds(pl.multiple_of(k * TOK, TOK), TOK)
        totals = jnp.zeros((TOK, 128), F32)
        tops = jnp.zeros((TOK, 128), F32)
        for g in range(3):
            two = S.qs[k, :, 128 * g : 128 * g + 128]
            mixed = jnp.zeros((TOK, 128), F32)
            for h in (2 * g, 2 * g + 1):
                before = jnp.concatenate([S.pv[0, h, rows, :], S.pv[1, h, rows, :]], axis=1)
                s = dot_nt(two, S.km[h]) + before.astype(F32) + S.madd[...]
                top = jnp.max(s, axis=1, keepdims=True)
                p = jnp.exp(s - top).astype(BF)
                S.pv[0, h, rows, :] = p[:, :128]
                S.pv[1, h, rows, :] = p[:, 128:]
                o = dot(p, S.ve[h])
                mixed = mixed + o[:, :128]
                totals = totals + o[:, 128:]
                tops = jnp.where(lane == 8 + h, top, tops)
            S.obuf[k, :, 128 * g : 128 * g + 128] = mixed.astype(BF)
        stats = jnp.where(lane < 8, totals, tops)
        S.st[k] = stats.T[:16, :]

        @pl.when(i > 0)
        def _():
            to = dev(dz=dz, dc=dc)
            out_send(k, to).start()
            st_send(k, to).start()

        return carry

    lax.fori_loop(0, BLOCKS, forward, 0)

    S.orecv[ki] = S.obuf[ki]
    S.strecv[ki] = S.st[ki]

    seven = pl.ds(0, 7)
    arrived(M.or_.at[0], S.orecv.at[seven])
    arrived(M.sr.at[0], S.strecv.at[seven])
    row8 = iota((8, 128), 0)
    spread = head_rows()
    lse = []
    for half in range(2):
        tops = [S.strecv[2 * zz + half, 8:16, :] for zz in range(4)]
        sums = [S.strecv[2 * zz + half, 0:8, :] for zz in range(4)]
        top = jnp.maximum(jnp.maximum(tops[0], tops[1]), jnp.maximum(tops[2], tops[3]))
        shares = [jnp.exp(t - top) for t in tops]
        total = shares[0] * sums[0] + shares[1] * sums[1] + shares[2] * sums[2] + shares[3] * sums[3]
        total = jnp.where(row8 < HEADS, total, 1.0)
        lse.append(jnp.where(row8 < HEADS, top + jnp.log(total), 0.0))
        acc = jnp.zeros((TOK, HALF), F32)
        for zz in range(4):
            factor = dot_tn(split_hi_lo(jnp.where(row8 < HEADS, shares[zz] / total, 0.0)), spread)
            acc = acc + S.orecv[2 * zz + half].astype(F32) * factor
        S.at[half] = acc
        S.atx[0, :, HALF * half : HALF * half + HALF] = acc.astype(BF)

    other = dev(dc=1)

    def swap(i, src, dst):
        copy = remote(src, dst, M.xs.at[i], M.xr.at[i], other)
        copy.start()
        return copy

    swap_at = swap(0, S.atx.at[0], S.atx.at[1])

    def vec(ref):
        return ref[...].reshape(1, -1)

    for cp in later[:9]:
        cp.wait()
    local(S.wi, S.wi, M.ld.at[15]).wait()
    local(S.wu, S.wu, M.ld.at[16]).wait()
    attn_low = S.atx[0]
    first_sum = S.hid[ki].astype(F32) + dot(attn_low, S.wo[...]) + vec(S.vo)
    normed, inverse_a = norm(first_sum)
    S.n1[...] = normed
    S.fx[0] = (normed * vec(S.ga) + vec(S.ba)).astype(BF)
    swap_fx = swap(1, S.fx.at[0], S.fx.at[1])
    second = normed * vec(S.ga) + vec(S.ba) + vec(S.vu)
    bias_i = vec(S.vi)
    for j in range(4):
        inner = dot(S.fx[0], S.wi[j]) + bias_i[:, D * j : D * j + D]
        cdf = 0.5 + 0.5 * lax.erf(inner * 0.7071067811865476)
        density = jnp.exp(inner * inner * -0.5) * 0.3989422804014327
        S.gp[j] = cdf + inner * density
        S.ax[0, :, D * j : D * j + D] = (inner * cdf).astype(BF)
        col = pl.ds(D * j, D)
        swap(2, S.ax.at[0, :, col], S.ax.at[1, :, col])
        second = second + dot(S.ax[0, :, D * j : D * j + D], S.wu[j])
    normed_f, inverse_f = norm(second)
    O.out_hidden[...] = (normed_f * vec(S.gf) + vec(S.bf)).astype(BF)
    upstream = S.go[...].astype(F32)

    def put_row(r, values):
        sums = row_sums(values)
        S.brow[0, r : r + 1, :] = sums[:, :HALF]
        S.brow[1, r : r + 1, :] = sums[:, HALF:]

    put_row(6, upstream * normed_f)
    put_row(7, upstream)
    grad_second = norm_back(upstream, normed_f, inverse_f, vec(S.gf))
    og = grad_second.astype(BF)
    put_row(3, og.astype(F32))
    S.ogs[0] = og[:, :HALF]
    S.ogs[1] = og[:, HALF:]
    swap_og = swap(3, S.ogs.at[oc], S.ogr)
    S.gs[...] = grad_second
    bsum = []
    for j in range(4):
        ig = (dot_nt(og, S.wu[j]) * S.gp[j]).astype(BF)
        S.igs[j // 2, :, D * (j % 2) : D * (j % 2) + D] = ig
        bsum.append(row_sums(ig.astype(F32)))
        S.gs[...] = S.gs[...] + dot_nt(ig, S.wi[j])
    swap_ig = swap(4, S.igs.at[oc], S.igr)

    grad_first = S.gs[...]
    normed = S.n1[...]
    put_row(4, grad_first * normed)
    put_row(5, grad_first)
    grad_first_sum = norm_back(grad_first, normed, inverse_a, vec(S.ga))
    S.gs[...] = grad_first_sum
    br = grad_first_sum.astype(BF)
    put_row(2, br.astype(F32))
    S.brs[0] = br[:, :HALF]
    S.brs[1] = br[:, HALF:]
    swap_br = swap(5, S.brs.at[oc], S.brr)
    ag = dot_nt(br, S.wo[...]).astype(BF)
    for half in range(2):
        S.ags[half] = ag[:, HALF * half : HALF * half + HALF]
        product = S.at[half] * ag[:, HALF * half : HALF * half + HALF].astype(F32)
        dots = jnp.zeros((16, TOK), F32)
        hi = product.astype(BF)
        lo = (product - hi.astype(F32)).astype(BF)
        dots = dot_nt(spread, hi) + dot_nt(spread, lo)
        S.s2[half, 0:8, :] = dots[0:8, :]
        S.s2[half, 8:16, :] = lse[half]

    def ag_send(i, src, k, rows, dz, dc):
        remote(src, S.dorecv.at[k, rows], M.ds.at[0], M.dr.at[i], dev(dz=dz, dc=dc)).start()

    def ag_arrival(i, dz, rows):
        arrived(M.dr.at[i], S.dorecv.at[pl.ds(lax.rem(z + dz, 4) * 2, 2), rows])

    def s2_send(i, dz, dc):
        half = lax.rem(c + dc, 2)
        remote(S.s2.at[half], S.s2recv.at[ki], M.es.at[0], M.er.at[i], dev(dz=dz, dc=dc)).start()

    def s2_arrival(i, dz):
        arrived(M.er.at[i], S.s2recv.at[pl.ds(lax.rem(z + dz, 4) * 2, 2)])

    for i, dz, rows in ((3, 1, low), (2, 3, high)):
        for dc in range(2):
            ag_send(i, S.ags.at[lax.rem(c + dc, 2), rows], ki, rows, dz, dc)
    ag_send(0, S.ags.at[oc], ki, whole, 0, 1)
    s2_send(0, 0, 1)
    for i, dz, rows in ((4, 1, high), (1, 3, low)):
        for dc in range(2):
            ag_send(i, S.ags.at[lax.rem(c + dc, 2), rows], ki, rows, dz, dc)
    for i, dz in ((2, 1), (1, 3), (3, 2)):
        for dc in range(2):
            s2_send(i, dz, dc)
    S.dorecv[ki] = S.ags[c]
    S.s2recv[ki] = S.s2[c]

    def weight_grad(left, right):
        return dot_tn(left, right).astype(BF)

    def along(axis, d):
        return dev(dx=d) if axis == 0 else dev(dy=d)

    def at_place(axis, d):
        return lax.rem((x if axis == 0 else y) + d, 4)

    class Ring:
        def __init__(self, n, axis, piece, held, landed):
            right, left = along(axis, 1), along(axis, 3)
            after, before, across = at_place(axis, 1), at_place(axis, 3), at_place(axis, 2)

            def copy(sem, src, dst, to):
                return remote(src, dst, M.rs.at[n], sem, to)

            here = M.rr.at[n]
            self.n = n

            self.first = [
                copy(M.rh.at[2 * n], piece(across, 0), held.at[0], right),
                copy(M.rh.at[2 * n + 1], piece(across, 1), held.at[1], left),
            ]
            self.own = [
                copy(here, piece(after, 1), landed(0, 1), right),
                copy(here, piece(before, 0), landed(1, 0), left),
            ]
            self.summed = [
                copy(here, held.at[0], landed(0, 0), right),
                copy(here, held.at[1], landed(1, 1), left),
            ]
            self.add = [(held.at[0], piece(after, 0)), (held.at[1], piece(before, 1))]

        def start(self, copies):
            for cp in copies:
                cp.start()

        def pass_on(self):
            for w in range(2):
                self.first[w].wait_recv()
                mine, extra = self.add[w]
                mine[...] = (mine[...].astype(F32) + extra[...].astype(F32)).astype(BF)
                self.summed[w].start()

        def landed(self, both):
            arrived(M.rr.at[self.n], both)

        def drain(self, three):
            sent(M.rs.at[self.n], three)

    for cp in [swap_fx, swap_ig]:
        cp.wait()
    first_two = S.fx[...].reshape(256, D)
    for j in range(4):
        col = slice(HALF * j, HALF * j + HALF)
        right = jnp.concatenate([S.igs[c, :, col], S.igr[:, col]], axis=0)
        S.a1s[:, :, col] = weight_grad(first_two, right).reshape(4, 192, HALF)
    for cp in [swap_at, swap_br]:
        cp.wait()
    right = jnp.concatenate([S.brs[c], S.brr[...]], axis=0)
    S.a1s[:, :, 1536:1920] = weight_grad(S.atx[...].reshape(256, D), right).reshape(4, 192, HALF)
    ring_a = Ring(
        0,
        0,
        lambda p, h: S.a1s.at[p, pl.ds(96 * h, 96)],
        S.a1p,
        lambda w, h: S.a1r.at[w, pl.ds(96 * h, 96)],
    )
    ring_a.start(ring_a.first)
    remote(S.ax.at[0], S.ax.at[1], M.xs.at[2], M.xr.at[2], other).wait()
    swap_og.wait()
    right = jnp.concatenate([S.ogs[c], S.ogr[...]], axis=0)
    for j in range(4):
        left = S.ax[:, :, D * j : D * j + D].reshape(256, D)
        S.b1s[j] = weight_grad(left, right).reshape(4, 192, HALF)
    ring_b = Ring(
        1,
        1,
        lambda p, h: S.b1s.at[pl.ds(2 * h, 2), p],
        S.b1p,
        lambda w, h: S.b1r.at[w, pl.ds(2 * h, 2)],
    )
    ring_b.start(ring_b.first)


    lane512 = iota((8, 512), 1)
    sub512 = iota((8, 512), 0)
    pick = jnp.where(
        iota((512, 128), 1) == (iota((512, 128), 0) // 128) * 32 + lax.rem(iota((512, 128), 0), 128) // 4,
        1.0,
        0.0,
    ).astype(BF)
    flat = jnp.concatenate(bsum, axis=1)
    for g in range(6):
        spread_out = jnp.where(lax.rem(lane512, 4) == sub512, flat[:, 512 * g : 512 * g + 512], 0.0)
        S.brow[g // 3, 8:16, 128 * (g % 3) : 128 * (g % 3) + 128] = dot(spread_out.astype(BF), pick)


    def scatter(n, axis, src, dst, inner):
        for d in (1, 2, 3):
            there = at_place(axis, d)
            piece = src.at[:, there] if inner else src.at[there]
            remote(piece, dst.at[d - 1], M.ts.at[n], M.tr.at[n], along(axis, d)).start()

    S.dkt[...] = jnp.zeros((HALF, 256), F32)
    S.dvt[...] = jnp.zeros((HALF, 256), F32)
    units = unit_rows()

    def dq_landing(w, half, h):
        return S.dqr.at[w, half, rows_half(h)], M.qr.at[2]

    def dq_copy(src, place, to):
        return remote(src, place[0], M.qs_.at[0], place[1], to)

    def dq_piece(dz, h):
        return S.dq.at[pl.ds(lax.rem(z + dz, 4) * 2, 2), rows_half(h)]

    dq_partner = dq_copy(S.dq.at[z * 2 + oc], (S.dqo.at[c], M.qr.at[3]), other)
    dq_first = [
        dq_copy(dq_piece(2, 0), (S.dqh.at[0], M.qr.at[0]), dev(dz=1)),
        dq_copy(dq_piece(2, 1), (S.dqh.at[1], M.qr.at[1]), dev(dz=3)),
    ]
    dq_own, dq_summed = [], []
    for w, dz in ((0, 1), (1, 3)):
        h = 1 - w
        dq_own.append(
            [
                dq_copy(
                    S.dq.at[lax.rem(z + dz, 4) * 2 + cc, rows_half(h)],
                    dq_landing(w, c, h),
                    (bi, lax.rem(z + dz, 4) * 2 + cc),
                )
                for cc in range(2)
            ]
        )
        h = w
        dq_summed.append(
            [
                dq_copy(
                    S.dqh.at[w, cc],
                    dq_landing(w, c, h),
                    (bi, lax.rem(z + dz, 4) * 2 + cc),
                )
                for cc in range(2)
            ]
        )

    def gl_rows(zz):
        return pl.ds(pl.multiple_of(zz * 256, 256), 256)

    def gl_local(k):
        rows = gl_rows(k)
        return local(
            S.pv.at[c, :, rows, :], O.gl.at[pl.ds(c * HEADS, HEADS), rows, :], M.gl_.at[0]
        )

    def gl_remote(k):
        rows = gl_rows(k)
        return remote(
            S.pv.at[oc, :, rows, :],
            O.gl.at[pl.ds(c * HEADS, HEADS), rows, :],
            M.gs_.at[0],
            M.gr.at[0],
            dev(dc=1),
        )

    def backward(i, carry):
        dz = far(i)
        zz = lax.rem(z + dz, 4)

        @pl.when(i == 2)
        def _():
            ring_a.start(ring_a.own)
            ring_b.start(ring_b.own)

        @pl.when(i == 0)
        def _():
            arrived(M.dr.at[0], S.dorecv.at[key_of(0, 1)])
            arrived(M.er.at[0], S.s2recv.at[key_of(0, 1)])

        @pl.when(i == 1)
        def _():
            ag_arrival(3, 3, low)
            for dc in range(2):
                k = key_of(3, dc)
                ag_send(5, S.dorecv.at[k, low], k, low, 1, 0)
            ag_arrival(2, 1, high)
            for dc in range(2):
                k = key_of(1, dc)
                ag_send(5, S.dorecv.at[k, high], k, high, 3, 0)
            ag_arrival(1, 1, low)
            s2_arrival(1, 1)

        @pl.when(i == 2)
        def _():
            ag_arrival(4, 3, high)
            s2_arrival(2, 3)

        @pl.when(i == 3)
        def _():
            ag_arrival(5, 2, whole)
            s2_arrival(3, 2)

        rows = pl.ds(pl.multiple_of(zz * 256, 256), 256)
        factors, minuses = [], []
        for half in range(2):
            k = zz * 2 + half
            share = jnp.exp(S.st[k, 8:16, :] - S.s2recv[k, 8:16, :])
            share = jnp.where(row8 < HEADS, share, 0.0)
            minuses.append(dot_tn(split_hi_lo(S.s2recv[k, 0:8, :] * share * -1.0), units).astype(BF))
            factors.append(dot_tn(split_hi_lo(share), spread))
        minus = jnp.concatenate(minuses, axis=0)
        two = pl.ds(zz * 2, 2)
        scaled = S.dorecv[two].reshape(256, HALF).astype(F32) * jnp.concatenate(factors, axis=0)
        scaled_t = scaled.T.astype(BF)
        scaled = scaled.astype(BF)
        queries_t = jnp.concatenate([S.qt[zz * 2], S.qt[zz * 2 + 1]], axis=1)
        for g in range(3):
            left = jnp.concatenate([scaled[:, 128 * g : 128 * g + 128], minus], axis=1)
            partial = jnp.zeros((256, 128), F32)
            for h in (2 * g, 2 * g + 1):
                p = jnp.concatenate([S.pv[0, h, rows, :], S.pv[1, h, rows, :]], axis=1)
                grad = (p.astype(F32) * dot_nt(left, S.ve[h])).astype(BF)
                S.pv[0, h, rows, :] = grad[:, :128]
                S.pv[1, h, rows, :] = grad[:, 128:]
                at = slice(64 * h, 64 * h + 64)
                S.dvt[at, :] = S.dvt[at, :] + dot(scaled_t[at, :], p)
                S.dkt[at, :] = S.dkt[at, :] + dot(queries_t[at, :], grad)
                partial = partial + dot(grad, S.km[h])
            partial = (partial * 0.125).astype(BF).reshape(2, TOK, 128)
            S.dq[two, :, 128 * g : 128 * g + 128] = partial

        @pl.when(i == 0)
        def _():
            dq_partner.start()

        @pl.when(i == 1)
        def _():
            for cp in dq_own[0]:
                cp.start()

        @pl.when(i == 2)
        def _():
            for cp in dq_own[1]:
                cp.start()

        @pl.when(i == 3)
        def _():
            for cp in dq_first:
                cp.start()

        gl_local(zz).start()
        gl_remote(zz).start()
        return carry

    lax.fori_loop(0, 4, backward, 0)
    S.dqo[c] = S.dq[ki]

    S.kvt[0] = S.dkt[...].astype(BF)
    S.kvt[1] = S.dvt[...].astype(BF)
    mine = pl.ds(pl.multiple_of(z * 256, 256), 256)
    for d in (1, 3, 2):
        there = pl.ds(pl.multiple_of(lax.rem(z + d, 4) * 96, 32), 96)
        for t in range(2):
            (
                remote(
                    S.kvt.at[t, there, :],
                    S.ykv.at[pl.ds(128 * t, 96), mine],
                    M.ys.at[0],
                    M.yr.at[0],
                    dev(dz=d),
                ).start()
            )
    here = pl.ds(pl.multiple_of(z * 96, 32), 96)
    for t in range(2):
        S.ykv[128 * t : 128 * t + 96, mine] = S.kvt[t, here, :]
    key_grad = S.dkt[...].T.astype(BF)
    value_grad = S.dvt[...].T.astype(BF)
    S.kgs[...] = key_grad.reshape(2, TOK, HALF)
    S.vgs[...] = value_grad.reshape(2, TOK, HALF)
    kv_swaps = [
        remote(S.kgs.at[oc], S.kgr, M.ks.at[0], M.kr.at[0], other),
        remote(S.vgs.at[oc], S.vgr, M.ks.at[0], M.kr.at[0], other),
    ]
    for cp in kv_swaps:
        cp.start()
    S.brow[c, 1:2, :] = row_sums(value_grad.astype(F32))
    ring_a.pass_on()
    ring_b.pass_on()

    for cp in last:
        cp.wait()
    arrived(M.kr.at[0], S.kgs)
    total = S.gs[...]
    total = total + dot_nt(S.kgs[c], S.wk[c]) + dot_nt(S.kgr[...], S.wk[oc])
    total = total + dot_nt(S.vgs[c], S.wv[c]) + dot_nt(S.vgr[...], S.wv[oc])
    S.gs[...] = total

    def sum_a(src, recv, dst):
        def step(j, carry):
            part = pl.ds(pl.multiple_of(j * 48, 16), 48)
            total = src[x, part, :].astype(F32)
            for d in range(recv.shape[0]):
                total = total + recv[d, part, :].astype(F32)
            dst[j] = total.astype(BF)
            return carry

        lax.fori_loop(0, 4, step, 0)

    def sum_b(src, recv, dst):
        def step(j, carry):
            total = src[j, y].astype(F32)
            for d in range(recv.shape[0]):
                total = total + recv[d, j].astype(F32)
            dst[j] = total.astype(BF)
            return carry

        lax.fori_loop(0, 4, step, 0)

    def finish(n, own, recv, dst):
        arrived(M.tr.at[n], recv)
        total = own.astype(F32)
        for d in range(3):
            total = total + recv[d].astype(F32)
        dst[...] = total

    for w in range(2):
        dq_first[w].wait_recv()
        add = dq_piece((1, 3)[w], w)[...].astype(F32)
        S.dqh[w] = (S.dqh[w].astype(F32) + add).astype(BF)
        for cp in dq_summed[w]:
            cp.start()
    dq_partner.wait_recv()
    arrived(M.qr.at[2], S.dqr)
    query_grads = []
    for half in range(2):
        grad = S.dqr[0, half].astype(F32) + S.dqr[1, half].astype(F32) + S.dqo[half].astype(F32)
        S.qgt[half] = grad.T.astype(BF)
        query_grads.append(grad.astype(BF))

    my_rows = pl.ds(pl.multiple_of(ki * TOK, TOK), TOK)

    def column_rows(k):
        return pl.ds(pl.multiple_of((k // 2) * 96, 32), 96)

    def yq_send(k, to):
        return remote(
            S.qgt.at[lax.rem(k, 2), column_rows(k), :],
            S.yq.at[pl.ds(0, 96), my_rows],
            M.us.at[0],
            M.ur.at[0],
            to,
        )

    def send_columns(i, carry):
        dz, dc = far(i // 2), lax.rem(i, 2)
        yq_send(key_of(dz, dc), dev(dz=dz, dc=dc)).start()
        return carry

    lax.fori_loop(1, BLOCKS, send_columns, 0)
    S.yq[0:96, my_rows] = S.qgt[c, here, :]

    arrived(M.yr.at[0], S.kvt.at[:, pl.ds(0, 288)])
    hid_all = S.hid[...].reshape(BLOCKS * TOK, D)
    flipped = dot(S.ykv[...], hid_all)
    for t in range(2):
        grad = flipped[128 * t : 128 * t + 128, :].T.astype(BF)
        S.b2s[:, :, :, 128 * t : 128 * t + 128] = grad.reshape(4, 4, 48, 128)
    scatter(0, 1, S.b2s, S.b2r, True)

    ring_b.landed(S.b1r)
    sum_b(S.b1s, S.b1r, S.b1t)
    scatter(2, 0, S.b1t, S.b1u, False)

    ring_a.landed(S.a1r)
    sum_a(S.a1s, S.a1r, S.a1t)
    scatter(3, 1, S.a1t, S.a1u, False)

    total = S.gs[...]
    for half in range(2):
        S.brow[half, 0:1, :] = row_sums(query_grads[half].astype(F32))
        total = total + dot_nt(query_grads[half], S.wq[half])
    O.grad_hidden[...] = total.astype(BF)

    arrived(M.tr.at[0], S.b2r)
    sum_b(S.b2s, S.b2r, S.b2t)
    scatter(4, 0, S.b2t, S.b2u, False)

    arrived(M.ur.at[0], S.qgt.at[:, pl.ds(0, 336)])
    beside = jnp.where(iota((16, 128), 1) == iota((16, 128), 0) + 96, 1.0, 0.0).astype(BF)
    flipped = dot(S.yq[...], hid_all).T
    for half in range(2):
        columns = dot_tn(S.brow[half].astype(BF), beside)
        columns = columns + flipped[HALF * half : HALF * half + HALF, :]
        S.a2s[2 * half : 2 * half + 2] = columns.astype(BF).reshape(2, 192, 128)
    scatter(1, 0, S.a2s, S.a2r, False)

    finish(2, S.b1t[x], S.b1u, S.fb1)
    for p in range(BLOCKS):
        S.zf[0:24, :] = S.fb1[24 * p : 24 * p + 24, :]
        S.zsb[p] = S.zf[...].astype(BF)

    def zb_send(k, to):
        return remote(S.zsb.at[k], O.zrb.at[ki], M.zs_.at[0], M.zr_.at[0], to)

    def za_send(k, to):
        return remote(S.zsa.at[k], O.zra.at[ki], M.vs.at[0], M.vr.at[0], to)

    def w_send(k, to):
        return remote(S.zs2.at[k], O.wr.at[ki], M.ws.at[0], M.wr.at[0], to)

    def to_all(send):
        def step(i, carry):
            dz, dc = far(i // 2), lax.rem(i, 2)
            send(key_of(dz, dc), dev(dz=dz, dc=dc)).start()
            return carry

        lax.fori_loop(1, BLOCKS, step, 0)

    to_all(zb_send)
    own = [
        local(S.zsb.at[ki], O.zrb.at[ki], M.own.at[0]),
        local(S.zsa.at[ki], O.zra.at[ki], M.own.at[1]),
        local(S.zs2.at[ki], O.wr.at[ki], M.own.at[2]),
    ]
    own[0].start()

    arrived(M.tr.at[1], S.a2r)
    sum_a(S.a2s, S.a2r, S.a2t)
    scatter(5, 1, S.a2t, S.a2u, False)

    finish(3, S.a1t[y], S.a1u, S.fa1)
    for p in range(BLOCKS):
        six = slice(6 * p, 6 * p + 6)
        S.zf[0:6, :] = S.fa1[six, 1536:1920]
        for j in range(4):
            S.zf[6 + 6 * j : 12 + 6 * j, :] = S.fa1[six, HALF * j : HALF * j + HALF]
        S.zsa[p] = S.zf[...].astype(BF)
    to_all(za_send)
    own[1].start()

    finish(4, S.b2t[x], S.b2u, S.fb2)
    finish(5, S.a2t[y], S.a2u, S.fa2)
    for p in range(BLOCKS):
        six = slice(6 * p, 6 * p + 6)
        S.zf2[0:6, :128] = S.fa2[six, :]
        S.zf2[0:6, 128:] = S.fb2[six, :]
        S.zs2[p] = S.zf2[...].astype(BF)
    to_all(w_send)
    own[2].start()

    sent(M.os.at[0], S.obuf.at[seven])
    sent(M.ss.at[0], S.st.at[seven])
    sent(M.es.at[0], S.s2recv.at[seven])
    sent(M.us.at[0], S.qgt.at[:, pl.ds(0, 336)])
    sent(M.ys.at[0], S.kvt.at[:, pl.ds(0, 288)])
    sent(M.ks.at[0], S.kgs)
    sent(M.ds.at[0], S.dorecv.at[seven])
    sent(M.qs_.at[0], S.dq.at[seven])
    for ssem, rsem, like in (
        (M.zs_, M.zr_, S.zsb),
        (M.vs, M.vr, S.zsa),
        (M.ws, M.wr, S.zs2),
    ):
        sent(ssem.at[0], like.at[seven])
        arrived(rsem.at[0], like.at[seven])
    local(S.pv.at[c], S.pv.at[c], M.gl_.at[0]).wait()
    sent(M.gs_.at[0], S.pv.at[oc])
    arrived(M.gr.at[0], S.pv.at[oc])
    sent(M.hs.at[0], S.hid.at[pl.ds(0, 7)])
    sent(M.ps.at[0], S.pv.at[0])
    for n, like in enumerate((S.b2r, S.a2r, S.b1u, S.a1u, S.b2u, S.a2u)):
        sent(M.ts.at[n], like)
    for cp in own:
        cp.wait()
    ring_a.drain(S.a1s.at[pl.ds(0, 3)])
    ring_b.drain(S.b1s.at[:, pl.ds(0, 3)])


def main_kernel(args):
    any_space = pl.BlockSpec(memory_space=pl.ANY)
    vmem = pl.BlockSpec(memory_space=pltpu.VMEM)
    return pl.pallas_call(
        body,
        out_shape=[
            jax.ShapeDtypeStruct((TOK, D), BF),
            jax.ShapeDtypeStruct((TOK, D), BF),
            jax.ShapeDtypeStruct((2 * HEADS, BLOCKS * TOK, 128), BF),
            jax.ShapeDtypeStruct((BLOCKS, 32, HALF), BF),
            jax.ShapeDtypeStruct((BLOCKS, 32, HALF), BF),
            jax.ShapeDtypeStruct((BLOCKS, 16, HALF), BF),
        ],
        in_specs=[any_space] * len(args),
        out_specs=[vmem, vmem] + [any_space] * 4,
        scratch_shapes=[pltpu.VMEM(s, t) for s, t in SCRATCH.values()]
        + [pltpu.SemaphoreType.DMA((n,)) for n in SEMS.values()]
        + [pltpu.SMEM((1, SEQS), jnp.int32)],
        compiler_params=pltpu.CompilerParams(
            collective_id=0, has_side_effects=True, vmem_limit_bytes=60 * 2**20
        ),
        name="layer",
    )(*args)


def lay_out(oh, gh, gl, zrb, zra, wr, *refs):
    outs = refs[:18]
    hold, v_oh, v_gh, v_zrb, v_zra, v_wr, sem, sem2 = refs[18:]
    copies = []
    for i in range(PARTS):
        heads = pl.ds(2 * HEADS // PARTS * i, 2 * HEADS // PARTS)
        copies.append(pltpu.make_async_copy(gl.at[heads], hold.at[i], sem.at[0, i]))
        copies[-1].start()
    small = [
        pltpu.make_async_copy(src, dst, sem2.at[i])
        for i, (src, dst) in enumerate(((zrb, v_zrb), (zra, v_zra), (wr, v_wr), (oh, v_oh), (gh, v_gh)))
    ]
    for copy in small:
        copy.start()
    for copy in small:
        copy.wait()
    small = [
        pltpu.make_async_copy(v_oh, outs[0], sem2.at[0]),
        pltpu.make_async_copy(v_gh, outs[1], sem2.at[1]),
    ]
    for copy in small:
        copy.start()

    def summed(ref):
        out = []
        for half in range(2):
            total = ref[half].astype(F32)
            for zz in range(1, 4):
                total = total + ref[2 * zz + half].astype(F32)
            out.append(total)
        return out

    sums, outer = summed(v_zra), summed(v_zrb)
    tail = jnp.zeros((8, 128), F32)
    for k in range(BLOCKS):
        rows = v_wr[k].astype(F32)
        tail = tail + rows[0:8, :128]
        at = (k % 2) * HALF + (k // 2) * 96
        for t in range(3):
            outs[3 + t][:, at : at + 96] = rows[0:6, 128 * t : 128 * t + 96]
    outs[6][...] = jnp.concatenate([sums[0][0:6, :], sums[1][0:6, :]], axis=1)
    for half in range(2):
        for j in range(4):
            at = (4 * half + j) * HALF
            outs[7][:, at : at + HALF] = sums[half][6 + 6 * j : 12 + 6 * j, :]
    outs[8][...] = jnp.concatenate([outer[0][0:24, :], outer[1][0:24, :]], axis=1)
    flipped = jnp.concatenate([tail, jnp.zeros((120, 128), F32)], axis=0).T
    for slot, row in ((9, 0), (10, 1), (11, 2), (13, 3), (14, 4), (15, 5), (16, 6), (17, 7)):
        outs[slot][...] = flipped[96 + row, 0:6]
    inner = jnp.zeros((1, 128), F32)
    lane = iota((1, 128), 1)
    for i in range(6):
        for j in range(4):
            inner = jnp.where(lane == 4 * i + j, flipped[104 + j : 105 + j, i : i + 1], inner)
    outs[12][...] = inner[0, 0:24]
    for i in range(PARTS):
        heads = pl.ds(2 * HEADS // PARTS * i, 2 * HEADS // PARTS)
        copies[i].wait()
        copies[i] = pltpu.make_async_copy(hold.at[i], outs[2].at[heads], sem.at[1, i])
        copies[i].start()
    for copy in small + copies:
        copy.wait()


def out_kernel(*args):
    vmem = pl.BlockSpec(memory_space=pltpu.VMEM)
    any_space = pl.BlockSpec(memory_space=pl.ANY)
    f = lambda *s: jax.ShapeDtypeStruct(s, F32)
    return pl.pallas_call(
        lay_out,
        out_shape=[
            jax.ShapeDtypeStruct((TOK, D), BF),
            jax.ShapeDtypeStruct((TOK, D), BF),
            jax.ShapeDtypeStruct((2 * HEADS, BLOCKS * TOK, 128), BF),
            f(6, D),
            f(6, D),
            f(6, D),
            f(6, D),
            f(6, FF),
            f(24, D),
            f(6),
            f(6),
            f(6),
            f(24),
            f(6),
            f(6),
            f(6),
            f(6),
            f(6),
        ],
        in_specs=[any_space] * 6,
        out_specs=[any_space] * 3 + [vmem] * 15,
        scratch_shapes=[
            pltpu.VMEM((PARTS, 2 * HEADS // PARTS, BLOCKS * TOK, 128), BF),
            pltpu.VMEM((TOK, D), BF),
            pltpu.VMEM((TOK, D), BF),
            pltpu.VMEM((BLOCKS, 32, HALF), BF),
            pltpu.VMEM((BLOCKS, 32, HALF), BF),
            pltpu.VMEM((BLOCKS, 16, HALF), BF),
            pltpu.SemaphoreType.DMA((2, PARTS)),
            pltpu.SemaphoreType.DMA((5,)),
        ],
        compiler_params=pltpu.CompilerParams(vmem_limit_bytes=60 * 2**20),
        name="lay_out",
    )(*args)


def on_device(*args):
    return tuple(out_kernel(*main_kernel(args)))


def solution(mesh):
    rows = P(("batch", "keys"), None)
    logits = P(None, "batch", "keys")
    flat = P(("batch", "keys"))
    return jax.shard_map(
        on_device,
        mesh=mesh,
        in_specs=(rows, logits, P("batch", None), rows) + (P(),) * 15,
        out_specs=(rows, rows, logits) + (rows,) * 6 + (flat,) * 9,
        check_vma=False,
    )
```

```python
from types import SimpleNamespace
from typing import Any, NamedTuple

import jax
import jax.numpy as jnp
from jax import lax
from jax.experimental import pallas as pl
from jax.experimental.pallas import tpu as pltpu
from jax.sharding import PartitionSpec as P

EPSILON = 1e-05
NEGATIVE = -1e30
MESH = pl.DeviceIdType.MESH
BF = jnp.bfloat16
F32 = jnp.float32

TOK = 128
D = 768
HALF = 384
HEADS = 6
FF = 3072
SEQS = 16
BLOCKS = 8


def dot(a, b):
    return lax.dot_general(a, b, (((1,), (0,)), ((), ())), preferred_element_type=F32)


def dot_nt(a, b):
    return lax.dot_general(a, b, (((1,), (1,)), ((), ())), preferred_element_type=F32)


def dot_tn(a, b):
    return lax.dot_general(a, b, (((0,), (0,)), ((), ())), preferred_element_type=F32)


def iota(shape, dim):
    return lax.broadcasted_iota(jnp.int32, shape, dim)


def split_hi_lo(v):
    hi = v.astype(BF)
    lo = (v - hi.astype(F32)).astype(BF)
    return jnp.concatenate([hi.astype(F32), lo.astype(F32)], axis=0).astype(BF)


def head_rows():
    return jnp.where(iota((16, HALF), 1) // 64 == iota((16, HALF), 0) % 8, 1.0, 0.0).astype(BF)


def unit_rows():
    return jnp.where(iota((16, 128), 1) == iota((16, 128), 0), 1.0, 0.0).astype(BF)


def row_sums(v):
    return jnp.sum(v, axis=0, keepdims=True)


def norm(values):
    average = jnp.mean(values, axis=-1, keepdims=True)
    centered = values - average
    variance = jnp.mean(centered * centered, axis=-1, keepdims=True)
    inverse = lax.rsqrt(variance + EPSILON)
    return centered * inverse, inverse


def norm_back(upstream, normed, inverse, gain):
    scaled = upstream * gain
    return inverse * (
        scaled
        - jnp.mean(scaled, axis=-1, keepdims=True)
        - normed * jnp.mean(scaled * normed, axis=-1, keepdims=True)
    )


class Args(NamedTuple):
    hidden: Any
    prev: Any
    lengths: Any
    gout: Any
    w_q: Any
    w_k: Any
    w_v: Any
    w_o: Any
    w_i: Any
    w_u: Any
    b_q: Any
    b_v: Any
    b_o: Any
    b_i: Any
    b_u: Any
    g_a: Any
    b_a: Any
    g_f: Any
    b_f: Any


class Outs(NamedTuple):
    out_hidden: Any
    grad_hidden: Any
    gl: Any
    zrb: Any
    zra: Any
    wr: Any


SCRATCH = dict(
    wq=((2, D, HALF), BF),
    wk=((2, D, HALF), BF),
    wv=((2, D, HALF), BF),
    wo=((D, D), BF),
    wi=((4, D, D), BF),
    wu=((4, D, D), BF),
    vq=((D,), F32),
    vv=((D,), F32),
    vo=((D,), F32),
    vi=((FF,), F32),
    vu=((D,), F32),
    ga=((D,), F32),
    ba=((D,), F32),
    gf=((D,), F32),
    bf=((D,), F32),
    go=((TOK, D), BF),
    hid=((BLOCKS, TOK, D), BF),
    pv=((2, HEADS, BLOCKS * TOK, 128), BF),
    qs=((BLOCKS, TOK, HALF), BF),
    km=((HEADS, 256, 128), BF),
    ve=((HEADS, 256, 256), BF),
    madd=((TOK, 256), F32),
    obuf=((BLOCKS, TOK, HALF), BF),
    orecv=((BLOCKS, TOK, HALF), BF),
    st=((BLOCKS, 16, 128), F32),
    strecv=((BLOCKS, 16, 128), F32),
    at=((2, TOK, HALF), F32),
    atx=((2, TOK, D), BF),
    n1=((TOK, D), F32),
    gs=((TOK, D), F32),
    gp=((4, TOK, D), F32),
    ogs=((2, TOK, HALF), BF),
    brs=((2, TOK, HALF), BF),
    brr=((TOK, HALF), BF),
    brow=((2, 16, HALF), F32),
    ags=((2, TOK, HALF), BF),
    dorecv=((BLOCKS, TOK, HALF), BF),
    s2=((2, 16, 128), F32),
    s2recv=((BLOCKS, 16, 128), F32),
    dkt=((HALF, 256), F32),
    dvt=((HALF, 256), F32),
    dq=((BLOCKS, TOK, HALF), BF),
    dqr=((2, 2, TOK, HALF), BF),
    dqo=((2, TOK, HALF), BF),
    dqh=((2, 2, 64, HALF), BF),
    kgs=((2, TOK, HALF), BF),
    kgr=((TOK, HALF), BF),
    vgs=((2, TOK, HALF), BF),
    vgr=((TOK, HALF), BF),
    a2s=((4, 192, 128), BF),
    a2r=((3, 192, 128), BF),
    a2t=((4, 48, 128), BF),
    a2u=((3, 48, 128), BF),
    b2s=((4, 4, 48, 256), BF),
    b2r=((3, 4, 48, 256), BF),
    b2t=((4, 48, 256), BF),
    b2u=((3, 48, 256), BF),
    fa2=((48, 128), F32),
    fb1=((192, HALF), F32),
    fx=((TOK, D), BF),
    ax=((4, TOK, D), BF),
    igs=((2, 4, TOK, HALF), BF),
    xi=((BLOCKS, TOK, D), BF),
    xo=((BLOCKS, TOK, D), BF),
    yi=((BLOCKS, TOK, HALF), BF),
    yo=((BLOCKS, TOK, HALF), BF),
    b1s=((4, 192, HALF), BF),
    b1r=((3, 192, HALF), BF),
    c1s=((4, 192, HALF), BF),
    c1r=((3, 192, HALF), BF),
    c1t=((4, 48, HALF), BF),
    c1u=((3, 48, HALF), BF),
    fc1=((48, HALF), F32),
    i1s=((4, 192, HALF), BF),
    i1r=((3, 192, HALF), BF),
    fi1=((192, HALF), F32),
    i1f=((48, HALF), F32),
    i1z=((4, 48, HALF), BF),
    i1u=((3, 48, HALF), BF),
    i1g=((16, HALF), F32),
    i1t=((BLOCKS, 16, HALF), BF),
    fb2=((48, 256), F32),
    zf=((32, HALF), F32),
    zsb=((BLOCKS, 32, HALF), BF),
    zf2=((16, HALF), F32),
    zs2=((BLOCKS, 16, HALF), BF),
    qt=((BLOCKS, HALF, TOK), BF),
    kvt=((2, HALF, 256), BF),
    qgt=((2, HALF, TOK), BF),
    ykv=((256, BLOCKS * TOK), BF),
    yq=((128, BLOCKS * TOK), BF),
)
SEMS = dict(
    ld=21,
    outs=3,
    pl_=4,
    ps=1,
    pr=4,
    hs=1,
    hr=9,
    os=1,
    or_=1,
    ss=1,
    sr=1,
    xs=2,
    xr=2,
    xis=1,
    xir=2,
    xos=1,
    xor_=2,
    yis=1,
    yir=1,
    yos=1,
    yor=1,
    ds=1,
    dr=6,
    es=1,
    er=4,
    ts=8,
    tr=8,
    is_=1,
    ir=1,
    qs_=1,
    qr=4,
    gl_=1,
    gs_=1,
    gr=1,
    ks=1,
    kr=1,
    ys=1,
    yr=1,
    us=1,
    ur=1,
    zs_=1,
    zr_=1,
    vs=1,
    vr=1,
    ws=1,
    wr=1,
    own=3,
)


def body(*refs):
    na, no, nsc = len(Args._fields), len(Outs._fields), len(SCRATCH)
    A = Args(*refs[:na])
    O = Outs(*refs[na : na + no])
    S = SimpleNamespace(**dict(zip(SCRATCH, refs[na + no : na + no + nsc])))
    M = SimpleNamespace(**dict(zip(SEMS, refs[na + no + nsc : -1])))
    LEN = refs[-1]

    bi = lax.axis_index("batch")
    ki = lax.axis_index("keys")
    x, y = bi // 4, lax.rem(bi, 4)
    z, c = ki // 2, lax.rem(ki, 2)
    oc = 1 - c

    def dev(dx=0, dy=0, dz=0, dc=0):
        nb = lax.rem(x + dx, 4) * 4 + lax.rem(y + dy, 4)
        return (nb, lax.rem(z + dz, 4) * 2 + lax.rem(c + dc, 2))

    def key_of(dz, dc):
        return lax.rem(z + dz, 4) * 2 + lax.rem(c + dc, 2)

    def far(d):
        return d + (d // 2) * (1 - 2 * lax.rem(d, 2))

    def remote(src, dst, ssem, rsem, to):
        return pltpu.make_async_remote_copy(
            src_ref=src, dst_ref=dst, send_sem=ssem, recv_sem=rsem, device_id=to, device_id_type=MESH
        )

    def sent(sem, like):
        remote(like, like, sem, sem, dev(dc=1)).wait_send()

    def arrived(sem, like):
        remote(like, like, sem, sem, dev(dc=1)).wait_recv()

    def local(src, dst, sem):
        return pltpu.make_async_copy(src, dst, sem)

    loads = [
        local(A.hidden, S.hid.at[ki], M.ld.at[0]),
        local(A.w_k.at[:, pl.ds(pl.multiple_of(c * HALF, 128), HALF)], S.wk.at[c], M.ld.at[1]),
        local(A.w_v.at[:, pl.ds(pl.multiple_of(c * HALF, 128), HALF)], S.wv.at[c], M.ld.at[2]),
        local(A.w_q.at[:, pl.ds(pl.multiple_of(c * HALF, 128), HALF)], S.wq.at[c], M.ld.at[3]),
        local(A.b_q, S.vq, M.ld.at[4]),
        local(A.b_v, S.vv, M.ld.at[5]),
    ]
    lengths = local(A.lengths, LEN, M.ld.at[17])
    lengths.start()
    later = [
        local(A.w_o, S.wo, M.ld.at[6]),
        local(A.b_o, S.vo, M.ld.at[7]),
        local(A.b_i, S.vi, M.ld.at[8]),
        local(A.b_u, S.vu, M.ld.at[9]),
        local(A.g_a, S.ga, M.ld.at[10]),
        local(A.b_a, S.ba, M.ld.at[11]),
        local(A.g_f, S.gf, M.ld.at[12]),
        local(A.b_f, S.bf, M.ld.at[13]),
        local(A.gout, S.go, M.ld.at[14]),
    ]
    for j in range(4):
        later.append(local(A.w_i.at[:, pl.ds(D * j, D)], S.wi.at[j], M.ld.at[15]))
        later.append(local(A.w_u.at[pl.ds(D * j, D)], S.wu.at[j], M.ld.at[16]))
    last = [
        local(a.at[:, pl.ds(pl.multiple_of(oc * HALF, 128), HALF)], s.at[oc], M.outs.at[i])
        for i, (a, s) in enumerate(((A.w_q, S.wq), (A.w_k, S.wk), (A.w_v, S.wv)))
    ]
    for cp in loads:
        cp.start()

    def prev_rows(dz):
        return pl.ds(pl.multiple_of(lax.rem(z + dz, 4) * 256, 256), 256)

    def prev_local(dz):
        rows = prev_rows(dz)
        return local(
            A.prev.at[pl.ds(c * HEADS, HEADS), rows, :], S.pv.at[c, :, rows, :], M.pl_.at[dz]
        )

    def prev_remote(dz):
        rows = prev_rows(dz)
        return remote(
            A.prev.at[pl.ds(oc * HEADS, HEADS), rows, :],
            S.pv.at[c, :, rows, :],
            M.ps.at[0],
            M.pr.at[dz],
            dev(dc=1),
        )

    for dz in (0, 1, 3, 2):
        prev_local(dz).start()

    peers = [(0, 0, dz, dc) for dz in range(4) for dc in range(2) if dz or dc]
    peers += [(d, 0, 0, dc) for d in (1, 2, 3) for dc in range(2)]
    peers += [(0, d, 0, dc) for d in (1, 2, 3) for dc in range(2)]
    barrier = pltpu.get_barrier_semaphore()
    for off in peers:
        pl.semaphore_signal(barrier, inc=1, device_id=dev(*off), device_id_type=MESH)
    pl.semaphore_wait(barrier, len(peers))

    def rows_half(h):
        return pl.ds(64 * h, 64)

    def hid_send(i, src, k, rows, dz, dc):
        remote(src, S.hid.at[k, rows], M.hs.at[0], M.hr.at[i], dev(dz=dz, dc=dc)).start()

    def hid_arrival(i, k, rows):
        arrived(M.hr.at[i], S.hid.at[k, rows])

    low, high, whole = rows_half(0), rows_half(1), pl.ds(0, TOK)
    hid_send(3, A.hidden.at[low], ki, low, 1, 0)
    hid_send(2, A.hidden.at[high], ki, high, 3, 0)
    hid_send(0, A.hidden, ki, whole, 0, 1)
    hid_send(4, A.hidden.at[high], ki, high, 1, 0)
    hid_send(1, A.hidden.at[low], ki, low, 3, 0)
    prev_remote(0).start()
    prev_remote(1).start()
    prev_remote(3).start()
    prev_remote(2).start()

    bounds = []
    running = jnp.int32(0)
    lengths.wait()
    for j in range(SEQS):
        running = running + LEN[0, j]
        bounds.append(running)

    def segment_of(places):
        counted = jnp.zeros(places.shape, jnp.int32)
        for bound in bounds:
            counted = counted + jnp.where(places >= bound, 1, 0)
        return jnp.where(places < bounds[-1], counted, -1 - places)

    lane8 = iota((8, 128), 1)
    key_segment = [segment_of(lane8 * BLOCKS + z * 2 + half)[0:1, :] for half in range(2)]
    lane = iota((TOK, 128), 1)

    for cp in loads[:1] + loads[1:3] + loads[5:6]:
        cp.wait()
    hid_arrival(0, key_of(0, 1), whole)
    pair = pl.ds(z * 2, 2)
    hid_pair = S.hid[pair].reshape(256, D)
    key_rows = dot(hid_pair, S.wk[c]).astype(BF).astype(F32)
    bias_v = S.vv[...].reshape(1, D)
    bias_q = S.vq
    bv = jnp.where(c == 0, bias_v[:, :HALF], bias_v[:, HALF:])
    value_rows = (dot(hid_pair, S.wv[c]) + bv).astype(BF).astype(F32)
    lane2 = iota((256, 128), 1)
    for h in range(HEADS):
        g, e = h // 2, h % 2
        mine = lane2 // 64 == e
        S.km[h] = jnp.where(mine, key_rows[:, 128 * g : 128 * g + 128], 0.0).astype(BF)
        S.ve[h, :, :128] = jnp.where(mine, value_rows[:, 128 * g : 128 * g + 128], 0.0).astype(BF)
        S.ve[h, :, 128:] = jnp.where((lane2 == h) | (lane2 == 8 + h), 1.0, 0.0).astype(BF)
    loads[3].wait()
    loads[4].wait()
    bias_q = S.vq[...].reshape(1, D)
    S.brow[...] = jnp.zeros((2, 16, HALF), F32)
    S.ykv[...] = jnp.zeros((256, BLOCKS * TOK), BF)
    S.yq[...] = jnp.zeros((128, BLOCKS * TOK), BF)
    S.zf[...] = jnp.zeros((32, HALF), F32)
    S.zf2[...] = jnp.zeros((16, HALF), F32)
    S.i1g[...] = jnp.zeros((16, HALF), F32)
    for cp in later + last:
        cp.start()

    def out_send(k, to):
        return remote(S.obuf.at[k], S.orecv.at[ki], M.os.at[0], M.or_.at[0], to)

    def st_send(k, to):
        return remote(S.st.at[k], S.strecv.at[ki], M.ss.at[0], M.sr.at[0], to)

    def forward(i, carry):
        ring = (i + 2) // 4
        odd = lax.rem(ring, 2)
        dz = ring + odd * 2 * lax.rem(i, 2)
        dc = (1 - odd) * lax.rem(i, 2) + odd * (i // 4)
        k = key_of(dz, dc)

        @pl.when(i == 2)
        def _():
            above, below = key_of(1, 0), key_of(3, 0)
            hid_arrival(3, below, low)
            hid_send(7, S.hid.at[below, low], below, low, 1, 0)
            hid_arrival(2, above, high)
            hid_send(7, S.hid.at[above, high], above, high, 3, 0)
            hid_arrival(1, above, low)
            hid_send(5, S.hid.at[above], above, whole, 0, 1)

        @pl.when(i == 3)
        def _():
            hid_arrival(4, k, high)
            hid_send(6, S.hid.at[k], k, whole, 0, 1)

        @pl.when(i >= 4)
        def _():
            hid_arrival(i + 1, k, whole)

        @pl.when(i == 6)
        def _():
            hid_send(8, S.hid.at[k], k, whole, 0, 1)

        @pl.when(dc == 0)
        def _():
            prev_local(dz).wait()
            prev_remote(dz).wait_recv()

        bq = jnp.where(c == 0, bias_q[:, :HALF], bias_q[:, HALF:])
        queries = (dot(S.hid[k], S.wq[c]) + bq).astype(BF).astype(F32) * 0.125
        S.qs[k] = queries.astype(BF)
        S.qt[k] = queries.T.astype(BF)
        row_segment = segment_of(iota((TOK, 128), 0) * BLOCKS + k)
        for half in range(2):
            S.madd[:, 128 * half : 128 * half + 128] = jnp.where(
                row_segment == key_segment[half], 0.0, NEGATIVE
            )
        rows = pl.ds(pl.multiple_of(k * TOK, TOK), TOK)
        totals = jnp.zeros((TOK, 128), F32)
        tops = jnp.zeros((TOK, 128), F32)
        for g in range(3):
            two = S.qs[k, :, 128 * g : 128 * g + 128]
            mixed = jnp.zeros((TOK, 128), F32)
            for h in (2 * g, 2 * g + 1):
                before = jnp.concatenate([S.pv[0, h, rows, :], S.pv[1, h, rows, :]], axis=1)
                s = dot_nt(two, S.km[h]) + before.astype(F32) + S.madd[...]
                top = jnp.max(s, axis=1, keepdims=True)
                p = jnp.exp(s - top).astype(BF)
                S.pv[0, h, rows, :] = p[:, :128]
                S.pv[1, h, rows, :] = p[:, 128:]
                o = dot(p, S.ve[h])
                mixed = mixed + o[:, :128]
                totals = totals + o[:, 128:]
                tops = jnp.where(lane == 8 + h, top, tops)
            S.obuf[k, :, 128 * g : 128 * g + 128] = mixed.astype(BF)
        stats = jnp.where(lane < 8, totals, tops)
        S.st[k] = stats.T[:16, :]

        @pl.when(i > 0)
        def _():
            to = dev(dz=dz, dc=dc)
            out_send(k, to).start()
            st_send(k, to).start()

        return carry

    lax.fori_loop(0, BLOCKS, forward, 0)

    S.orecv[ki] = S.obuf[ki]
    S.strecv[ki] = S.st[ki]

    seven = pl.ds(0, 7)
    arrived(M.or_.at[0], S.orecv.at[seven])
    arrived(M.sr.at[0], S.strecv.at[seven])
    row8 = iota((8, 128), 0)
    spread = head_rows()
    lse = []
    for half in range(2):
        tops = [S.strecv[2 * zz + half, 8:16, :] for zz in range(4)]
        sums = [S.strecv[2 * zz + half, 0:8, :] for zz in range(4)]
        top = jnp.maximum(jnp.maximum(tops[0], tops[1]), jnp.maximum(tops[2], tops[3]))
        shares = [jnp.exp(t - top) for t in tops]
        total = shares[0] * sums[0] + shares[1] * sums[1] + shares[2] * sums[2] + shares[3] * sums[3]
        total = jnp.where(row8 < HEADS, total, 1.0)
        lse.append(jnp.where(row8 < HEADS, top + jnp.log(total), 0.0))
        acc = jnp.zeros((TOK, HALF), F32)
        for zz in range(4):
            factor = dot_tn(split_hi_lo(jnp.where(row8 < HEADS, shares[zz] / total, 0.0)), spread)
            acc = acc + S.orecv[2 * zz + half].astype(F32) * factor
        S.at[half] = acc
        S.atx[0, :, HALF * half : HALF * half + HALF] = acc.astype(BF)

    other = dev(dc=1)

    def swap(i, src, dst):
        copy = remote(src, dst, M.xs.at[i], M.xr.at[i], other)
        copy.start()
        return copy

    swap_at = swap(0, S.atx.at[0], S.atx.at[1])

    def vec(ref):
        return ref[...].reshape(1, -1)

    for cp in later[:9]:
        cp.wait()
    local(S.wi, S.wi, M.ld.at[15]).wait()
    local(S.wu, S.wu, M.ld.at[16]).wait()
    attn_low = S.atx[0]
    first_sum = S.hid[ki].astype(F32) + dot(attn_low, S.wo[...]) + vec(S.vo)
    normed, inverse_a = norm(first_sum)
    S.n1[...] = normed
    first_low = (normed * vec(S.ga) + vec(S.ba)).astype(BF)
    S.fx[...] = first_low
    in_y, in_x = y * 2 + c, x * 2 + c
    S.xi[in_y] = first_low

    def xi_send(i, src, k, **to):
        remote(src, S.xi.at[k], M.xis.at[0], M.xir.at[i], dev(**to)).start()

    for d in (1, 3, 2):
        xi_send(0, S.fx, in_y, dy=d)
    xi_send(1, S.fx, in_y, dc=1)
    second = normed * vec(S.ga) + vec(S.ba) + vec(S.vu)
    bias_i = vec(S.vi)
    for j in range(4):
        inner = dot(S.fx[...], S.wi[j]) + bias_i[:, D * j : D * j + D]
        cdf = 0.5 + 0.5 * lax.erf(inner * 0.7071067811865476)
        density = jnp.exp(inner * inner * -0.5) * 0.3989422804014327
        S.gp[j] = cdf + inner * density
        S.ax[j] = (inner * cdf).astype(BF)

        @pl.when(x != j)
        def _():
            remote(S.ax.at[j], S.xo.at[in_x], M.xos.at[0], M.xor_.at[0], (j * 4 + y, ki)).start()

        @pl.when(x == j)
        def _():
            remote(S.ax.at[j], S.xo.at[in_x], M.xos.at[0], M.xor_.at[1], other).start()
            S.xo[in_x] = S.ax[j]

        second = second + dot(S.ax[j], S.wu[j])
    normed_f, inverse_f = norm(second)
    O.out_hidden[...] = (normed_f * vec(S.gf) + vec(S.bf)).astype(BF)
    upstream = S.go[...].astype(F32)

    def put_row(r, values):
        sums = row_sums(values)
        S.brow[0, r : r + 1, :] = sums[:, :HALF]
        S.brow[1, r : r + 1, :] = sums[:, HALF:]

    put_row(6, upstream * normed_f)
    put_row(7, upstream)
    grad_second = norm_back(upstream, normed_f, inverse_f, vec(S.gf))
    og = grad_second.astype(BF)
    put_row(3, og.astype(F32))
    S.ogs[0] = og[:, :HALF]
    S.ogs[1] = og[:, HALF:]
    ring_places = [(d, dc) for d in (1, 3, 2) for dc in range(2)]
    for d, dc in ring_places + [(0, 1)]:
        src = S.ogs.at[lax.rem(c + dc, 2)]
        remote(src, S.yo.at[in_x], M.yos.at[0], M.yor.at[0], dev(dx=d, dc=dc)).start()
    S.yo[in_x] = S.ogs[c]
    S.gs[...] = grad_second
    bsum = []
    for j in range(4):
        ig = (dot_nt(og, S.wu[j]) * S.gp[j]).astype(BF)
        S.igs[j // 2, 2 * (j % 2)] = ig[:, :HALF]
        S.igs[j // 2, 2 * (j % 2) + 1] = ig[:, HALF:]
        bsum.append(row_sums(ig.astype(F32)))
        S.gs[...] = S.gs[...] + dot_nt(ig, S.wi[j])
    for d, dc in ring_places + [(0, 1)]:
        src = S.igs.at[lax.rem(c + dc, 2), lax.rem(y + d, 4)]
        remote(src, S.yi.at[in_y], M.yis.at[0], M.yir.at[0], dev(dy=d, dc=dc)).start()
    S.yi[in_y] = S.igs[c, y]

    grad_first = S.gs[...]
    normed = S.n1[...]
    put_row(4, grad_first * normed)
    put_row(5, grad_first)
    grad_first_sum = norm_back(grad_first, normed, inverse_a, vec(S.ga))
    S.gs[...] = grad_first_sum
    br = grad_first_sum.astype(BF)
    put_row(2, br.astype(F32))
    S.brs[0] = br[:, :HALF]
    S.brs[1] = br[:, HALF:]
    swap_br = swap(1, S.brs.at[oc], S.brr)
    ag = dot_nt(br, S.wo[...]).astype(BF)
    for half in range(2):
        S.ags[half] = ag[:, HALF * half : HALF * half + HALF]
        product = S.at[half] * ag[:, HALF * half : HALF * half + HALF].astype(F32)
        dots = jnp.zeros((16, TOK), F32)
        hi = product.astype(BF)
        lo = (product - hi.astype(F32)).astype(BF)
        dots = dot_nt(spread, hi) + dot_nt(spread, lo)
        S.s2[half, 0:8, :] = dots[0:8, :]
        S.s2[half, 8:16, :] = lse[half]

    def ag_send(i, src, k, rows, dz, dc):
        remote(src, S.dorecv.at[k, rows], M.ds.at[0], M.dr.at[i], dev(dz=dz, dc=dc)).start()

    def ag_arrival(i, dz, rows):
        arrived(M.dr.at[i], S.dorecv.at[pl.ds(lax.rem(z + dz, 4) * 2, 2), rows])

    def s2_send(i, dz, dc):
        half = lax.rem(c + dc, 2)
        remote(S.s2.at[half], S.s2recv.at[ki], M.es.at[0], M.er.at[i], dev(dz=dz, dc=dc)).start()

    def s2_arrival(i, dz):
        arrived(M.er.at[i], S.s2recv.at[pl.ds(lax.rem(z + dz, 4) * 2, 2)])

    for i, dz, rows in ((3, 1, low), (2, 3, high)):
        for dc in range(2):
            ag_send(i, S.ags.at[lax.rem(c + dc, 2), rows], ki, rows, dz, dc)
    ag_send(0, S.ags.at[oc], ki, whole, 0, 1)
    s2_send(0, 0, 1)
    for i, dz, rows in ((4, 1, high), (1, 3, low)):
        for dc in range(2):
            ag_send(i, S.ags.at[lax.rem(c + dc, 2), rows], ki, rows, dz, dc)
    for i, dz in ((2, 1), (1, 3), (3, 2)):
        for dc in range(2):
            s2_send(i, dz, dc)
    S.dorecv[ki] = S.ags[c]
    S.s2recv[ki] = S.s2[c]

    def weight_grad(left, right):
        return dot_tn(left, right).astype(BF)

    def along(axis, d):
        return dev(dx=d) if axis == 0 else dev(dy=d)

    def at_place(axis, d):
        return lax.rem((x if axis == 0 else y) + d, 4)

    def scatter(n, axis, src, dst, inner):
        for d in (1, 2, 3):
            there = at_place(axis, d)
            piece = src.at[:, there] if inner else src.at[there]
            remote(piece, dst.at[d - 1], M.ts.at[n], M.tr.at[n], along(axis, d)).start()

    for cp in [swap_at, swap_br]:
        cp.wait()
    right = jnp.concatenate([S.brs[c], S.brr[...]], axis=0)
    S.c1s[...] = weight_grad(S.atx[...].reshape(256, D), right).reshape(4, 192, HALF)
    scatter(6, 0, S.c1s, S.c1r, False)

    lane512 = iota((8, 512), 1)
    sub512 = iota((8, 512), 0)
    pick = jnp.where(
        iota((512, 128), 1) == (iota((512, 128), 0) // 128) * 32 + lax.rem(iota((512, 128), 0), 128) // 4,
        1.0,
        0.0,
    ).astype(BF)
    flat = jnp.concatenate(bsum, axis=1)
    for g in range(6):
        spread_out = jnp.where(lax.rem(lane512, 4) == sub512, flat[:, 512 * g : 512 * g + 512], 0.0)
        S.brow[g // 3, 8:16, 128 * (g % 3) : 128 * (g % 3) + 128] = dot(spread_out.astype(BF), pick)

    S.dkt[...] = jnp.zeros((HALF, 256), F32)
    S.dvt[...] = jnp.zeros((HALF, 256), F32)
    units = unit_rows()

    def dq_landing(w, half, h):
        return S.dqr.at[w, half, rows_half(h)], M.qr.at[2]

    def dq_copy(src, place, to):
        return remote(src, place[0], M.qs_.at[0], place[1], to)

    def dq_piece(dz, h):
        return S.dq.at[pl.ds(lax.rem(z + dz, 4) * 2, 2), rows_half(h)]

    dq_partner = dq_copy(S.dq.at[z * 2 + oc], (S.dqo.at[c], M.qr.at[3]), other)
    dq_first = [
        dq_copy(dq_piece(2, 0), (S.dqh.at[0], M.qr.at[0]), dev(dz=1)),
        dq_copy(dq_piece(2, 1), (S.dqh.at[1], M.qr.at[1]), dev(dz=3)),
    ]
    dq_own, dq_summed = [], []
    for w, dz in ((0, 1), (1, 3)):
        h = 1 - w
        dq_own.append(
            [
                dq_copy(
                    S.dq.at[lax.rem(z + dz, 4) * 2 + cc, rows_half(h)],
                    dq_landing(w, c, h),
                    (bi, lax.rem(z + dz, 4) * 2 + cc),
                )
                for cc in range(2)
            ]
        )
        h = w
        dq_summed.append(
            [
                dq_copy(
                    S.dqh.at[w, cc],
                    dq_landing(w, c, h),
                    (bi, lax.rem(z + dz, 4) * 2 + cc),
                )
                for cc in range(2)
            ]
        )

    def gl_rows(zz):
        return pl.ds(pl.multiple_of(zz * 256, 256), 256)

    def gl_local(k):
        rows = gl_rows(k)
        return local(
            S.pv.at[c, :, rows, :], O.gl.at[pl.ds(c * HEADS, HEADS), rows, :], M.gl_.at[0]
        )

    def gl_remote(k):
        rows = gl_rows(k)
        return remote(
            S.pv.at[oc, :, rows, :],
            O.gl.at[pl.ds(c * HEADS, HEADS), rows, :],
            M.gs_.at[0],
            M.gr.at[0],
            dev(dc=1),
        )

    def backward(i, carry):
        dz = far(i)
        zz = lax.rem(z + dz, 4)

        @pl.when(i == 2)
        def _():
            arrived(M.xir.at[0], S.xi.at[pl.ds(0, 3)])
            for d in (1, 3, 2):
                k = lax.rem(y + d, 4) * 2 + c
                xi_send(1, S.xi.at[k], k, dc=1)

        @pl.when(i == 3)
        def _():
            arrived(M.xor_.at[0], S.xo.at[pl.ds(0, 3)])
            for d in (1, 3, 2):
                k = lax.rem(x + d, 4) * 2 + c
                remote(S.xo.at[k], S.xo.at[k], M.xos.at[0], M.xor_.at[1], other).start()

        @pl.when(i == 0)
        def _():
            arrived(M.dr.at[0], S.dorecv.at[key_of(0, 1)])
            arrived(M.er.at[0], S.s2recv.at[key_of(0, 1)])

        @pl.when(i == 1)
        def _():
            ag_arrival(3, 3, low)
            for dc in range(2):
                k = key_of(3, dc)
                ag_send(5, S.dorecv.at[k, low], k, low, 1, 0)
            ag_arrival(2, 1, high)
            for dc in range(2):
                k = key_of(1, dc)
                ag_send(5, S.dorecv.at[k, high], k, high, 3, 0)
            ag_arrival(1, 1, low)
            s2_arrival(1, 1)

        @pl.when(i == 2)
        def _():
            ag_arrival(4, 3, high)
            s2_arrival(2, 3)

        @pl.when(i == 3)
        def _():
            ag_arrival(5, 2, whole)
            s2_arrival(3, 2)

        rows = pl.ds(pl.multiple_of(zz * 256, 256), 256)
        factors, minuses = [], []
        for half in range(2):
            k = zz * 2 + half
            share = jnp.exp(S.st[k, 8:16, :] - S.s2recv[k, 8:16, :])
            share = jnp.where(row8 < HEADS, share, 0.0)
            minuses.append(dot_tn(split_hi_lo(S.s2recv[k, 0:8, :] * share * -1.0), units).astype(BF))
            factors.append(dot_tn(split_hi_lo(share), spread))
        minus = jnp.concatenate(minuses, axis=0)
        two = pl.ds(zz * 2, 2)
        scaled = S.dorecv[two].reshape(256, HALF).astype(F32) * jnp.concatenate(factors, axis=0)
        scaled_t = scaled.T.astype(BF)
        scaled = scaled.astype(BF)
        queries_t = jnp.concatenate([S.qt[zz * 2], S.qt[zz * 2 + 1]], axis=1)
        for g in range(3):
            left = jnp.concatenate([scaled[:, 128 * g : 128 * g + 128], minus], axis=1)
            partial = jnp.zeros((256, 128), F32)
            for h in (2 * g, 2 * g + 1):
                p = jnp.concatenate([S.pv[0, h, rows, :], S.pv[1, h, rows, :]], axis=1)
                grad = (p.astype(F32) * dot_nt(left, S.ve[h])).astype(BF)
                S.pv[0, h, rows, :] = grad[:, :128]
                S.pv[1, h, rows, :] = grad[:, 128:]
                at = slice(64 * h, 64 * h + 64)
                S.dvt[at, :] = S.dvt[at, :] + dot(scaled_t[at, :], p)
                S.dkt[at, :] = S.dkt[at, :] + dot(queries_t[at, :], grad)
                partial = partial + dot(grad, S.km[h])
            partial = (partial * 0.125).astype(BF).reshape(2, TOK, 128)
            S.dq[two, :, 128 * g : 128 * g + 128] = partial

        @pl.when(i == 0)
        def _():
            dq_partner.start()

        @pl.when(i == 1)
        def _():
            for cp in dq_own[0]:
                cp.start()

        @pl.when(i == 2)
        def _():
            for cp in dq_own[1]:
                cp.start()

        @pl.when(i == 3)
        def _():
            for cp in dq_first:
                cp.start()

        gl_local(zz).start()
        gl_remote(zz).start()
        return carry

    lax.fori_loop(0, 4, backward, 0)
    S.dqo[c] = S.dq[ki]

    S.kvt[0] = S.dkt[...].astype(BF)
    S.kvt[1] = S.dvt[...].astype(BF)
    mine = pl.ds(pl.multiple_of(z * 256, 256), 256)
    for d in (1, 3, 2):
        there = pl.ds(pl.multiple_of(lax.rem(z + d, 4) * 96, 32), 96)
        for t in range(2):
            place = S.ykv.at[pl.ds(128 * t, 96), mine]
            remote(S.kvt.at[t, there, :], place, M.ys.at[0], M.yr.at[0], dev(dz=d)).start()
    here = pl.ds(pl.multiple_of(z * 96, 32), 96)
    for t in range(2):
        S.ykv[128 * t : 128 * t + 96, mine] = S.kvt[t, here, :]
    key_grad = S.dkt[...].T.astype(BF)
    value_grad = S.dvt[...].T.astype(BF)
    S.kgs[...] = key_grad.reshape(2, TOK, HALF)
    S.vgs[...] = value_grad.reshape(2, TOK, HALF)
    kv_swaps = [
        remote(S.kgs.at[oc], S.kgr, M.ks.at[0], M.kr.at[0], other),
        remote(S.vgs.at[oc], S.vgr, M.ks.at[0], M.kr.at[0], other),
    ]
    for cp in kv_swaps:
        cp.start()
    S.brow[c, 1:2, :] = row_sums(value_grad.astype(F32))
    arrived(M.yir.at[0], S.yi.at[seven])
    arrived(M.xir.at[1], S.xi.at[pl.ds(0, 4)])
    grad = weight_grad(S.xi[...].reshape(BLOCKS * TOK, D), S.yi[...].reshape(BLOCKS * TOK, HALF))
    S.i1s[...] = grad.reshape(4, 192, HALF)
    scatter(3, 0, S.i1s, S.i1r, False)
    arrived(M.yor.at[0], S.yo.at[seven])
    arrived(M.xor_.at[1], S.xo.at[pl.ds(0, 4)])
    grad = weight_grad(S.xo[...].reshape(BLOCKS * TOK, D), S.yo[...].reshape(BLOCKS * TOK, HALF))
    S.b1s[...] = grad.reshape(4, 192, HALF)
    scatter(2, 1, S.b1s, S.b1r, False)

    for cp in last:
        cp.wait()
    arrived(M.kr.at[0], S.kgs)
    total = S.gs[...]
    total = total + dot_nt(S.kgs[c], S.wk[c]) + dot_nt(S.kgr[...], S.wk[oc])
    total = total + dot_nt(S.vgs[c], S.wv[c]) + dot_nt(S.vgr[...], S.wv[oc])
    S.gs[...] = total

    def sum_a(src, recv, dst):
        def step(j, carry):
            part = pl.ds(pl.multiple_of(j * 48, 16), 48)
            total = src[x, part, :].astype(F32)
            for d in range(recv.shape[0]):
                total = total + recv[d, part, :].astype(F32)
            dst[j] = total.astype(BF)
            return carry

        lax.fori_loop(0, 4, step, 0)

    def sum_b(src, recv, dst):
        def step(j, carry):
            total = src[j, y].astype(F32)
            for d in range(recv.shape[0]):
                total = total + recv[d, j].astype(F32)
            dst[j] = total.astype(BF)
            return carry

        lax.fori_loop(0, 4, step, 0)

    def finish(n, own, recv, dst):
        arrived(M.tr.at[n], recv)
        total = own.astype(F32)
        for d in range(3):
            total = total + recv[d].astype(F32)
        dst[...] = total

    for w in range(2):
        dq_first[w].wait_recv()
        add = dq_piece((1, 3)[w], w)[...].astype(F32)
        S.dqh[w] = (S.dqh[w].astype(F32) + add).astype(BF)
        for cp in dq_summed[w]:
            cp.start()
    arrived(M.yr.at[0], S.kvt.at[:, pl.ds(0, 288)])
    hid_all = S.hid[...].reshape(BLOCKS * TOK, D)
    flipped = dot(S.ykv[...], hid_all)
    for t in range(2):
        grad = flipped[128 * t : 128 * t + 128, :].T.astype(BF)
        S.b2s[:, :, :, 128 * t : 128 * t + 128] = grad.reshape(4, 4, 48, 128)
    scatter(0, 1, S.b2s, S.b2r, True)

    arrived(M.tr.at[6], S.c1r)
    sum_a(S.c1s, S.c1r, S.c1t)
    scatter(7, 1, S.c1t, S.c1u, False)
    dq_partner.wait_recv()
    arrived(M.qr.at[2], S.dqr)
    query_grads = []
    for half in range(2):
        grad = S.dqr[0, half].astype(F32) + S.dqr[1, half].astype(F32) + S.dqo[half].astype(F32)
        S.qgt[half] = grad.T.astype(BF)
        query_grads.append(grad.astype(BF))

    my_rows = pl.ds(pl.multiple_of(ki * TOK, TOK), TOK)

    def column_rows(k):
        return pl.ds(pl.multiple_of((k // 2) * 96, 32), 96)

    def yq_send(k, to):
        return remote(
            S.qgt.at[lax.rem(k, 2), column_rows(k), :],
            S.yq.at[pl.ds(0, 96), my_rows],
            M.us.at[0],
            M.ur.at[0],
            to,
        )

    def send_columns(i, carry):
        dz, dc = far(i // 2), lax.rem(i, 2)
        yq_send(key_of(dz, dc), dev(dz=dz, dc=dc)).start()
        return carry

    lax.fori_loop(1, BLOCKS, send_columns, 0)
    S.yq[0:96, my_rows] = S.qgt[c, here, :]

    total = S.gs[...]
    for half in range(2):
        S.brow[half, 0:1, :] = row_sums(query_grads[half].astype(F32))
        total = total + dot_nt(query_grads[half], S.wq[half])
    O.grad_hidden[...] = total.astype(BF)

    finish(3, S.i1s[x], S.i1r, S.fi1)
    for p in range(4):
        for k in range(BLOCKS):
            at = 48 * (k // 2) + 12 * p + 6 * (k % 2)
            S.i1f[6 * k : 6 * k + 6, :] = S.fi1[at : at + 6, :]
        S.i1z[p] = S.i1f[...].astype(BF)
    for d in (1, 3, 2):
        there = lax.rem(z + d, 4)
        remote(S.i1z.at[there], S.i1u.at[d - 1], M.is_.at[0], M.ir.at[0], dev(dz=d)).start()

    arrived(M.ur.at[0], S.qgt.at[:, pl.ds(0, 336)])
    beside = jnp.where(iota((16, 128), 1) == iota((16, 128), 0) + 96, 1.0, 0.0).astype(BF)
    flipped = dot(S.yq[...], hid_all).T
    for half in range(2):
        columns = dot_tn(S.brow[half].astype(BF), beside)
        columns = columns + flipped[HALF * half : HALF * half + HALF, :]
        S.a2s[2 * half : 2 * half + 2] = columns.astype(BF).reshape(2, 192, 128)
    scatter(1, 0, S.a2s, S.a2r, False)

    finish(2, S.b1s[y], S.b1r, S.fb1)
    finish(7, S.c1t[y], S.c1u, S.fc1)
    for p in range(BLOCKS):
        S.zf[0:24, :] = S.fb1[24 * p : 24 * p + 24, :]
        S.zf[24:30, :] = S.fc1[6 * p : 6 * p + 6, :]
        S.zsb[p] = S.zf[...].astype(BF)

    def zb_send(k, to):
        return remote(S.zsb.at[k], O.zrb.at[ki], M.zs_.at[0], M.zr_.at[0], to)

    def w_send(k, to):
        return remote(S.zs2.at[k], O.wr.at[ki], M.ws.at[0], M.wr.at[0], to)

    def to_all(send):
        def step(i, carry):
            dz, dc = far(i // 2), lax.rem(i, 2)
            send(key_of(dz, dc), dev(dz=dz, dc=dc)).start()
            return carry

        lax.fori_loop(1, BLOCKS, step, 0)

    to_all(zb_send)
    own = [
        local(S.zsb.at[ki], O.zrb.at[ki], M.own.at[0]),
        local(S.zs2.at[ki], O.wr.at[ki], M.own.at[1]),
    ]
    own[0].start()

    arrived(M.tr.at[0], S.b2r)
    sum_b(S.b2s, S.b2r, S.b2t)
    scatter(4, 0, S.b2t, S.b2u, False)

    arrived(M.ir.at[0], S.i1u)
    total = S.i1z[z].astype(F32)
    for d in range(3):
        total = total + S.i1u[d].astype(F32)
    S.i1f[...] = total
    for k in range(BLOCKS):
        S.i1g[0:6, :] = S.i1f[6 * k : 6 * k + 6, :]
        S.i1t[k] = S.i1g[...].astype(BF)
    for d, dc in ring_places + [(0, 1)]:
        src = S.i1t.at[lax.rem(y + d, 4) * 2 + lax.rem(c + dc, 2)]
        remote(src, O.zra.at[in_y], M.vs.at[0], M.vr.at[0], dev(dy=d, dc=dc)).start()
    own.append(local(S.i1t.at[in_y], O.zra.at[in_y], M.own.at[2]))
    own[2].start()

    arrived(M.tr.at[1], S.a2r)
    sum_a(S.a2s, S.a2r, S.a2t)
    scatter(5, 1, S.a2t, S.a2u, False)

    finish(4, S.b2t[x], S.b2u, S.fb2)
    finish(5, S.a2t[y], S.a2u, S.fa2)
    for p in range(BLOCKS):
        six = slice(6 * p, 6 * p + 6)
        S.zf2[0:6, :128] = S.fa2[six, :]
        S.zf2[0:6, 128:] = S.fb2[six, :]
        S.zs2[p] = S.zf2[...].astype(BF)
    to_all(w_send)
    own[1].start()

    sent(M.os.at[0], S.obuf.at[seven])
    sent(M.ss.at[0], S.st.at[seven])
    sent(M.es.at[0], S.s2recv.at[seven])
    sent(M.us.at[0], S.qgt.at[:, pl.ds(0, 336)])
    sent(M.ys.at[0], S.kvt.at[:, pl.ds(0, 288)])
    sent(M.ks.at[0], S.kgs)
    sent(M.ds.at[0], S.dorecv.at[seven])
    sent(M.qs_.at[0], S.dq.at[seven])
    for ssem, rsem, like in (
        (M.zs_, M.zr_, S.zsb),
        (M.vs, M.vr, S.i1t),
        (M.ws, M.wr, S.zs2),
    ):
        sent(ssem.at[0], like.at[seven])
        arrived(rsem.at[0], like.at[seven])
    local(S.pv.at[c], S.pv.at[c], M.gl_.at[0]).wait()
    sent(M.gs_.at[0], S.pv.at[oc])
    arrived(M.gr.at[0], S.pv.at[oc])
    sent(M.hs.at[0], S.hid.at[pl.ds(0, 7)])
    sent(M.ps.at[0], S.pv.at[0])
    for n, like in enumerate((S.b2r, S.a2r, S.b1r, S.i1r, S.b2u, S.a2u, S.c1r, S.c1u)):
        sent(M.ts.at[n], like)
    for cp in own:
        cp.wait()
    sent(M.is_.at[0], S.i1u)
    for sem, like in ((M.xis, S.xi), (M.xos, S.xo), (M.yis, S.yi), (M.yos, S.yo)):
        sent(sem.at[0], like.at[seven])


def main_kernel(args):
    any_space = pl.BlockSpec(memory_space=pl.ANY)
    vmem = pl.BlockSpec(memory_space=pltpu.VMEM)
    return pl.pallas_call(
        body,
        out_shape=[
            pltpu.VMEM((TOK, D), BF),
            pltpu.VMEM((TOK, D), BF),
            pltpu.VMEM((2 * HEADS, BLOCKS * TOK, 128), BF),
            pltpu.VMEM((BLOCKS, 32, HALF), BF),
            pltpu.VMEM((BLOCKS, 16, HALF), BF),
            pltpu.VMEM((BLOCKS, 16, HALF), BF),
        ],
        in_specs=[any_space] * len(args),
        out_specs=[vmem, vmem] + [any_space] * 4,
        scratch_shapes=[pltpu.VMEM(s, t) for s, t in SCRATCH.values()]
        + [pltpu.SemaphoreType.DMA((n,)) for n in SEMS.values()]
        + [pltpu.SMEM((1, SEQS), jnp.int32)],
        compiler_params=pltpu.CompilerParams(
            collective_id=0, has_side_effects=True, vmem_limit_bytes=52 * 2**20
        ),
        name="layer",
    )(*args)


def lay_out(oh, gh, gl, zrb, zra, wr, *refs):
    outs, sem = refs[:18], refs[18]
    copies = [
        pltpu.make_async_copy(src, dst, sem.at[i])
        for i, (src, dst) in enumerate(((gl, outs[2]), (oh, outs[0]), (gh, outs[1])))
    ]
    for copy in copies:
        copy.start()

    def summed(ref):
        out = []
        for half in range(2):
            total = ref[half].astype(F32)
            for zz in range(1, 4):
                total = total + ref[2 * zz + half].astype(F32)
            out.append(total)
        return out

    outer = summed(zrb)
    tail = jnp.zeros((8, 128), F32)
    for k in range(BLOCKS):
        rows = wr[k].astype(F32)
        tail = tail + rows[0:8, :128]
        at = (k % 2) * HALF + (k // 2) * 96
        for t in range(3):
            outs[3 + t][:, at : at + 96] = rows[0:6, 128 * t : 128 * t + 96]
    outs[6][...] = jnp.concatenate([outer[0][24:30, :], outer[1][24:30, :]], axis=1)
    for k in range(BLOCKS):
        at = (k % 2) * (FF // 2) + (k // 2) * HALF
        outs[7][:, at : at + HALF] = zra[k].astype(F32)[0:6, :]
    outs[8][...] = jnp.concatenate([outer[0][0:24, :], outer[1][0:24, :]], axis=1)
    flipped = jnp.concatenate([tail, jnp.zeros((120, 128), F32)], axis=0).T
    for slot, row in ((9, 0), (10, 1), (11, 2), (13, 3), (14, 4), (15, 5), (16, 6), (17, 7)):
        outs[slot][...] = flipped[96 + row, 0:6]
    inner = jnp.zeros((1, 128), F32)
    lane = iota((1, 128), 1)
    for i in range(6):
        for j in range(4):
            inner = jnp.where(lane == 4 * i + j, flipped[104 + j : 105 + j, i : i + 1], inner)
    outs[12][...] = inner[0, 0:24]
    for copy in copies:
        copy.wait()


def out_kernel(*args):
    vmem = pl.BlockSpec(memory_space=pltpu.VMEM)
    any_space = pl.BlockSpec(memory_space=pl.ANY)
    f = lambda *s: jax.ShapeDtypeStruct(s, F32)
    return pl.pallas_call(
        lay_out,
        out_shape=[
            jax.ShapeDtypeStruct((TOK, D), BF),
            jax.ShapeDtypeStruct((TOK, D), BF),
            jax.ShapeDtypeStruct((2 * HEADS, BLOCKS * TOK, 128), BF),
            f(6, D),
            f(6, D),
            f(6, D),
            f(6, D),
            f(6, FF),
            f(24, D),
            f(6),
            f(6),
            f(6),
            f(24),
            f(6),
            f(6),
            f(6),
            f(6),
            f(6),
        ],
        in_specs=[any_space] * 3 + [vmem] * 3,
        out_specs=[any_space] * 3 + [vmem] * 15,
        scratch_shapes=[pltpu.SemaphoreType.DMA((3,))],
        compiler_params=pltpu.CompilerParams(vmem_limit_bytes=8 * 2**20),
        name="lay_out",
    )(*args)


def on_device(*args):
    parts = main_kernel(args)
    return tuple(out_kernel(*[pltpu.with_memory_space_constraint(p, pltpu.VMEM) for p in parts]))


def solution(mesh):
    rows = P(("batch", "keys"), None)
    logits = P(None, "batch", "keys")
    flat = P(("batch", "keys"))
    return jax.shard_map(
        on_device,
        mesh=mesh,
        in_specs=(rows, logits, P("batch", None), rows) + (P(),) * 15,
        out_specs=(rows, rows, logits) + (rows,) * 6 + (flat,) * 9,
        check_vma=False,
    )
```

```python
from types import SimpleNamespace
from typing import Any, NamedTuple

import jax
import jax.numpy as jnp
from jax import lax
from jax.experimental import pallas as pl
from jax.experimental.pallas import tpu as pltpu
from jax.sharding import PartitionSpec as P

EPSILON = 1e-05
NEGATIVE = -1e30
MESH = pl.DeviceIdType.MESH
BF = jnp.bfloat16
F32 = jnp.float32

TOK = 128
D = 768
HALF = 384
HEADS = 6
FF = 3072
SEQS = 16
BLOCKS = 8


def dot(a, b):
    return lax.dot_general(a, b, (((1,), (0,)), ((), ())), preferred_element_type=F32)


def dot_nt(a, b):
    return lax.dot_general(a, b, (((1,), (1,)), ((), ())), preferred_element_type=F32)


def dot_tn(a, b):
    return lax.dot_general(a, b, (((0,), (0,)), ((), ())), preferred_element_type=F32)


def iota(shape, dim):
    return lax.broadcasted_iota(jnp.int32, shape, dim)


def split_hi_lo(v):
    hi = v.astype(BF)
    lo = (v - hi.astype(F32)).astype(BF)
    return jnp.concatenate([hi.astype(F32), lo.astype(F32)], axis=0).astype(BF)


def head_rows():
    return jnp.where(iota((16, HALF), 1) // 64 == iota((16, HALF), 0) % 8, 1.0, 0.0).astype(BF)


def unit_rows():
    return jnp.where(iota((16, 128), 1) == iota((16, 128), 0), 1.0, 0.0).astype(BF)


def row_sums(v):
    return jnp.sum(v, axis=0, keepdims=True)


def norm(values):
    average = jnp.mean(values, axis=-1, keepdims=True)
    centered = values - average
    variance = jnp.mean(centered * centered, axis=-1, keepdims=True)
    inverse = lax.rsqrt(variance + EPSILON)
    return centered * inverse, inverse


def norm_back(upstream, normed, inverse, gain):
    scaled = upstream * gain
    return inverse * (
        scaled
        - jnp.mean(scaled, axis=-1, keepdims=True)
        - normed * jnp.mean(scaled * normed, axis=-1, keepdims=True)
    )


class Args(NamedTuple):
    hidden: Any
    prev: Any
    lengths: Any
    gout: Any
    w_q: Any
    w_k: Any
    w_v: Any
    w_o: Any
    w_i: Any
    w_u: Any
    b_q: Any
    b_v: Any
    b_o: Any
    b_i: Any
    b_u: Any
    g_a: Any
    b_a: Any
    g_f: Any
    b_f: Any


class Outs(NamedTuple):
    out_hidden: Any
    grad_hidden: Any
    gl: Any
    zrb: Any
    zra: Any
    wr: Any


SCRATCH = dict(
    wq=((2, D, HALF), BF),
    wk=((2, D, HALF), BF),
    wv=((2, D, HALF), BF),
    wo=((D, D), BF),
    wi=((4, D, D), BF),
    wu=((4, D, D), BF),
    wot=((D, D), BF),
    wit=((4, D, D), BF),
    wut=((4, D, D), BF),
    vq=((D,), F32),
    vv=((D,), F32),
    vo=((D,), F32),
    vi=((FF,), F32),
    vu=((D,), F32),
    ga=((D,), F32),
    ba=((D,), F32),
    gf=((D,), F32),
    bf=((D,), F32),
    go=((TOK, D), BF),
    hid=((BLOCKS, TOK, D), BF),
    pv=((2, HEADS, BLOCKS * TOK, 128), BF),
    qs=((TOK, HALF), BF),
    km=((HEADS, 256, 128), BF),
    ve=((HEADS, 256, 256), BF),
    madd=((BLOCKS, TOK, 256), F32),
    obuf=((BLOCKS, TOK, HALF), BF),
    orecv=((BLOCKS, TOK, HALF), BF),
    st=((BLOCKS, 16, 128), F32),
    strecv=((BLOCKS, 16, 128), F32),
    at=((2, TOK, HALF), F32),
    atx=((2, TOK, D), BF),
    n1=((TOK, D), F32),
    gs=((TOK, D), F32),
    gp=((4, TOK, D), F32),
    ogs=((2, TOK, HALF), BF),
    brs=((2, TOK, HALF), BF),
    brr=((TOK, HALF), BF),
    brow=((2, 16, HALF), F32),
    ags=((2, TOK, HALF), BF),
    dorecv=((BLOCKS, TOK, HALF), BF),
    s2=((2, 16, 128), F32),
    s2recv=((BLOCKS, 16, 128), F32),
    dkt=((HALF, 256), F32),
    dvt=((HALF, 256), F32),
    dq=((BLOCKS, TOK, HALF), BF),
    dqr=((2, 2, TOK, HALF), BF),
    dqo=((2, TOK, HALF), BF),
    dqh=((2, 2, 64, HALF), BF),
    kgs=((2, TOK, HALF), BF),
    kgr=((TOK, HALF), BF),
    vgs=((2, TOK, HALF), BF),
    vgr=((TOK, HALF), BF),
    a2s=((4, 192, HALF), BF),
    a2p=((2, 96, HALF), BF),
    a2r=((2, 192, HALF), BF),
    a2t=((4, 48, HALF), BF),
    a2u=((3, 48, HALF), BF),
    b2s=((4, 4, 48, 256), BF),
    b2r=((3, 4, 48, 256), BF),
    b2t=((4, 48, 256), BF),
    b2u=((3, 48, 256), BF),
    fa2=((48, HALF), F32),
    fb1=((192, HALF), F32),
    fx=((TOK, D), BF),
    ax=((4, TOK, D), BF),
    igs=((2, 4, TOK, HALF), BF),
    xi=((BLOCKS, TOK, D), BF),
    xo=((BLOCKS, TOK, D), BF),
    yi=((BLOCKS, TOK, HALF), BF),
    yo=((BLOCKS, TOK, HALF), BF),
    b1s=((4, 192, HALF), BF),
    b1p=((2, 96, HALF), BF),
    b1r=((2, 192, HALF), BF),
    c1s=((4, 4, 48, HALF), BF),
    c1p=((2, 2, 48, HALF), BF),
    c1r=((2, 4, 48, HALF), BF),
    c1t=((4, 48, HALF), BF),
    c1u=((3, 48, HALF), BF),
    fc1=((48, HALF), F32),
    i1s=((4, 192, HALF), BF),
    i1p=((2, 96, HALF), BF),
    i1r=((2, 192, HALF), BF),
    fi1=((192, HALF), F32),
    i1f=((48, HALF), F32),
    i1z=((4, 48, HALF), BF),
    i1u=((3, 48, HALF), BF),
    i1g=((16, HALF), F32),
    i1t=((BLOCKS, 16, HALF), BF),
    fb2=((48, 256), F32),
    zf=((32, HALF), F32),
    zsb=((BLOCKS, 32, HALF), BF),
    zf2=((16, HALF), F32),
    zs2=((BLOCKS, 16, HALF), BF),
    qt=((BLOCKS, HALF, TOK), BF),
    kvt=((2, HALF, 256), BF),
    ykv=((256, BLOCKS * TOK), BF),
)
SEMS = dict(
    ld=21,
    outs=3,
    pl_=4,
    ps=1,
    pr=4,
    hs=1,
    hr=9,
    os=1,
    or_=1,
    ss=1,
    sr=1,
    xs=2,
    xr=2,
    xis=1,
    xir=2,
    xos=1,
    xor_=2,
    yis=1,
    yir=1,
    yos=1,
    yor=1,
    ds=1,
    dr=6,
    es=1,
    er=4,
    ts=4,
    tr=4,
    rs=4,
    rh=8,
    rr=4,
    is_=1,
    ir=1,
    qs_=1,
    qr=4,
    gl_=1,
    gs_=1,
    gr=1,
    ks=1,
    kr=1,
    ys=1,
    yr=1,
    zs_=1,
    zr_=1,
    vs=1,
    vr=1,
    ws=1,
    wr=1,
    own=3,
)


def body(*refs):
    na, no, nsc = len(Args._fields), len(Outs._fields), len(SCRATCH)
    A = Args(*refs[:na])
    O = Outs(*refs[na : na + no])
    S = SimpleNamespace(**dict(zip(SCRATCH, refs[na + no : na + no + nsc])))
    M = SimpleNamespace(**dict(zip(SEMS, refs[na + no + nsc : -1])))
    LEN = refs[-1]

    bi = lax.axis_index("batch")
    ki = lax.axis_index("keys")
    x, y = bi // 4, lax.rem(bi, 4)
    z, c = ki // 2, lax.rem(ki, 2)
    oc = 1 - c

    def dev(dx=0, dy=0, dz=0, dc=0):
        nb = lax.rem(x + dx, 4) * 4 + lax.rem(y + dy, 4)
        return (nb, lax.rem(z + dz, 4) * 2 + lax.rem(c + dc, 2))

    def key_of(dz, dc):
        return lax.rem(z + dz, 4) * 2 + lax.rem(c + dc, 2)

    def far(d):
        return d + (d // 2) * (1 - 2 * lax.rem(d, 2))

    def remote(src, dst, ssem, rsem, to):
        return pltpu.make_async_remote_copy(
            src_ref=src, dst_ref=dst, send_sem=ssem, recv_sem=rsem, device_id=to, device_id_type=MESH
        )

    def sent(sem, like):
        remote(like, like, sem, sem, dev(dc=1)).wait_send()

    def arrived(sem, like):
        remote(like, like, sem, sem, dev(dc=1)).wait_recv()

    def local(src, dst, sem):
        return pltpu.make_async_copy(src, dst, sem)

    loads = [
        local(A.hidden, S.hid.at[ki], M.ld.at[0]),
        local(A.w_k.at[:, pl.ds(pl.multiple_of(c * HALF, 128), HALF)], S.wk.at[c], M.ld.at[1]),
        local(A.w_v.at[:, pl.ds(pl.multiple_of(c * HALF, 128), HALF)], S.wv.at[c], M.ld.at[2]),
        local(A.w_q.at[:, pl.ds(pl.multiple_of(c * HALF, 128), HALF)], S.wq.at[c], M.ld.at[3]),
        local(A.b_q, S.vq, M.ld.at[4]),
        local(A.b_v, S.vv, M.ld.at[5]),
    ]
    lengths = local(A.lengths, LEN, M.ld.at[17])
    lengths.start()
    later = [
        local(A.w_o, S.wo, M.ld.at[6]),
        local(A.b_o, S.vo, M.ld.at[7]),
        local(A.b_i, S.vi, M.ld.at[8]),
        local(A.b_u, S.vu, M.ld.at[9]),
        local(A.g_a, S.ga, M.ld.at[10]),
        local(A.b_a, S.ba, M.ld.at[11]),
        local(A.g_f, S.gf, M.ld.at[12]),
        local(A.b_f, S.bf, M.ld.at[13]),
        local(A.gout, S.go, M.ld.at[14]),
    ]
    for j in range(4):
        later.append(local(A.w_i.at[:, pl.ds(D * j, D)], S.wi.at[j], M.ld.at[15]))
        later.append(local(A.w_u.at[pl.ds(D * j, D)], S.wu.at[j], M.ld.at[16]))
    last = [
        local(a.at[:, pl.ds(pl.multiple_of(oc * HALF, 128), HALF)], s.at[oc], M.outs.at[i])
        for i, (a, s) in enumerate(((A.w_q, S.wq), (A.w_k, S.wk), (A.w_v, S.wv)))
    ]
    for cp in loads:
        cp.start()

    def prev_rows(dz):
        return pl.ds(pl.multiple_of(lax.rem(z + dz, 4) * 256, 256), 256)

    def prev_local(dz):
        rows = prev_rows(dz)
        return local(
            A.prev.at[pl.ds(c * HEADS, HEADS), rows, :], S.pv.at[c, :, rows, :], M.pl_.at[dz]
        )

    def prev_remote(dz):
        rows = prev_rows(dz)
        return remote(
            A.prev.at[pl.ds(oc * HEADS, HEADS), rows, :],
            S.pv.at[c, :, rows, :],
            M.ps.at[0],
            M.pr.at[dz],
            dev(dc=1),
        )

    for dz in (0, 1, 3, 2):
        prev_local(dz).start()

    peers = [(0, 0, dz, dc) for dz in range(4) for dc in range(2) if dz or dc]
    peers += [(d, 0, 0, dc) for d in (1, 2, 3) for dc in range(2)]
    peers += [(0, d, 0, dc) for d in (1, 2, 3) for dc in range(2)]
    barrier = pltpu.get_barrier_semaphore()
    for off in peers:
        pl.semaphore_signal(barrier, inc=1, device_id=dev(*off), device_id_type=MESH)
    pl.semaphore_wait(barrier, len(peers))

    def rows_half(h):
        return pl.ds(64 * h, 64)

    def hid_send(i, src, k, rows, dz, dc):
        remote(src, S.hid.at[k, rows], M.hs.at[0], M.hr.at[i], dev(dz=dz, dc=dc)).start()

    def hid_arrival(i, k, rows):
        arrived(M.hr.at[i], S.hid.at[k, rows])

    low, high, whole = rows_half(0), rows_half(1), pl.ds(0, TOK)
    hid_send(3, A.hidden.at[low], ki, low, 1, 0)
    hid_send(2, A.hidden.at[high], ki, high, 3, 0)
    hid_send(0, A.hidden, ki, whole, 0, 1)
    hid_send(4, A.hidden.at[high], ki, high, 1, 0)
    hid_send(1, A.hidden.at[low], ki, low, 3, 0)
    prev_remote(0).start()
    prev_remote(1).start()
    prev_remote(3).start()
    prev_remote(2).start()

    bounds = []
    running = jnp.int32(0)
    lengths.wait()
    for j in range(SEQS):
        running = running + LEN[0, j]
        bounds.append(running)

    def segment_of(places):
        counted = jnp.zeros(places.shape, jnp.int32)
        for bound in bounds:
            counted = counted + jnp.where(places >= bound, 1, 0)
        return jnp.where(places < bounds[-1], counted, -1 - places)

    lane8 = iota((8, 128), 1)
    key_segment = [segment_of(lane8 * BLOCKS + z * 2 + half)[0:1, :] for half in range(2)]
    lane = iota((TOK, 128), 1)

    in_block = iota((TOK, 128), 0)

    def mask(k, carry):
        row_segment = segment_of(in_block * BLOCKS + k)
        for half in range(2):
            allowed = row_segment == key_segment[half]
            S.madd[k, :, 128 * half : 128 * half + 128] = jnp.where(allowed, 0.0, NEGATIVE)
        return carry

    lax.fori_loop(0, BLOCKS, mask, 0)

    for cp in loads[:1] + loads[1:3] + loads[5:6]:
        cp.wait()
    hid_arrival(0, key_of(0, 1), whole)
    pair = pl.ds(z * 2, 2)
    hid_pair = S.hid[pair].reshape(256, D)
    key_rows = dot(hid_pair, S.wk[c]).astype(BF).astype(F32)
    bias_v = S.vv[...].reshape(1, D)
    bias_q = S.vq
    bv = jnp.where(c == 0, bias_v[:, :HALF], bias_v[:, HALF:])
    value_rows = (dot(hid_pair, S.wv[c]) + bv).astype(BF).astype(F32)
    lane2 = iota((256, 128), 1)
    for h in range(HEADS):
        g, e = h // 2, h % 2
        mine = lane2 // 64 == e
        S.km[h] = jnp.where(mine, key_rows[:, 128 * g : 128 * g + 128], 0.0).astype(BF)
        S.ve[h, :, :128] = jnp.where(mine, value_rows[:, 128 * g : 128 * g + 128], 0.0).astype(BF)
        S.ve[h, :, 128:] = jnp.where((lane2 == h) | (lane2 == 8 + h), 1.0, 0.0).astype(BF)
    loads[3].wait()
    loads[4].wait()
    bias_q = S.vq[...].reshape(1, D)
    S.brow[...] = jnp.zeros((2, 16, HALF), F32)
    S.ykv[...] = jnp.zeros((256, BLOCKS * TOK), BF)
    S.zf[...] = jnp.zeros((32, HALF), F32)
    S.zf2[...] = jnp.zeros((16, HALF), F32)
    S.i1g[...] = jnp.zeros((16, HALF), F32)
    for cp in later + last:
        cp.start()

    def out_send(k, to):
        return remote(S.obuf.at[k], S.orecv.at[ki], M.os.at[0], M.or_.at[0], to)

    def st_send(k, to):
        return remote(S.st.at[k], S.strecv.at[ki], M.ss.at[0], M.sr.at[0], to)

    def forward(i, carry):
        ring = (i + 2) // 4
        odd = lax.rem(ring, 2)
        dz = ring + odd * 2 * lax.rem(i, 2)
        dc = (1 - odd) * lax.rem(i, 2) + odd * (i // 4)
        k = key_of(dz, dc)

        @pl.when(i == 2)
        def _():
            above, below = key_of(1, 0), key_of(3, 0)
            hid_arrival(3, below, low)
            hid_send(7, S.hid.at[below, low], below, low, 1, 0)
            hid_arrival(2, above, high)
            hid_send(7, S.hid.at[above, high], above, high, 3, 0)
            hid_arrival(1, above, low)
            hid_send(5, S.hid.at[above], above, whole, 0, 1)

        @pl.when(i == 3)
        def _():
            hid_arrival(4, k, high)
            hid_send(6, S.hid.at[k], k, whole, 0, 1)

        @pl.when(i >= 4)
        def _():
            hid_arrival(i + 1, k, whole)

        @pl.when(i == 6)
        def _():
            hid_send(8, S.hid.at[k], k, whole, 0, 1)

        @pl.when(dc == 0)
        def _():
            prev_local(dz).wait()
            prev_remote(dz).wait_recv()

        bq = jnp.where(c == 0, bias_q[:, :HALF], bias_q[:, HALF:])
        queries = (dot(S.hid[k], S.wq[c]) + bq).astype(BF).astype(F32) * 0.125
        S.qs[...] = queries.astype(BF)
        S.qt[k] = queries.T.astype(BF)
        rows = pl.ds(pl.multiple_of(k * TOK, TOK), TOK)
        totals = jnp.zeros((TOK, 128), F32)
        tops = jnp.zeros((TOK, 128), F32)
        for g in range(3):
            two = S.qs[:, 128 * g : 128 * g + 128]
            mixed = jnp.zeros((TOK, 128), F32)
            for h in (2 * g, 2 * g + 1):
                before = jnp.concatenate([S.pv[0, h, rows, :], S.pv[1, h, rows, :]], axis=1)
                s = dot_nt(two, S.km[h]) + before.astype(F32) + S.madd[k]
                top = jnp.max(s, axis=1, keepdims=True)
                p = jnp.exp(s - top).astype(BF)
                S.pv[0, h, rows, :] = p[:, :128]
                S.pv[1, h, rows, :] = p[:, 128:]
                o = dot(p, S.ve[h])
                mixed = mixed + o[:, :128]
                totals = totals + o[:, 128:]
                tops = jnp.where(lane == 8 + h, top, tops)
            S.obuf[k, :, 128 * g : 128 * g + 128] = mixed.astype(BF)
        stats = jnp.where(lane < 8, totals, tops)
        S.st[k] = stats.T[:16, :]

        @pl.when(i > 0)
        def _():
            to = dev(dz=dz, dc=dc)
            out_send(k, to).start()
            st_send(k, to).start()

        return carry

    lax.fori_loop(0, BLOCKS, forward, 0)

    S.orecv[ki] = S.obuf[ki]
    S.strecv[ki] = S.st[ki]

    seven = pl.ds(0, 7)
    for cp in later[:9]:
        cp.wait()
    local(S.wi, S.wi, M.ld.at[15]).wait()
    local(S.wu, S.wu, M.ld.at[16]).wait()
    S.wot[...] = S.wo[...].T
    for j in range(4):
        S.wit[j] = S.wi[j].T
        S.wut[j] = S.wu[j].T
    arrived(M.or_.at[0], S.orecv.at[seven])
    arrived(M.sr.at[0], S.strecv.at[seven])
    row8 = iota((8, 128), 0)
    spread = head_rows()
    lse = []
    for half in range(2):
        tops = [S.strecv[2 * zz + half, 8:16, :] for zz in range(4)]
        sums = [S.strecv[2 * zz + half, 0:8, :] for zz in range(4)]
        top = jnp.maximum(jnp.maximum(tops[0], tops[1]), jnp.maximum(tops[2], tops[3]))
        shares = [jnp.exp(t - top) for t in tops]
        total = shares[0] * sums[0] + shares[1] * sums[1] + shares[2] * sums[2] + shares[3] * sums[3]
        total = jnp.where(row8 < HEADS, total, 1.0)
        lse.append(jnp.where(row8 < HEADS, top + jnp.log(total), 0.0))
        acc = jnp.zeros((TOK, HALF), F32)
        for zz in range(4):
            factor = dot_tn(split_hi_lo(jnp.where(row8 < HEADS, shares[zz] / total, 0.0)), spread)
            acc = acc + S.orecv[2 * zz + half].astype(F32) * factor
        S.at[half] = acc
        S.atx[0, :, HALF * half : HALF * half + HALF] = acc.astype(BF)

    other = dev(dc=1)

    def swap(i, src, dst):
        copy = remote(src, dst, M.xs.at[i], M.xr.at[i], other)
        copy.start()
        return copy

    swap_at = swap(0, S.atx.at[0], S.atx.at[1])

    def vec(ref):
        return ref[...].reshape(1, -1)

    attn_low = S.atx[0]
    first_sum = S.hid[ki].astype(F32) + dot(attn_low, S.wo[...]) + vec(S.vo)
    normed, inverse_a = norm(first_sum)
    S.n1[...] = normed
    first_low = (normed * vec(S.ga) + vec(S.ba)).astype(BF)
    S.fx[...] = first_low
    in_y, in_x = y * 2 + c, x * 2 + c
    S.xi[in_y] = first_low

    def xi_send(i, src, k, **to):
        remote(src, S.xi.at[k], M.xis.at[0], M.xir.at[i], dev(**to)).start()

    for d in (1, 3, 2):
        xi_send(0, S.fx, in_y, dy=d)
    xi_send(1, S.fx, in_y, dc=1)
    second = normed * vec(S.ga) + vec(S.ba) + vec(S.vu)
    bias_i = vec(S.vi)
    for j in range(4):
        inner = dot(S.fx[...], S.wi[j]) + bias_i[:, D * j : D * j + D]
        cdf = 0.5 + 0.5 * lax.erf(inner * 0.7071067811865476)
        density = jnp.exp(inner * inner * -0.5) * 0.3989422804014327
        S.gp[j] = cdf + inner * density
        S.ax[j] = (inner * cdf).astype(BF)

        @pl.when(x != j)
        def _():
            remote(S.ax.at[j], S.xo.at[in_x], M.xos.at[0], M.xor_.at[0], (j * 4 + y, ki)).start()

        @pl.when(x == j)
        def _():
            remote(S.ax.at[j], S.xo.at[in_x], M.xos.at[0], M.xor_.at[1], other).start()
            S.xo[in_x] = S.ax[j]

        second = second + dot(S.ax[j], S.wu[j])
    normed_f, inverse_f = norm(second)
    O.out_hidden[...] = (normed_f * vec(S.gf) + vec(S.bf)).astype(BF)
    upstream = S.go[...].astype(F32)

    def put_row(r, values):
        sums = row_sums(values)
        S.brow[0, r : r + 1, :] = sums[:, :HALF]
        S.brow[1, r : r + 1, :] = sums[:, HALF:]

    put_row(6, upstream * normed_f)
    put_row(7, upstream)
    grad_second = norm_back(upstream, normed_f, inverse_f, vec(S.gf))
    og = grad_second.astype(BF)
    put_row(3, og.astype(F32))
    S.ogs[0] = og[:, :HALF]
    S.ogs[1] = og[:, HALF:]
    ring_places = [(d, dc) for d in (1, 3, 2) for dc in range(2)]

    for d, dc in ring_places + [(0, 1)]:
        src = S.ogs.at[lax.rem(c + dc, 2)]
        remote(src, S.yo.at[in_x], M.yos.at[0], M.yor.at[0], dev(dx=d, dc=dc)).start()
    S.yo[in_x] = S.ogs[c]
    S.gs[...] = grad_second
    bsum = []
    for j in range(4):
        ig = (dot(og, S.wut[j]) * S.gp[j]).astype(BF)
        S.igs[j // 2, 2 * (j % 2)] = ig[:, :HALF]
        S.igs[j // 2, 2 * (j % 2) + 1] = ig[:, HALF:]
        bsum.append(row_sums(ig.astype(F32)))
        S.gs[...] = S.gs[...] + dot(ig, S.wit[j])
    for d, dc in ring_places + [(0, 1)]:
        src = S.igs.at[lax.rem(c + dc, 2), lax.rem(y + d, 4)]
        remote(src, S.yi.at[in_y], M.yis.at[0], M.yir.at[0], dev(dy=d, dc=dc)).start()
    S.yi[in_y] = S.igs[c, y]

    grad_first = S.gs[...]
    normed = S.n1[...]
    put_row(4, grad_first * normed)
    put_row(5, grad_first)
    grad_first_sum = norm_back(grad_first, normed, inverse_a, vec(S.ga))
    S.gs[...] = grad_first_sum
    br = grad_first_sum.astype(BF)
    put_row(2, br.astype(F32))
    S.brs[0] = br[:, :HALF]
    S.brs[1] = br[:, HALF:]
    swap_br = swap(1, S.brs.at[oc], S.brr)
    ag = dot(br, S.wot[...]).astype(BF)
    for half in range(2):
        S.ags[half] = ag[:, HALF * half : HALF * half + HALF]
        product = S.at[half] * ag[:, HALF * half : HALF * half + HALF].astype(F32)
        dots = jnp.zeros((16, TOK), F32)
        hi = product.astype(BF)
        lo = (product - hi.astype(F32)).astype(BF)
        dots = dot_nt(spread, hi) + dot_nt(spread, lo)
        S.s2[half, 0:8, :] = dots[0:8, :]
        S.s2[half, 8:16, :] = lse[half]

    def ag_send(i, src, k, rows, dz, dc):
        remote(src, S.dorecv.at[k, rows], M.ds.at[0], M.dr.at[i], dev(dz=dz, dc=dc)).start()

    def ag_arrival(i, dz, rows):
        arrived(M.dr.at[i], S.dorecv.at[pl.ds(lax.rem(z + dz, 4) * 2, 2), rows])

    def s2_send(i, dz, dc):
        half = lax.rem(c + dc, 2)
        remote(S.s2.at[half], S.s2recv.at[ki], M.es.at[0], M.er.at[i], dev(dz=dz, dc=dc)).start()

    def s2_arrival(i, dz):
        arrived(M.er.at[i], S.s2recv.at[pl.ds(lax.rem(z + dz, 4) * 2, 2)])

    for i, dz, rows in ((3, 1, low), (2, 3, high)):
        for dc in range(2):
            ag_send(i, S.ags.at[lax.rem(c + dc, 2), rows], ki, rows, dz, dc)
    ag_send(0, S.ags.at[oc], ki, whole, 0, 1)
    s2_send(0, 0, 1)
    for i, dz in ((2, 1), (1, 3), (3, 2)):
        for dc in range(2):
            s2_send(i, dz, dc)
    for i, dz, rows in ((4, 1, high), (1, 3, low)):
        for dc in range(2):
            ag_send(i, S.ags.at[lax.rem(c + dc, 2), rows], ki, rows, dz, dc)
    S.dorecv[ki] = S.ags[c]
    S.s2recv[ki] = S.s2[c]

    def weight_grad(left, right):
        return dot_tn(left, right).astype(BF)

    def along(axis, d):
        return dev(dx=d) if axis == 0 else dev(dy=d)

    def at_place(axis, d):
        return lax.rem((x if axis == 0 else y) + d, 4)

    def scatter(n, axis, src, dst, inner):
        for d in (1, 2, 3):
            there = at_place(axis, d)
            piece = src.at[:, there] if inner else src.at[there]
            remote(piece, dst.at[d - 1], M.ts.at[n], M.tr.at[n], along(axis, d)).start()

    class Ring:
        def __init__(self, n, axis, piece, held, landed):
            right, left = along(axis, 1), along(axis, 3)
            after, before, across = at_place(axis, 1), at_place(axis, 3), at_place(axis, 2)

            def copy(sem, src, dst, to):
                return remote(src, dst, M.rs.at[n], sem, to)

            here = M.rr.at[n]
            self.n = n

            self.first = [
                copy(M.rh.at[2 * n], piece(across, 0), held.at[0], right),
                copy(M.rh.at[2 * n + 1], piece(across, 1), held.at[1], left),
            ]
            self.own = [
                copy(here, piece(after, 1), landed(0, 1), right),
                copy(here, piece(before, 0), landed(1, 0), left),
            ]
            self.summed = [
                copy(here, held.at[0], landed(0, 0), right),
                copy(here, held.at[1], landed(1, 1), left),
            ]
            self.add = [(held.at[0], piece(after, 0)), (held.at[1], piece(before, 1))]

        def start(self, copies):
            for cp in copies:
                cp.start()

        def pass_on(self):
            for w in range(2):
                self.first[w].wait_recv()
                mine, extra = self.add[w]
                mine[...] = (mine[...].astype(F32) + extra[...].astype(F32)).astype(BF)
                self.summed[w].start()

        def landed(self, both):
            arrived(M.rr.at[self.n], both)

        def drain(self, three):
            sent(M.rs.at[self.n], three)

    def quarter_ring(n, axis, send, held, recv):
        return Ring(
            n,
            axis,
            lambda p, h: send.at[p, pl.ds(96 * h, 96)],
            held,
            lambda w, h: recv.at[w, pl.ds(96 * h, 96)],
        )

    ring_q = quarter_ring(0, 0, S.a2s, S.a2p, S.a2r)
    ring_i = quarter_ring(1, 0, S.i1s, S.i1p, S.i1r)
    ring_u = quarter_ring(2, 1, S.b1s, S.b1p, S.b1r)
    ring_o = Ring(
        3,
        1,
        lambda p, h: S.c1s.at[pl.ds(2 * h, 2), p],
        S.c1p,
        lambda w, h: S.c1r.at[w, pl.ds(2 * h, 2)],
    )
    for cp in [swap_at, swap_br]:
        cp.wait()
    right = jnp.concatenate([S.brs[c], S.brr[...]], axis=0)
    S.c1s[...] = weight_grad(S.atx[...].reshape(256, D), right).reshape(4, 4, 48, HALF)

    lane512 = iota((8, 512), 1)
    sub512 = iota((8, 512), 0)
    pick = jnp.where(
        iota((512, 128), 1) == (iota((512, 128), 0) // 128) * 32 + lax.rem(iota((512, 128), 0), 128) // 4,
        1.0,
        0.0,
    ).astype(BF)
    flat = jnp.concatenate(bsum, axis=1)
    for g in range(6):
        spread_out = jnp.where(lax.rem(lane512, 4) == sub512, flat[:, 512 * g : 512 * g + 512], 0.0)
        S.brow[g // 3, 8:16, 128 * (g % 3) : 128 * (g % 3) + 128] = dot(spread_out.astype(BF), pick)

    def unit(u):
        dc = lax.rem(u, 2)
        dz = far(u // 2)
        return key_of(lax.rem(4 - dz, 4), dc), key_of(dz, dc)

    def unit_rows_of(u):
        ka, kb = unit(u)
        start_a = pl.multiple_of(ka * TOK, 64)
        start_b = pl.multiple_of(kb * TOK + 64, 64)
        return pl.ds(start_a, 64), pl.ds(start_b, 64)

    S.dkt[...] = jnp.zeros((HALF, 256), F32)
    S.dvt[...] = jnp.zeros((HALF, 256), F32)
    units = unit_rows()

    def dq_landing(w, half, h):
        return S.dqr.at[w, half, rows_half(h)], M.qr.at[2]

    def dq_copy(src, place, to):
        return remote(src, place[0], M.qs_.at[0], place[1], to)

    def dq_piece(dz, h):
        return S.dq.at[pl.ds(lax.rem(z + dz, 4) * 2, 2), rows_half(h)]

    dq_partner = dq_copy(S.dq.at[z * 2 + oc], (S.dqo.at[c], M.qr.at[3]), other)
    dq_first = [
        dq_copy(dq_piece(2, 0), (S.dqh.at[0], M.qr.at[0]), dev(dz=1)),
        dq_copy(dq_piece(2, 1), (S.dqh.at[1], M.qr.at[1]), dev(dz=3)),
    ]
    dq_own, dq_summed = [], []
    for w, dz in ((0, 1), (1, 3)):
        h = 1 - w
        dq_own.append(
            [
                dq_copy(
                    S.dq.at[lax.rem(z + dz, 4) * 2 + cc, rows_half(h)],
                    dq_landing(w, c, h),
                    (bi, lax.rem(z + dz, 4) * 2 + cc),
                )
                for cc in range(2)
            ]
        )
        h = w
        dq_summed.append(
            [
                dq_copy(
                    S.dqh.at[w, cc],
                    dq_landing(w, c, h),
                    (bi, lax.rem(z + dz, 4) * 2 + cc),
                )
                for cc in range(2)
            ]
        )

    def gl_rows(zz):
        return pl.ds(pl.multiple_of(zz * 256, 256), 256)

    def gl_local(k):
        rows = gl_rows(k)
        return local(
            S.pv.at[c, :, rows, :], O.gl.at[pl.ds(c * HEADS, HEADS), rows, :], M.gl_.at[0]
        )

    def gl_remote(k):
        rows = gl_rows(k)
        return remote(
            S.pv.at[oc, :, rows, :],
            O.gl.at[pl.ds(c * HEADS, HEADS), rows, :],
            M.gs_.at[0],
            M.gr.at[0],
            dev(dc=1),
        )

    def backward(i, carry):
        @pl.when(i == 2)
        def _():
            arrived(M.xir.at[0], S.xi.at[pl.ds(0, 3)])
            for d in (1, 3, 2):
                k = lax.rem(y + d, 4) * 2 + c
                xi_send(1, S.xi.at[k], k, dc=1)

        @pl.when(i == 3)
        def _():
            ring_o.start(ring_o.first)
            arrived(M.xor_.at[0], S.xo.at[pl.ds(0, 3)])
            for d in (1, 3, 2):
                k = lax.rem(x + d, 4) * 2 + c
                remote(S.xo.at[k], S.xo.at[k], M.xos.at[0], M.xor_.at[1], other).start()

        @pl.when(i == 0)
        def _():
            arrived(M.dr.at[0], S.dorecv.at[key_of(0, 1)])
            arrived(M.er.at[0], S.s2recv.at[key_of(0, 1)])

        @pl.when(i == 1)
        def _():
            ag_arrival(3, 3, low)
            for dc in range(2):
                k = key_of(3, dc)
                ag_send(5, S.dorecv.at[k, low], k, low, 1, 0)
            ag_arrival(2, 1, high)
            for dc in range(2):
                k = key_of(1, dc)
                ag_send(5, S.dorecv.at[k, high], k, high, 3, 0)
            s2_arrival(1, 1)
            s2_arrival(2, 3)

        @pl.when(i == 2)
        def _():
            ag_arrival(1, 1, low)
            ag_arrival(4, 3, high)

        @pl.when(i == 3)
        def _():
            ag_arrival(5, 2, whole)
            s2_arrival(3, 2)

        places, factors, minuses, pieces = [], [], [], []
        for half in range(2):
            u = 2 * i + half
            ka, kb = unit(u)
            places.append((ka, low))
            places.append((kb, high))
            here = jnp.where(lane[:16] < 64, S.s2recv[ka], S.s2recv[kb])
            tops = jnp.where(lane[:8] < 64, S.st[ka, 8:16, :], S.st[kb, 8:16, :])
            share = jnp.exp(tops - here[8:16, :])
            share = jnp.where(row8 < HEADS, share, 0.0)
            minuses.append(dot_tn(split_hi_lo(here[0:8, :] * share * -1.0), units).astype(BF))
            factors.append(dot_tn(split_hi_lo(share), spread))
            pieces += [S.dorecv[ka, low], S.dorecv[kb, high]]
        rows = unit_rows_of(2 * i) + unit_rows_of(2 * i + 1)
        minus = jnp.concatenate(minuses, axis=0)
        scaled = jnp.concatenate(pieces, axis=0).astype(F32) * jnp.concatenate(factors, axis=0)
        scaled_t = scaled.T.astype(BF)
        scaled = scaled.astype(BF)
        in_low = iota((HALF, TOK), 1) < 64
        queries_t = []
        for half in range(2):
            ka, kb = unit(2 * i + half)
            queries_t.append(jnp.where(in_low, S.qt[ka].astype(F32), S.qt[kb].astype(F32)))
        queries_t = jnp.concatenate(queries_t, axis=1).astype(BF)
        for g in range(3):
            left = jnp.concatenate([scaled[:, 128 * g : 128 * g + 128], minus], axis=1)
            partial = jnp.zeros((256, 128), F32)
            for h in (2 * g, 2 * g + 1):
                p = jnp.concatenate(
                    [
                        jnp.concatenate([S.pv[half, h, r, :] for r in rows], axis=0)
                        for half in range(2)
                    ],
                    axis=1,
                )
                grad = (p.astype(F32) * dot_nt(left, S.ve[h])).astype(BF)
                for half in range(2):
                    for e, r in enumerate(rows):
                        at = slice(64 * e, 64 * e + 64)
                        S.pv[half, h, r, :] = grad[at, 128 * half : 128 * half + 128]
                at = slice(64 * h, 64 * h + 64)
                S.dvt[at, :] = S.dvt[at, :] + dot(scaled_t[at, :], p)
                S.dkt[at, :] = S.dkt[at, :] + dot(queries_t[at, :], grad)
                partial = partial + dot(grad, S.km[h])
            partial = (partial * 0.125).astype(BF)
            for e, (k, half_rows) in enumerate(places):
                S.dq[k, half_rows, 128 * g : 128 * g + 128] = partial[64 * e : 64 * e + 64, :]

        @pl.when(i == 0)
        def _():
            dq_partner.start()

        @pl.when(i == 1)
        def _():
            for cp in dq_own[0] + dq_own[1]:
                cp.start()

        def logits_out(zz):
            gl_local(zz).start()
            gl_remote(zz).start()

        @pl.when(i == 0)
        def _():
            logits_out(z)

        @pl.when(i == 2)
        def _():
            logits_out(lax.rem(z + 1, 4))
            logits_out(lax.rem(z + 3, 4))

        @pl.when(i == 3)
        def _():
            logits_out(lax.rem(z + 2, 4))

        return carry

    lax.fori_loop(0, 4, backward, 0)
    S.dqo[c] = S.dq[ki]

    S.kvt[0] = S.dkt[...].astype(BF)
    S.kvt[1] = S.dvt[...].astype(BF)
    mine = pl.ds(pl.multiple_of(z * 256, 256), 256)
    for d in (1, 3, 2):
        there = pl.ds(pl.multiple_of(lax.rem(z + d, 4) * 96, 32), 96)
        for t in range(2):
            place = S.ykv.at[pl.ds(128 * t, 96), mine]
            remote(S.kvt.at[t, there, :], place, M.ys.at[0], M.yr.at[0], dev(dz=d)).start()
    here = pl.ds(pl.multiple_of(z * 96, 32), 96)
    for t in range(2):
        S.ykv[128 * t : 128 * t + 96, mine] = S.kvt[t, here, :]
    key_grad = S.dkt[...].T.astype(BF)
    value_grad = S.dvt[...].T.astype(BF)
    S.kgs[...] = key_grad.reshape(2, TOK, HALF)
    S.vgs[...] = value_grad.reshape(2, TOK, HALF)
    kv_swaps = [
        remote(S.kgs.at[oc], S.kgr, M.ks.at[0], M.kr.at[0], other),
        remote(S.vgs.at[oc], S.vgr, M.ks.at[0], M.kr.at[0], other),
    ]
    for cp in kv_swaps:
        cp.start()
    S.brow[c, 1:2, :] = row_sums(value_grad.astype(F32))
    hid_all = S.hid[...].reshape(BLOCKS * TOK, D)
    query_parts = S.dq[...].reshape(BLOCKS * TOK, HALF)
    S.a2s[...] = weight_grad(hid_all, query_parts).reshape(4, 192, HALF)
    ring_q.start(ring_q.first)
    ring_o.start(ring_o.own)
    S.brow[c, 0:1, :] = row_sums(query_parts.astype(F32))

    arrived(M.yir.at[0], S.yi.at[seven])
    arrived(M.xir.at[1], S.xi.at[pl.ds(0, 4)])
    grad = weight_grad(S.xi[...].reshape(BLOCKS * TOK, D), S.yi[...].reshape(BLOCKS * TOK, HALF))
    S.i1s[...] = grad.reshape(4, 192, HALF)
    ring_i.start(ring_i.first)
    ring_q.start(ring_q.own)
    arrived(M.yor.at[0], S.yo.at[seven])
    arrived(M.xor_.at[1], S.xo.at[pl.ds(0, 4)])
    grad = weight_grad(S.xo[...].reshape(BLOCKS * TOK, D), S.yo[...].reshape(BLOCKS * TOK, HALF))
    S.b1s[...] = grad.reshape(4, 192, HALF)
    ring_u.start(ring_u.first)
    ring_i.start(ring_i.own)
    for cp in dq_first:
        cp.start()

    for cp in last:
        cp.wait()
    arrived(M.kr.at[0], S.kgs)
    total = S.gs[...]
    total = total + dot_nt(S.kgs[c], S.wk[c]) + dot_nt(S.kgr[...], S.wk[oc])
    total = total + dot_nt(S.vgs[c], S.wv[c]) + dot_nt(S.vgr[...], S.wv[oc])
    S.gs[...] = total

    def sum_a(src, recv, dst):
        def step(j, carry):
            part = pl.ds(pl.multiple_of(j * 48, 16), 48)
            total = src[x, part, :].astype(F32)
            for d in range(recv.shape[0]):
                total = total + recv[d, part, :].astype(F32)
            dst[j] = total.astype(BF)
            return carry

        lax.fori_loop(0, 4, step, 0)

    def sum_b(src, recv, dst):
        def step(j, carry):
            total = src[j, y].astype(F32)
            for d in range(recv.shape[0]):
                total = total + recv[d, j].astype(F32)
            dst[j] = total.astype(BF)
            return carry

        lax.fori_loop(0, 4, step, 0)

    def finish(own, recv, dst):
        total = own.astype(F32)
        for d in range(recv.shape[0]):
            total = total + recv[d].astype(F32)
        dst[...] = total

    ring_u.start(ring_u.own)
    ring_o.pass_on()
    ring_q.pass_on()
    arrived(M.yr.at[0], S.kvt.at[:, pl.ds(0, 288)])
    beside = jnp.where(iota((16, 128), 1) == iota((16, 128), 0) + 96, 1.0, 0.0).astype(BF)
    columns = [dot_tn(S.brow[half].astype(BF), beside) for half in range(2)]
    flipped = dot(S.ykv[...], hid_all)
    grad = (flipped[:128, :].T + jnp.concatenate(columns, axis=0)).astype(BF)
    S.b2s[:, :, :, :128] = grad.reshape(4, 4, 48, 128)
    S.b2s[:, :, :, 128:] = flipped[128:, :].T.astype(BF).reshape(4, 4, 48, 128)
    scatter(0, 1, S.b2s, S.b2r, True)

    ring_i.pass_on()
    for w in range(2):
        dq_first[w].wait_recv()
        add = dq_piece((1, 3)[w], w)[...].astype(F32)
        S.dqh[w] = (S.dqh[w].astype(F32) + add).astype(BF)
        for cp in dq_summed[w]:
            cp.start()
    ring_u.pass_on()

    ring_o.landed(S.c1r)
    sum_b(S.c1s, S.c1r, S.c1t)
    scatter(3, 0, S.c1t, S.c1u, False)

    ring_q.landed(S.a2r)
    sum_a(S.a2s, S.a2r, S.a2t)
    scatter(2, 1, S.a2t, S.a2u, False)

    ring_i.landed(S.i1r)
    finish(S.i1s[x], S.i1r, S.fi1)
    for p in range(4):
        for k in range(BLOCKS):
            at = 48 * (k // 2) + 12 * p + 6 * (k % 2)
            S.i1f[6 * k : 6 * k + 6, :] = S.fi1[at : at + 6, :]
        S.i1z[p] = S.i1f[...].astype(BF)
    for d in (1, 3, 2):
        there = lax.rem(z + d, 4)
        remote(S.i1z.at[there], S.i1u.at[d - 1], M.is_.at[0], M.ir.at[0], dev(dz=d)).start()

    dq_partner.wait_recv()
    arrived(M.qr.at[2], S.dqr)
    query_grads = []
    for half in range(2):
        grad = S.dqr[0, half].astype(F32) + S.dqr[1, half].astype(F32) + S.dqo[half].astype(F32)
        query_grads.append(grad.astype(BF))

    total = S.gs[...]
    for half in range(2):
        total = total + dot_nt(query_grads[half], S.wq[half])
    O.grad_hidden[...] = total.astype(BF)

    ring_u.landed(S.b1r)
    finish(S.b1s[y], S.b1r, S.fb1)
    arrived(M.tr.at[3], S.c1u)
    finish(S.c1t[x], S.c1u, S.fc1)
    for p in range(BLOCKS):
        S.zf[0:24, :] = S.fb1[24 * p : 24 * p + 24, :]
        S.zf[24:30, :] = S.fc1[6 * p : 6 * p + 6, :]
        S.zsb[p] = S.zf[...].astype(BF)

    def zb_send(k, to):
        return remote(S.zsb.at[k], O.zrb.at[ki], M.zs_.at[0], M.zr_.at[0], to)

    def w_send(k, to):
        return remote(S.zs2.at[k], O.wr.at[ki], M.ws.at[0], M.wr.at[0], to)

    def to_all(send):
        def step(i, carry):
            dz, dc = far(i // 2), lax.rem(i, 2)
            send(key_of(dz, dc), dev(dz=dz, dc=dc)).start()
            return carry

        lax.fori_loop(1, BLOCKS, step, 0)

    to_all(zb_send)
    own = [
        local(S.zsb.at[ki], O.zrb.at[ki], M.own.at[0]),
        local(S.zs2.at[ki], O.wr.at[ki], M.own.at[1]),
    ]
    own[0].start()

    arrived(M.tr.at[0], S.b2r)
    sum_b(S.b2s, S.b2r, S.b2t)
    scatter(1, 0, S.b2t, S.b2u, False)

    arrived(M.ir.at[0], S.i1u)
    total = S.i1z[z].astype(F32)
    for d in range(3):
        total = total + S.i1u[d].astype(F32)
    S.i1f[...] = total
    for k in range(BLOCKS):
        S.i1g[0:6, :] = S.i1f[6 * k : 6 * k + 6, :]
        S.i1t[k] = S.i1g[...].astype(BF)
    for d, dc in ring_places + [(0, 1)]:
        src = S.i1t.at[lax.rem(y + d, 4) * 2 + lax.rem(c + dc, 2)]
        remote(src, O.zra.at[in_y], M.vs.at[0], M.vr.at[0], dev(dy=d, dc=dc)).start()
    own.append(local(S.i1t.at[in_y], O.zra.at[in_y], M.own.at[2]))
    own[2].start()

    arrived(M.tr.at[1], S.b2u)
    finish(S.b2t[x], S.b2u, S.fb2)
    arrived(M.tr.at[2], S.a2u)
    finish(S.a2t[y], S.a2u, S.fa2)
    for p in range(BLOCKS):
        six = slice(6 * p, 6 * p + 6)
        S.zf2[0:6, :256] = S.fb2[six, :]
        S.zf2[6:12, :] = S.fa2[six, :]
        S.zs2[p] = S.zf2[...].astype(BF)
    to_all(w_send)
    own[1].start()

    sent(M.os.at[0], S.obuf.at[seven])
    sent(M.ss.at[0], S.st.at[seven])
    sent(M.es.at[0], S.s2recv.at[seven])
    sent(M.ys.at[0], S.kvt.at[:, pl.ds(0, 288)])
    sent(M.ks.at[0], S.kgs)
    sent(M.ds.at[0], S.dorecv.at[seven])
    sent(M.qs_.at[0], S.dq.at[seven])
    for ssem, rsem, like in (
        (M.zs_, M.zr_, S.zsb),
        (M.vs, M.vr, S.i1t),
        (M.ws, M.wr, S.zs2),
    ):
        sent(ssem.at[0], like.at[seven])
        arrived(rsem.at[0], like.at[seven])
    local(S.pv.at[c], S.pv.at[c], M.gl_.at[0]).wait()
    sent(M.gs_.at[0], S.pv.at[oc])
    arrived(M.gr.at[0], S.pv.at[oc])
    sent(M.hs.at[0], S.hid.at[pl.ds(0, 7)])
    sent(M.ps.at[0], S.pv.at[0])
    for n, like in enumerate((S.b2r, S.b2u, S.a2u, S.c1u)):
        sent(M.ts.at[n], like)
    for cp in own:
        cp.wait()
    for ring, like in ((ring_q, S.a2s), (ring_i, S.i1s), (ring_u, S.b1s)):
        ring.drain(like.at[pl.ds(0, 3)])
    ring_o.drain(S.c1s.at[:, pl.ds(0, 3)])
    sent(M.is_.at[0], S.i1u)
    for sem, like in ((M.xis, S.xi), (M.xos, S.xo), (M.yis, S.yi), (M.yos, S.yo)):
        sent(sem.at[0], like.at[seven])


def main_kernel(args):
    any_space = pl.BlockSpec(memory_space=pl.ANY)
    vmem = pl.BlockSpec(memory_space=pltpu.VMEM)
    return pl.pallas_call(
        body,
        out_shape=[
            pltpu.VMEM((TOK, D), BF),
            pltpu.VMEM((TOK, D), BF),
            pltpu.VMEM((2 * HEADS, BLOCKS * TOK, 128), BF),
            pltpu.VMEM((BLOCKS, 32, HALF), BF),
            pltpu.VMEM((BLOCKS, 16, HALF), BF),
            pltpu.VMEM((BLOCKS, 16, HALF), BF),
        ],
        in_specs=[any_space] * len(args),
        out_specs=[vmem, vmem] + [any_space] * 4,
        scratch_shapes=[pltpu.VMEM(s, t) for s, t in SCRATCH.values()]
        + [pltpu.SemaphoreType.DMA((n,)) for n in SEMS.values()]
        + [pltpu.SMEM((1, SEQS), jnp.int32)],
        compiler_params=pltpu.CompilerParams(
            collective_id=0, has_side_effects=True, vmem_limit_bytes=58 * 2**20
        ),
        name="layer",
    )(*args)


def lay_out(oh, gh, gl, zrb, zra, wr, *refs):
    outs, sem = refs[:18], refs[18]
    copies = [
        pltpu.make_async_copy(src, dst, sem.at[i])
        for i, (src, dst) in enumerate(((gl, outs[2]), (oh, outs[0]), (gh, outs[1])))
    ]
    for copy in copies:
        copy.start()

    def summed(ref):
        out = []
        for half in range(2):
            total = ref[half].astype(F32)
            for zz in range(1, 4):
                total = total + ref[2 * zz + half].astype(F32)
            out.append(total)
        return out

    outer = summed(zrb)
    tail = jnp.zeros((8, 128), F32)
    for k in range(BLOCKS):
        rows = wr[k].astype(F32)
        tail = tail + rows[0:8, :128]
        at = (k % 2) * HALF + (k // 2) * 96
        for t in range(2):
            outs[4 + t][:, at : at + 96] = rows[0:6, 128 * t : 128 * t + 96]
    query = summed(wr)
    outs[3][...] = jnp.concatenate([query[0][6:12, :], query[1][6:12, :]], axis=1)
    outs[6][...] = jnp.concatenate([outer[0][24:30, :], outer[1][24:30, :]], axis=1)
    for k in range(BLOCKS):
        at = (k % 2) * (FF // 2) + (k // 2) * HALF
        outs[7][:, at : at + HALF] = zra[k].astype(F32)[0:6, :]
    outs[8][...] = jnp.concatenate([outer[0][0:24, :], outer[1][0:24, :]], axis=1)
    flipped = jnp.concatenate([tail, jnp.zeros((120, 128), F32)], axis=0).T
    for slot, row in ((9, 0), (10, 1), (11, 2), (13, 3), (14, 4), (15, 5), (16, 6), (17, 7)):
        outs[slot][...] = flipped[96 + row, 0:6]
    inner = jnp.zeros((1, 128), F32)
    lane = iota((1, 128), 1)
    for i in range(6):
        for j in range(4):
            inner = jnp.where(lane == 4 * i + j, flipped[104 + j : 105 + j, i : i + 1], inner)
    outs[12][...] = inner[0, 0:24]
    for copy in copies:
        copy.wait()


def out_kernel(*args):
    vmem = pl.BlockSpec(memory_space=pltpu.VMEM)
    any_space = pl.BlockSpec(memory_space=pl.ANY)
    f = lambda *s: jax.ShapeDtypeStruct(s, F32)
    return pl.pallas_call(
        lay_out,
        out_shape=[
            jax.ShapeDtypeStruct((TOK, D), BF),
            jax.ShapeDtypeStruct((TOK, D), BF),
            jax.ShapeDtypeStruct((2 * HEADS, BLOCKS * TOK, 128), BF),
            f(6, D),
            f(6, D),
            f(6, D),
            f(6, D),
            f(6, FF),
            f(24, D),
            f(6),
            f(6),
            f(6),
            f(24),
            f(6),
            f(6),
            f(6),
            f(6),
            f(6),
        ],
        in_specs=[any_space] * 3 + [vmem] * 3,
        out_specs=[any_space] * 3 + [vmem] * 15,
        scratch_shapes=[pltpu.SemaphoreType.DMA((3,))],
        compiler_params=pltpu.CompilerParams(vmem_limit_bytes=8 * 2**20),
        name="lay_out",
    )(*args)


def on_device(*args):
    parts = main_kernel(args)
    return tuple(out_kernel(*[pltpu.with_memory_space_constraint(p, pltpu.VMEM) for p in parts]))


def solution(mesh):
    rows = P(("batch", "keys"), None)
    logits = P(None, "batch", "keys")
    flat = P(("batch", "keys"))
    return jax.shard_map(
        on_device,
        mesh=mesh,
        in_specs=(rows, logits, P("batch", None), rows) + (P(),) * 15,
        out_specs=(rows, rows, logits) + (rows,) * 6 + (flat,) * 9,
        check_vma=False,
    )
```

```python
from types import SimpleNamespace
from typing import Any, NamedTuple

import jax
import jax.numpy as jnp
from jax import lax
from jax.experimental import pallas as pl
from jax.experimental.pallas import tpu as pltpu
from jax.sharding import PartitionSpec as P

EPSILON = 1e-05
NEGATIVE = -1e30
MESH = pl.DeviceIdType.MESH
BF = jnp.bfloat16
F32 = jnp.float32

TOK = 128
D = 768
HALF = 384
HEADS = 6
FF = 3072
SEQS = 16
BLOCKS = 8


def dot(a, b):
    return lax.dot_general(a, b, (((1,), (0,)), ((), ())), preferred_element_type=F32)


def dot_nt(a, b):
    return lax.dot_general(a, b, (((1,), (1,)), ((), ())), preferred_element_type=F32)


def dot_tn(a, b):
    return lax.dot_general(a, b, (((0,), (0,)), ((), ())), preferred_element_type=F32)


def iota(shape, dim):
    return lax.broadcasted_iota(jnp.int32, shape, dim)


def split_hi_lo(v):
    hi = v.astype(BF)
    lo = (v - hi.astype(F32)).astype(BF)
    return jnp.concatenate([hi.astype(F32), lo.astype(F32)], axis=0).astype(BF)


def head_rows():
    return jnp.where(iota((16, HALF), 1) // 64 == iota((16, HALF), 0) % 8, 1.0, 0.0).astype(BF)


def unit_rows():
    return jnp.where(iota((16, 128), 1) == iota((16, 128), 0), 1.0, 0.0).astype(BF)


def row_sums(v):
    return jnp.sum(v, axis=0, keepdims=True)


def norm(values):
    average = jnp.mean(values, axis=-1, keepdims=True)
    centered = values - average
    variance = jnp.mean(centered * centered, axis=-1, keepdims=True)
    inverse = lax.rsqrt(variance + EPSILON)
    return centered * inverse, inverse


def norm_back(upstream, normed, inverse, gain):
    scaled = upstream * gain
    return inverse * (
        scaled
        - jnp.mean(scaled, axis=-1, keepdims=True)
        - normed * jnp.mean(scaled * normed, axis=-1, keepdims=True)
    )


class Args(NamedTuple):
    hidden: Any
    prev: Any
    lengths: Any
    gout: Any
    w_q: Any
    w_k: Any
    w_v: Any
    w_o: Any
    w_i: Any
    w_u: Any
    b_q: Any
    b_v: Any
    b_o: Any
    b_i: Any
    b_u: Any
    g_a: Any
    b_a: Any
    g_f: Any
    b_f: Any


class Outs(NamedTuple):
    out_hidden: Any
    grad_hidden: Any
    gl: Any
    zrb: Any
    zra: Any
    wr: Any


SCRATCH = dict(
    wq=((2, D, HALF), BF),
    wk=((2, D, HALF), BF),
    wv=((2, D, HALF), BF),
    wo=((D, D), BF),
    wi=((4, D, D), BF),
    wu=((4, D, D), BF),
    wot=((D, D), BF),
    wit=((4, D, D), BF),
    wut=((4, D, D), BF),
    vq=((D,), F32),
    vv=((D,), F32),
    vo=((D,), F32),
    vi=((FF,), F32),
    vu=((D,), F32),
    ga=((D,), F32),
    ba=((D,), F32),
    gf=((D,), F32),
    bf=((D,), F32),
    go=((TOK, D), BF),
    hid=((BLOCKS, TOK, D), BF),
    pv=((2, HEADS, BLOCKS * TOK, 128), BF),
    pw=((BLOCKS, HEADS, TOK, 256), BF),
    qs=((TOK, HALF), BF),
    km=((HEADS, 256, 128), BF),
    ve=((HEADS, 256, 256), BF),
    madd=((BLOCKS, TOK, 256), F32),
    obuf=((BLOCKS, TOK, HALF), BF),
    orecv=((BLOCKS, TOK, HALF), BF),
    st=((BLOCKS, 16, 128), F32),
    stu=((BLOCKS, 16, 128), F32),
    strecv=((BLOCKS, 16, 128), F32),
    at=((2, TOK, HALF), F32),
    atx=((2, TOK, D), BF),
    n1=((TOK, D), F32),
    gs=((TOK, D), F32),
    gp=((4, TOK, D), BF),
    ogs=((2, TOK, HALF), BF),
    brs=((2, TOK, HALF), BF),
    brr=((TOK, HALF), BF),
    brow=((2, 16, HALF), F32),
    ags=((2, TOK, HALF), BF),
    dorecv=((BLOCKS, TOK, HALF), BF),
    s2=((2, 16, 128), F32),
    s2recv=((BLOCKS, 16, 128), F32),
    dkt=((HALF, 256), F32),
    dvt=((HALF, 256), F32),
    dqr=((2, 2, TOK, HALF), BF),
    dqo=((2, TOK, HALF), BF),
    dqh=((2, 2, 64, HALF), BF),
    kgs=((2, TOK, HALF), BF),
    kgr=((TOK, HALF), BF),
    vgs=((2, TOK, HALF), BF),
    vgr=((TOK, HALF), BF),
    a2s=((4, 192, HALF), BF),
    a2p=((2, 96, HALF), BF),
    a2r=((2, 192, HALF), BF),
    a2t=((4, 48, HALF), BF),
    a2u=((3, 48, HALF), BF),
    b2ks=((4, 192, 128), BF),
    b2kr=((3, 192, 128), BF),
    b2kt=((4, 48, 128), BF),
    b2ku=((3, 48, 128), BF),
    b2vs=((4, 4, 48, 128), BF),
    b2vr=((3, 4, 48, 128), BF),
    b2vt=((4, 48, 128), BF),
    b2vu=((3, 48, 128), BF),
    fa2=((48, HALF), F32),
    fb1=((192, HALF), F32),
    fx=((TOK, D), BF),
    ax=((4, TOK, D), BF),
    igs=((2, 4, TOK, HALF), BF),
    xi=((BLOCKS, TOK, D), BF),
    xo=((BLOCKS, TOK, D), BF),
    yi=((BLOCKS, TOK, HALF), BF),
    yo=((BLOCKS, TOK, HALF), BF),
    b1s=((4, 192, HALF), BF),
    b1p=((2, 96, HALF), BF),
    b1r=((2, 192, HALF), BF),
    c1s=((4, 4, 48, HALF), BF),
    c1p=((2, 2, 48, HALF), BF),
    c1r=((2, 4, 48, HALF), BF),
    c1t=((4, 48, HALF), BF),
    c1u=((3, 48, HALF), BF),
    fc1=((48, HALF), F32),
    i1s=((4, 192, HALF), BF),
    i1p=((2, 96, HALF), BF),
    i1r=((2, 192, HALF), BF),
    fi1=((192, HALF), F32),
    i1f=((48, HALF), F32),
    i1z=((4, 48, HALF), BF),
    i1u=((3, 48, HALF), BF),
    i1g=((16, HALF), F32),
    i1t=((BLOCKS, 16, HALF), BF),
    fb2k=((48, 128), F32),
    fb2v=((48, 128), F32),
    zf=((32, HALF), F32),
    zsb=((BLOCKS, 32, HALF), BF),
    zf2=((16, HALF), F32),
    zs2=((BLOCKS, 16, HALF), BF),
    qt=((BLOCKS, HALF, TOK), BF),
    kvt=((2, HALF, 256), BF),
    ykv=((256, BLOCKS * TOK), BF),
)
SEMS = dict(
    ld=21,
    outs=3,
    pl_=4,
    ps=1,
    pr=4,
    hs=1,
    hr=9,
    os=1,
    or_=1,
    ss=1,
    sr=1,
    xs=2,
    xr=2,
    xis=1,
    xir=2,
    xos=1,
    xor_=2,
    yis=1,
    yir=1,
    yos=1,
    yor=1,
    ds=1,
    dr=6,
    es=1,
    er=4,
    ts=6,
    tr=6,
    rs=4,
    rh=8,
    rr=4,
    is_=1,
    ir=1,
    qs_=1,
    qr=4,
    gl_=1,
    gs_=1,
    gr=1,
    ks=1,
    kr=1,
    ys=1,
    yr=1,
    zs_=1,
    zr_=1,
    vs=1,
    vr=1,
    ws=1,
    wr=1,
    own=3,
)


def body(*refs):
    na, no, nsc = len(Args._fields), len(Outs._fields), len(SCRATCH)
    A = Args(*refs[:na])
    O = Outs(*refs[na : na + no])
    S = SimpleNamespace(**dict(zip(SCRATCH, refs[na + no : na + no + nsc])))
    M = SimpleNamespace(**dict(zip(SEMS, refs[na + no + nsc : -1])))
    LEN = refs[-1]

    bi = lax.axis_index("batch")
    ki = lax.axis_index("keys")
    x, y = bi // 4, lax.rem(bi, 4)
    z, c = ki // 2, lax.rem(ki, 2)
    oc = 1 - c

    def dev(dx=0, dy=0, dz=0, dc=0):
        nb = lax.rem(x + dx, 4) * 4 + lax.rem(y + dy, 4)
        return (nb, lax.rem(z + dz, 4) * 2 + lax.rem(c + dc, 2))

    def key_of(dz, dc):
        return lax.rem(z + dz, 4) * 2 + lax.rem(c + dc, 2)

    def far(d):
        return d + (d // 2) * (1 - 2 * lax.rem(d, 2))

    def remote(src, dst, ssem, rsem, to):
        return pltpu.make_async_remote_copy(
            src_ref=src, dst_ref=dst, send_sem=ssem, recv_sem=rsem, device_id=to, device_id_type=MESH
        )

    def sent(sem, like):
        remote(like, like, sem, sem, dev(dc=1)).wait_send()

    def arrived(sem, like):
        remote(like, like, sem, sem, dev(dc=1)).wait_recv()

    def local(src, dst, sem):
        return pltpu.make_async_copy(src, dst, sem)

    loads = [
        local(A.hidden, S.hid.at[ki], M.ld.at[0]),
        local(A.w_k.at[:, pl.ds(pl.multiple_of(c * HALF, 128), HALF)], S.wk.at[c], M.ld.at[1]),
        local(A.w_v.at[:, pl.ds(pl.multiple_of(c * HALF, 128), HALF)], S.wv.at[c], M.ld.at[2]),
        local(A.w_q.at[:, pl.ds(pl.multiple_of(c * HALF, 128), HALF)], S.wq.at[c], M.ld.at[3]),
        local(A.b_q, S.vq, M.ld.at[4]),
        local(A.b_v, S.vv, M.ld.at[5]),
    ]
    lengths = local(A.lengths, LEN, M.ld.at[17])
    lengths.start()
    later = [
        local(A.w_o, S.wo, M.ld.at[6]),
        local(A.b_o, S.vo, M.ld.at[7]),
        local(A.b_i, S.vi, M.ld.at[8]),
        local(A.b_u, S.vu, M.ld.at[9]),
        local(A.g_a, S.ga, M.ld.at[10]),
        local(A.b_a, S.ba, M.ld.at[11]),
        local(A.g_f, S.gf, M.ld.at[12]),
        local(A.b_f, S.bf, M.ld.at[13]),
        local(A.gout, S.go, M.ld.at[14]),
    ]
    for j in range(4):
        later.append(local(A.w_i.at[:, pl.ds(D * j, D)], S.wi.at[j], M.ld.at[15]))
        later.append(local(A.w_u.at[pl.ds(D * j, D)], S.wu.at[j], M.ld.at[16]))
    last = [
        local(a.at[:, pl.ds(pl.multiple_of(oc * HALF, 128), HALF)], s.at[oc], M.outs.at[i])
        for i, (a, s) in enumerate(((A.w_q, S.wq), (A.w_k, S.wk), (A.w_v, S.wv)))
    ]
    for cp in loads:
        cp.start()

    def prev_rows(dz):
        return pl.ds(pl.multiple_of(lax.rem(z + dz, 4) * 256, 256), 256)

    def prev_local(dz):
        rows = prev_rows(dz)
        return local(
            A.prev.at[pl.ds(c * HEADS, HEADS), rows, :], S.pv.at[c, :, rows, :], M.pl_.at[dz]
        )

    def prev_remote(dz):
        rows = prev_rows(dz)
        return remote(
            A.prev.at[pl.ds(oc * HEADS, HEADS), rows, :],
            S.pv.at[c, :, rows, :],
            M.ps.at[0],
            M.pr.at[dz],
            dev(dc=1),
        )

    for dz in (0, 1, 3, 2):
        prev_local(dz).start()

    peers = [(0, 0, dz, dc) for dz in range(4) for dc in range(2) if dz or dc]
    peers += [(d, 0, 0, dc) for d in (1, 2, 3) for dc in range(2)]
    peers += [(0, d, 0, dc) for d in (1, 2, 3) for dc in range(2)]
    barrier = pltpu.get_barrier_semaphore()
    for off in peers:
        pl.semaphore_signal(barrier, inc=1, device_id=dev(*off), device_id_type=MESH)
    pl.semaphore_wait(barrier, len(peers))

    def rows_half(h):
        return pl.ds(64 * h, 64)

    def hid_send(i, src, k, rows, dz, dc):
        remote(src, S.hid.at[k, rows], M.hs.at[0], M.hr.at[i], dev(dz=dz, dc=dc)).start()

    def hid_arrival(i, k, rows):
        arrived(M.hr.at[i], S.hid.at[k, rows])

    low, high, whole = rows_half(0), rows_half(1), pl.ds(0, TOK)
    hid_send(3, A.hidden.at[low], ki, low, 1, 0)
    hid_send(2, A.hidden.at[high], ki, high, 3, 0)
    hid_send(0, A.hidden, ki, whole, 0, 1)
    prev_remote(0).start()
    prev_remote(1).start()
    prev_remote(3).start()
    prev_remote(2).start()

    bounds = []
    running = jnp.int32(0)
    lengths.wait()
    for j in range(SEQS):
        running = running + LEN[0, j]
        bounds.append(running)

    def segment_of(places):
        counted = jnp.zeros(places.shape, jnp.int32)
        for bound in bounds:
            counted = counted + jnp.where(places >= bound, 1, 0)
        return jnp.where(places < bounds[-1], counted, -1 - places)

    lane8 = iota((8, 128), 1)
    key_segment = [segment_of(lane8 * BLOCKS + z * 2 + half)[0:1, :] for half in range(2)]
    lane = iota((TOK, 128), 1)

    def unit(u):
        dc = lax.rem(u, 2)
        dz = far(u // 2)
        return key_of(lax.rem(4 - dz, 4), dc), key_of(dz, dc)

    def unit_rows_of(u):
        ka, kb = unit(u)
        start_a = pl.multiple_of(ka * TOK, 64)
        start_b = pl.multiple_of(kb * TOK + 64, 64)
        return pl.ds(start_a, 64), pl.ds(start_b, 64)

    in_block = iota((TOK, 128), 0)
    low_half = in_block < 64

    def mask(u, carry):
        ka, kb = unit(u)
        row_segment = segment_of(in_block * BLOCKS + jnp.where(low_half, ka, kb))
        for half in range(2):
            allowed = row_segment == key_segment[half]
            S.madd[u, :, 128 * half : 128 * half + 128] = jnp.where(allowed, 0.0, NEGATIVE)
        return carry

    lax.fori_loop(0, BLOCKS, mask, 0)
    hid_send(4, A.hidden.at[high], ki, high, 1, 0)
    hid_send(1, A.hidden.at[low], ki, low, 3, 0)

    for cp in loads[:1] + loads[1:3] + loads[5:6]:
        cp.wait()
    hid_arrival(0, key_of(0, 1), whole)
    pair = pl.ds(z * 2, 2)
    hid_pair = S.hid[pair].reshape(256, D)
    key_rows = dot(hid_pair, S.wk[c]).astype(BF).astype(F32)
    bias_v = S.vv[...].reshape(1, D)
    bias_q = S.vq
    bv = jnp.where(c == 0, bias_v[:, :HALF], bias_v[:, HALF:])
    value_rows = (dot(hid_pair, S.wv[c]) + bv).astype(BF).astype(F32)
    lane2 = iota((256, 128), 1)
    for h in range(HEADS):
        g, e = h // 2, h % 2
        mine = lane2 // 64 == e
        S.km[h] = jnp.where(mine, key_rows[:, 128 * g : 128 * g + 128], 0.0).astype(BF)
        S.ve[h, :, :128] = jnp.where(mine, value_rows[:, 128 * g : 128 * g + 128], 0.0).astype(BF)
        S.ve[h, :, 128:] = jnp.where((lane2 == h) | (lane2 == 8 + h), 1.0, 0.0).astype(BF)
    loads[3].wait()
    loads[4].wait()
    bias_q = S.vq[...].reshape(1, D)
    S.brow[...] = jnp.zeros((2, 16, HALF), F32)
    S.ykv[...] = jnp.zeros((256, BLOCKS * TOK), BF)
    S.zf[...] = jnp.zeros((32, HALF), F32)
    S.zf2[...] = jnp.zeros((16, HALF), F32)
    S.i1g[...] = jnp.zeros((16, HALF), F32)
    for cp in later + last:
        cp.start()

    def out_send(k, rows, to):
        return remote(S.obuf.at[k, rows], S.orecv.at[ki, rows], M.os.at[0], M.or_.at[0], to)

    def st_send(k, to):
        return remote(S.st.at[k], S.strecv.at[ki], M.ss.at[0], M.sr.at[0], to)

    def forward(i, carry):
        ka, kb = unit(i)
        above, below = key_of(1, 0), key_of(3, 0)

        @pl.when(i == 0)
        def _():
            prev_local(0).wait()
            prev_remote(0).wait_recv()

        @pl.when(i == 2)
        def _():
            hid_arrival(3, below, low)
            hid_send(7, S.hid.at[below, low], below, low, 1, 0)
            hid_send(5, S.hid.at[below, low], below, low, 0, 1)
            hid_arrival(2, above, high)
            hid_send(7, S.hid.at[above, high], above, high, 3, 0)
            hid_send(5, S.hid.at[above, high], above, high, 0, 1)
            for dz in (1, 3):
                prev_local(dz).wait()
                prev_remote(dz).wait_recv()

        @pl.when(i == 4)
        def _():
            hid_arrival(1, above, low)
            hid_send(6, S.hid.at[above, low], above, low, 0, 1)
            hid_arrival(4, below, high)
            hid_send(6, S.hid.at[below, high], below, high, 0, 1)

        @pl.when(i == 6)
        def _():
            hid_arrival(7, ka, whole)
            hid_send(8, S.hid.at[ka], ka, whole, 0, 1)
            prev_local(2).wait()
            prev_remote(2).wait_recv()

        @pl.when(jnp.logical_or(i == 3, i == 5))
        def _():
            hid_arrival((i + 7) // 2, ka, whole)

        @pl.when(i == 7)
        def _():
            hid_arrival(8, ka, whole)

        bq = jnp.where(c == 0, bias_q[:, :HALF], bias_q[:, HALF:])
        hidden = jnp.concatenate([S.hid[ka, low], S.hid[kb, high]], axis=0)
        queries = (dot(hidden, S.wq[c]) + bq).astype(BF).astype(F32) * 0.125
        S.qs[...] = queries.astype(BF)
        S.qt[i] = queries.T.astype(BF)
        rows_a, rows_b = unit_rows_of(i)
        totals = jnp.zeros((TOK, 128), F32)
        tops = jnp.zeros((TOK, 128), F32)
        for g in range(3):
            two = S.qs[:, 128 * g : 128 * g + 128]
            mixed = jnp.zeros((TOK, 128), F32)
            for h in (2 * g, 2 * g + 1):
                s = dot_nt(two, S.km[h])
                parts = []
                for e, r in enumerate((rows_a, rows_b)):
                    at = slice(64 * e, 64 * e + 64)
                    before = [S.pv[half, h, r, :].astype(F32) for half in range(2)]
                    parts.append(s[at, :] + jnp.concatenate(before, axis=1) + S.madd[i, at, :])
                s = jnp.concatenate(parts, axis=0)
                top = jnp.max(s, axis=1, keepdims=True)
                p = jnp.exp(s - top).astype(BF)
                S.pw[i, h] = p
                o = dot(p, S.ve[h])
                mixed = mixed + o[:, :128]
                totals = totals + o[:, 128:]
                tops = jnp.where(lane == 8 + h, top, tops)
            mixed = mixed.astype(BF)
            S.obuf[ka, low, 128 * g : 128 * g + 128] = mixed[:64, :]
            S.obuf[kb, high, 128 * g : 128 * g + 128] = mixed[64:, :]
        stats = jnp.where(lane < 8, totals, tops).T[:16, :]
        S.stu[i] = stats

        def owner(k):
            return (bi, k)

        @pl.when(i > 0)
        def _():
            out_send(ka, low, owner(ka)).start()
            out_send(kb, high, owner(kb)).start()

        @pl.when(jnp.logical_or(i == 1, i >= 6))
        def _():
            S.st[ka] = stats
            st_send(ka, owner(ka)).start()

        @pl.when(jnp.logical_or(i == 4, i == 5))
        def _():
            first = S.stu[i - 2]
            S.st[ka] = jnp.where(lane[:16] < 64, stats, first)
            S.st[kb] = jnp.where(lane[:16] < 64, first, stats)
            st_send(ka, owner(ka)).start()
            st_send(kb, owner(kb)).start()

        return carry

    lax.fori_loop(0, BLOCKS, forward, 0)

    S.orecv[ki] = S.obuf[ki]
    S.strecv[ki] = S.stu[0]

    seven = pl.ds(0, 7)
    for cp in later[:9]:
        cp.wait()
    local(S.wi, S.wi, M.ld.at[15]).wait()
    local(S.wu, S.wu, M.ld.at[16]).wait()
    S.wot[...] = S.wo[...].T
    for j in range(4):
        S.wit[j] = S.wi[j].T
        S.wut[j] = S.wu[j].T
    arrived(M.or_.at[0], S.orecv.at[seven])
    arrived(M.sr.at[0], S.strecv.at[seven])
    row8 = iota((8, 128), 0)
    spread = head_rows()
    lse = []
    for half in range(2):
        tops = [S.strecv[2 * zz + half, 8:16, :] for zz in range(4)]
        sums = [S.strecv[2 * zz + half, 0:8, :] for zz in range(4)]
        top = jnp.maximum(jnp.maximum(tops[0], tops[1]), jnp.maximum(tops[2], tops[3]))
        shares = [jnp.exp(t - top) for t in tops]
        total = shares[0] * sums[0] + shares[1] * sums[1] + shares[2] * sums[2] + shares[3] * sums[3]
        total = jnp.where(row8 < HEADS, total, 1.0)
        lse.append(jnp.where(row8 < HEADS, top + jnp.log(total), 0.0))
        acc = jnp.zeros((TOK, HALF), F32)
        for zz in range(4):
            factor = dot_tn(split_hi_lo(jnp.where(row8 < HEADS, shares[zz] / total, 0.0)), spread)
            acc = acc + S.orecv[2 * zz + half].astype(F32) * factor
        S.at[half] = acc
        S.atx[0, :, HALF * half : HALF * half + HALF] = acc.astype(BF)

    other = dev(dc=1)

    def swap(i, src, dst):
        copy = remote(src, dst, M.xs.at[i], M.xr.at[i], other)
        copy.start()
        return copy

    swap_at = swap(0, S.atx.at[0], S.atx.at[1])

    def vec(ref):
        return ref[...].reshape(1, -1)

    attn_low = S.atx[0]
    first_sum = S.hid[ki].astype(F32) + dot(attn_low, S.wo[...]) + vec(S.vo)
    normed, inverse_a = norm(first_sum)
    S.n1[...] = normed
    first_low = (normed * vec(S.ga) + vec(S.ba)).astype(BF)
    S.fx[...] = first_low
    in_y, in_x = y * 2 + c, x * 2 + c
    S.xi[in_y] = first_low

    def xi_send(i, src, k, **to):
        remote(src, S.xi.at[k], M.xis.at[0], M.xir.at[i], dev(**to)).start()

    for d in (1, 3, 2):
        xi_send(0, S.fx, in_y, dy=d)
    xi_send(1, S.fx, in_y, dc=1)
    second = normed * vec(S.ga) + vec(S.ba) + vec(S.vu)
    bias_i = vec(S.vi)
    for j in range(4):
        inner = dot(S.fx[...], S.wi[j]) + bias_i[:, D * j : D * j + D]
        cdf = 0.5 + 0.5 * lax.erf(inner * 0.7071067811865476)
        density = jnp.exp(inner * inner * -0.5) * 0.3989422804014327
        S.gp[j] = (cdf + inner * density).astype(BF)
        S.ax[j] = (inner * cdf).astype(BF)

        @pl.when(x != j)
        def _():
            remote(S.ax.at[j], S.xo.at[in_x], M.xos.at[0], M.xor_.at[0], (j * 4 + y, ki)).start()

        @pl.when(x == j)
        def _():
            remote(S.ax.at[j], S.xo.at[in_x], M.xos.at[0], M.xor_.at[1], other).start()
            S.xo[in_x] = S.ax[j]

        second = second + dot(S.ax[j], S.wu[j])
    normed_f, inverse_f = norm(second)
    O.out_hidden[...] = (normed_f * vec(S.gf) + vec(S.bf)).astype(BF)
    upstream = S.go[...].astype(F32)

    def put_row(r, values):
        sums = row_sums(values)
        S.brow[0, r : r + 1, :] = sums[:, :HALF]
        S.brow[1, r : r + 1, :] = sums[:, HALF:]

    put_row(6, upstream * normed_f)
    put_row(7, upstream)
    grad_second = norm_back(upstream, normed_f, inverse_f, vec(S.gf))
    og = grad_second.astype(BF)
    put_row(3, og.astype(F32))
    S.ogs[0] = og[:, :HALF]
    S.ogs[1] = og[:, HALF:]
    ring_places = [(d, dc) for d in (1, 3, 2) for dc in range(2)]

    for d, dc in ring_places + [(0, 1)]:
        src = S.ogs.at[lax.rem(c + dc, 2)]
        remote(src, S.yo.at[in_x], M.yos.at[0], M.yor.at[0], dev(dx=d, dc=dc)).start()
    S.yo[in_x] = S.ogs[c]
    S.gs[...] = grad_second
    bsum = []
    for j in range(4):
        ig = (dot(og, S.wut[j]) * S.gp[j].astype(F32)).astype(BF)
        S.igs[j // 2, 2 * (j % 2)] = ig[:, :HALF]
        S.igs[j // 2, 2 * (j % 2) + 1] = ig[:, HALF:]
        bsum.append(row_sums(ig.astype(F32)))
        S.gs[...] = S.gs[...] + dot(ig, S.wit[j])
    for d, dc in ring_places + [(0, 1)]:
        src = S.igs.at[lax.rem(c + dc, 2), lax.rem(y + d, 4)]
        remote(src, S.yi.at[in_y], M.yis.at[0], M.yir.at[0], dev(dy=d, dc=dc)).start()
    S.yi[in_y] = S.igs[c, y]

    grad_first = S.gs[...]
    normed = S.n1[...]
    put_row(4, grad_first * normed)
    put_row(5, grad_first)
    grad_first_sum = norm_back(grad_first, normed, inverse_a, vec(S.ga))
    S.gs[...] = grad_first_sum
    br = grad_first_sum.astype(BF)
    put_row(2, br.astype(F32))
    S.brs[0] = br[:, :HALF]
    S.brs[1] = br[:, HALF:]
    swap_br = swap(1, S.brs.at[oc], S.brr)
    ag = dot(br, S.wot[...]).astype(BF)
    for half in range(2):
        S.ags[half] = ag[:, HALF * half : HALF * half + HALF]
        product = S.at[half] * ag[:, HALF * half : HALF * half + HALF].astype(F32)
        dots = jnp.zeros((16, TOK), F32)
        hi = product.astype(BF)
        lo = (product - hi.astype(F32)).astype(BF)
        dots = dot_nt(spread, hi) + dot_nt(spread, lo)
        S.s2[half, 0:8, :] = dots[0:8, :]
        S.s2[half, 8:16, :] = lse[half]

    def ag_send(i, src, k, rows, dz, dc):
        remote(src, S.dorecv.at[k, rows], M.ds.at[0], M.dr.at[i], dev(dz=dz, dc=dc)).start()

    def ag_arrival(i, dz, rows):
        arrived(M.dr.at[i], S.dorecv.at[pl.ds(lax.rem(z + dz, 4) * 2, 2), rows])

    def s2_send(i, dz, dc):
        half = lax.rem(c + dc, 2)
        remote(S.s2.at[half], S.s2recv.at[ki], M.es.at[0], M.er.at[i], dev(dz=dz, dc=dc)).start()

    def s2_arrival(i, dz):
        arrived(M.er.at[i], S.s2recv.at[pl.ds(lax.rem(z + dz, 4) * 2, 2)])

    for i, dz, rows in ((3, 1, low), (2, 3, high)):
        for dc in range(2):
            ag_send(i, S.ags.at[lax.rem(c + dc, 2), rows], ki, rows, dz, dc)
    ag_send(0, S.ags.at[oc], ki, whole, 0, 1)
    s2_send(0, 0, 1)
    for i, dz in ((2, 1), (1, 3), (3, 2)):
        for dc in range(2):
            s2_send(i, dz, dc)
    S.dorecv[ki] = S.ags[c]
    S.s2recv[ki] = S.s2[c]

    def weight_grad(left, right):
        return dot_tn(left, right).astype(BF)

    def along(axis, d):
        return dev(dx=d) if axis == 0 else dev(dy=d)

    def at_place(axis, d):
        return lax.rem((x if axis == 0 else y) + d, 4)

    def scatter(n, axis, src, dst, inner):
        for d in (1, 2, 3):
            there = at_place(axis, d)
            piece = src.at[:, there] if inner else src.at[there]
            remote(piece, dst.at[d - 1], M.ts.at[n], M.tr.at[n], along(axis, d)).start()

    class Ring:
        def __init__(self, n, axis, piece, held, landed):
            right, left = along(axis, 1), along(axis, 3)
            after, before, across = at_place(axis, 1), at_place(axis, 3), at_place(axis, 2)

            def copy(sem, src, dst, to):
                return remote(src, dst, M.rs.at[n], sem, to)

            here = M.rr.at[n]
            self.n = n

            self.first = [
                copy(M.rh.at[2 * n], piece(across, 0), held.at[0], right),
                copy(M.rh.at[2 * n + 1], piece(across, 1), held.at[1], left),
            ]
            self.own = [
                copy(here, piece(after, 1), landed(0, 1), right),
                copy(here, piece(before, 0), landed(1, 0), left),
            ]
            self.summed = [
                copy(here, held.at[0], landed(0, 0), right),
                copy(here, held.at[1], landed(1, 1), left),
            ]
            self.add = [(held.at[0], piece(after, 0)), (held.at[1], piece(before, 1))]

        def start(self, copies):
            for cp in copies:
                cp.start()

        def pass_on(self):
            for w in range(2):
                self.first[w].wait_recv()
                mine, extra = self.add[w]
                mine[...] = (mine[...].astype(F32) + extra[...].astype(F32)).astype(BF)
                self.summed[w].start()

        def landed(self, both):
            arrived(M.rr.at[self.n], both)

        def drain(self, three):
            sent(M.rs.at[self.n], three)

    def quarter_ring(n, axis, send, held, recv):
        return Ring(
            n,
            axis,
            lambda p, h: send.at[p, pl.ds(96 * h, 96)],
            held,
            lambda w, h: recv.at[w, pl.ds(96 * h, 96)],
        )

    ring_q = quarter_ring(0, 0, S.a2s, S.a2p, S.a2r)
    ring_i = quarter_ring(1, 0, S.i1s, S.i1p, S.i1r)
    ring_u = quarter_ring(2, 1, S.b1s, S.b1p, S.b1r)
    ring_o = Ring(
        3,
        1,
        lambda p, h: S.c1s.at[pl.ds(2 * h, 2), p],
        S.c1p,
        lambda w, h: S.c1r.at[w, pl.ds(2 * h, 2)],
    )
    for cp in [swap_at, swap_br]:
        cp.wait()
    right = jnp.concatenate([S.brs[c], S.brr[...]], axis=0)
    S.c1s[...] = weight_grad(S.atx[...].reshape(256, D), right).reshape(4, 4, 48, HALF)

    for i, dz, rows in ((4, 1, high), (1, 3, low)):
        for dc in range(2):
            ag_send(i, S.ags.at[lax.rem(c + dc, 2), rows], ki, rows, dz, dc)

    lane512 = iota((8, 512), 1)
    sub512 = iota((8, 512), 0)
    pick = jnp.where(
        iota((512, 128), 1) == (iota((512, 128), 0) // 128) * 32 + lax.rem(iota((512, 128), 0), 128) // 4,
        1.0,
        0.0,
    ).astype(BF)
    flat = jnp.concatenate(bsum, axis=1)
    for g in range(6):
        spread_out = jnp.where(lax.rem(lane512, 4) == sub512, flat[:, 512 * g : 512 * g + 512], 0.0)
        S.brow[g // 3, 8:16, 128 * (g % 3) : 128 * (g % 3) + 128] = dot(spread_out.astype(BF), pick)

    S.dkt[...] = jnp.zeros((HALF, 256), F32)
    S.dvt[...] = jnp.zeros((HALF, 256), F32)
    units = unit_rows()

    sent(M.os.at[0], S.obuf.at[seven])

    def dq_landing(w, half, h):
        return S.dqr.at[w, half, rows_half(h)], M.qr.at[2]

    def dq_copy(src, place, to):
        return remote(src, place[0], M.qs_.at[0], place[1], to)

    def dq_piece(dz, h):
        return S.obuf.at[pl.ds(lax.rem(z + dz, 4) * 2, 2), rows_half(h)]

    dq_partner = dq_copy(S.obuf.at[z * 2 + oc], (S.dqo.at[c], M.qr.at[3]), other)
    dq_first = [
        dq_copy(dq_piece(2, 0), (S.dqh.at[0], M.qr.at[0]), dev(dz=1)),
        dq_copy(dq_piece(2, 1), (S.dqh.at[1], M.qr.at[1]), dev(dz=3)),
    ]
    dq_own, dq_summed = [], []
    for w, dz in ((0, 1), (1, 3)):
        h = 1 - w
        dq_own.append(
            [
                dq_copy(
                    S.obuf.at[lax.rem(z + dz, 4) * 2 + cc, rows_half(h)],
                    dq_landing(w, c, h),
                    (bi, lax.rem(z + dz, 4) * 2 + cc),
                )
                for cc in range(2)
            ]
        )
        h = w
        dq_summed.append(
            [
                dq_copy(
                    S.dqh.at[w, cc],
                    dq_landing(w, c, h),
                    (bi, lax.rem(z + dz, 4) * 2 + cc),
                )
                for cc in range(2)
            ]
        )

    def gl_rows(zz):
        return pl.ds(pl.multiple_of(zz * 256, 256), 256)

    def gl_local(k):
        rows = gl_rows(k)
        return local(
            S.pv.at[c, :, rows, :], O.gl.at[pl.ds(c * HEADS, HEADS), rows, :], M.gl_.at[0]
        )

    def gl_remote(k):
        rows = gl_rows(k)
        return remote(
            S.pv.at[oc, :, rows, :],
            O.gl.at[pl.ds(c * HEADS, HEADS), rows, :],
            M.gs_.at[0],
            M.gr.at[0],
            dev(dc=1),
        )

    def backward(i, carry):
        @pl.when(i == 2)
        def _():
            arrived(M.xir.at[0], S.xi.at[pl.ds(0, 3)])
            for d in (1, 3, 2):
                k = lax.rem(y + d, 4) * 2 + c
                xi_send(1, S.xi.at[k], k, dc=1)

        @pl.when(i == 3)
        def _():
            ring_o.start(ring_o.first)
            arrived(M.xor_.at[0], S.xo.at[pl.ds(0, 3)])
            for d in (1, 3, 2):
                k = lax.rem(x + d, 4) * 2 + c
                remote(S.xo.at[k], S.xo.at[k], M.xos.at[0], M.xor_.at[1], other).start()

        @pl.when(i == 0)
        def _():
            arrived(M.dr.at[0], S.dorecv.at[key_of(0, 1)])
            arrived(M.er.at[0], S.s2recv.at[key_of(0, 1)])

        @pl.when(i == 1)
        def _():
            ag_arrival(3, 3, low)
            for dc in range(2):
                k = key_of(3, dc)
                ag_send(5, S.dorecv.at[k, low], k, low, 1, 0)
            ag_arrival(2, 1, high)
            for dc in range(2):
                k = key_of(1, dc)
                ag_send(5, S.dorecv.at[k, high], k, high, 3, 0)
            s2_arrival(1, 1)
            s2_arrival(2, 3)

        @pl.when(i == 2)
        def _():
            ag_arrival(1, 1, low)
            ag_arrival(4, 3, high)

        @pl.when(i == 3)
        def _():
            ag_arrival(5, 2, whole)
            s2_arrival(3, 2)

        places, factors, minuses, pieces = [], [], [], []
        for half in range(2):
            u = 2 * i + half
            ka, kb = unit(u)
            places.append((ka, low))
            places.append((kb, high))
            here = jnp.where(lane[:16] < 64, S.s2recv[ka], S.s2recv[kb])
            share = jnp.exp(S.stu[u, 8:16, :] - here[8:16, :])
            share = jnp.where(row8 < HEADS, share, 0.0)
            minuses.append(dot_tn(split_hi_lo(here[0:8, :] * share * -1.0), units).astype(BF))
            factors.append(dot_tn(split_hi_lo(share), spread))
            pieces += [S.dorecv[ka, low], S.dorecv[kb, high]]
        rows = unit_rows_of(2 * i) + unit_rows_of(2 * i + 1)
        minus = jnp.concatenate(minuses, axis=0)
        scaled = jnp.concatenate(pieces, axis=0).astype(F32) * jnp.concatenate(factors, axis=0)
        scaled_t = scaled.T.astype(BF)
        scaled = scaled.astype(BF)
        queries_t = jnp.concatenate([S.qt[2 * i], S.qt[2 * i + 1]], axis=1)
        for g in range(3):
            left = jnp.concatenate([scaled[:, 128 * g : 128 * g + 128], minus], axis=1)
            partial = jnp.zeros((256, 128), F32)
            for h in (2 * g, 2 * g + 1):
                p = S.pw[pl.ds(2 * i, 2), h].reshape(256, 256)
                grad = (p.astype(F32) * dot_nt(left, S.ve[h])).astype(BF)
                for half in range(2):
                    for e, r in enumerate(rows):
                        at = slice(64 * e, 64 * e + 64)
                        S.pv[half, h, r, :] = grad[at, 128 * half : 128 * half + 128]
                at = slice(64 * h, 64 * h + 64)
                S.dvt[at, :] = S.dvt[at, :] + dot(scaled_t[at, :], p)
                S.dkt[at, :] = S.dkt[at, :] + dot(queries_t[at, :], grad)
                partial = partial + dot(grad, S.km[h])
            partial = (partial * 0.125).astype(BF)
            for e, (k, half_rows) in enumerate(places):
                S.obuf[k, half_rows, 128 * g : 128 * g + 128] = partial[64 * e : 64 * e + 64, :]

        @pl.when(i == 0)
        def _():
            dq_partner.start()

        @pl.when(i == 1)
        def _():
            for cp in dq_own[0] + dq_own[1]:
                cp.start()

        def logits_out(zz):
            gl_local(zz).start()
            gl_remote(zz).start()

        @pl.when(i == 0)
        def _():
            logits_out(z)

        @pl.when(i == 2)
        def _():
            logits_out(lax.rem(z + 1, 4))
            logits_out(lax.rem(z + 3, 4))

        @pl.when(i == 3)
        def _():
            logits_out(lax.rem(z + 2, 4))

        return carry

    lax.fori_loop(0, 4, backward, 0)
    S.dqo[c] = S.obuf[ki]

    S.kvt[0] = S.dkt[...].astype(BF)
    S.kvt[1] = S.dvt[...].astype(BF)
    mine = pl.ds(pl.multiple_of(z * 256, 256), 256)
    for d in (1, 3, 2):
        there = pl.ds(pl.multiple_of(lax.rem(z + d, 4) * 96, 32), 96)
        for t in range(2):
            place = S.ykv.at[pl.ds(128 * t, 96), mine]
            remote(S.kvt.at[t, there, :], place, M.ys.at[0], M.yr.at[0], dev(dz=d)).start()
    here = pl.ds(pl.multiple_of(z * 96, 32), 96)
    for t in range(2):
        S.ykv[128 * t : 128 * t + 96, mine] = S.kvt[t, here, :]
    key_grad = S.dkt[...].T.astype(BF)
    value_grad = S.dvt[...].T.astype(BF)
    S.kgs[...] = key_grad.reshape(2, TOK, HALF)
    S.vgs[...] = value_grad.reshape(2, TOK, HALF)
    kv_swaps = [
        remote(S.kgs.at[oc], S.kgr, M.ks.at[0], M.kr.at[0], other),
        remote(S.vgs.at[oc], S.vgr, M.ks.at[0], M.kr.at[0], other),
    ]
    for cp in kv_swaps:
        cp.start()
    S.brow[c, 1:2, :] = row_sums(value_grad.astype(F32))
    hid_all = S.hid[...].reshape(BLOCKS * TOK, D)
    query_parts = S.obuf[...].reshape(BLOCKS * TOK, HALF)
    S.a2s[...] = weight_grad(hid_all, query_parts).reshape(4, 192, HALF)
    ring_q.start(ring_q.first)
    ring_o.start(ring_o.own)
    S.brow[c, 0:1, :] = row_sums(query_parts.astype(F32))

    arrived(M.yir.at[0], S.yi.at[seven])
    arrived(M.xir.at[1], S.xi.at[pl.ds(0, 4)])
    grad = weight_grad(S.xi[...].reshape(BLOCKS * TOK, D), S.yi[...].reshape(BLOCKS * TOK, HALF))
    S.i1s[...] = grad.reshape(4, 192, HALF)
    ring_i.start(ring_i.first)
    ring_q.start(ring_q.own)
    arrived(M.yor.at[0], S.yo.at[seven])
    arrived(M.xor_.at[1], S.xo.at[pl.ds(0, 4)])
    grad = weight_grad(S.xo[...].reshape(BLOCKS * TOK, D), S.yo[...].reshape(BLOCKS * TOK, HALF))
    S.b1s[...] = grad.reshape(4, 192, HALF)
    ring_u.start(ring_u.first)
    ring_i.start(ring_i.own)
    for cp in dq_first:
        cp.start()

    for cp in last:
        cp.wait()
    arrived(M.kr.at[0], S.kgs)
    total = S.gs[...]
    total = total + dot_nt(S.kgs[c], S.wk[c]) + dot_nt(S.kgr[...], S.wk[oc])
    total = total + dot_nt(S.vgs[c], S.wv[c]) + dot_nt(S.vgr[...], S.wv[oc])
    S.gs[...] = total

    def sum_a(src, recv, dst):
        def step(j, carry):
            part = pl.ds(pl.multiple_of(j * 48, 16), 48)
            total = src[x, part, :].astype(F32)
            for d in range(recv.shape[0]):
                total = total + recv[d, part, :].astype(F32)
            dst[j] = total.astype(BF)
            return carry

        lax.fori_loop(0, 4, step, 0)

    def sum_b(src, recv, dst):
        def step(j, carry):
            total = src[j, y].astype(F32)
            for d in range(recv.shape[0]):
                total = total + recv[d, j].astype(F32)
            dst[j] = total.astype(BF)
            return carry

        lax.fori_loop(0, 4, step, 0)

    def finish(own, recv, dst):
        total = own.astype(F32)
        for d in range(recv.shape[0]):
            total = total + recv[d].astype(F32)
        dst[...] = total

    ring_u.start(ring_u.own)
    ring_o.pass_on()
    ring_q.pass_on()
    arrived(M.yr.at[0], S.kvt.at[:, pl.ds(0, 288)])
    beside = jnp.where(iota((16, 128), 1) == iota((16, 128), 0) + 96, 1.0, 0.0).astype(BF)
    columns = [dot_tn(S.brow[half].astype(BF), beside) for half in range(2)]
    flipped = dot(S.ykv[...], hid_all)
    grad = (flipped[:128, :].T + jnp.concatenate(columns, axis=0)).astype(BF)
    S.b2ks[...] = grad.reshape(4, 192, 128)
    scatter(0, 0, S.b2ks, S.b2kr, False)
    S.b2vs[...] = flipped[128:, :].T.astype(BF).reshape(4, 4, 48, 128)
    scatter(4, 1, S.b2vs, S.b2vr, True)

    ring_i.pass_on()
    ring_u.pass_on()
    for w in range(2):
        dq_first[w].wait_recv()
        add = dq_piece((1, 3)[w], w)[...].astype(F32)
        S.dqh[w] = (S.dqh[w].astype(F32) + add).astype(BF)
        for cp in dq_summed[w]:
            cp.start()
    ring_q.landed(S.a2r)
    sum_a(S.a2s, S.a2r, S.a2t)
    scatter(2, 1, S.a2t, S.a2u, False)

    arrived(M.tr.at[0], S.b2kr)
    sum_a(S.b2ks, S.b2kr, S.b2kt)
    scatter(1, 1, S.b2kt, S.b2ku, False)
    arrived(M.tr.at[4], S.b2vr)
    sum_b(S.b2vs, S.b2vr, S.b2vt)
    scatter(5, 0, S.b2vt, S.b2vu, False)

    ring_i.landed(S.i1r)
    finish(S.i1s[x], S.i1r, S.fi1)
    for p in range(4):
        for k in range(BLOCKS):
            at = 48 * (k // 2) + 12 * p + 6 * (k % 2)
            S.i1f[6 * k : 6 * k + 6, :] = S.fi1[at : at + 6, :]
        S.i1z[p] = S.i1f[...].astype(BF)
    for d in (1, 3, 2):
        there = lax.rem(z + d, 4)
        remote(S.i1z.at[there], S.i1u.at[d - 1], M.is_.at[0], M.ir.at[0], dev(dz=d)).start()

    ring_o.landed(S.c1r)
    sum_b(S.c1s, S.c1r, S.c1t)
    scatter(3, 0, S.c1t, S.c1u, False)

    dq_partner.wait_recv()
    arrived(M.qr.at[2], S.dqr)
    query_grads = []
    for half in range(2):
        grad = S.dqr[0, half].astype(F32) + S.dqr[1, half].astype(F32) + S.dqo[half].astype(F32)
        query_grads.append(grad.astype(BF))

    total = S.gs[...]
    for half in range(2):
        total = total + dot_nt(query_grads[half], S.wq[half])
    O.grad_hidden[...] = total.astype(BF)

    def zb_send(k, to):
        return remote(S.zsb.at[k], O.zrb.at[ki], M.zs_.at[0], M.zr_.at[0], to)

    def w_send(k, to):
        return remote(S.zs2.at[k], O.wr.at[ki], M.ws.at[0], M.wr.at[0], to)

    def to_all(send):
        def step(i, carry):
            dz, dc = far(i // 2), lax.rem(i, 2)
            send(key_of(dz, dc), dev(dz=dz, dc=dc)).start()
            return carry

        lax.fori_loop(1, BLOCKS, step, 0)

    own = [
        local(S.i1t.at[in_y], O.zra.at[in_y], M.own.at[2]),
        local(S.zsb.at[ki], O.zrb.at[ki], M.own.at[0]),
        local(S.zs2.at[ki], O.wr.at[ki], M.own.at[1]),
    ]
    arrived(M.tr.at[1], S.b2ku)
    finish(S.b2kt[y], S.b2ku, S.fb2k)
    arrived(M.tr.at[5], S.b2vu)
    finish(S.b2vt[x], S.b2vu, S.fb2v)
    arrived(M.tr.at[2], S.a2u)
    finish(S.a2t[y], S.a2u, S.fa2)
    for p in range(BLOCKS):
        six = slice(6 * p, 6 * p + 6)
        S.zf2[0:6, :128] = S.fb2k[six, :]
        S.zf2[0:6, 128:256] = S.fb2v[six, :]
        S.zf2[6:12, :] = S.fa2[six, :]
        S.zs2[p] = S.zf2[...].astype(BF)
    to_all(w_send)
    own[2].start()

    ring_u.landed(S.b1r)
    finish(S.b1s[y], S.b1r, S.fb1)
    arrived(M.tr.at[3], S.c1u)
    finish(S.c1t[x], S.c1u, S.fc1)
    for p in range(BLOCKS):
        S.zf[0:24, :] = S.fb1[24 * p : 24 * p + 24, :]
        S.zf[24:30, :] = S.fc1[6 * p : 6 * p + 6, :]
        S.zsb[p] = S.zf[...].astype(BF)

    to_all(zb_send)
    own[1].start()

    arrived(M.ir.at[0], S.i1u)
    total = S.i1z[z].astype(F32)
    for d in range(3):
        total = total + S.i1u[d].astype(F32)
    S.i1f[...] = total
    for k in range(BLOCKS):
        S.i1g[0:6, :] = S.i1f[6 * k : 6 * k + 6, :]
        S.i1t[k] = S.i1g[...].astype(BF)
    for d, dc in ring_places + [(0, 1)]:
        src = S.i1t.at[lax.rem(y + d, 4) * 2 + lax.rem(c + dc, 2)]
        remote(src, O.zra.at[in_y], M.vs.at[0], M.vr.at[0], dev(dy=d, dc=dc)).start()
    own[0].start()

    sent(M.ss.at[0], S.st.at[seven])
    sent(M.es.at[0], S.s2recv.at[seven])
    sent(M.ys.at[0], S.kvt.at[:, pl.ds(0, 288)])
    sent(M.ks.at[0], S.kgs)
    sent(M.ds.at[0], S.dorecv.at[seven])
    sent(M.qs_.at[0], S.obuf.at[seven])
    for ssem, rsem, like in (
        (M.zs_, M.zr_, S.zsb),
        (M.vs, M.vr, S.i1t),
        (M.ws, M.wr, S.zs2),
    ):
        sent(ssem.at[0], like.at[seven])
        arrived(rsem.at[0], like.at[seven])
    local(S.pv.at[c], S.pv.at[c], M.gl_.at[0]).wait()
    sent(M.gs_.at[0], S.pv.at[oc])
    arrived(M.gr.at[0], S.pv.at[oc])
    sent(M.hs.at[0], S.hid.at[pl.ds(0, 7)])
    sent(M.ps.at[0], S.pv.at[0])
    for n, like in enumerate((S.b2kr, S.b2ku, S.a2u, S.c1u, S.b2vr, S.b2vu)):
        sent(M.ts.at[n], like)
    for cp in own:
        cp.wait()
    for ring, like in ((ring_q, S.a2s), (ring_i, S.i1s), (ring_u, S.b1s)):
        ring.drain(like.at[pl.ds(0, 3)])
    ring_o.drain(S.c1s.at[:, pl.ds(0, 3)])
    sent(M.is_.at[0], S.i1u)
    for sem, like in ((M.xis, S.xi), (M.xos, S.xo), (M.yis, S.yi), (M.yos, S.yo)):
        sent(sem.at[0], like.at[seven])


def main_kernel(args):
    any_space = pl.BlockSpec(memory_space=pl.ANY)
    vmem = pl.BlockSpec(memory_space=pltpu.VMEM)
    return pl.pallas_call(
        body,
        out_shape=[
            pltpu.VMEM((TOK, D), BF),
            pltpu.VMEM((TOK, D), BF),
            pltpu.VMEM((2 * HEADS, BLOCKS * TOK, 128), BF),
            pltpu.VMEM((BLOCKS, 32, HALF), BF),
            pltpu.VMEM((BLOCKS, 16, HALF), BF),
            pltpu.VMEM((BLOCKS, 16, HALF), BF),
        ],
        in_specs=[any_space] * len(args),
        out_specs=[vmem, vmem] + [any_space] * 4,
        scratch_shapes=[pltpu.VMEM(s, t) for s, t in SCRATCH.values()]
        + [pltpu.SemaphoreType.DMA((n,)) for n in SEMS.values()]
        + [pltpu.SMEM((1, SEQS), jnp.int32)],
        compiler_params=pltpu.CompilerParams(
            collective_id=0, has_side_effects=True, vmem_limit_bytes=59 * 2**20
        ),
        name="layer",
    )(*args)


def lay_out(oh, gh, gl, zrb, zra, wr, *refs):
    outs, hold, sem = refs[:18], (None,) * 3 + refs[18:33], refs[33]
    copies = [
        pltpu.make_async_copy(src, dst, sem.at[i])
        for i, (src, dst) in enumerate(
            [(gl.at[pl.ds(3 * j, 3)], outs[2].at[pl.ds(3 * j, 3)]) for j in range(4)]
            + [(oh, outs[0]), (gh, outs[1])]
        )
    ]
    for copy in copies:
        copy.start()

    def summed(ref):
        out = []
        for half in range(2):
            total = ref[half].astype(F32)
            for zz in range(1, 4):
                total = total + ref[2 * zz + half].astype(F32)
            out.append(total)
        return out


    def leave(i):
        copies.append(pltpu.make_async_copy(hold[i], outs[i], sem.at[i + 3]))
        copies[-1].start()

    outer = summed(zrb)
    tail = jnp.zeros((8, 128), F32)
    for k in range(BLOCKS):
        rows = wr[k].astype(F32)
        tail = tail + rows[0:8, :128]
        at = (k % 2) * HALF + (k // 2) * 96
        for t in range(2):
            hold[4 + t][:, at : at + 96] = rows[0:6, 128 * t : 128 * t + 96]
    query = summed(wr)
    hold[3][...] = jnp.concatenate([query[0][6:12, :], query[1][6:12, :]], axis=1)
    for i in (3, 4, 5):
        leave(i)
    hold[6][...] = jnp.concatenate([outer[0][24:30, :], outer[1][24:30, :]], axis=1)
    for k in range(BLOCKS):
        at = (k % 2) * (FF // 2) + (k // 2) * HALF
        hold[7][:, at : at + HALF] = zra[k].astype(F32)[0:6, :]
    hold[8][...] = jnp.concatenate([outer[0][0:24, :], outer[1][0:24, :]], axis=1)
    for i in (6, 7, 8):
        leave(i)
    flipped = jnp.concatenate([tail, jnp.zeros((120, 128), F32)], axis=0).T
    for slot, row in ((9, 0), (10, 1), (11, 2), (13, 3), (14, 4), (15, 5), (16, 6), (17, 7)):
        hold[slot][...] = flipped[96 + row, 0:6]
        leave(slot)
    inner = jnp.zeros((1, 128), F32)
    lane = iota((1, 128), 1)
    for i in range(6):
        for j in range(4):
            inner = jnp.where(lane == 4 * i + j, flipped[104 + j : 105 + j, i : i + 1], inner)
    hold[12][...] = inner[0, 0:24]
    leave(12)
    for copy in copies:
        copy.wait()


def out_kernel(*args):
    vmem = pl.BlockSpec(memory_space=pltpu.VMEM)
    any_space = pl.BlockSpec(memory_space=pl.ANY)
    f = lambda *s: jax.ShapeDtypeStruct(s, F32)
    shapes = [
            jax.ShapeDtypeStruct((TOK, D), BF),
            jax.ShapeDtypeStruct((TOK, D), BF),
            jax.ShapeDtypeStruct((2 * HEADS, BLOCKS * TOK, 128), BF),
            f(6, D),
            f(6, D),
            f(6, D),
            f(6, D),
            f(6, FF),
            f(24, D),
            f(6),
            f(6),
            f(6),
            f(24),
            f(6),
            f(6),
            f(6),
            f(6),
            f(6),
        ]
    return pl.pallas_call(
        lay_out,
        out_shape=shapes,
        in_specs=[any_space] * 3 + [vmem] * 3,
        out_specs=[any_space] * 18,
        scratch_shapes=[pltpu.VMEM(o.shape, F32) for o in shapes[3:]]
        + [pltpu.SemaphoreType.DMA((21,))],
        compiler_params=pltpu.CompilerParams(vmem_limit_bytes=8 * 2**20),
        name="lay_out",
    )(*args)


def on_device(*args):
    parts = main_kernel(args)
    return tuple(out_kernel(*[pltpu.with_memory_space_constraint(p, pltpu.VMEM) for p in parts]))


def solution(mesh):
    rows = P(("batch", "keys"), None)
    logits = P(None, "batch", "keys")
    flat = P(("batch", "keys"))
    return jax.shard_map(
        on_device,
        mesh=mesh,
        in_specs=(rows, logits, P("batch", None), rows) + (P(),) * 15,
        out_specs=(rows, rows, logits) + (rows,) * 6 + (flat,) * 9,
        check_vma=False,
    )
```

```python
from types import SimpleNamespace
from typing import Any, NamedTuple

import jax
import jax.numpy as jnp
from jax import lax
from jax.experimental import pallas as pl
from jax.experimental.pallas import tpu as pltpu
from jax.sharding import PartitionSpec as P

EPSILON = 1e-05
NEGATIVE = -1e30
MESH = pl.DeviceIdType.MESH
BF = jnp.bfloat16
F32 = jnp.float32

TOK = 128
D = 768
HALF = 384
HEADS = 6
FF = 3072
SEQS = 16
BLOCKS = 8


def dot(a, b):
    return lax.dot_general(a, b, (((1,), (0,)), ((), ())), preferred_element_type=F32)


def dot_nt(a, b):
    return lax.dot_general(a, b, (((1,), (1,)), ((), ())), preferred_element_type=F32)


def dot_tn(a, b):
    return lax.dot_general(a, b, (((0,), (0,)), ((), ())), preferred_element_type=F32)


def iota(shape, dim):
    return lax.broadcasted_iota(jnp.int32, shape, dim)


def split_hi_lo(v):
    hi = v.astype(BF)
    lo = (v - hi.astype(F32)).astype(BF)
    return jnp.concatenate([hi.astype(F32), lo.astype(F32)], axis=0).astype(BF)


def head_rows():
    return jnp.where(iota((16, HALF), 1) // 64 == iota((16, HALF), 0) % 8, 1.0, 0.0).astype(BF)


def unit_rows():
    return jnp.where(iota((16, 128), 1) == iota((16, 128), 0), 1.0, 0.0).astype(BF)


def row_sums(v):
    return jnp.sum(v, axis=0, keepdims=True)


def norm(values):
    average = jnp.mean(values, axis=-1, keepdims=True)
    centered = values - average
    variance = jnp.mean(centered * centered, axis=-1, keepdims=True)
    inverse = lax.rsqrt(variance + EPSILON)
    return centered * inverse, inverse


def norm_back(upstream, normed, inverse, gain):
    scaled = upstream * gain
    return inverse * (
        scaled
        - jnp.mean(scaled, axis=-1, keepdims=True)
        - normed * jnp.mean(scaled * normed, axis=-1, keepdims=True)
    )


class Args(NamedTuple):
    hidden: Any
    prev: Any
    lengths: Any
    gout: Any
    w_q: Any
    w_k: Any
    w_v: Any
    w_o: Any
    w_i: Any
    w_u: Any
    b_q: Any
    b_v: Any
    b_o: Any
    b_i: Any
    b_u: Any
    g_a: Any
    b_a: Any
    g_f: Any
    b_f: Any


class Outs(NamedTuple):
    out_hidden: Any
    grad_hidden: Any
    gl: Any
    zrb: Any
    zra: Any
    wr: Any


SCRATCH = dict(
    wq=((2, D, HALF), BF),
    wk=((2, D, HALF), BF),
    wv=((2, D, HALF), BF),
    wo=((D, D), BF),
    wi=((4, D, D), BF),
    wu=((4, D, D), BF),
    wot=((D, D), BF),
    wit=((4, D, D), BF),
    wut=((4, D, D), BF),
    vq=((D,), F32),
    vv=((D,), F32),
    vo=((D,), F32),
    vi=((FF,), F32),
    vu=((D,), F32),
    ga=((D,), F32),
    ba=((D,), F32),
    gf=((D,), F32),
    bf=((D,), F32),
    go=((TOK, D), BF),
    hid=((BLOCKS, TOK, D), BF),
    pv=((2, HEADS, BLOCKS * TOK, 128), BF),
    pw=((BLOCKS, HEADS, TOK, 256), BF),
    qs=((TOK, HALF), BF),
    km=((HEADS, 256, 128), BF),
    ve=((HEADS, 256, 256), BF),
    madd=((BLOCKS, TOK, 256), F32),
    obuf=((BLOCKS, TOK, HALF), BF),
    orecv=((BLOCKS, TOK, HALF), BF),
    st=((BLOCKS, 16, 128), F32),
    stu=((BLOCKS, 16, 128), F32),
    strecv=((BLOCKS, 16, 128), F32),
    at=((2, TOK, HALF), F32),
    atx=((2, TOK, D), BF),
    n1=((TOK, D), F32),
    gs=((TOK, D), F32),
    gp=((4, TOK, D), BF),
    ogs=((2, TOK, HALF), BF),
    brs=((2, TOK, HALF), BF),
    brr=((TOK, HALF), BF),
    brow=((2, 16, HALF), F32),
    ags=((2, TOK, HALF), BF),
    dorecv=((BLOCKS, TOK, HALF), BF),
    s2=((2, 16, 128), F32),
    s2recv=((BLOCKS, 16, 128), F32),
    dkt=((HALF, 256), F32),
    dvt=((HALF, 256), F32),
    dqr=((2, 2, TOK, HALF), BF),
    dqo=((2, TOK, HALF), BF),
    dqh=((2, 2, 64, HALF), BF),
    kgs=((2, TOK, HALF), BF),
    kgr=((TOK, HALF), BF),
    vgs=((2, TOK, HALF), BF),
    vgr=((TOK, HALF), BF),
    a2s=((4, 192, HALF), BF),
    a2p=((2, 96, HALF), BF),
    a2r=((2, 192, HALF), BF),
    a2t=((4, 48, HALF), BF),
    a2u=((3, 48, HALF), BF),
    b2ks=((4, 192, 128), BF),
    b2kr=((3, 192, 128), BF),
    b2kt=((4, 48, 128), BF),
    b2ku=((3, 48, 128), BF),
    b2vs=((4, 4, 48, 128), BF),
    b2vr=((3, 4, 48, 128), BF),
    b2vt=((4, 48, 128), BF),
    b2vu=((3, 48, 128), BF),
    fa2=((48, HALF), F32),
    fb1=((192, HALF), F32),
    fx=((TOK, D), BF),
    ax=((4, TOK, D), BF),
    igs=((2, 4, TOK, HALF), BF),
    xi=((BLOCKS, TOK, D), BF),
    xo=((BLOCKS, TOK, D), BF),
    yi=((BLOCKS, TOK, HALF), BF),
    yo=((BLOCKS, TOK, HALF), BF),
    b1s=((4, 192, HALF), BF),
    b1p=((2, 96, HALF), BF),
    b1r=((2, 192, HALF), BF),
    c1s=((4, 4, 48, HALF), BF),
    c1p=((2, 2, 48, HALF), BF),
    c1r=((2, 4, 48, HALF), BF),
    c1t=((4, 48, HALF), BF),
    c1u=((3, 48, HALF), BF),
    fc1=((48, HALF), F32),
    i1s=((4, 192, HALF), BF),
    i1p=((2, 96, HALF), BF),
    i1r=((2, 192, HALF), BF),
    fi1=((192, HALF), F32),
    i1f=((48, HALF), F32),
    i1z=((4, 48, HALF), BF),
    i1u=((3, 48, HALF), BF),
    i1g=((16, HALF), F32),
    i1t=((BLOCKS, 16, HALF), BF),
    fb2k=((48, 128), F32),
    fb2v=((48, 128), F32),
    zf=((32, HALF), F32),
    zsb=((BLOCKS, 32, HALF), BF),
    zf2=((16, HALF), F32),
    zs2=((BLOCKS, 16, HALF), BF),
    qt=((BLOCKS, HALF, TOK), BF),
    kvt=((2, HALF, 256), BF),
    ykv=((256, BLOCKS * TOK), BF),
)
SEMS = dict(
    ld=21,
    outs=3,
    pl_=4,
    ps=1,
    pr=4,
    hs=1,
    hr=9,
    os=1,
    or_=1,
    ss=1,
    sr=1,
    xs=2,
    xr=2,
    xis=1,
    xir=2,
    xos=1,
    xor_=2,
    yis=1,
    yir=1,
    yos=1,
    yor=1,
    ds=1,
    dr=6,
    es=1,
    er=4,
    ts=6,
    tr=6,
    rs=4,
    rh=8,
    rr=4,
    is_=1,
    ir=1,
    qs_=1,
    qr=4,
    gl_=1,
    gs_=1,
    gr=1,
    ks=1,
    kr=1,
    ys=1,
    yr=1,
    zs_=1,
    zr_=1,
    vs=1,
    vr=1,
    ws=1,
    wr=1,
    own=3,
)


def body(*refs):
    na, no, nsc = len(Args._fields), len(Outs._fields), len(SCRATCH)
    A = Args(*refs[:na])
    O = Outs(*refs[na : na + no])
    S = SimpleNamespace(**dict(zip(SCRATCH, refs[na + no : na + no + nsc])))
    M = SimpleNamespace(**dict(zip(SEMS, refs[na + no + nsc : -1])))
    LEN = refs[-1]

    bi = lax.axis_index("batch")
    ki = lax.axis_index("keys")
    x, y = bi // 4, lax.rem(bi, 4)
    z, c = ki // 2, lax.rem(ki, 2)
    oc = 1 - c

    def dev(dx=0, dy=0, dz=0, dc=0):
        nb = lax.rem(x + dx, 4) * 4 + lax.rem(y + dy, 4)
        return (nb, lax.rem(z + dz, 4) * 2 + lax.rem(c + dc, 2))

    def key_of(dz, dc):
        return lax.rem(z + dz, 4) * 2 + lax.rem(c + dc, 2)

    def far(d):
        return d + (d // 2) * (1 - 2 * lax.rem(d, 2))

    def remote(src, dst, ssem, rsem, to):
        return pltpu.make_async_remote_copy(
            src_ref=src, dst_ref=dst, send_sem=ssem, recv_sem=rsem, device_id=to, device_id_type=MESH
        )

    def sent(sem, like):
        remote(like, like, sem, sem, dev(dc=1)).wait_send()

    def arrived(sem, like):
        remote(like, like, sem, sem, dev(dc=1)).wait_recv()

    def local(src, dst, sem):
        return pltpu.make_async_copy(src, dst, sem)

    loads = [
        local(A.hidden, S.hid.at[ki], M.ld.at[0]),
        local(A.w_k.at[:, pl.ds(pl.multiple_of(c * HALF, 128), HALF)], S.wk.at[c], M.ld.at[1]),
        local(A.w_v.at[:, pl.ds(pl.multiple_of(c * HALF, 128), HALF)], S.wv.at[c], M.ld.at[2]),
        local(A.w_q.at[:, pl.ds(pl.multiple_of(c * HALF, 128), HALF)], S.wq.at[c], M.ld.at[3]),
        local(A.b_q, S.vq, M.ld.at[4]),
        local(A.b_v, S.vv, M.ld.at[5]),
    ]
    lengths = local(A.lengths, LEN, M.ld.at[17])
    lengths.start()
    later = [
        local(A.w_o, S.wo, M.ld.at[6]),
        local(A.b_o, S.vo, M.ld.at[7]),
        local(A.b_i, S.vi, M.ld.at[8]),
        local(A.b_u, S.vu, M.ld.at[9]),
        local(A.g_a, S.ga, M.ld.at[10]),
        local(A.b_a, S.ba, M.ld.at[11]),
        local(A.g_f, S.gf, M.ld.at[12]),
        local(A.b_f, S.bf, M.ld.at[13]),
        local(A.gout, S.go, M.ld.at[14]),
    ]
    for j in range(4):
        later.append(local(A.w_i.at[:, pl.ds(D * j, D)], S.wi.at[j], M.ld.at[15]))
        later.append(local(A.w_u.at[pl.ds(D * j, D)], S.wu.at[j], M.ld.at[16]))
    last = [
        local(a.at[:, pl.ds(pl.multiple_of(oc * HALF, 128), HALF)], s.at[oc], M.outs.at[i])
        for i, (a, s) in enumerate(((A.w_q, S.wq), (A.w_k, S.wk), (A.w_v, S.wv)))
    ]
    for cp in loads:
        cp.start()

    def prev_rows(dz):
        return pl.ds(pl.multiple_of(lax.rem(z + dz, 4) * 256, 256), 256)

    def prev_local(dz):
        rows = prev_rows(dz)
        return local(
            A.prev.at[pl.ds(c * HEADS, HEADS), rows, :], S.pv.at[c, :, rows, :], M.pl_.at[dz]
        )

    def prev_remote(dz):
        rows = prev_rows(dz)
        return remote(
            A.prev.at[pl.ds(oc * HEADS, HEADS), rows, :],
            S.pv.at[c, :, rows, :],
            M.ps.at[0],
            M.pr.at[dz],
            dev(dc=1),
        )

    for dz in (0, 1, 3, 2):
        prev_local(dz).start()

    peers = [(0, 0, dz, dc) for dz in range(4) for dc in range(2) if dz or dc]
    peers += [(d, 0, 0, dc) for d in (1, 2, 3) for dc in range(2)]
    peers += [(0, d, 0, dc) for d in (1, 2, 3) for dc in range(2)]
    barrier = pltpu.get_barrier_semaphore()
    for off in peers:
        pl.semaphore_signal(barrier, inc=1, device_id=dev(*off), device_id_type=MESH)
    pl.semaphore_wait(barrier, len(peers))

    def rows_half(h):
        return pl.ds(64 * h, 64)

    def hid_send(i, src, k, rows, dz, dc):
        remote(src, S.hid.at[k, rows], M.hs.at[0], M.hr.at[i], dev(dz=dz, dc=dc)).start()

    def hid_arrival(i, k, rows):
        arrived(M.hr.at[i], S.hid.at[k, rows])

    low, high, whole = rows_half(0), rows_half(1), pl.ds(0, TOK)
    hid_send(3, A.hidden.at[low], ki, low, 1, 0)
    hid_send(2, A.hidden.at[high], ki, high, 3, 0)
    hid_send(0, A.hidden, ki, whole, 0, 1)
    prev_remote(0).start()
    prev_remote(1).start()
    prev_remote(3).start()
    prev_remote(2).start()

    bounds = []
    running = jnp.int32(0)
    lengths.wait()
    for j in range(SEQS):
        running = running + LEN[0, j]
        bounds.append(running)

    def segment_of(places):
        counted = jnp.zeros(places.shape, jnp.int32)
        for bound in bounds:
            counted = counted + jnp.where(places >= bound, 1, 0)
        return jnp.where(places < bounds[-1], counted, -1 - places)

    lane8 = iota((8, 128), 1)
    key_segment = [segment_of(lane8 * BLOCKS + z * 2 + half)[0:1, :] for half in range(2)]
    lane = iota((TOK, 128), 1)

    def unit(u):
        dc = lax.rem(u, 2)
        dz = far(u // 2)
        return key_of(lax.rem(4 - dz, 4), dc), key_of(dz, dc)

    def unit_rows_of(u):
        ka, kb = unit(u)
        start_a = pl.multiple_of(ka * TOK, 64)
        start_b = pl.multiple_of(kb * TOK + 64, 64)
        return pl.ds(start_a, 64), pl.ds(start_b, 64)

    in_block = iota((TOK, 128), 0)
    low_half = in_block < 64

    def mask(u, carry):
        ka, kb = unit(u)
        row_segment = segment_of(in_block * BLOCKS + jnp.where(low_half, ka, kb))
        for half in range(2):
            allowed = row_segment == key_segment[half]
            S.madd[u, :, 128 * half : 128 * half + 128] = jnp.where(allowed, 0.0, NEGATIVE)
        return carry

    lax.fori_loop(0, BLOCKS, mask, 0)
    hid_send(4, A.hidden.at[high], ki, high, 1, 0)
    hid_send(1, A.hidden.at[low], ki, low, 3, 0)

    for cp in loads[:1] + loads[1:3] + loads[5:6]:
        cp.wait()
    hid_arrival(0, key_of(0, 1), whole)
    pair = pl.ds(z * 2, 2)
    hid_pair = S.hid[pair].reshape(256, D)
    key_rows = dot(hid_pair, S.wk[c]).astype(BF).astype(F32)
    bias_v = S.vv[...].reshape(1, D)
    bias_q = S.vq
    bv = jnp.where(c == 0, bias_v[:, :HALF], bias_v[:, HALF:])
    value_rows = (dot(hid_pair, S.wv[c]) + bv).astype(BF).astype(F32)
    lane2 = iota((256, 128), 1)
    for h in range(HEADS):
        g, e = h // 2, h % 2
        mine = lane2 // 64 == e
        S.km[h] = jnp.where(mine, key_rows[:, 128 * g : 128 * g + 128], 0.0).astype(BF)
        S.ve[h, :, :128] = jnp.where(mine, value_rows[:, 128 * g : 128 * g + 128], 0.0).astype(BF)
        S.ve[h, :, 128:] = jnp.where((lane2 == h) | (lane2 == 8 + h), 1.0, 0.0).astype(BF)
    loads[3].wait()
    loads[4].wait()
    bias_q = S.vq[...].reshape(1, D)
    S.brow[...] = jnp.zeros((2, 16, HALF), F32)
    S.ykv[...] = jnp.zeros((256, BLOCKS * TOK), BF)
    S.zf[...] = jnp.zeros((32, HALF), F32)
    S.zf2[...] = jnp.zeros((16, HALF), F32)
    S.i1g[...] = jnp.zeros((16, HALF), F32)
    for cp in later + last:
        cp.start()

    def out_send(k, rows, to):
        return remote(S.obuf.at[k, rows], S.orecv.at[ki, rows], M.os.at[0], M.or_.at[0], to)

    def st_send(k, to):
        return remote(S.st.at[k], S.strecv.at[ki], M.ss.at[0], M.sr.at[0], to)

    def forward(i, carry):
        ka, kb = unit(i)
        above, below = key_of(1, 0), key_of(3, 0)

        @pl.when(i == 0)
        def _():
            prev_local(0).wait()
            prev_remote(0).wait_recv()

        @pl.when(i == 2)
        def _():
            hid_arrival(3, below, low)
            hid_send(7, S.hid.at[below, low], below, low, 1, 0)
            hid_send(5, S.hid.at[below, low], below, low, 0, 1)
            hid_arrival(2, above, high)
            hid_send(7, S.hid.at[above, high], above, high, 3, 0)
            hid_send(5, S.hid.at[above, high], above, high, 0, 1)
            for dz in (1, 3):
                prev_local(dz).wait()
                prev_remote(dz).wait_recv()

        @pl.when(i == 4)
        def _():
            hid_arrival(1, above, low)
            hid_send(6, S.hid.at[above, low], above, low, 0, 1)
            hid_arrival(4, below, high)
            hid_send(6, S.hid.at[below, high], below, high, 0, 1)

        @pl.when(i == 6)
        def _():
            hid_arrival(7, ka, whole)
            hid_send(8, S.hid.at[ka], ka, whole, 0, 1)
            prev_local(2).wait()
            prev_remote(2).wait_recv()

        @pl.when(jnp.logical_or(i == 3, i == 5))
        def _():
            hid_arrival((i + 7) // 2, ka, whole)

        @pl.when(i == 7)
        def _():
            hid_arrival(8, ka, whole)

        bq = jnp.where(c == 0, bias_q[:, :HALF], bias_q[:, HALF:])
        hidden = jnp.concatenate([S.hid[ka, low], S.hid[kb, high]], axis=0)
        queries = (dot(hidden, S.wq[c]) + bq).astype(BF).astype(F32) * 0.125
        S.qs[...] = queries.astype(BF)
        S.qt[i] = queries.T.astype(BF)
        rows_a, rows_b = unit_rows_of(i)
        totals = jnp.zeros((TOK, 128), F32)
        tops = jnp.zeros((TOK, 128), F32)
        for g in range(3):
            two = S.qs[:, 128 * g : 128 * g + 128]
            mixed = jnp.zeros((TOK, 128), F32)
            for h in (2 * g, 2 * g + 1):
                s = dot_nt(two, S.km[h])
                parts = []
                for e, r in enumerate((rows_a, rows_b)):
                    at = slice(64 * e, 64 * e + 64)
                    before = [S.pv[half, h, r, :].astype(F32) for half in range(2)]
                    parts.append(s[at, :] + jnp.concatenate(before, axis=1) + S.madd[i, at, :])
                s = jnp.concatenate(parts, axis=0)
                top = jnp.max(s, axis=1, keepdims=True)
                p = jnp.exp(s - top).astype(BF)
                S.pw[i, h] = p
                o = dot(p, S.ve[h])
                mixed = mixed + o[:, :128]
                totals = totals + o[:, 128:]
                tops = jnp.where(lane == 8 + h, top, tops)
            mixed = mixed.astype(BF)
            S.obuf[ka, low, 128 * g : 128 * g + 128] = mixed[:64, :]
            S.obuf[kb, high, 128 * g : 128 * g + 128] = mixed[64:, :]
        stats = jnp.where(lane < 8, totals, tops).T[:16, :]
        S.stu[i] = stats

        def owner(k):
            return (bi, k)

        @pl.when(i > 0)
        def _():
            out_send(ka, low, owner(ka)).start()
            out_send(kb, high, owner(kb)).start()

        @pl.when(jnp.logical_or(i == 1, i >= 6))
        def _():
            S.st[ka] = stats
            st_send(ka, owner(ka)).start()

        @pl.when(jnp.logical_or(i == 4, i == 5))
        def _():
            first = S.stu[i - 2]
            S.st[ka] = jnp.where(lane[:16] < 64, stats, first)
            S.st[kb] = jnp.where(lane[:16] < 64, first, stats)
            st_send(ka, owner(ka)).start()
            st_send(kb, owner(kb)).start()

        return carry

    lax.fori_loop(0, BLOCKS, forward, 0)

    S.orecv[ki] = S.obuf[ki]
    S.strecv[ki] = S.stu[0]

    seven = pl.ds(0, 7)
    for cp in later[:9]:
        cp.wait()
    local(S.wi, S.wi, M.ld.at[15]).wait()
    local(S.wu, S.wu, M.ld.at[16]).wait()
    S.wot[...] = S.wo[...].T
    for j in range(4):
        S.wit[j] = S.wi[j].T
        S.wut[j] = S.wu[j].T
    arrived(M.or_.at[0], S.orecv.at[seven])
    arrived(M.sr.at[0], S.strecv.at[seven])
    row8 = iota((8, 128), 0)
    spread = head_rows()
    lse = []
    for half in range(2):
        tops = [S.strecv[2 * zz + half, 8:16, :] for zz in range(4)]
        sums = [S.strecv[2 * zz + half, 0:8, :] for zz in range(4)]
        top = jnp.maximum(jnp.maximum(tops[0], tops[1]), jnp.maximum(tops[2], tops[3]))
        shares = [jnp.exp(t - top) for t in tops]
        total = shares[0] * sums[0] + shares[1] * sums[1] + shares[2] * sums[2] + shares[3] * sums[3]
        total = jnp.where(row8 < HEADS, total, 1.0)
        lse.append(jnp.where(row8 < HEADS, top + jnp.log(total), 0.0))
        acc = jnp.zeros((TOK, HALF), F32)
        for zz in range(4):
            factor = dot_tn(split_hi_lo(jnp.where(row8 < HEADS, shares[zz] / total, 0.0)), spread)
            acc = acc + S.orecv[2 * zz + half].astype(F32) * factor
        S.at[half] = acc
        S.atx[0, :, HALF * half : HALF * half + HALF] = acc.astype(BF)

    other = dev(dc=1)

    def swap(i, src, dst):
        copy = remote(src, dst, M.xs.at[i], M.xr.at[i], other)
        copy.start()
        return copy

    swap_at = swap(0, S.atx.at[0], S.atx.at[1])

    def vec(ref):
        return ref[...].reshape(1, -1)

    attn_low = S.atx[0]
    first_sum = S.hid[ki].astype(F32) + dot(attn_low, S.wo[...]) + vec(S.vo)
    normed, inverse_a = norm(first_sum)
    S.n1[...] = normed
    first_low = (normed * vec(S.ga) + vec(S.ba)).astype(BF)
    S.fx[...] = first_low
    in_y, in_x = y * 2 + c, x * 2 + c
    S.xi[in_y] = first_low

    def xi_send(i, src, k, **to):
        remote(src, S.xi.at[k], M.xis.at[0], M.xir.at[i], dev(**to)).start()

    for d in (1, 3, 2):
        xi_send(0, S.fx, in_y, dy=d)
    xi_send(1, S.fx, in_y, dc=1)
    second = normed * vec(S.ga) + vec(S.ba) + vec(S.vu)
    bias_i = vec(S.vi)
    for j in range(4):
        inner = dot(S.fx[...], S.wi[j]) + bias_i[:, D * j : D * j + D]
        cdf = 0.5 + 0.5 * lax.erf(inner * 0.7071067811865476)
        density = jnp.exp(inner * inner * -0.5) * 0.3989422804014327
        S.gp[j] = (cdf + inner * density).astype(BF)
        S.ax[j] = (inner * cdf).astype(BF)

        @pl.when(x != j)
        def _():
            remote(S.ax.at[j], S.xo.at[in_x], M.xos.at[0], M.xor_.at[0], (j * 4 + y, ki)).start()

        @pl.when(x == j)
        def _():
            remote(S.ax.at[j], S.xo.at[in_x], M.xos.at[0], M.xor_.at[1], other).start()
            S.xo[in_x] = S.ax[j]

        second = second + dot(S.ax[j], S.wu[j])
    normed_f, inverse_f = norm(second)
    O.out_hidden[...] = (normed_f * vec(S.gf) + vec(S.bf)).astype(BF)
    upstream = S.go[...].astype(F32)

    def put_row(r, values):
        sums = row_sums(values)
        S.brow[0, r : r + 1, :] = sums[:, :HALF]
        S.brow[1, r : r + 1, :] = sums[:, HALF:]

    put_row(6, upstream * normed_f)
    put_row(7, upstream)
    grad_second = norm_back(upstream, normed_f, inverse_f, vec(S.gf))
    og = grad_second.astype(BF)
    put_row(3, og.astype(F32))
    S.ogs[0] = og[:, :HALF]
    S.ogs[1] = og[:, HALF:]
    ring_places = [(d, dc) for d in (1, 3, 2) for dc in range(2)]

    for d, dc in ring_places + [(0, 1)]:
        src = S.ogs.at[lax.rem(c + dc, 2)]
        remote(src, S.yo.at[in_x], M.yos.at[0], M.yor.at[0], dev(dx=d, dc=dc)).start()
    S.yo[in_x] = S.ogs[c]
    S.gs[...] = grad_second
    bsum = []
    for j in range(4):
        ig = (dot(og, S.wut[j]) * S.gp[j].astype(F32)).astype(BF)
        S.igs[j // 2, 2 * (j % 2)] = ig[:, :HALF]
        S.igs[j // 2, 2 * (j % 2) + 1] = ig[:, HALF:]
        bsum.append(row_sums(ig.astype(F32)))
        S.gs[...] = S.gs[...] + dot(ig, S.wit[j])
    for d, dc in ring_places + [(0, 1)]:
        src = S.igs.at[lax.rem(c + dc, 2), lax.rem(y + d, 4)]
        remote(src, S.yi.at[in_y], M.yis.at[0], M.yir.at[0], dev(dy=d, dc=dc)).start()
    S.yi[in_y] = S.igs[c, y]

    grad_first = S.gs[...]
    normed = S.n1[...]
    put_row(4, grad_first * normed)
    put_row(5, grad_first)
    grad_first_sum = norm_back(grad_first, normed, inverse_a, vec(S.ga))
    S.gs[...] = grad_first_sum
    br = grad_first_sum.astype(BF)
    put_row(2, br.astype(F32))
    S.brs[0] = br[:, :HALF]
    S.brs[1] = br[:, HALF:]
    swap_br = swap(1, S.brs.at[oc], S.brr)
    ag = dot(br, S.wot[...]).astype(BF)
    for half in range(2):
        S.ags[half] = ag[:, HALF * half : HALF * half + HALF]

    def ag_send(i, src, k, rows, dz, dc):
        remote(src, S.dorecv.at[k, rows], M.ds.at[0], M.dr.at[i], dev(dz=dz, dc=dc)).start()

    def ag_arrival(i, dz, rows):
        arrived(M.dr.at[i], S.dorecv.at[pl.ds(lax.rem(z + dz, 4) * 2, 2), rows])

    def s2_send(i, dz, dc):
        half = lax.rem(c + dc, 2)
        remote(S.s2.at[half], S.s2recv.at[ki], M.es.at[0], M.er.at[i], dev(dz=dz, dc=dc)).start()

    def s2_arrival(i, dz):
        arrived(M.er.at[i], S.s2recv.at[pl.ds(lax.rem(z + dz, 4) * 2, 2)])

    for i, dz, rows in ((3, 1, low), (2, 3, high)):
        for dc in range(2):
            ag_send(i, S.ags.at[lax.rem(c + dc, 2), rows], ki, rows, dz, dc)
    ag_send(0, S.ags.at[oc], ki, whole, 0, 1)

    for half in range(2):
        product = S.at[half] * ag[:, HALF * half : HALF * half + HALF].astype(F32)
        dots = jnp.zeros((16, TOK), F32)
        hi = product.astype(BF)
        lo = (product - hi.astype(F32)).astype(BF)
        dots = dot_nt(spread, hi) + dot_nt(spread, lo)
        S.s2[half, 0:8, :] = dots[0:8, :]
        S.s2[half, 8:16, :] = lse[half]
    s2_send(0, 0, 1)
    for i, dz in ((2, 1), (1, 3), (3, 2)):
        for dc in range(2):
            s2_send(i, dz, dc)
    S.dorecv[ki] = S.ags[c]
    S.s2recv[ki] = S.s2[c]

    def weight_grad(left, right):
        return dot_tn(left, right).astype(BF)

    def along(axis, d):
        return dev(dx=d) if axis == 0 else dev(dy=d)

    def at_place(axis, d):
        return lax.rem((x if axis == 0 else y) + d, 4)

    def scatter(n, axis, src, dst, inner):
        for d in (1, 2, 3):
            there = at_place(axis, d)
            piece = src.at[:, there] if inner else src.at[there]
            remote(piece, dst.at[d - 1], M.ts.at[n], M.tr.at[n], along(axis, d)).start()

    class Ring:
        def __init__(self, n, axis, piece, held, landed):
            right, left = along(axis, 1), along(axis, 3)
            after, before, across = at_place(axis, 1), at_place(axis, 3), at_place(axis, 2)

            def copy(sem, src, dst, to):
                return remote(src, dst, M.rs.at[n], sem, to)

            here = M.rr.at[n]
            self.n = n

            self.first = [
                copy(M.rh.at[2 * n], piece(across, 0), held.at[0], right),
                copy(M.rh.at[2 * n + 1], piece(across, 1), held.at[1], left),
            ]
            self.own = [
                copy(here, piece(after, 1), landed(0, 1), right),
                copy(here, piece(before, 0), landed(1, 0), left),
            ]
            self.summed = [
                copy(here, held.at[0], landed(0, 0), right),
                copy(here, held.at[1], landed(1, 1), left),
            ]
            self.add = [(held.at[0], piece(after, 0)), (held.at[1], piece(before, 1))]

        def start(self, copies):
            for cp in copies:
                cp.start()

        def pass_on(self):
            for w in range(2):
                self.first[w].wait_recv()
                mine, extra = self.add[w]
                mine[...] = (mine[...].astype(F32) + extra[...].astype(F32)).astype(BF)
                self.summed[w].start()

        def landed(self, both):
            arrived(M.rr.at[self.n], both)

        def drain(self, three):
            sent(M.rs.at[self.n], three)

    def quarter_ring(n, axis, send, held, recv):
        return Ring(
            n,
            axis,
            lambda p, h: send.at[p, pl.ds(96 * h, 96)],
            held,
            lambda w, h: recv.at[w, pl.ds(96 * h, 96)],
        )

    ring_q = quarter_ring(0, 0, S.a2s, S.a2p, S.a2r)
    ring_i = quarter_ring(1, 0, S.i1s, S.i1p, S.i1r)
    ring_u = quarter_ring(2, 1, S.b1s, S.b1p, S.b1r)
    ring_o = Ring(
        3,
        1,
        lambda p, h: S.c1s.at[pl.ds(2 * h, 2), p],
        S.c1p,
        lambda w, h: S.c1r.at[w, pl.ds(2 * h, 2)],
    )
    for cp in [swap_at, swap_br]:
        cp.wait()
    right = jnp.concatenate([S.brs[c], S.brr[...]], axis=0)
    S.c1s[...] = weight_grad(S.atx[...].reshape(256, D), right).reshape(4, 4, 48, HALF)

    for i, dz, rows in ((4, 1, high), (1, 3, low)):
        for dc in range(2):
            ag_send(i, S.ags.at[lax.rem(c + dc, 2), rows], ki, rows, dz, dc)

    lane512 = iota((8, 512), 1)
    sub512 = iota((8, 512), 0)
    pick = jnp.where(
        iota((512, 128), 1) == (iota((512, 128), 0) // 128) * 32 + lax.rem(iota((512, 128), 0), 128) // 4,
        1.0,
        0.0,
    ).astype(BF)
    flat = jnp.concatenate(bsum, axis=1)
    for g in range(6):
        spread_out = jnp.where(lax.rem(lane512, 4) == sub512, flat[:, 512 * g : 512 * g + 512], 0.0)
        S.brow[g // 3, 8:16, 128 * (g % 3) : 128 * (g % 3) + 128] = dot(spread_out.astype(BF), pick)

    S.dkt[...] = jnp.zeros((HALF, 256), F32)
    S.dvt[...] = jnp.zeros((HALF, 256), F32)
    units = unit_rows()

    sent(M.os.at[0], S.obuf.at[seven])

    def dq_landing(w, half, h):
        return S.dqr.at[w, half, rows_half(h)], M.qr.at[2]

    def dq_copy(src, place, to):
        return remote(src, place[0], M.qs_.at[0], place[1], to)

    def dq_piece(dz, h):
        return S.obuf.at[pl.ds(lax.rem(z + dz, 4) * 2, 2), rows_half(h)]

    dq_partner = dq_copy(S.obuf.at[z * 2 + oc], (S.dqo.at[c], M.qr.at[3]), other)
    dq_first = [
        dq_copy(dq_piece(2, 0), (S.dqh.at[0], M.qr.at[0]), dev(dz=1)),
        dq_copy(dq_piece(2, 1), (S.dqh.at[1], M.qr.at[1]), dev(dz=3)),
    ]
    dq_own, dq_summed = [], []
    for w, dz in ((0, 1), (1, 3)):
        h = 1 - w
        dq_own.append(
            [
                dq_copy(
                    S.obuf.at[lax.rem(z + dz, 4) * 2 + cc, rows_half(h)],
                    dq_landing(w, c, h),
                    (bi, lax.rem(z + dz, 4) * 2 + cc),
                )
                for cc in range(2)
            ]
        )
        h = w
        dq_summed.append(
            [
                dq_copy(
                    S.dqh.at[w, cc],
                    dq_landing(w, c, h),
                    (bi, lax.rem(z + dz, 4) * 2 + cc),
                )
                for cc in range(2)
            ]
        )

    def gl_rows(zz):
        return pl.ds(pl.multiple_of(zz * 256, 256), 256)

    def gl_local(k):
        rows = gl_rows(k)
        return local(
            S.pv.at[c, :, rows, :], O.gl.at[pl.ds(c * HEADS, HEADS), rows, :], M.gl_.at[0]
        )

    def gl_remote(k):
        rows = gl_rows(k)
        return remote(
            S.pv.at[oc, :, rows, :],
            O.gl.at[pl.ds(c * HEADS, HEADS), rows, :],
            M.gs_.at[0],
            M.gr.at[0],
            dev(dc=1),
        )

    def backward(i, carry):
        @pl.when(i == 2)
        def _():
            arrived(M.xir.at[0], S.xi.at[pl.ds(0, 3)])
            for d in (1, 3, 2):
                k = lax.rem(y + d, 4) * 2 + c
                xi_send(1, S.xi.at[k], k, dc=1)

        @pl.when(i == 3)
        def _():
            ring_o.start(ring_o.first)
            arrived(M.xor_.at[0], S.xo.at[pl.ds(0, 3)])
            for d in (1, 3, 2):
                k = lax.rem(x + d, 4) * 2 + c
                remote(S.xo.at[k], S.xo.at[k], M.xos.at[0], M.xor_.at[1], other).start()

        @pl.when(i == 0)
        def _():
            arrived(M.dr.at[0], S.dorecv.at[key_of(0, 1)])
            arrived(M.er.at[0], S.s2recv.at[key_of(0, 1)])

        @pl.when(i == 1)
        def _():
            ag_arrival(3, 3, low)
            for dc in range(2):
                k = key_of(3, dc)
                ag_send(5, S.dorecv.at[k, low], k, low, 1, 0)
            ag_arrival(2, 1, high)
            for dc in range(2):
                k = key_of(1, dc)
                ag_send(5, S.dorecv.at[k, high], k, high, 3, 0)
            s2_arrival(1, 1)
            s2_arrival(2, 3)

        @pl.when(i == 2)
        def _():
            ag_arrival(1, 1, low)
            ag_arrival(4, 3, high)

        @pl.when(i == 3)
        def _():
            ag_arrival(5, 2, whole)
            s2_arrival(3, 2)

        places, factors, minuses, pieces = [], [], [], []
        for half in range(2):
            u = 2 * i + half
            ka, kb = unit(u)
            places.append((ka, low))
            places.append((kb, high))
            here = jnp.where(lane[:16] < 64, S.s2recv[ka], S.s2recv[kb])
            share = jnp.exp(S.stu[u, 8:16, :] - here[8:16, :])
            share = jnp.where(row8 < HEADS, share, 0.0)
            minuses.append(dot_tn(split_hi_lo(here[0:8, :] * share * -1.0), units).astype(BF))
            factors.append(dot_tn(split_hi_lo(share), spread))
            pieces += [S.dorecv[ka, low], S.dorecv[kb, high]]
        rows = unit_rows_of(2 * i) + unit_rows_of(2 * i + 1)
        minus = jnp.concatenate(minuses, axis=0)
        scaled = jnp.concatenate(pieces, axis=0).astype(F32) * jnp.concatenate(factors, axis=0)
        scaled_t = scaled.T.astype(BF)
        scaled = scaled.astype(BF)
        queries_t = jnp.concatenate([S.qt[2 * i], S.qt[2 * i + 1]], axis=1)
        for g in range(3):
            left = jnp.concatenate([scaled[:, 128 * g : 128 * g + 128], minus], axis=1)
            partial = jnp.zeros((256, 128), F32)
            for h in (2 * g, 2 * g + 1):
                p = S.pw[pl.ds(2 * i, 2), h].reshape(256, 256)
                grad = (p.astype(F32) * dot_nt(left, S.ve[h])).astype(BF)
                for half in range(2):
                    for e, r in enumerate(rows):
                        at = slice(64 * e, 64 * e + 64)
                        S.pv[half, h, r, :] = grad[at, 128 * half : 128 * half + 128]
                at = slice(64 * h, 64 * h + 64)
                S.dvt[at, :] = S.dvt[at, :] + dot(scaled_t[at, :], p)
                S.dkt[at, :] = S.dkt[at, :] + dot(queries_t[at, :], grad)
                partial = partial + dot(grad, S.km[h])
            partial = (partial * 0.125).astype(BF)
            for e, (k, half_rows) in enumerate(places):
                S.obuf[k, half_rows, 128 * g : 128 * g + 128] = partial[64 * e : 64 * e + 64, :]

        @pl.when(i == 0)
        def _():
            dq_partner.start()

        @pl.when(i == 1)
        def _():
            for cp in dq_own[0] + dq_own[1]:
                cp.start()

        def logits_out(zz):
            gl_local(zz).start()
            gl_remote(zz).start()

        @pl.when(i == 0)
        def _():
            logits_out(z)

        @pl.when(i == 2)
        def _():
            logits_out(lax.rem(z + 1, 4))
            logits_out(lax.rem(z + 3, 4))

        @pl.when(i == 3)
        def _():
            logits_out(lax.rem(z + 2, 4))

        return carry

    lax.fori_loop(0, 4, backward, 0)
    S.dqo[c] = S.obuf[ki]

    S.kvt[0] = S.dkt[...].astype(BF)
    S.kvt[1] = S.dvt[...].astype(BF)
    mine = pl.ds(pl.multiple_of(z * 256, 256), 256)
    for d in (1, 3, 2):
        there = pl.ds(pl.multiple_of(lax.rem(z + d, 4) * 96, 32), 96)
        for t in range(2):
            place = S.ykv.at[pl.ds(128 * t, 96), mine]
            remote(S.kvt.at[t, there, :], place, M.ys.at[0], M.yr.at[0], dev(dz=d)).start()
    here = pl.ds(pl.multiple_of(z * 96, 32), 96)
    for t in range(2):
        S.ykv[128 * t : 128 * t + 96, mine] = S.kvt[t, here, :]
    key_grad = S.dkt[...].T.astype(BF)
    value_grad = S.dvt[...].T.astype(BF)
    S.kgs[...] = key_grad.reshape(2, TOK, HALF)
    S.vgs[...] = value_grad.reshape(2, TOK, HALF)
    kv_swaps = [
        remote(S.kgs.at[oc], S.kgr, M.ks.at[0], M.kr.at[0], other),
        remote(S.vgs.at[oc], S.vgr, M.ks.at[0], M.kr.at[0], other),
    ]
    for cp in kv_swaps:
        cp.start()
    S.brow[c, 1:2, :] = row_sums(value_grad.astype(F32))
    hid_all = S.hid[...].reshape(BLOCKS * TOK, D)
    query_parts = S.obuf[...].reshape(BLOCKS * TOK, HALF)
    S.a2s[...] = weight_grad(hid_all, query_parts).reshape(4, 192, HALF)
    ring_q.start(ring_q.first)
    ring_o.start(ring_o.own)
    S.brow[c, 0:1, :] = row_sums(query_parts.astype(F32))

    for cp in last:
        cp.wait()
    arrived(M.kr.at[0], S.kgs)
    total = S.gs[...]
    total = total + dot_nt(S.kgs[c], S.wk[c]) + dot_nt(S.kgr[...], S.wk[oc])
    total = total + dot_nt(S.vgs[c], S.wv[c]) + dot_nt(S.vgr[...], S.wv[oc])
    S.gs[...] = total

    arrived(M.yir.at[0], S.yi.at[seven])
    arrived(M.xir.at[1], S.xi.at[pl.ds(0, 4)])
    grad = weight_grad(S.xi[...].reshape(BLOCKS * TOK, D), S.yi[...].reshape(BLOCKS * TOK, HALF))
    S.i1s[...] = grad.reshape(4, 192, HALF)
    ring_i.start(ring_i.first)
    ring_q.start(ring_q.own)
    arrived(M.yor.at[0], S.yo.at[seven])
    arrived(M.xor_.at[1], S.xo.at[pl.ds(0, 4)])
    grad = weight_grad(S.xo[...].reshape(BLOCKS * TOK, D), S.yo[...].reshape(BLOCKS * TOK, HALF))
    S.b1s[...] = grad.reshape(4, 192, HALF)
    ring_u.start(ring_u.first)
    ring_i.start(ring_i.own)
    for cp in dq_first:
        cp.start()

    def sum_a(src, recv, dst):
        def step(j, carry):
            part = pl.ds(pl.multiple_of(j * 48, 16), 48)
            total = src[x, part, :].astype(F32)
            for d in range(recv.shape[0]):
                total = total + recv[d, part, :].astype(F32)
            dst[j] = total.astype(BF)
            return carry

        lax.fori_loop(0, 4, step, 0)

    def sum_b(src, recv, dst):
        def step(j, carry):
            total = src[j, y].astype(F32)
            for d in range(recv.shape[0]):
                total = total + recv[d, j].astype(F32)
            dst[j] = total.astype(BF)
            return carry

        lax.fori_loop(0, 4, step, 0)

    def finish(own, recv, dst):
        total = own.astype(F32)
        for d in range(recv.shape[0]):
            total = total + recv[d].astype(F32)
        dst[...] = total

    ring_u.start(ring_u.own)
    ring_o.pass_on()
    ring_q.pass_on()
    arrived(M.yr.at[0], S.kvt.at[:, pl.ds(0, 288)])
    beside = jnp.where(iota((16, 128), 1) == iota((16, 128), 0) + 96, 1.0, 0.0).astype(BF)
    columns = [dot_tn(S.brow[half].astype(BF), beside) for half in range(2)]
    flipped = dot(S.ykv[...], hid_all)
    grad = (flipped[:128, :].T + jnp.concatenate(columns, axis=0)).astype(BF)
    S.b2ks[...] = grad.reshape(4, 192, 128)
    scatter(0, 0, S.b2ks, S.b2kr, False)
    S.b2vs[...] = flipped[128:, :].T.astype(BF).reshape(4, 4, 48, 128)
    scatter(4, 1, S.b2vs, S.b2vr, True)

    ring_i.pass_on()
    ring_u.pass_on()
    for w in range(2):
        dq_first[w].wait_recv()
        add = dq_piece((1, 3)[w], w)[...].astype(F32)
        S.dqh[w] = (S.dqh[w].astype(F32) + add).astype(BF)
        for cp in dq_summed[w]:
            cp.start()
    ring_q.landed(S.a2r)
    sum_a(S.a2s, S.a2r, S.a2t)
    scatter(2, 1, S.a2t, S.a2u, False)

    ring_o.landed(S.c1r)
    sum_b(S.c1s, S.c1r, S.c1t)
    scatter(3, 0, S.c1t, S.c1u, False)

    arrived(M.tr.at[0], S.b2kr)
    sum_a(S.b2ks, S.b2kr, S.b2kt)
    scatter(1, 1, S.b2kt, S.b2ku, False)
    arrived(M.tr.at[4], S.b2vr)
    sum_b(S.b2vs, S.b2vr, S.b2vt)
    scatter(5, 0, S.b2vt, S.b2vu, False)

    ring_i.landed(S.i1r)
    finish(S.i1s[x], S.i1r, S.fi1)
    for p in range(4):
        for k in range(BLOCKS):
            at = 48 * (k // 2) + 12 * p + 6 * (k % 2)
            S.i1f[6 * k : 6 * k + 6, :] = S.fi1[at : at + 6, :]
        S.i1z[p] = S.i1f[...].astype(BF)
    for d in (1, 3, 2):
        there = lax.rem(z + d, 4)
        remote(S.i1z.at[there], S.i1u.at[d - 1], M.is_.at[0], M.ir.at[0], dev(dz=d)).start()

    dq_partner.wait_recv()
    arrived(M.qr.at[2], S.dqr)
    query_grads = []
    for half in range(2):
        grad = S.dqr[0, half].astype(F32) + S.dqr[1, half].astype(F32) + S.dqo[half].astype(F32)
        query_grads.append(grad.astype(BF))

    total = S.gs[...]
    for half in range(2):
        total = total + dot_nt(query_grads[half], S.wq[half])
    O.grad_hidden[...] = total.astype(BF)

    def zb_send(k, to):
        return remote(S.zsb.at[k], O.zrb.at[ki], M.zs_.at[0], M.zr_.at[0], to)

    def w_send(k, to):
        return remote(S.zs2.at[k], O.wr.at[ki], M.ws.at[0], M.wr.at[0], to)

    def to_all(send):
        def step(i, carry):
            dz, dc = far(i // 2), lax.rem(i, 2)
            send(key_of(dz, dc), dev(dz=dz, dc=dc)).start()
            return carry

        lax.fori_loop(1, BLOCKS, step, 0)

    own = [
        local(S.i1t.at[in_y], O.zra.at[in_y], M.own.at[2]),
        local(S.zsb.at[ki], O.zrb.at[ki], M.own.at[0]),
        local(S.zs2.at[ki], O.wr.at[ki], M.own.at[1]),
    ]
    arrived(M.tr.at[1], S.b2ku)
    finish(S.b2kt[y], S.b2ku, S.fb2k)
    arrived(M.tr.at[5], S.b2vu)
    finish(S.b2vt[x], S.b2vu, S.fb2v)
    arrived(M.tr.at[2], S.a2u)
    finish(S.a2t[y], S.a2u, S.fa2)
    for p in range(BLOCKS):
        six = slice(6 * p, 6 * p + 6)
        S.zf2[0:6, :128] = S.fb2k[six, :]
        S.zf2[0:6, 128:256] = S.fb2v[six, :]
        S.zf2[6:12, :] = S.fa2[six, :]
        S.zs2[p] = S.zf2[...].astype(BF)
    to_all(w_send)
    own[2].start()

    ring_u.landed(S.b1r)
    finish(S.b1s[y], S.b1r, S.fb1)
    arrived(M.tr.at[3], S.c1u)
    finish(S.c1t[x], S.c1u, S.fc1)
    for p in range(BLOCKS):
        S.zf[0:24, :] = S.fb1[24 * p : 24 * p + 24, :]
        S.zf[24:30, :] = S.fc1[6 * p : 6 * p + 6, :]
        S.zsb[p] = S.zf[...].astype(BF)

    to_all(zb_send)
    own[1].start()

    arrived(M.ir.at[0], S.i1u)
    total = S.i1z[z].astype(F32)
    for d in range(3):
        total = total + S.i1u[d].astype(F32)
    S.i1f[...] = total
    for k in range(BLOCKS):
        S.i1g[0:6, :] = S.i1f[6 * k : 6 * k + 6, :]
        S.i1t[k] = S.i1g[...].astype(BF)
    for d, dc in ring_places + [(0, 1)]:
        src = S.i1t.at[lax.rem(y + d, 4) * 2 + lax.rem(c + dc, 2)]
        remote(src, O.zra.at[in_y], M.vs.at[0], M.vr.at[0], dev(dy=d, dc=dc)).start()
    own[0].start()

    sent(M.ss.at[0], S.st.at[seven])
    sent(M.es.at[0], S.s2recv.at[seven])
    sent(M.ys.at[0], S.kvt.at[:, pl.ds(0, 288)])
    sent(M.ks.at[0], S.kgs)
    sent(M.ds.at[0], S.dorecv.at[seven])
    sent(M.qs_.at[0], S.obuf.at[seven])
    for ssem, rsem, like in (
        (M.zs_, M.zr_, S.zsb),
        (M.vs, M.vr, S.i1t),
        (M.ws, M.wr, S.zs2),
    ):
        sent(ssem.at[0], like.at[seven])
        arrived(rsem.at[0], like.at[seven])
    local(S.pv.at[c], S.pv.at[c], M.gl_.at[0]).wait()
    sent(M.gs_.at[0], S.pv.at[oc])
    arrived(M.gr.at[0], S.pv.at[oc])
    sent(M.hs.at[0], S.hid.at[pl.ds(0, 7)])
    sent(M.ps.at[0], S.pv.at[0])
    for n, like in enumerate((S.b2kr, S.b2ku, S.a2u, S.c1u, S.b2vr, S.b2vu)):
        sent(M.ts.at[n], like)
    for cp in own:
        cp.wait()
    for ring, like in ((ring_q, S.a2s), (ring_i, S.i1s), (ring_u, S.b1s)):
        ring.drain(like.at[pl.ds(0, 3)])
    ring_o.drain(S.c1s.at[:, pl.ds(0, 3)])
    sent(M.is_.at[0], S.i1u)
    for sem, like in ((M.xis, S.xi), (M.xos, S.xo), (M.yis, S.yi), (M.yos, S.yo)):
        sent(sem.at[0], like.at[seven])


def main_kernel(args):
    any_space = pl.BlockSpec(memory_space=pl.ANY)
    vmem = pl.BlockSpec(memory_space=pltpu.VMEM)
    return pl.pallas_call(
        body,
        out_shape=[
            pltpu.VMEM((TOK, D), BF),
            pltpu.VMEM((TOK, D), BF),
            pltpu.VMEM((2 * HEADS, BLOCKS * TOK, 128), BF),
            pltpu.VMEM((BLOCKS, 32, HALF), BF),
            pltpu.VMEM((BLOCKS, 16, HALF), BF),
            pltpu.VMEM((BLOCKS, 16, HALF), BF),
        ],
        in_specs=[any_space] * len(args),
        out_specs=[vmem, vmem] + [any_space] * 4,
        scratch_shapes=[pltpu.VMEM(s, t) for s, t in SCRATCH.values()]
        + [pltpu.SemaphoreType.DMA((n,)) for n in SEMS.values()]
        + [pltpu.SMEM((1, SEQS), jnp.int32)],
        compiler_params=pltpu.CompilerParams(
            collective_id=0, has_side_effects=True, vmem_limit_bytes=59 * 2**20
        ),
        name="layer",
    )(*args)


def lay_out(oh, gh, gl, zrb, zra, wr, *refs):
    outs, hold, sem = refs[:18], (None,) * 3 + refs[18:33], refs[33]
    copies = [
        pltpu.make_async_copy(src, dst, sem.at[i])
        for i, (src, dst) in enumerate(
            [(gl.at[pl.ds(3 * j, 3)], outs[2].at[pl.ds(3 * j, 3)]) for j in range(4)]
            + [(oh, outs[0]), (gh, outs[1])]
        )
    ]
    for copy in copies:
        copy.start()

    def summed(ref):
        out = []
        for half in range(2):
            total = ref[half].astype(F32)
            for zz in range(1, 4):
                total = total + ref[2 * zz + half].astype(F32)
            out.append(total)
        return out


    def leave(i):
        copies.append(pltpu.make_async_copy(hold[i], outs[i], sem.at[i + 3]))
        copies[-1].start()

    outer = summed(zrb)
    tail = jnp.zeros((8, 128), F32)
    for k in range(BLOCKS):
        rows = wr[k].astype(F32)
        tail = tail + rows[0:8, :128]
        at = (k % 2) * HALF + (k // 2) * 96
        for t in range(2):
            hold[4 + t][:, at : at + 96] = rows[0:6, 128 * t : 128 * t + 96]
    query = summed(wr)
    hold[3][...] = jnp.concatenate([query[0][6:12, :], query[1][6:12, :]], axis=1)
    for i in (3, 4, 5):
        leave(i)
    hold[6][...] = jnp.concatenate([outer[0][24:30, :], outer[1][24:30, :]], axis=1)
    for k in range(BLOCKS):
        at = (k % 2) * (FF // 2) + (k // 2) * HALF
        hold[7][:, at : at + HALF] = zra[k].astype(F32)[0:6, :]
    hold[8][...] = jnp.concatenate([outer[0][0:24, :], outer[1][0:24, :]], axis=1)
    for i in (6, 7, 8):
        leave(i)
    flipped = jnp.concatenate([tail, jnp.zeros((120, 128), F32)], axis=0).T
    for slot, row in ((9, 0), (10, 1), (11, 2), (13, 3), (14, 4), (15, 5), (16, 6), (17, 7)):
        hold[slot][...] = flipped[96 + row, 0:6]
        leave(slot)
    inner = jnp.zeros((1, 128), F32)
    lane = iota((1, 128), 1)
    for i in range(6):
        for j in range(4):
            inner = jnp.where(lane == 4 * i + j, flipped[104 + j : 105 + j, i : i + 1], inner)
    hold[12][...] = inner[0, 0:24]
    leave(12)
    for copy in copies:
        copy.wait()


def out_kernel(*args):
    vmem = pl.BlockSpec(memory_space=pltpu.VMEM)
    any_space = pl.BlockSpec(memory_space=pl.ANY)
    f = lambda *s: jax.ShapeDtypeStruct(s, F32)
    shapes = [
            jax.ShapeDtypeStruct((TOK, D), BF),
            jax.ShapeDtypeStruct((TOK, D), BF),
            jax.ShapeDtypeStruct((2 * HEADS, BLOCKS * TOK, 128), BF),
            f(6, D),
            f(6, D),
            f(6, D),
            f(6, D),
            f(6, FF),
            f(24, D),
            f(6),
            f(6),
            f(6),
            f(24),
            f(6),
            f(6),
            f(6),
            f(6),
            f(6),
        ]
    return pl.pallas_call(
        lay_out,
        out_shape=shapes,
        in_specs=[any_space] * 3 + [vmem] * 3,
        out_specs=[any_space] * 18,
        scratch_shapes=[pltpu.VMEM(o.shape, F32) for o in shapes[3:]]
        + [pltpu.SemaphoreType.DMA((21,))],
        compiler_params=pltpu.CompilerParams(vmem_limit_bytes=8 * 2**20),
        name="lay_out",
    )(*args)


def on_device(*args):
    parts = main_kernel(args)
    return tuple(out_kernel(*[pltpu.with_memory_space_constraint(p, pltpu.VMEM) for p in parts]))


def solution(mesh):
    rows = P(("batch", "keys"), None)
    logits = P(None, "batch", "keys")
    flat = P(("batch", "keys"))
    return jax.shard_map(
        on_device,
        mesh=mesh,
        in_specs=(rows, logits, P("batch", None), rows) + (P(),) * 15,
        out_specs=(rows, rows, logits) + (rows,) * 6 + (flat,) * 9,
        check_vma=False,
    )
```

```python
from types import SimpleNamespace
from typing import Any, NamedTuple

import jax
import jax.numpy as jnp
from jax import lax
from jax.experimental import pallas as pl
from jax.experimental.pallas import tpu as pltpu
from jax.sharding import PartitionSpec as P

EPSILON = 1e-05
NEGATIVE = -1e30
MESH = pl.DeviceIdType.MESH
BF = jnp.bfloat16
F32 = jnp.float32

TOK = 128
D = 768
HALF = 384
HEADS = 6
FF = 3072
SEQS = 16
BLOCKS = 8


def dot(a, b):
    return lax.dot_general(a, b, (((1,), (0,)), ((), ())), preferred_element_type=F32)


def dot_nt(a, b):
    return lax.dot_general(a, b, (((1,), (1,)), ((), ())), preferred_element_type=F32)


def dot_tn(a, b):
    return lax.dot_general(a, b, (((0,), (0,)), ((), ())), preferred_element_type=F32)


def iota(shape, dim):
    return lax.broadcasted_iota(jnp.int32, shape, dim)


def split_hi_lo(v):
    hi = v.astype(BF)
    lo = (v - hi.astype(F32)).astype(BF)
    return jnp.concatenate([hi.astype(F32), lo.astype(F32)], axis=0).astype(BF)


def head_rows():
    return jnp.where(iota((16, HALF), 1) // 64 == iota((16, HALF), 0) % 8, 1.0, 0.0).astype(BF)


def unit_rows():
    return jnp.where(iota((16, 128), 1) == iota((16, 128), 0), 1.0, 0.0).astype(BF)


def row_sums(v):
    return jnp.sum(v, axis=0, keepdims=True)


def norm(values):
    average = jnp.mean(values, axis=-1, keepdims=True)
    centered = values - average
    variance = jnp.mean(centered * centered, axis=-1, keepdims=True)
    inverse = lax.rsqrt(variance + EPSILON)
    return centered * inverse, inverse


def norm_back(upstream, normed, inverse, gain):
    scaled = upstream * gain
    return inverse * (
        scaled
        - jnp.mean(scaled, axis=-1, keepdims=True)
        - normed * jnp.mean(scaled * normed, axis=-1, keepdims=True)
    )


class Args(NamedTuple):
    hidden: Any
    prev: Any
    lengths: Any
    gout: Any
    w_q: Any
    w_k: Any
    w_v: Any
    w_o: Any
    w_i: Any
    w_u: Any
    b_q: Any
    b_v: Any
    b_o: Any
    b_i: Any
    b_u: Any
    g_a: Any
    b_a: Any
    g_f: Any
    b_f: Any


class Outs(NamedTuple):
    out_hidden: Any
    grad_hidden: Any
    gl: Any
    zrb: Any
    zra: Any
    wr: Any


SCRATCH = dict(
    wq=((2, D, HALF), BF),
    wk=((2, D, HALF), BF),
    wv=((2, D, HALF), BF),
    wo=((D, D), BF),
    wi=((4, D, D), BF),
    wu=((4, D, D), BF),
    wot=((D, D), BF),
    wit=((4, D, D), BF),
    wut=((4, D, D), BF),
    vq=((D,), F32),
    vv=((D,), F32),
    vo=((D,), F32),
    vi=((FF,), F32),
    vu=((D,), F32),
    ga=((D,), F32),
    ba=((D,), F32),
    gf=((D,), F32),
    bf=((D,), F32),
    go=((TOK, D), BF),
    hid=((BLOCKS, TOK, D), BF),
    pv=((2, HEADS, BLOCKS * TOK, 128), BF),
    pw=((BLOCKS, HEADS, TOK, 256), BF),
    qs=((TOK, HALF), BF),
    km=((HEADS, 256, 128), BF),
    ve=((HEADS, 256, 256), BF),
    madd=((BLOCKS, TOK, 256), F32),
    obuf=((BLOCKS, TOK, HALF), BF),
    orecv=((BLOCKS, TOK, HALF), BF),
    st=((BLOCKS, 16, 128), F32),
    stu=((BLOCKS, 16, 128), F32),
    strecv=((BLOCKS, 16, 128), F32),
    at=((2, TOK, HALF), F32),
    atx=((2, TOK, D), BF),
    n1=((TOK, D), F32),
    gs=((TOK, D), F32),
    gp=((4, TOK, D), BF),
    ogs=((2, TOK, HALF), BF),
    brs=((2, TOK, HALF), BF),
    brr=((TOK, HALF), BF),
    brow=((2, 16, HALF), F32),
    ags=((2, TOK, HALF), BF),
    dorecv=((BLOCKS, TOK, HALF), BF),
    s2=((2, 16, 128), F32),
    s2recv=((BLOCKS, 16, 128), F32),
    dkt=((HALF, 256), F32),
    dvt=((HALF, 256), F32),
    dqr=((2, 2, TOK, HALF), BF),
    dqo=((2, TOK, HALF), BF),
    dqh=((2, 2, 64, HALF), BF),
    kgs=((2, TOK, HALF), BF),
    kgr=((TOK, HALF), BF),
    vgs=((2, TOK, HALF), BF),
    vgr=((TOK, HALF), BF),
    a2s=((4, 192, HALF), BF),
    a2p=((2, 96, HALF), BF),
    a2r=((2, 192, HALF), BF),
    a2t=((4, 48, HALF), BF),
    a2u=((3, 48, HALF), BF),
    b2ks=((4, 192, 128), BF),
    b2kr=((3, 192, 128), BF),
    b2kt=((4, 48, 128), BF),
    b2ku=((3, 48, 128), BF),
    b2vs=((4, 4, 48, 128), BF),
    b2vr=((3, 4, 48, 128), BF),
    b2vt=((4, 48, 128), BF),
    b2vu=((3, 48, 128), BF),
    fa2=((48, HALF), F32),
    fb1=((192, HALF), F32),
    fx=((TOK, D), BF),
    ax=((4, TOK, D), BF),
    igs=((2, 4, TOK, HALF), BF),
    xi=((BLOCKS, TOK, D), BF),
    xo=((BLOCKS, TOK, D), BF),
    yi=((BLOCKS, TOK, HALF), BF),
    yo=((BLOCKS, TOK, HALF), BF),
    b1s=((4, 192, HALF), BF),
    b1p=((2, 96, HALF), BF),
    b1r=((2, 192, HALF), BF),
    c1s=((4, 4, 48, HALF), BF),
    c1p=((2, 2, 48, HALF), BF),
    c1r=((2, 4, 48, HALF), BF),
    c1t=((4, 48, HALF), BF),
    c1u=((3, 48, HALF), BF),
    fc1=((48, HALF), F32),
    i1s=((4, 192, HALF), BF),
    i1p=((2, 96, HALF), BF),
    i1r=((2, 192, HALF), BF),
    fi1=((192, HALF), F32),
    i1f=((48, HALF), F32),
    i1z=((4, 48, HALF), BF),
    i1u=((3, 48, HALF), BF),
    i1g=((16, HALF), F32),
    i1t=((BLOCKS, 16, HALF), BF),
    fb2k=((48, 128), F32),
    fb2v=((48, 128), F32),
    zf=((32, HALF), F32),
    zsb=((BLOCKS, 32, HALF), BF),
    zf2=((16, HALF), F32),
    zs2=((BLOCKS, 16, HALF), BF),
    qt=((BLOCKS, HALF, TOK), BF),
    kvt=((2, HALF, 256), BF),
    ykv=((256, BLOCKS * TOK), BF),
)
SEMS = dict(
    ld=21,
    outs=3,
    pl_=4,
    ps=1,
    pr=4,
    hs=1,
    hr=9,
    os=1,
    or_=1,
    ss=1,
    sr=1,
    xs=2,
    xr=2,
    xis=1,
    xir=2,
    xos=1,
    xor_=2,
    yis=1,
    yir=1,
    yos=1,
    yor=1,
    ds=1,
    dr=6,
    es=1,
    er=4,
    ts=6,
    tr=6,
    rs=4,
    rh=8,
    rr=4,
    is_=1,
    ir=1,
    qs_=1,
    qr=4,
    gl_=1,
    gs_=1,
    gr=1,
    ks=1,
    kr=1,
    ys=1,
    yr=1,
    zs_=1,
    zr_=1,
    vs=1,
    vr=1,
    ws=1,
    wr=1,
    own=3,
)


def body(*refs):
    na, no, nsc = len(Args._fields), len(Outs._fields), len(SCRATCH)
    A = Args(*refs[:na])
    O = Outs(*refs[na : na + no])
    S = SimpleNamespace(**dict(zip(SCRATCH, refs[na + no : na + no + nsc])))
    M = SimpleNamespace(**dict(zip(SEMS, refs[na + no + nsc : -1])))
    LEN = refs[-1]

    bi = lax.axis_index("batch")
    ki = lax.axis_index("keys")
    x, y = bi // 4, lax.rem(bi, 4)
    z, c = ki // 2, lax.rem(ki, 2)
    oc = 1 - c

    def dev(dx=0, dy=0, dz=0, dc=0):
        nb = lax.rem(x + dx, 4) * 4 + lax.rem(y + dy, 4)
        return (nb, lax.rem(z + dz, 4) * 2 + lax.rem(c + dc, 2))

    def key_of(dz, dc):
        return lax.rem(z + dz, 4) * 2 + lax.rem(c + dc, 2)

    def far(d):
        return d + (d // 2) * (1 - 2 * lax.rem(d, 2))

    def remote(src, dst, ssem, rsem, to):
        return pltpu.make_async_remote_copy(
            src_ref=src, dst_ref=dst, send_sem=ssem, recv_sem=rsem, device_id=to, device_id_type=MESH
        )

    def sent(sem, like):
        remote(like, like, sem, sem, dev(dc=1)).wait_send()

    def arrived(sem, like):
        remote(like, like, sem, sem, dev(dc=1)).wait_recv()

    def local(src, dst, sem):
        return pltpu.make_async_copy(src, dst, sem)

    loads = [
        local(A.hidden, S.hid.at[ki], M.ld.at[0]),
        local(A.w_k.at[:, pl.ds(pl.multiple_of(c * HALF, 128), HALF)], S.wk.at[c], M.ld.at[1]),
        local(A.w_v.at[:, pl.ds(pl.multiple_of(c * HALF, 128), HALF)], S.wv.at[c], M.ld.at[2]),
        local(A.w_q.at[:, pl.ds(pl.multiple_of(c * HALF, 128), HALF)], S.wq.at[c], M.ld.at[3]),
        local(A.b_q, S.vq, M.ld.at[4]),
        local(A.b_v, S.vv, M.ld.at[5]),
    ]
    lengths = local(A.lengths, LEN, M.ld.at[17])
    lengths.start()
    later = [
        local(A.w_o, S.wo, M.ld.at[6]),
        local(A.b_o, S.vo, M.ld.at[7]),
        local(A.b_i, S.vi, M.ld.at[8]),
        local(A.b_u, S.vu, M.ld.at[9]),
        local(A.g_a, S.ga, M.ld.at[10]),
        local(A.b_a, S.ba, M.ld.at[11]),
        local(A.g_f, S.gf, M.ld.at[12]),
        local(A.b_f, S.bf, M.ld.at[13]),
        local(A.gout, S.go, M.ld.at[14]),
    ]
    for j in range(4):
        later.append(local(A.w_i.at[:, pl.ds(D * j, D)], S.wi.at[j], M.ld.at[15]))
        later.append(local(A.w_u.at[pl.ds(D * j, D)], S.wu.at[j], M.ld.at[16]))
    last = [
        local(a.at[:, pl.ds(pl.multiple_of(oc * HALF, 128), HALF)], s.at[oc], M.outs.at[i])
        for i, (a, s) in enumerate(((A.w_q, S.wq), (A.w_k, S.wk), (A.w_v, S.wv)))
    ]
    for cp in loads:
        cp.start()

    def prev_rows(dz):
        return pl.ds(pl.multiple_of(lax.rem(z + dz, 4) * 256, 256), 256)

    def prev_local(dz):
        rows = prev_rows(dz)
        return local(
            A.prev.at[pl.ds(c * HEADS, HEADS), rows, :], S.pv.at[c, :, rows, :], M.pl_.at[dz]
        )

    def prev_remote(dz):
        rows = prev_rows(dz)
        return remote(
            A.prev.at[pl.ds(oc * HEADS, HEADS), rows, :],
            S.pv.at[c, :, rows, :],
            M.ps.at[0],
            M.pr.at[dz],
            dev(dc=1),
        )

    for dz in (0, 1, 3, 2):
        prev_local(dz).start()

    peers = [(0, 0, dz, dc) for dz in range(4) for dc in range(2) if dz or dc]
    peers += [(d, 0, 0, dc) for d in (1, 2, 3) for dc in range(2)]
    peers += [(0, d, 0, dc) for d in (1, 2, 3) for dc in range(2)]
    barrier = pltpu.get_barrier_semaphore()
    for off in peers:
        pl.semaphore_signal(barrier, inc=1, device_id=dev(*off), device_id_type=MESH)
    pl.semaphore_wait(barrier, len(peers))

    def rows_half(h):
        return pl.ds(64 * h, 64)

    def hid_send(i, src, k, rows, dz, dc):
        remote(src, S.hid.at[k, rows], M.hs.at[0], M.hr.at[i], dev(dz=dz, dc=dc)).start()

    def hid_arrival(i, k, rows):
        arrived(M.hr.at[i], S.hid.at[k, rows])

    low, high, whole = rows_half(0), rows_half(1), pl.ds(0, TOK)
    hid_send(3, A.hidden.at[low], ki, low, 1, 0)
    hid_send(2, A.hidden.at[high], ki, high, 3, 0)
    hid_send(0, A.hidden, ki, whole, 0, 1)
    prev_remote(0).start()
    prev_remote(1).start()
    prev_remote(3).start()
    prev_remote(2).start()

    bounds = []
    running = jnp.int32(0)
    lengths.wait()
    for j in range(SEQS):
        running = running + LEN[0, j]
        bounds.append(running)

    def segment_of(places):
        counted = jnp.zeros(places.shape, jnp.int32)
        for bound in bounds:
            counted = counted + jnp.where(places >= bound, 1, 0)
        return jnp.where(places < bounds[-1], counted, -1 - places)

    lane8 = iota((8, 128), 1)
    key_segment = [segment_of(lane8 * BLOCKS + z * 2 + half)[0:1, :] for half in range(2)]
    lane = iota((TOK, 128), 1)

    def unit(u):
        dc = lax.rem(u, 2)
        dz = far(u // 2)
        return key_of(lax.rem(4 - dz, 4), dc), key_of(dz, dc)

    def unit_rows_of(u):
        ka, kb = unit(u)
        start_a = pl.multiple_of(ka * TOK, 64)
        start_b = pl.multiple_of(kb * TOK + 64, 64)
        return pl.ds(start_a, 64), pl.ds(start_b, 64)

    in_block = iota((TOK, 128), 0)
    low_half = in_block < 64

    def mask(u, carry):
        ka, kb = unit(u)
        row_segment = segment_of(in_block * BLOCKS + jnp.where(low_half, ka, kb))
        for half in range(2):
            allowed = row_segment == key_segment[half]
            S.madd[u, :, 128 * half : 128 * half + 128] = jnp.where(allowed, 0.0, NEGATIVE)
        return carry

    lax.fori_loop(0, BLOCKS, mask, 0)
    hid_send(4, A.hidden.at[high], ki, high, 1, 0)
    hid_send(1, A.hidden.at[low], ki, low, 3, 0)

    for cp in loads[:1] + loads[1:3] + loads[5:6]:
        cp.wait()
    hid_arrival(0, key_of(0, 1), whole)
    pair = pl.ds(z * 2, 2)
    hid_pair = S.hid[pair].reshape(256, D)
    key_rows = dot(hid_pair, S.wk[c]).astype(BF).astype(F32)
    bias_v = S.vv[...].reshape(1, D)
    bias_q = S.vq
    bv = jnp.where(c == 0, bias_v[:, :HALF], bias_v[:, HALF:])
    value_rows = (dot(hid_pair, S.wv[c]) + bv).astype(BF).astype(F32)
    lane2 = iota((256, 128), 1)
    for h in range(HEADS):
        g, e = h // 2, h % 2
        mine = lane2 // 64 == e
        S.km[h] = jnp.where(mine, key_rows[:, 128 * g : 128 * g + 128], 0.0).astype(BF)
        S.ve[h, :, :128] = jnp.where(mine, value_rows[:, 128 * g : 128 * g + 128], 0.0).astype(BF)
        S.ve[h, :, 128:] = jnp.where((lane2 == h) | (lane2 == 8 + h), 1.0, 0.0).astype(BF)
    loads[3].wait()
    loads[4].wait()
    bias_q = S.vq[...].reshape(1, D)
    S.brow[...] = jnp.zeros((2, 16, HALF), F32)
    S.ykv[...] = jnp.zeros((256, BLOCKS * TOK), BF)
    S.zf[...] = jnp.zeros((32, HALF), F32)
    S.zf2[...] = jnp.zeros((16, HALF), F32)
    S.i1g[...] = jnp.zeros((16, HALF), F32)
    for cp in later + last:
        cp.start()

    def out_send(k, rows, to):
        return remote(S.obuf.at[k, rows], S.orecv.at[ki, rows], M.os.at[0], M.or_.at[0], to)

    def st_send(k, to):
        return remote(S.st.at[k], S.strecv.at[ki], M.ss.at[0], M.sr.at[0], to)

    def forward(i, carry):
        ka, kb = unit(i)
        above, below = key_of(1, 0), key_of(3, 0)

        @pl.when(i == 0)
        def _():
            prev_local(0).wait()
            prev_remote(0).wait_recv()

        @pl.when(i == 2)
        def _():
            hid_arrival(3, below, low)
            hid_send(7, S.hid.at[below, low], below, low, 1, 0)
            hid_send(5, S.hid.at[below, low], below, low, 0, 1)
            hid_arrival(2, above, high)
            hid_send(7, S.hid.at[above, high], above, high, 3, 0)
            hid_send(5, S.hid.at[above, high], above, high, 0, 1)
            for dz in (1, 3):
                prev_local(dz).wait()
                prev_remote(dz).wait_recv()

        @pl.when(i == 4)
        def _():
            hid_arrival(1, above, low)
            hid_send(6, S.hid.at[above, low], above, low, 0, 1)
            hid_arrival(4, below, high)
            hid_send(6, S.hid.at[below, high], below, high, 0, 1)

        @pl.when(i == 6)
        def _():
            hid_arrival(7, ka, whole)
            hid_send(8, S.hid.at[ka], ka, whole, 0, 1)
            prev_local(2).wait()
            prev_remote(2).wait_recv()

        @pl.when(jnp.logical_or(i == 3, i == 5))
        def _():
            hid_arrival((i + 7) // 2, ka, whole)

        @pl.when(i == 7)
        def _():
            hid_arrival(8, ka, whole)

        bq = jnp.where(c == 0, bias_q[:, :HALF], bias_q[:, HALF:])
        hidden = jnp.concatenate([S.hid[ka, low], S.hid[kb, high]], axis=0)
        queries = (dot(hidden, S.wq[c]) + bq).astype(BF).astype(F32) * 0.125
        S.qs[...] = queries.astype(BF)
        S.qt[i] = queries.T.astype(BF)
        rows_a, rows_b = unit_rows_of(i)
        totals = jnp.zeros((TOK, 128), F32)
        tops = jnp.zeros((TOK, 128), F32)
        for g in range(3):
            two = S.qs[:, 128 * g : 128 * g + 128]
            mixed = jnp.zeros((TOK, 128), F32)
            for h in (2 * g, 2 * g + 1):
                s = dot_nt(two, S.km[h])
                parts = []
                for e, r in enumerate((rows_a, rows_b)):
                    at = slice(64 * e, 64 * e + 64)
                    before = [S.pv[half, h, r, :].astype(F32) for half in range(2)]
                    parts.append(s[at, :] + jnp.concatenate(before, axis=1) + S.madd[i, at, :])
                s = jnp.concatenate(parts, axis=0)
                top = jnp.max(s, axis=1, keepdims=True)
                p = jnp.exp(s - top).astype(BF)
                S.pw[i, h] = p
                o = dot(p, S.ve[h])
                mixed = mixed + o[:, :128]
                totals = totals + o[:, 128:]
                tops = jnp.where(lane == 8 + h, top, tops)
            mixed = mixed.astype(BF)
            S.obuf[ka, low, 128 * g : 128 * g + 128] = mixed[:64, :]
            S.obuf[kb, high, 128 * g : 128 * g + 128] = mixed[64:, :]
        stats = jnp.where(lane < 8, totals, tops).T[:16, :]
        S.stu[i] = stats

        def owner(k):
            return (bi, k)

        @pl.when(i > 0)
        def _():
            out_send(ka, low, owner(ka)).start()
            out_send(kb, high, owner(kb)).start()

        @pl.when(jnp.logical_or(i == 1, i >= 6))
        def _():
            S.st[ka] = stats
            st_send(ka, owner(ka)).start()

        @pl.when(jnp.logical_or(i == 4, i == 5))
        def _():
            first = S.stu[i - 2]
            S.st[ka] = jnp.where(lane[:16] < 64, stats, first)
            S.st[kb] = jnp.where(lane[:16] < 64, first, stats)
            st_send(ka, owner(ka)).start()
            st_send(kb, owner(kb)).start()

        return carry

    lax.fori_loop(0, BLOCKS, forward, 0)

    S.orecv[ki] = S.obuf[ki]
    S.strecv[ki] = S.stu[0]

    seven = pl.ds(0, 7)
    for cp in later[:9]:
        cp.wait()
    local(S.wi, S.wi, M.ld.at[15]).wait()
    local(S.wu, S.wu, M.ld.at[16]).wait()
    S.wot[...] = S.wo[...].T
    for j in range(4):
        S.wit[j] = S.wi[j].T
        S.wut[j] = S.wu[j].T
    arrived(M.or_.at[0], S.orecv.at[seven])
    arrived(M.sr.at[0], S.strecv.at[seven])
    row8 = iota((8, 128), 0)
    spread = head_rows()
    lse = []
    for half in range(2):
        tops = [S.strecv[2 * zz + half, 8:16, :] for zz in range(4)]
        sums = [S.strecv[2 * zz + half, 0:8, :] for zz in range(4)]
        top = jnp.maximum(jnp.maximum(tops[0], tops[1]), jnp.maximum(tops[2], tops[3]))
        shares = [jnp.exp(t - top) for t in tops]
        total = shares[0] * sums[0] + shares[1] * sums[1] + shares[2] * sums[2] + shares[3] * sums[3]
        total = jnp.where(row8 < HEADS, total, 1.0)
        lse.append(jnp.where(row8 < HEADS, top + jnp.log(total), 0.0))
        acc = jnp.zeros((TOK, HALF), F32)
        for zz in range(4):
            factor = dot_tn(split_hi_lo(jnp.where(row8 < HEADS, shares[zz] / total, 0.0)), spread)
            acc = acc + S.orecv[2 * zz + half].astype(F32) * factor
        S.at[half] = acc
        S.atx[0, :, HALF * half : HALF * half + HALF] = acc.astype(BF)

    other = dev(dc=1)

    def swap(i, src, dst):
        copy = remote(src, dst, M.xs.at[i], M.xr.at[i], other)
        copy.start()
        return copy

    swap_at = swap(0, S.atx.at[0], S.atx.at[1])

    def vec(ref):
        return ref[...].reshape(1, -1)

    attn_low = S.atx[0]
    first_sum = S.hid[ki].astype(F32) + dot(attn_low, S.wo[...]) + vec(S.vo)
    normed, inverse_a = norm(first_sum)
    S.n1[...] = normed
    first_low = (normed * vec(S.ga) + vec(S.ba)).astype(BF)
    S.fx[...] = first_low
    in_y, in_x = y * 2 + c, x * 2 + c
    S.xi[in_y] = first_low

    def xi_send(i, src, k, **to):
        remote(src, S.xi.at[k], M.xis.at[0], M.xir.at[i], dev(**to)).start()

    for d in (1, 3, 2):
        xi_send(0, S.fx, in_y, dy=d)
    xi_send(1, S.fx, in_y, dc=1)
    second = normed * vec(S.ga) + vec(S.ba) + vec(S.vu)
    bias_i = vec(S.vi)
    for j in range(4):
        inner = dot(S.fx[...], S.wi[j]) + bias_i[:, D * j : D * j + D]
        cdf = 0.5 + 0.5 * lax.erf(inner * 0.7071067811865476)
        density = jnp.exp(inner * inner * -0.5) * 0.3989422804014327
        S.gp[j] = (cdf + inner * density).astype(BF)
        S.ax[j] = (inner * cdf).astype(BF)

        own = 1 - (lax.rem(x + 4 - j, 4) + 3) // 4
        to = (j * 4 + y, z * 2 + lax.rem(c + own, 2))
        remote(S.ax.at[j], S.xo.at[in_x], M.xos.at[0], M.xor_.at[own], to).start()
        second = second + dot(S.ax[j], S.wu[j])
    S.xo[in_x] = S.ax[x]
    normed_f, inverse_f = norm(second)
    O.out_hidden[...] = (normed_f * vec(S.gf) + vec(S.bf)).astype(BF)
    upstream = S.go[...].astype(F32)

    def put_row(r, values):
        sums = row_sums(values)
        S.brow[0, r : r + 1, :] = sums[:, :HALF]
        S.brow[1, r : r + 1, :] = sums[:, HALF:]

    put_row(6, upstream * normed_f)
    put_row(7, upstream)
    grad_second = norm_back(upstream, normed_f, inverse_f, vec(S.gf))
    og = grad_second.astype(BF)
    put_row(3, og.astype(F32))
    S.ogs[0] = og[:, :HALF]
    S.ogs[1] = og[:, HALF:]
    ring_places = [(d, dc) for d in (1, 3, 2) for dc in range(2)]

    for d, dc in ring_places + [(0, 1)]:
        src = S.ogs.at[lax.rem(c + dc, 2)]
        remote(src, S.yo.at[in_x], M.yos.at[0], M.yor.at[0], dev(dx=d, dc=dc)).start()
    S.yo[in_x] = S.ogs[c]
    S.gs[...] = grad_second
    bsum = []
    for j in range(4):
        ig = (dot(og, S.wut[j]) * S.gp[j].astype(F32)).astype(BF)
        S.igs[j // 2, 2 * (j % 2)] = ig[:, :HALF]
        S.igs[j // 2, 2 * (j % 2) + 1] = ig[:, HALF:]
        bsum.append(row_sums(ig.astype(F32)))
        S.gs[...] = S.gs[...] + dot(ig, S.wit[j])
    for d, dc in ring_places + [(0, 1)]:
        src = S.igs.at[lax.rem(c + dc, 2), lax.rem(y + d, 4)]
        remote(src, S.yi.at[in_y], M.yis.at[0], M.yir.at[0], dev(dy=d, dc=dc)).start()
    S.yi[in_y] = S.igs[c, y]

    grad_first = S.gs[...]
    normed = S.n1[...]
    put_row(4, grad_first * normed)
    put_row(5, grad_first)
    grad_first_sum = norm_back(grad_first, normed, inverse_a, vec(S.ga))
    S.gs[...] = grad_first_sum
    br = grad_first_sum.astype(BF)
    put_row(2, br.astype(F32))
    S.brs[0] = br[:, :HALF]
    S.brs[1] = br[:, HALF:]
    swap_br = swap(1, S.brs.at[oc], S.brr)
    ag = dot(br, S.wot[...]).astype(BF)
    for half in range(2):
        S.ags[half] = ag[:, HALF * half : HALF * half + HALF]

    def ag_send(i, src, k, rows, dz, dc):
        remote(src, S.dorecv.at[k, rows], M.ds.at[0], M.dr.at[i], dev(dz=dz, dc=dc)).start()

    def ag_arrival(i, dz, rows):
        arrived(M.dr.at[i], S.dorecv.at[pl.ds(lax.rem(z + dz, 4) * 2, 2), rows])

    def s2_send(i, dz, dc):
        half = lax.rem(c + dc, 2)
        remote(S.s2.at[half], S.s2recv.at[ki], M.es.at[0], M.er.at[i], dev(dz=dz, dc=dc)).start()

    def s2_arrival(i, dz):
        arrived(M.er.at[i], S.s2recv.at[pl.ds(lax.rem(z + dz, 4) * 2, 2)])

    for i, dz, rows in ((3, 1, low), (2, 3, high)):
        for dc in range(2):
            ag_send(i, S.ags.at[lax.rem(c + dc, 2), rows], ki, rows, dz, dc)
    ag_send(0, S.ags.at[oc], ki, whole, 0, 1)

    for half in range(2):
        product = S.at[half] * ag[:, HALF * half : HALF * half + HALF].astype(F32)
        dots = jnp.zeros((16, TOK), F32)
        hi = product.astype(BF)
        lo = (product - hi.astype(F32)).astype(BF)
        dots = dot_nt(spread, hi) + dot_nt(spread, lo)
        S.s2[half, 0:8, :] = dots[0:8, :]
        S.s2[half, 8:16, :] = lse[half]
    s2_send(0, 0, 1)
    for i, dz in ((2, 1), (1, 3), (3, 2)):
        for dc in range(2):
            s2_send(i, dz, dc)
    S.dorecv[ki] = S.ags[c]
    S.s2recv[ki] = S.s2[c]

    def weight_grad(left, right):
        return dot_tn(left, right).astype(BF)

    def along(axis, d):
        return dev(dx=d) if axis == 0 else dev(dy=d)

    def at_place(axis, d):
        return lax.rem((x if axis == 0 else y) + d, 4)

    def scatter(n, axis, src, dst, inner):
        for d in (1, 2, 3):
            there = at_place(axis, d)
            piece = src.at[:, there] if inner else src.at[there]
            remote(piece, dst.at[d - 1], M.ts.at[n], M.tr.at[n], along(axis, d)).start()

    class Ring:
        def __init__(self, n, axis, piece, held, landed):
            right, left = along(axis, 1), along(axis, 3)
            after, before, across = at_place(axis, 1), at_place(axis, 3), at_place(axis, 2)

            def copy(sem, src, dst, to):
                return remote(src, dst, M.rs.at[n], sem, to)

            here = M.rr.at[n]
            self.n = n

            self.first = [
                copy(M.rh.at[2 * n], piece(across, 0), held.at[0], right),
                copy(M.rh.at[2 * n + 1], piece(across, 1), held.at[1], left),
            ]
            self.own = [
                copy(here, piece(after, 1), landed(0, 1), right),
                copy(here, piece(before, 0), landed(1, 0), left),
            ]
            self.summed = [
                copy(here, held.at[0], landed(0, 0), right),
                copy(here, held.at[1], landed(1, 1), left),
            ]
            self.add = [(held.at[0], piece(after, 0)), (held.at[1], piece(before, 1))]

        def start(self, copies):
            for cp in copies:
                cp.start()

        def pass_on(self):
            for w in range(2):
                self.first[w].wait_recv()
                mine, extra = self.add[w]
                mine[...] = (mine[...].astype(F32) + extra[...].astype(F32)).astype(BF)
                self.summed[w].start()

        def landed(self, both):
            arrived(M.rr.at[self.n], both)

        def drain(self, three):
            sent(M.rs.at[self.n], three)

    def quarter_ring(n, axis, send, held, recv):
        return Ring(
            n,
            axis,
            lambda p, h: send.at[p, pl.ds(96 * h, 96)],
            held,
            lambda w, h: recv.at[w, pl.ds(96 * h, 96)],
        )

    ring_q = quarter_ring(0, 0, S.a2s, S.a2p, S.a2r)
    ring_i = quarter_ring(1, 0, S.i1s, S.i1p, S.i1r)
    ring_u = quarter_ring(2, 1, S.b1s, S.b1p, S.b1r)
    ring_o = Ring(
        3,
        1,
        lambda p, h: S.c1s.at[pl.ds(2 * h, 2), p],
        S.c1p,
        lambda w, h: S.c1r.at[w, pl.ds(2 * h, 2)],
    )
    for cp in [swap_at, swap_br]:
        cp.wait()
    right = jnp.concatenate([S.brs[c], S.brr[...]], axis=0)
    S.c1s[...] = weight_grad(S.atx[...].reshape(256, D), right).reshape(4, 4, 48, HALF)

    for i, dz, rows in ((4, 1, high), (1, 3, low)):
        for dc in range(2):
            ag_send(i, S.ags.at[lax.rem(c + dc, 2), rows], ki, rows, dz, dc)

    lane512 = iota((8, 512), 1)
    sub512 = iota((8, 512), 0)
    pick = jnp.where(
        iota((512, 128), 1) == (iota((512, 128), 0) // 128) * 32 + lax.rem(iota((512, 128), 0), 128) // 4,
        1.0,
        0.0,
    ).astype(BF)
    flat = jnp.concatenate(bsum, axis=1)
    for g in range(6):
        spread_out = jnp.where(lax.rem(lane512, 4) == sub512, flat[:, 512 * g : 512 * g + 512], 0.0)
        S.brow[g // 3, 8:16, 128 * (g % 3) : 128 * (g % 3) + 128] = dot(spread_out.astype(BF), pick)

    S.dkt[...] = jnp.zeros((HALF, 256), F32)
    S.dvt[...] = jnp.zeros((HALF, 256), F32)
    units = unit_rows()

    sent(M.os.at[0], S.obuf.at[seven])

    def dq_landing(w, half, h):
        return S.dqr.at[w, half, rows_half(h)], M.qr.at[2]

    def dq_copy(src, place, to):
        return remote(src, place[0], M.qs_.at[0], place[1], to)

    def dq_piece(dz, h):
        return S.obuf.at[pl.ds(lax.rem(z + dz, 4) * 2, 2), rows_half(h)]

    dq_partner = dq_copy(S.obuf.at[z * 2 + oc], (S.dqo.at[c], M.qr.at[3]), other)
    dq_first = [
        dq_copy(dq_piece(2, 0), (S.dqh.at[0], M.qr.at[0]), dev(dz=1)),
        dq_copy(dq_piece(2, 1), (S.dqh.at[1], M.qr.at[1]), dev(dz=3)),
    ]
    dq_own, dq_summed = [], []
    for w, dz in ((0, 1), (1, 3)):
        h = 1 - w
        dq_own.append(
            [
                dq_copy(
                    S.obuf.at[lax.rem(z + dz, 4) * 2 + cc, rows_half(h)],
                    dq_landing(w, c, h),
                    (bi, lax.rem(z + dz, 4) * 2 + cc),
                )
                for cc in range(2)
            ]
        )
        h = w
        dq_summed.append(
            [
                dq_copy(
                    S.dqh.at[w, cc],
                    dq_landing(w, c, h),
                    (bi, lax.rem(z + dz, 4) * 2 + cc),
                )
                for cc in range(2)
            ]
        )

    def gl_rows(zz):
        return pl.ds(pl.multiple_of(zz * 256, 256), 256)

    def gl_local(k):
        rows = gl_rows(k)
        return local(
            S.pv.at[c, :, rows, :], O.gl.at[pl.ds(c * HEADS, HEADS), rows, :], M.gl_.at[0]
        )

    def gl_remote(k):
        rows = gl_rows(k)
        return remote(
            S.pv.at[oc, :, rows, :],
            O.gl.at[pl.ds(c * HEADS, HEADS), rows, :],
            M.gs_.at[0],
            M.gr.at[0],
            dev(dc=1),
        )

    def backward(i, carry):
        @pl.when(i == 2)
        def _():
            arrived(M.xir.at[0], S.xi.at[pl.ds(0, 3)])
            for d in (1, 3, 2):
                k = lax.rem(y + d, 4) * 2 + c
                xi_send(1, S.xi.at[k], k, dc=1)

        @pl.when(i == 3)
        def _():
            ring_o.start(ring_o.first)
            arrived(M.xor_.at[0], S.xo.at[pl.ds(0, 3)])
            for d in (1, 3, 2):
                k = lax.rem(x + d, 4) * 2 + c
                remote(S.xo.at[k], S.xo.at[k], M.xos.at[0], M.xor_.at[1], other).start()

        @pl.when(i == 0)
        def _():
            arrived(M.dr.at[0], S.dorecv.at[key_of(0, 1)])
            arrived(M.er.at[0], S.s2recv.at[key_of(0, 1)])

        @pl.when(i == 1)
        def _():
            ag_arrival(3, 3, low)
            for dc in range(2):
                k = key_of(3, dc)
                ag_send(5, S.dorecv.at[k, low], k, low, 1, 0)
            ag_arrival(2, 1, high)
            for dc in range(2):
                k = key_of(1, dc)
                ag_send(5, S.dorecv.at[k, high], k, high, 3, 0)
            s2_arrival(1, 1)
            s2_arrival(2, 3)

        @pl.when(i == 2)
        def _():
            ag_arrival(1, 1, low)
            ag_arrival(4, 3, high)

        @pl.when(i == 3)
        def _():
            ag_arrival(5, 2, whole)
            s2_arrival(3, 2)

        places, factors, minuses, pieces = [], [], [], []
        for half in range(2):
            u = 2 * i + half
            ka, kb = unit(u)
            places.append((ka, low))
            places.append((kb, high))
            here = jnp.where(lane[:16] < 64, S.s2recv[ka], S.s2recv[kb])
            share = jnp.exp(S.stu[u, 8:16, :] - here[8:16, :])
            share = jnp.where(row8 < HEADS, share, 0.0)
            minuses.append(dot_tn(split_hi_lo(here[0:8, :] * share * -1.0), units).astype(BF))
            factors.append(dot_tn(split_hi_lo(share), spread))
            pieces += [S.dorecv[ka, low], S.dorecv[kb, high]]
        rows = unit_rows_of(2 * i) + unit_rows_of(2 * i + 1)
        minus = jnp.concatenate(minuses, axis=0)
        scaled = jnp.concatenate(pieces, axis=0).astype(F32) * jnp.concatenate(factors, axis=0)
        scaled_t = scaled.T.astype(BF)
        scaled = scaled.astype(BF)
        queries_t = jnp.concatenate([S.qt[2 * i], S.qt[2 * i + 1]], axis=1)
        for g in range(3):
            left = jnp.concatenate([scaled[:, 128 * g : 128 * g + 128], minus], axis=1)
            partial = jnp.zeros((256, 128), F32)
            for h in (2 * g, 2 * g + 1):
                p = S.pw[pl.ds(2 * i, 2), h].reshape(256, 256)
                grad = (p.astype(F32) * dot_nt(left, S.ve[h])).astype(BF)
                for half in range(2):
                    for e, r in enumerate(rows):
                        at = slice(64 * e, 64 * e + 64)
                        S.pv[half, h, r, :] = grad[at, 128 * half : 128 * half + 128]
                at = slice(64 * h, 64 * h + 64)
                S.dvt[at, :] = S.dvt[at, :] + dot(scaled_t[at, :], p)
                S.dkt[at, :] = S.dkt[at, :] + dot(queries_t[at, :], grad)
                partial = partial + dot(grad, S.km[h])
            partial = (partial * 0.125).astype(BF)
            for e, (k, half_rows) in enumerate(places):
                S.obuf[k, half_rows, 128 * g : 128 * g + 128] = partial[64 * e : 64 * e + 64, :]

        @pl.when(i == 0)
        def _():
            dq_partner.start()

        @pl.when(i == 1)
        def _():
            for cp in dq_own[0] + dq_own[1]:
                cp.start()

        def logits_out(zz):
            gl_local(zz).start()
            gl_remote(zz).start()

        @pl.when(i == 0)
        def _():
            logits_out(z)

        @pl.when(i == 2)
        def _():
            logits_out(lax.rem(z + 1, 4))
            logits_out(lax.rem(z + 3, 4))

        @pl.when(i == 3)
        def _():
            logits_out(lax.rem(z + 2, 4))

        return carry

    lax.fori_loop(0, 4, backward, 0)
    S.dqo[c] = S.obuf[ki]

    S.kvt[0] = S.dkt[...].astype(BF)
    S.kvt[1] = S.dvt[...].astype(BF)
    mine = pl.ds(pl.multiple_of(z * 256, 256), 256)
    for d in (1, 3, 2):
        there = pl.ds(pl.multiple_of(lax.rem(z + d, 4) * 96, 32), 96)
        for t in range(2):
            place = S.ykv.at[pl.ds(128 * t, 96), mine]
            remote(S.kvt.at[t, there, :], place, M.ys.at[0], M.yr.at[0], dev(dz=d)).start()
    here = pl.ds(pl.multiple_of(z * 96, 32), 96)
    for t in range(2):
        S.ykv[128 * t : 128 * t + 96, mine] = S.kvt[t, here, :]
    key_grad = S.dkt[...].T.astype(BF)
    value_grad = S.dvt[...].T.astype(BF)
    S.kgs[...] = key_grad.reshape(2, TOK, HALF)
    S.vgs[...] = value_grad.reshape(2, TOK, HALF)
    kv_swaps = [
        remote(S.kgs.at[oc], S.kgr, M.ks.at[0], M.kr.at[0], other),
        remote(S.vgs.at[oc], S.vgr, M.ks.at[0], M.kr.at[0], other),
    ]
    for cp in kv_swaps:
        cp.start()
    S.brow[c, 1:2, :] = row_sums(value_grad.astype(F32))
    hid_all = S.hid[...].reshape(BLOCKS * TOK, D)
    query_parts = S.obuf[...].reshape(BLOCKS * TOK, HALF)
    S.a2s[...] = weight_grad(hid_all, query_parts).reshape(4, 192, HALF)
    ring_q.start(ring_q.first)
    ring_o.start(ring_o.own)
    S.brow[c, 0:1, :] = row_sums(query_parts.astype(F32))

    for cp in last:
        cp.wait()
    arrived(M.kr.at[0], S.kgs)
    total = S.gs[...]
    total = total + dot_nt(S.kgs[c], S.wk[c]) + dot_nt(S.kgr[...], S.wk[oc])
    total = total + dot_nt(S.vgs[c], S.wv[c]) + dot_nt(S.vgr[...], S.wv[oc])
    S.gs[...] = total

    arrived(M.yir.at[0], S.yi.at[seven])
    arrived(M.xir.at[1], S.xi.at[pl.ds(0, 4)])
    grad = weight_grad(S.xi[...].reshape(BLOCKS * TOK, D), S.yi[...].reshape(BLOCKS * TOK, HALF))
    S.i1s[...] = grad.reshape(4, 192, HALF)
    ring_i.start(ring_i.first)
    ring_q.start(ring_q.own)
    arrived(M.yor.at[0], S.yo.at[seven])
    arrived(M.xor_.at[1], S.xo.at[pl.ds(0, 4)])
    grad = weight_grad(S.xo[...].reshape(BLOCKS * TOK, D), S.yo[...].reshape(BLOCKS * TOK, HALF))
    S.b1s[...] = grad.reshape(4, 192, HALF)
    ring_u.start(ring_u.first)
    ring_i.start(ring_i.own)
    for cp in dq_first:
        cp.start()

    def sum_a(src, recv, dst):
        def step(j, carry):
            part = pl.ds(pl.multiple_of(j * 48, 16), 48)
            total = src[x, part, :].astype(F32)
            for d in range(recv.shape[0]):
                total = total + recv[d, part, :].astype(F32)
            dst[j] = total.astype(BF)
            return carry

        lax.fori_loop(0, 4, step, 0)

    def sum_b(src, recv, dst):
        def step(j, carry):
            total = src[j, y].astype(F32)
            for d in range(recv.shape[0]):
                total = total + recv[d, j].astype(F32)
            dst[j] = total.astype(BF)
            return carry

        lax.fori_loop(0, 4, step, 0)

    def finish(own, recv, dst):
        total = own.astype(F32)
        for d in range(recv.shape[0]):
            total = total + recv[d].astype(F32)
        dst[...] = total

    ring_u.start(ring_u.own)
    ring_o.pass_on()
    ring_q.pass_on()
    arrived(M.yr.at[0], S.kvt.at[:, pl.ds(0, 288)])
    beside = jnp.where(iota((16, 128), 1) == iota((16, 128), 0) + 96, 1.0, 0.0).astype(BF)
    columns = [dot_tn(S.brow[half].astype(BF), beside) for half in range(2)]
    flipped = dot(S.ykv[...], hid_all)
    grad = (flipped[:128, :].T + jnp.concatenate(columns, axis=0)).astype(BF)
    S.b2ks[...] = grad.reshape(4, 192, 128)
    scatter(0, 0, S.b2ks, S.b2kr, False)
    S.b2vs[...] = flipped[128:, :].T.astype(BF).reshape(4, 4, 48, 128)
    scatter(4, 1, S.b2vs, S.b2vr, True)

    ring_i.pass_on()
    ring_u.pass_on()
    for w in range(2):
        dq_first[w].wait_recv()
        add = dq_piece((1, 3)[w], w)[...].astype(F32)
        S.dqh[w] = (S.dqh[w].astype(F32) + add).astype(BF)
        for cp in dq_summed[w]:
            cp.start()
    ring_q.landed(S.a2r)
    sum_a(S.a2s, S.a2r, S.a2t)
    scatter(2, 1, S.a2t, S.a2u, False)

    ring_o.landed(S.c1r)
    sum_b(S.c1s, S.c1r, S.c1t)
    scatter(3, 0, S.c1t, S.c1u, False)

    arrived(M.tr.at[0], S.b2kr)
    sum_a(S.b2ks, S.b2kr, S.b2kt)
    scatter(1, 1, S.b2kt, S.b2ku, False)
    arrived(M.tr.at[4], S.b2vr)
    sum_b(S.b2vs, S.b2vr, S.b2vt)
    scatter(5, 0, S.b2vt, S.b2vu, False)

    ring_i.landed(S.i1r)
    finish(S.i1s[x], S.i1r, S.fi1)
    for p in range(4):
        for k in range(BLOCKS):
            at = 48 * (k // 2) + 12 * p + 6 * (k % 2)
            S.i1f[6 * k : 6 * k + 6, :] = S.fi1[at : at + 6, :]
        S.i1z[p] = S.i1f[...].astype(BF)
    for d in (1, 3, 2):
        there = lax.rem(z + d, 4)
        remote(S.i1z.at[there], S.i1u.at[d - 1], M.is_.at[0], M.ir.at[0], dev(dz=d)).start()

    dq_partner.wait_recv()
    arrived(M.qr.at[2], S.dqr)
    query_grads = []
    for half in range(2):
        grad = S.dqr[0, half].astype(F32) + S.dqr[1, half].astype(F32) + S.dqo[half].astype(F32)
        query_grads.append(grad.astype(BF))

    total = S.gs[...]
    for half in range(2):
        total = total + dot_nt(query_grads[half], S.wq[half])
    O.grad_hidden[...] = total.astype(BF)

    def zb_send(k, to):
        return remote(S.zsb.at[k], O.zrb.at[ki], M.zs_.at[0], M.zr_.at[0], to)

    def w_send(k, to):
        return remote(S.zs2.at[k], O.wr.at[ki], M.ws.at[0], M.wr.at[0], to)

    def to_all(send):
        def step(i, carry):
            dz, dc = far(i // 2), lax.rem(i, 2)
            send(key_of(dz, dc), dev(dz=dz, dc=dc)).start()
            return carry

        lax.fori_loop(1, BLOCKS, step, 0)

    own = [
        local(S.i1t.at[in_y], O.zra.at[in_y], M.own.at[2]),
        local(S.zsb.at[ki], O.zrb.at[ki], M.own.at[0]),
        local(S.zs2.at[ki], O.wr.at[ki], M.own.at[1]),
    ]
    arrived(M.tr.at[1], S.b2ku)
    finish(S.b2kt[y], S.b2ku, S.fb2k)
    arrived(M.tr.at[5], S.b2vu)
    finish(S.b2vt[x], S.b2vu, S.fb2v)
    arrived(M.tr.at[2], S.a2u)
    finish(S.a2t[y], S.a2u, S.fa2)
    for p in range(BLOCKS):
        six = slice(6 * p, 6 * p + 6)
        S.zf2[0:6, :128] = S.fb2k[six, :]
        S.zf2[0:6, 128:256] = S.fb2v[six, :]
        S.zf2[6:12, :] = S.fa2[six, :]
        S.zs2[p] = S.zf2[...].astype(BF)
    to_all(w_send)
    own[2].start()

    ring_u.landed(S.b1r)
    finish(S.b1s[y], S.b1r, S.fb1)
    arrived(M.tr.at[3], S.c1u)
    finish(S.c1t[x], S.c1u, S.fc1)
    for p in range(BLOCKS):
        S.zf[0:24, :] = S.fb1[24 * p : 24 * p + 24, :]
        S.zf[24:30, :] = S.fc1[6 * p : 6 * p + 6, :]
        S.zsb[p] = S.zf[...].astype(BF)

    to_all(zb_send)
    own[1].start()

    arrived(M.ir.at[0], S.i1u)
    total = S.i1z[z].astype(F32)
    for d in range(3):
        total = total + S.i1u[d].astype(F32)
    S.i1f[...] = total
    for k in range(BLOCKS):
        S.i1g[0:6, :] = S.i1f[6 * k : 6 * k + 6, :]
        S.i1t[k] = S.i1g[...].astype(BF)
    for d, dc in ring_places + [(0, 1)]:
        src = S.i1t.at[lax.rem(y + d, 4) * 2 + lax.rem(c + dc, 2)]
        remote(src, O.zra.at[in_y], M.vs.at[0], M.vr.at[0], dev(dy=d, dc=dc)).start()
    own[0].start()

    sent(M.ss.at[0], S.st.at[seven])
    sent(M.es.at[0], S.s2recv.at[seven])
    sent(M.ys.at[0], S.kvt.at[:, pl.ds(0, 288)])
    sent(M.ks.at[0], S.kgs)
    sent(M.ds.at[0], S.dorecv.at[seven])
    sent(M.qs_.at[0], S.obuf.at[seven])
    for ssem, rsem, like in (
        (M.zs_, M.zr_, S.zsb),
        (M.vs, M.vr, S.i1t),
        (M.ws, M.wr, S.zs2),
    ):
        sent(ssem.at[0], like.at[seven])
        arrived(rsem.at[0], like.at[seven])
    local(S.pv.at[c], S.pv.at[c], M.gl_.at[0]).wait()
    sent(M.gs_.at[0], S.pv.at[oc])
    arrived(M.gr.at[0], S.pv.at[oc])
    sent(M.hs.at[0], S.hid.at[pl.ds(0, 7)])
    sent(M.ps.at[0], S.pv.at[0])
    for n, like in enumerate((S.b2kr, S.b2ku, S.a2u, S.c1u, S.b2vr, S.b2vu)):
        sent(M.ts.at[n], like)
    for cp in own:
        cp.wait()
    for ring, like in ((ring_q, S.a2s), (ring_i, S.i1s), (ring_u, S.b1s)):
        ring.drain(like.at[pl.ds(0, 3)])
    ring_o.drain(S.c1s.at[:, pl.ds(0, 3)])
    sent(M.is_.at[0], S.i1u)
    for sem, like in ((M.xis, S.xi), (M.xos, S.xo), (M.yis, S.yi), (M.yos, S.yo)):
        sent(sem.at[0], like.at[seven])


def main_kernel(args):
    any_space = pl.BlockSpec(memory_space=pl.ANY)
    vmem = pl.BlockSpec(memory_space=pltpu.VMEM)
    return pl.pallas_call(
        body,
        out_shape=[
            pltpu.VMEM((TOK, D), BF),
            pltpu.VMEM((TOK, D), BF),
            pltpu.VMEM((2 * HEADS, BLOCKS * TOK, 128), BF),
            pltpu.VMEM((BLOCKS, 32, HALF), BF),
            pltpu.VMEM((BLOCKS, 16, HALF), BF),
            pltpu.VMEM((BLOCKS, 16, HALF), BF),
        ],
        in_specs=[any_space] * len(args),
        out_specs=[vmem, vmem] + [any_space] * 4,
        scratch_shapes=[pltpu.VMEM(s, t) for s, t in SCRATCH.values()]
        + [pltpu.SemaphoreType.DMA((n,)) for n in SEMS.values()]
        + [pltpu.SMEM((1, SEQS), jnp.int32)],
        compiler_params=pltpu.CompilerParams(
            collective_id=0, has_side_effects=True, vmem_limit_bytes=59 * 2**20
        ),
        name="layer",
    )(*args)


def lay_out(oh, gh, gl, zrb, zra, wr, *refs):
    outs, hold, sem = refs[:18], (None,) * 3 + refs[18:33], refs[33]
    copies = [
        pltpu.make_async_copy(src, dst, sem.at[i])
        for i, (src, dst) in enumerate(
            [(gl.at[pl.ds(3 * j, 3)], outs[2].at[pl.ds(3 * j, 3)]) for j in range(4)]
            + [(oh, outs[0]), (gh, outs[1])]
        )
    ]
    for copy in copies:
        copy.start()

    def summed(ref):
        out = []
        for half in range(2):
            total = ref[half].astype(F32)
            for zz in range(1, 4):
                total = total + ref[2 * zz + half].astype(F32)
            out.append(total)
        return out


    def leave(i):
        copies.append(pltpu.make_async_copy(hold[i], outs[i], sem.at[i + 3]))
        copies[-1].start()

    outer = summed(zrb)
    tail = jnp.zeros((8, 128), F32)
    for k in range(BLOCKS):
        rows = wr[k].astype(F32)
        tail = tail + rows[0:8, :128]
        at = (k % 2) * HALF + (k // 2) * 96
        for t in range(2):
            hold[4 + t][:, at : at + 96] = rows[0:6, 128 * t : 128 * t + 96]
    query = summed(wr)
    hold[3][...] = jnp.concatenate([query[0][6:12, :], query[1][6:12, :]], axis=1)
    for i in (3, 4, 5):
        leave(i)
    hold[6][...] = jnp.concatenate([outer[0][24:30, :], outer[1][24:30, :]], axis=1)
    for k in range(BLOCKS):
        at = (k % 2) * (FF // 2) + (k // 2) * HALF
        hold[7][:, at : at + HALF] = zra[k].astype(F32)[0:6, :]
    hold[8][...] = jnp.concatenate([outer[0][0:24, :], outer[1][0:24, :]], axis=1)
    for i in (6, 7, 8):
        leave(i)
    flipped = jnp.concatenate([tail, jnp.zeros((120, 128), F32)], axis=0).T
    for slot, row in ((9, 0), (10, 1), (11, 2), (13, 3), (14, 4), (15, 5), (16, 6), (17, 7)):
        hold[slot][...] = flipped[96 + row, 0:6]
        leave(slot)
    inner = jnp.zeros((1, 128), F32)
    lane = iota((1, 128), 1)
    for i in range(6):
        for j in range(4):
            inner = jnp.where(lane == 4 * i + j, flipped[104 + j : 105 + j, i : i + 1], inner)
    hold[12][...] = inner[0, 0:24]
    leave(12)
    for copy in copies:
        copy.wait()


def out_kernel(*args):
    vmem = pl.BlockSpec(memory_space=pltpu.VMEM)
    any_space = pl.BlockSpec(memory_space=pl.ANY)
    f = lambda *s: jax.ShapeDtypeStruct(s, F32)
    shapes = [
            jax.ShapeDtypeStruct((TOK, D), BF),
            jax.ShapeDtypeStruct((TOK, D), BF),
            jax.ShapeDtypeStruct((2 * HEADS, BLOCKS * TOK, 128), BF),
            f(6, D),
            f(6, D),
            f(6, D),
            f(6, D),
            f(6, FF),
            f(24, D),
            f(6),
            f(6),
            f(6),
            f(24),
            f(6),
            f(6),
            f(6),
            f(6),
            f(6),
        ]
    return pl.pallas_call(
        lay_out,
        out_shape=shapes,
        in_specs=[any_space] * 3 + [vmem] * 3,
        out_specs=[any_space] * 18,
        scratch_shapes=[pltpu.VMEM(o.shape, F32) for o in shapes[3:]]
        + [pltpu.SemaphoreType.DMA((21,))],
        compiler_params=pltpu.CompilerParams(vmem_limit_bytes=8 * 2**20),
        name="lay_out",
    )(*args)


def on_device(*args):
    parts = main_kernel(args)
    return tuple(out_kernel(*[pltpu.with_memory_space_constraint(p, pltpu.VMEM) for p in parts]))


def solution(mesh):
    rows = P(("batch", "keys"), None)
    logits = P(None, "batch", "keys")
    flat = P(("batch", "keys"))
    return jax.shard_map(
        on_device,
        mesh=mesh,
        in_specs=(rows, logits, P("batch", None), rows) + (P(),) * 15,
        out_specs=(rows, rows, logits) + (rows,) * 6 + (flat,) * 9,
        check_vma=False,
    )
```
